32 devices in a mesh: groups: 2 (over x), vir: 16 (over z, y, core).
Axes of the slice: x: 2, y: 2, z: 4, core: 2. Of those that a mesh axis runs over, the one named last changes fastest.
Arguments:
- amps: bfloat16 [16, 8, 640, 640], P('groups', None, 'vir'), parts along dimension 0, may hold values from -6 to 6
- fock_vir: bfloat16 [1280, 640], P('groups'), parts along dimension 0, may hold values from -0.25 to 0.25
- fock_occ: bfloat16 [16, 8], P('groups'), parts along dimension 0, may hold values from -2 to 2
- ladder_ints: bfloat16 [640, 1280, 128], P('vir', 'groups'), parts along dimension 1, may hold values from -0.75 to 0.75
- cycle_ints: bfloat16 [640, 16, 128], P('vir', 'groups'), parts along dimension 1, may hold values from -0.5 to 0.5
- occ_irrep: int32 [16], P('groups'), parts along dimension 0, may hold values from 0 to 3, as said below
- vir_irrep: int32 [1280], P('groups'), parts along dimension 0, may hold values from 0 to 3
Outputs:
- residual: float32 [16, 8, 640, 640], P('groups', None, 'vir'), parts along dimension 0
The draws below stay inside these ranges and needn't reach their ends.
There are 2 independent parts, one for each index of `groups`. The reference program is written for one: setup_inputs(seed, part) draws one part's arguments, and reference() takes and returns one part's arrays. A program takes and returns all parts, laid end to end along the dimension named above; each array names one. Nothing has to cross between parts.
Inputs may be any that keep to these rules, and one draw needn't show every extreme that they name: `occ_irrep`: labels of the four irreps of the point group, each labelling exactly 2 occupied orbitals; irreps multiply as the exclusive or of labels. `vir_irrep`: labels of the four irreps of the point group.
All inputs are finite; a program needn't handle non-finite values.
Results may differ from the reference program's by a relative error of at most 0.0003.
Values may be sent and summed in bfloat16 or wider, within the bound.
No kernel may reach another device: no remote copies, remote signals or barrier semaphores. Data moves between devices by JAX's collectives and lax.ppermute only.
A program may use at most 128 MiB of HBM per device.

```python
import jax
import jax.numpy as jnp
from jax import lax

OCC = 8
VIRT = 640
DW = 8
CW = 16
VDEV = 40
KW = 128


def draw_occ_irrep(key, part):
    key = jax.random.fold_in(key, 11)
    labels = jnp.arange(OCC, dtype=jnp.int32) % 4
    return jax.random.permutation(key, labels).astype(jnp.int32)


def set_ends(values, own_key, smallest, largest):
    index_at = [jax.random.randint(jax.random.fold_in(own_key, axis), (), 0, length) for axis, length in enumerate(values.shape)]
    main_axis = values.shape.index(max(values.shape))
    beside = index_at[:main_axis] + [(index_at[main_axis] + 1) % values.shape[main_axis]] + index_at[main_axis + 1:]
    return values.at[tuple(index_at)].set(smallest).at[tuple(beside)].set(largest)


def strengthened(drawn, rng, source, target, parts, factor):
    def block_of(dim):
        return (jnp.arange(drawn.shape[dim]) // (drawn.shape[dim] // parts)).reshape((-1,) + (1,) * (drawn.ndim - 1 - dim))

    first = jax.random.permutation(rng, parts)[block_of(target)]
    second = (block_of(target) + parts // 2) % parts
    return jnp.where((block_of(source) == first) | (block_of(source) == second), factor * drawn, drawn)


def levels(rng, dims, split, low, largest):
    def one(position, parts):
        heights = jax.random.uniform(jax.random.fold_in(jax.random.fold_in(rng, 6), position), (parts,), jnp.float32, low / len(split), largest / len(split))
        return jnp.repeat(jnp.exp(heights), dims[position] // parts).reshape((-1,) + (1,) * (len(dims) - position - 1))

    gain = one(*split[0])
    for cut in split[1:]:
        gain = gain * one(*cut)
    return gain


def scatter_about(stream_key, shape, spread, bound, cuts=(), held_as=jnp.bfloat16):
    factor_of = levels(stream_key, shape, cuts, -0.22, 0.18) if cuts else 1.0
    entries = jax.random.normal(stream_key, shape, jnp.float32) * spread * factor_of
    return jnp.minimum(jnp.maximum(entries, -bound), bound).astype(held_as)


def heavy_noise(own_key, shape, spread, most, shards, heavy, held_as=jnp.bfloat16):
    values = spread * jax.random.normal(own_key, shape, jnp.float32)
    if shards:
        values = values * levels(own_key, shape, shards, -0.22, 0.18)
    return jnp.clip(strengthened(values, jax.random.fold_in(own_key, 3), *heavy), -most, most).astype(held_as)


def setup_inputs(seed: int = 0, part: int = 0) -> dict:
    arg_keys = jax.random.split(jax.random.key(seed), 8)
    part_keys = jax.random.split(jax.random.fold_in(arg_keys[7], part), 8)
    amps = scatter_about(part_keys[0], (OCC, OCC, VIRT, VIRT), 1.0, 6.0, ((2, 16),))
    fock_vir = scatter_about(part_keys[1], (VIRT, VIRT), VIRT ** -0.5, 0.25)
    fock_occ = scatter_about(part_keys[2], (OCC, OCC), OCC ** -0.5, 2.0)
    ladder_ints = heavy_noise(part_keys[3], (VIRT, VIRT, KW), KW ** -0.5, 0.75, ((0, 16),), (2, 0, 16, 2.0))
    cycle_ints = scatter_about(part_keys[4], (VIRT, OCC, OCC * CW), (OCC * CW) ** -0.5, 0.5, ((0, 16),))
    occ_irrep = draw_occ_irrep(jax.random.fold_in(jax.random.fold_in(arg_keys[7], part), 71), part)
    vir_irrep = set_ends(jax.random.randint(part_keys[6], (VIRT,), 0, 4), jax.random.fold_in(part_keys[6], 1), 0, 3).astype(jnp.int32)
    return dict(amps=amps, fock_vir=fock_vir, fock_occ=fock_occ, ladder_ints=ladder_ints, cycle_ints=cycle_ints, occ_irrep=occ_irrep, vir_irrep=vir_irrep)


def symmetry_allowed(occ_irrep, vir_irrep):
    occ_pair = jnp.bitwise_xor(occ_irrep[:, None], occ_irrep[None, :])
    vir_pair = jnp.bitwise_xor(vir_irrep[:, None], vir_irrep[None, :])
    product_irrep = jnp.bitwise_xor(occ_pair[:, :, None, None], vir_pair[None, None, :, :])
    return jnp.where(product_irrep == 0, jnp.float32(1.0), jnp.float32(0.0))


def reference(amps, fock_vir, fock_occ, ladder_ints, cycle_ints, occ_irrep, vir_irrep):
    pair_count = OCC * OCC
    fock_term = jnp.dot(amps.reshape(pair_count * VIRT, VIRT), fock_vir,
                        preferred_element_type=jnp.float32).reshape(OCC, OCC, VIRT, VIRT)
    occ_term = jnp.einsum("ikab,kj->ijab", amps.astype(jnp.float32), fock_occ.astype(jnp.float32),
                          precision=lax.Precision.HIGHEST)
    window = amps[:, :, ::VDEV, :DW].reshape(pair_count, KW)
    ladder = lax.dot_general(window, ladder_ints.reshape(VIRT * VIRT, KW),
                             (((1,), (1,)), ((), ())),
                             preferred_element_type=jnp.float32).reshape(OCC, OCC, VIRT, VIRT)
    left_side = jnp.transpose(amps[:, :, :, :CW], (0, 2, 1, 3)).reshape(OCC * VIRT, OCC * CW)
    right_side = cycle_ints.reshape(VIRT * OCC, OCC * CW)
    cycle_block = lax.dot_general(left_side, right_side, (((1,), (1,)), ((), ())),
                                 preferred_element_type=jnp.float32).reshape(OCC, VIRT, VIRT, OCC)
    cycle = jnp.transpose(cycle_block, (0, 3, 1, 2))
    half_sum = fock_term - occ_term + ladder + cycle
    mirrored = jnp.transpose(half_sum, (1, 0, 3, 2))
    return symmetry_allowed(occ_irrep, vir_irrep) * (half_sum + mirrored)
```

```python
import functools

import jax
import jax.numpy as jnp
from jax import lax
from jax.experimental import pallas as pl
from jax.experimental.pallas import tpu as pltpu
from jax.sharding import PartitionSpec as P

DW = 8
CW = 16
LANES = 128
POWER = 9
TOP_EXPONENT = 13


def contract_last(left_side, right_side):
    return lax.dot_general(
        left_side, right_side, (((1,), (1,)), ((), ())), preferred_element_type=jnp.float32
    )


def plain_body(amps, fock_vir, fock_occ, ladder_ints, cycle_ints, occ_irrep, vir_irrep):
    occupied = amps.shape[0]
    per_device = amps.shape[2]
    virtuals = amps.shape[3]
    pair_count = occupied * occupied
    position = lax.axis_index("vir")
    fock_term = jnp.dot(
        amps.reshape(pair_count * per_device, virtuals),
        fock_vir,
        preferred_element_type=jnp.float32,
    ).reshape(occupied, occupied, per_device, virtuals)
    occ_term = jnp.einsum("ikab,kj->ijab", amps, fock_occ, preferred_element_type=jnp.float32)
    flat_ints = ladder_ints.reshape(per_device * virtuals, ladder_ints.shape[2])
    local_window = amps[:, :, 0:1, :DW]
    local_cycle = amps[:, :, :, :CW]
    segment = lax.all_gather(local_window, "vir", axis=2, tiled=True)
    width = segment.shape[2] * DW
    ladder = contract_last(segment.reshape(pair_count, width), flat_ints)
    left_side = jnp.transpose(local_cycle, (0, 2, 1, 3)).reshape(
        occupied * per_device, occupied * CW
    )
    segment = lax.all_gather(cycle_ints, "vir", axis=0, tiled=True)
    right_side = segment.reshape(segment.shape[0] * occupied, occupied * CW)
    cycle_block = contract_last(left_side, right_side).reshape(
        occupied, per_device, segment.shape[0], occupied
    )
    cycle_part = jnp.transpose(cycle_block, (0, 3, 1, 2))
    half_sum = (
        fock_term - occ_term + ladder.reshape(occupied, occupied, per_device, virtuals) + cycle_part
    )
    vir_local = lax.dynamic_slice_in_dim(vir_irrep, position * per_device, per_device)
    occ_pair = jnp.bitwise_xor(occ_irrep[:, None], occ_irrep[None, :])
    vir_pair = jnp.bitwise_xor(vir_local[:, None], vir_irrep[None, :])
    received = lax.all_to_all(half_sum, "vir", split_axis=3, concat_axis=2, tiled=True)
    mirrored = jnp.transpose(received, (1, 0, 3, 2))
    product_irrep = jnp.bitwise_xor(occ_pair[:, :, None, None], vir_pair[None, None, :, :])
    allowed = jnp.where(product_irrep == 0, jnp.float32(1.0), jnp.float32(0.0))
    return allowed * (half_sum + mirrored)


def labels_and_copies(occ_ref, occupied):
    labels = [occ_ref[j] for j in range(occupied)]
    copies = []
    for j in range(occupied):
        s = jnp.int32(0)
        for k in range(j):
            s = s + (labels[k] == labels[j]).astype(jnp.int32)
        copies.append(s)
    return labels, copies


def prep_kernel(pos_ref, cyc_ref, amps_ref, out_ref):
    per_device, occupied, _ = cyc_ref.shape
    cyc = jnp.swapaxes(cyc_ref[...].astype(jnp.float32), 0, 1)
    rows = occupied * per_device
    out_ref[0:rows, :] = cyc.reshape(rows, LANES).astype(jnp.bfloat16)
    win = amps_ref[:, :, 0, :].astype(jnp.float32).reshape(occupied * occupied, LANES)
    lane = lax.broadcasted_iota(jnp.int32, win.shape, 1)
    win = jnp.where(lane < DW, win, 0.0)
    win = pltpu.roll(win, pos_ref[0] * DW, axis=1)
    out_ref[rows:, :] = win.astype(jnp.bfloat16)


def fock_kernel(occ_ref, amps_ref, fock_ref, mix_ref, u_ref, half_ref, cyc_ref, hs_ref):
    i = pl.program_id(0)
    _, per_device, virtuals = half_ref.shape
    occupied = occ_ref.shape[0]
    labels, copies = labels_and_copies(occ_ref, occupied)
    a = amps_ref[0]
    h = jnp.dot(a, fock_ref[...], preferred_element_type=jnp.float32)
    h = h - jnp.dot(mix_ref[...], a, preferred_element_type=jnp.float32)
    hs_ref[...] = h.reshape(occupied, per_device, virtuals)
    own = occ_ref[i]
    u = u_ref[...]
    for j in range(occupied):
        s = copies[j]
        half_ref[s] = jnp.where(u == (own ^ labels[j]), hs_ref[j], half_ref[s])
    head = a[:, :LANES].astype(jnp.float32)
    lane = lax.broadcasted_iota(jnp.int32, (per_device, LANES), 1)
    acc = jnp.zeros((per_device, LANES), jnp.float32)
    for k in range(occupied):
        piece = jnp.where(lane < CW, head[k * per_device : (k + 1) * per_device], 0.0)
        acc = acc + (pltpu.roll(piece, k * CW, axis=1) if k else piece)
    cyc_ref[0] = acc.astype(jnp.bfloat16)


def payload_pieces(per_device, pairs, dests):
    out = {}
    for q in range(dests):
        for e in range(pairs):
            start = 0
            while start < per_device:
                src = q * per_device + start
                dst = e * per_device + start
                length = min(LANES - src % LANES, LANES - dst % LANES, per_device - start)
                out.setdefault((q, dst // LANES), []).append(
                    (dst % LANES, e, src // LANES, (dst - src) % LANES)
                )
                start += length
    return out


def half_kernel(
    pos_ref, occ_ref, own_ref, mate_ref, cyc_ref, half_ref, u_ref, lad_ref,
    out_ref, send_ref, xs_ref, w1_ref, w2_ref, hs_ref, ls_ref, pay_ref, max_ref,
):
    step = pl.program_id(0)
    steps = pl.num_programs(0)
    occupied = occ_ref.shape[0]
    pairs, per_device, virtuals = hs_ref.shape
    dests = send_ref.shape[0]
    rows = occupied * per_device
    labels, copies = labels_and_copies(occ_ref, occupied)

    @pl.when(step == 0)
    def _():
        win = jnp.zeros((occupied * occupied, LANES), jnp.float32)
        for r in range(dests):
            ref = mate_ref if r & 1 else own_ref
            block = ref[((r >> 1) & 1) * (dests // 4) + (r >> 2)].astype(jnp.float32)
            win = win + block[rows:]
            p = jnp.int32(r) ^ pos_ref[0]
            at = pl.ds(pl.multiple_of(p * per_device, 8), per_device)
            for j in range(occupied):
                xs_ref[j, at, :] = block[j * per_device : (j + 1) * per_device]
        w1_ref[...] = win
        for i in range(occupied):
            for j in range(occupied):
                row = (labels[i] ^ labels[j]) * pairs + 2 * i + copies[j]
                w2_ref[pl.ds(row, 1), :] = w1_ref[i * occupied + j : i * occupied + j + 1, :]
        hs_ref[...] = half_ref[...]
        u = u_ref[...]
        for j in range(occupied):
            c = contract_last(cyc_ref[...], xs_ref[j].astype(jnp.bfloat16))
            for i in range(occupied):
                e = 2 * i + copies[j]
                part = c[i * per_device : (i + 1) * per_device]
                hs_ref[e] = hs_ref[e] + jnp.where(u == (labels[i] ^ labels[j]), part, 0.0)
        max_ref[...] = jnp.zeros_like(max_ref)

    w2 = w2_ref[...].astype(jnp.bfloat16)
    group = pl.ds(pl.multiple_of(step * 8, 8), 8)
    u8 = u_ref[group, :]
    for a in range(8):
        ladder = contract_last(w2, lad_ref[a])
        ua = u8[a : a + 1, :]
        sel = ladder[0:pairs]
        for v in range(1, 4):
            sel = jnp.where(ua == v, ladder[v * pairs : (v + 1) * pairs], sel)
        ls_ref[:, a, :] = sel
    top = max_ref[...]
    lane = lax.broadcasted_iota(jnp.int32, (8, LANES), 1)
    tiles = {}
    for e in range(pairs):
        for v in range(virtuals // LANES):
            at = slice(v * LANES, (v + 1) * LANES)
            x = hs_ref[e, group, at] + ls_ref[e, :, at]
            out_ref[e, :, at] = x
            top = jnp.maximum(top, jnp.abs(x))
            tiles[e, v] = x
    max_ref[...] = top
    rolled = {}
    for (q, t), pieces in payload_pieces(per_device, pairs, dests).items():
        acc = None
        for first, e, v, shift in pieces:
            if (e, v, shift) not in rolled:
                x = tiles[e, v]
                rolled[e, v, shift] = pltpu.roll(x, shift, axis=1) if shift else x
            x = rolled[e, v, shift]
            acc = x if acc is None else jnp.where(lane >= first, x, acc)
        at = pl.ds(pl.multiple_of(t * per_device + step * 8, 8), 8)
        pay_ref[q, at, :] = acc

    @pl.when(step == steps - 1)
    def _():
        top = jnp.max(jnp.max(max_ref[...], axis=0, keepdims=True), axis=1, keepdims=True)
        k = jnp.floor(TOP_EXPONENT - jnp.log2(jnp.maximum(top, 1e-30)))
        scale = jnp.exp2(k)
        count = pay_ref.shape[1]
        row = lax.broadcasted_iota(jnp.int32, (count, LANES), 0)
        data_rows = (virtuals // LANES) * per_device
        for q in range(dests):
            z = pay_ref[q] * scale
            z2 = z * z
            z4 = z2 * z2
            y = jnp.where(row >= data_rows, k, z4 * z4 * z)
            send_ref[q] = y.astype(jnp.bfloat16)


def join_kernel(occ_ref, half_ref, recv_ref, u_ref, out_ref, dec_ref, mir_ref):
    i = pl.program_id(0)
    occupied = occ_ref.shape[0]
    _, per_device, virtuals = half_ref.shape
    dests = recv_ref.shape[0]
    tiles = virtuals // LANES
    labels, copies = labels_and_copies(occ_ref, occupied)

    @pl.when(i == 0)
    def _():
        for p in range(dests):
            block = recv_ref[p].astype(jnp.float32)
            k = block[tiles * per_device : tiles * per_device + 1, 0:1]
            y = block[: tiles * per_device]
            size = jnp.exp2(jnp.log2(jnp.maximum(jnp.abs(y), 2.0**-126)) * (1.0 / POWER) - k)
            x = jnp.where(y < 0, -size, jnp.where(y > 0, size, 0.0))
            for t in range(tiles):
                dec_ref[t, p * per_device : (p + 1) * per_device, :] = x[
                    t * per_device : (t + 1) * per_device
                ]
        for t in range(tiles):
            mir_ref[t * LANES : (t + 1) * LANES, :] = dec_ref[t].T

    own = occ_ref[i]
    copy = jnp.int32(0)
    for k in range(occupied):
        copy = copy + jnp.logical_and(labels[k] == own, k < i).astype(jnp.int32)
    u = u_ref[...]
    for j in range(occupied):
        at = pl.ds(pl.multiple_of((2 * j + copy) * per_device, 8), per_device)
        total = half_ref[copies[j]] + mir_ref[at, :]
        out_ref[0, j] = jnp.where(u == (own ^ labels[j]), total, 0.0)


def permute(x, flip, size):
    return lax.ppermute(x, "vir", [(n, n ^ flip) for n in range(size)])


def body(dests, amps, fock_vir, fock_occ, ladder_ints, cycle_ints, occ_irrep, vir_irrep):
    occupied, _, per_device, virtuals = amps.shape
    pairs = 2 * occupied
    tiles = virtuals // LANES
    rows = occupied * per_device
    kw = ladder_ints.shape[2]
    f32, bf16 = jnp.float32, jnp.bfloat16
    position = lax.axis_index("vir").astype(jnp.int32)
    pos = position.reshape(1)
    vir_local = lax.dynamic_slice_in_dim(vir_irrep, position * per_device, per_device)
    u = jnp.bitwise_xor(vir_local[:, None], vir_irrep[None, :])
    smem = pl.BlockSpec(memory_space=pltpu.SMEM)
    limit = 40 * 2**20

    def whole(shape):
        return pl.BlockSpec(shape, lambda n: (0,) * len(shape))

    gather_rows = rows + occupied * occupied
    block = pl.pallas_call(
        prep_kernel,
        grid=(1,),
        out_shape=jax.ShapeDtypeStruct((gather_rows, LANES), bf16),
        in_specs=[
            smem,
            whole(cycle_ints.shape),
            pl.BlockSpec((occupied, occupied, 16, LANES), lambda n: (0, 0, 0, 0)),
        ],
        out_specs=whole((gather_rows, LANES)),
        compiler_params=pltpu.CompilerParams(vmem_limit_bytes=limit),
        cost_estimate=pl.CostEstimate(flops=0, bytes_accessed=600000, transcendentals=0),
    )(pos, cycle_ints, amps)

    along_z = [block] + [permute(block, m << 2, dests) for m in range(1, dests // 4)]
    along_y = [permute(b, 2, dests) for b in along_z]
    own_blocks = jnp.stack(along_z + along_y)
    mate_blocks = permute(own_blocks, 1, dests)

    mix = jnp.kron(fock_occ.T, jnp.eye(per_device, dtype=bf16))
    half, cyc = pl.pallas_call(
        fock_kernel,
        grid=(occupied,),
        out_shape=(
            jax.ShapeDtypeStruct((pairs, per_device, virtuals), f32),
            jax.ShapeDtypeStruct((occupied, per_device, LANES), bf16),
        ),
        in_specs=[
            smem,
            pl.BlockSpec((1, rows, virtuals), lambda n: (n, 0, 0)),
            whole(fock_vir.shape),
            whole(mix.shape),
            whole(u.shape),
        ],
        out_specs=(
            pl.BlockSpec((2, per_device, virtuals), lambda n: (n, 0, 0)),
            pl.BlockSpec((1, per_device, LANES), lambda n: (n, 0, 0)),
        ),
        scratch_shapes=[pltpu.VMEM((occupied, per_device, virtuals), f32)],
        compiler_params=pltpu.CompilerParams(vmem_limit_bytes=limit),
        cost_estimate=pl.CostEstimate(
            flops=3 * occupied * rows * virtuals * virtuals,
            bytes_accessed=6 * 10**6,
            transcendentals=0,
        ),
    )(occ_irrep, amps.reshape(occupied, rows, virtuals), fock_vir, mix, u)

    send_rows = tiles * per_device + 8
    half, send = pl.pallas_call(
        half_kernel,
        grid=(per_device // 8,),
        out_shape=(
            jax.ShapeDtypeStruct((pairs, per_device, virtuals), f32),
            jax.ShapeDtypeStruct((dests, send_rows, LANES), bf16),
        ),
        in_specs=[
            smem,
            smem,
            whole(own_blocks.shape),
            whole(mate_blocks.shape),
            whole((rows, LANES)),
            whole(half.shape),
            whole(u.shape),
            pl.BlockSpec((8, virtuals, kw), lambda n: (n, 0, 0)),
        ],
        out_specs=(
            pl.BlockSpec((pairs, 8, virtuals), lambda n: (0, n, 0)),
            whole((dests, send_rows, LANES)),
        ),
        scratch_shapes=[
            pltpu.VMEM((occupied, virtuals, LANES), f32),
            pltpu.VMEM((occupied * occupied, LANES), f32),
            pltpu.VMEM((occupied * occupied, LANES), f32),
            pltpu.VMEM((pairs, per_device, virtuals), f32),
            pltpu.VMEM((pairs, 8, virtuals), f32),
            pltpu.VMEM((dests, send_rows, LANES), f32),
            pltpu.VMEM((8, LANES), f32),
        ],
        compiler_params=pltpu.CompilerParams(vmem_limit_bytes=limit),
        cost_estimate=pl.CostEstimate(
            flops=4 * occupied * rows * virtuals * LANES,
            bytes_accessed=12 * 10**6,
            transcendentals=0,
        ),
    )(pos, occ_irrep, own_blocks, mate_blocks, cyc.reshape(rows, LANES), half, u, ladder_ints)

    recv = lax.all_to_all(send, "vir", split_axis=0, concat_axis=0, tiled=True)

    return pl.pallas_call(
        join_kernel,
        grid=(occupied,),
        out_shape=jax.ShapeDtypeStruct((occupied, occupied, per_device, virtuals), f32),
        in_specs=[
            smem,
            pl.BlockSpec((2, per_device, virtuals), lambda n: (n, 0, 0)),
            whole(recv.shape),
            whole(u.shape),
        ],
        out_specs=pl.BlockSpec((1, occupied, per_device, virtuals), lambda n: (n, 0, 0, 0)),
        scratch_shapes=[
            pltpu.VMEM((tiles, virtuals, LANES), f32),
            pltpu.VMEM((tiles * LANES, virtuals), f32),
        ],
        compiler_params=pltpu.CompilerParams(vmem_limit_bytes=limit),
        cost_estimate=pl.CostEstimate(flops=10**6, bytes_accessed=10**7, transcendentals=0),
    )(occ_irrep, half, recv, u)


def solution(mesh):
    dests = mesh.shape["vir"]

    def run(amps, *rest):
        occupied, _, per_device, virtuals = amps.shape
        tiled = (
            dests == 16
            and per_device % 8 == 0
            and virtuals % LANES == 0
            and 2 * occupied * per_device == virtuals
            and rest[2].shape[2] == LANES
            and rest[3].shape[2] == LANES
        )
        return body(dests, amps, *rest) if tiled else plain_body(amps, *rest)

    return jax.shard_map(
        run,
        mesh=mesh,
        in_specs=(
            P("groups", None, "vir", None),
            P("groups", None),
            P("groups", None),
            P("vir", "groups", None),
            P("vir", "groups", None),
            P("groups"),
            P("groups"),
        ),
        out_specs=P("groups", None, "vir", None),
        check_vma=False,
    )
```

```python
import functools

import jax
import jax.numpy as jnp
from jax import lax
from jax.experimental import pallas as pl
from jax.experimental.pallas import tpu as pltpu
from jax.sharding import PartitionSpec as P

DW = 8
CW = 16
LANES = 128
POWER = 9
TOP_EXPONENT = 13


def contract_last(left_side, right_side):
    return lax.dot_general(
        left_side, right_side, (((1,), (1,)), ((), ())), preferred_element_type=jnp.float32
    )


def plain_body(amps, fock_vir, fock_occ, ladder_ints, cycle_ints, occ_irrep, vir_irrep):
    occupied = amps.shape[0]
    per_device = amps.shape[2]
    virtuals = amps.shape[3]
    pair_count = occupied * occupied
    position = lax.axis_index("vir")
    fock_term = jnp.dot(
        amps.reshape(pair_count * per_device, virtuals),
        fock_vir,
        preferred_element_type=jnp.float32,
    ).reshape(occupied, occupied, per_device, virtuals)
    occ_term = jnp.einsum("ikab,kj->ijab", amps, fock_occ, preferred_element_type=jnp.float32)
    flat_ints = ladder_ints.reshape(per_device * virtuals, ladder_ints.shape[2])
    local_window = amps[:, :, 0:1, :DW]
    local_cycle = amps[:, :, :, :CW]
    segment = lax.all_gather(local_window, "vir", axis=2, tiled=True)
    width = segment.shape[2] * DW
    ladder = contract_last(segment.reshape(pair_count, width), flat_ints)
    left_side = jnp.transpose(local_cycle, (0, 2, 1, 3)).reshape(
        occupied * per_device, occupied * CW
    )
    segment = lax.all_gather(cycle_ints, "vir", axis=0, tiled=True)
    right_side = segment.reshape(segment.shape[0] * occupied, occupied * CW)
    cycle_block = contract_last(left_side, right_side).reshape(
        occupied, per_device, segment.shape[0], occupied
    )
    cycle_part = jnp.transpose(cycle_block, (0, 3, 1, 2))
    half_sum = (
        fock_term - occ_term + ladder.reshape(occupied, occupied, per_device, virtuals) + cycle_part
    )
    vir_local = lax.dynamic_slice_in_dim(vir_irrep, position * per_device, per_device)
    occ_pair = jnp.bitwise_xor(occ_irrep[:, None], occ_irrep[None, :])
    vir_pair = jnp.bitwise_xor(vir_local[:, None], vir_irrep[None, :])
    received = lax.all_to_all(half_sum, "vir", split_axis=3, concat_axis=2, tiled=True)
    mirrored = jnp.transpose(received, (1, 0, 3, 2))
    product_irrep = jnp.bitwise_xor(occ_pair[:, :, None, None], vir_pair[None, None, :, :])
    allowed = jnp.where(product_irrep == 0, jnp.float32(1.0), jnp.float32(0.0))
    return allowed * (half_sum + mirrored)


def labels_and_copies(occ_ref, occupied):
    labels = [occ_ref[j] for j in range(occupied)]
    copies = []
    for j in range(occupied):
        s = jnp.int32(0)
        for k in range(j):
            s = s + (labels[k] == labels[j]).astype(jnp.int32)
        copies.append(s)
    return labels, copies


def prep_kernel(pos_ref, occ_vals_ref, amps_ref, win_ref, mix_ref):
    occupied, _, _, _ = amps_ref.shape
    rows = mix_ref.shape[0]
    per_device = rows // occupied
    win = amps_ref[:, :, 0, :].astype(jnp.float32).reshape(occupied * occupied, LANES)
    lane = lax.broadcasted_iota(jnp.int32, win.shape, 1)
    win = jnp.where(lane < DW, win, 0.0)
    win_ref[...] = pltpu.roll(win, pos_ref[0] * DW, axis=1).astype(jnp.bfloat16)
    r = lax.broadcasted_iota(jnp.int32, (rows, rows), 0)
    c = lax.broadcasted_iota(jnp.int32, (rows, rows), 1)
    mix = jnp.zeros((rows, rows), jnp.float32)
    one = lax.broadcasted_iota(jnp.int32, (rows, occupied), 0)
    col = lax.broadcasted_iota(jnp.int32, (rows, occupied), 1) * per_device
    pick = jnp.logical_and(one >= col, one < col + per_device).astype(jnp.bfloat16)
    left = lax.dot_general(
        pick, occ_vals_ref[...], (((1,), (1,)), ((), ())), preferred_element_type=jnp.float32
    ).astype(jnp.bfloat16)
    mix = contract_last(left, pick)
    gap = r - c
    same = gap == 0
    for n in range(1, occupied):
        same = jnp.logical_or(same, jnp.abs(gap) == n * per_device)
    mix_ref[...] = jnp.where(same, mix, 0.0).astype(jnp.bfloat16)


def fock_kernel(first, occ_ref, amps_ref, fock_ref, mix_ref, u_ref, after_ref, half_ref, cyc_ref, hs_ref):
    i = pl.program_id(0) + first
    _, per_device, virtuals = half_ref.shape
    occupied = occ_ref.shape[0]
    labels, copies = labels_and_copies(occ_ref, occupied)
    a = amps_ref[0]
    h = jnp.dot(a, fock_ref[...], preferred_element_type=jnp.float32)
    h = h - jnp.dot(mix_ref[...], a, preferred_element_type=jnp.float32)
    hs_ref[...] = h.reshape(occupied, per_device, virtuals)
    own = occ_ref[i]
    u = u_ref[...]
    for j in range(occupied):
        s = copies[j]
        half_ref[s] = jnp.where(u == (own ^ labels[j]), hs_ref[j], half_ref[s])
    head = a[:, :LANES].astype(jnp.float32)
    lane = lax.broadcasted_iota(jnp.int32, (per_device, LANES), 1)
    acc = jnp.zeros((per_device, LANES), jnp.float32)
    for k in range(occupied):
        piece = jnp.where(lane < CW, head[k * per_device : (k + 1) * per_device], 0.0)
        acc = acc + (pltpu.roll(piece, k * CW, axis=1) if k else piece)
    cyc_ref[0] = acc.astype(jnp.bfloat16)


def tie(blocks, windows, after):
    count = len(blocks)

    def kernel(*refs):
        ins, outs = refs[: count + len(windows) + 1], refs[count + len(windows) + 1 :]
        if windows:
            total = ins[count][...]
            for ref in ins[count + 1 : count + len(windows)]:
                total = total + ref[...]
            outs[count][...] = total

    anywhere = pl.BlockSpec(memory_space=pl.ANY)
    vmem = pl.BlockSpec(memory_space=pltpu.VMEM)
    return pl.pallas_call(
        kernel,
        out_shape=tuple(jax.ShapeDtypeStruct(b.shape, b.dtype) for b in blocks)
        + tuple(jax.ShapeDtypeStruct(w.shape, w.dtype) for w in windows[:1]),
        in_specs=[anywhere] * count + [vmem] * len(windows) + [anywhere],
        out_specs=(anywhere,) * count + (vmem,) * len(windows[:1]),
        input_output_aliases={n: n for n in range(count)},
        cost_estimate=pl.CostEstimate(flops=0, bytes_accessed=0, transcendentals=0),
    )(*blocks, *windows, after)


def payload_pieces(per_device, pairs, dests):
    out = {}
    for q in range(dests):
        for e in range(pairs):
            start = 0
            while start < per_device:
                src = q * per_device + start
                dst = e * per_device + start
                length = min(LANES - src % LANES, LANES - dst % LANES, per_device - start)
                out.setdefault((q, dst // LANES), []).append(
                    (dst % LANES, e, src // LANES, (dst - src) % LANES)
                )
                start += length
    return out


def ladder_kernel(occ_ref, win0_ref, win1_ref, half0, half1, half2, half3, u_ref, lad_ref, out_ref, w1_ref, w2_ref, ls_ref):
    step = pl.program_id(0)
    occupied = occ_ref.shape[0]
    pairs, _, virtuals = out_ref.shape
    labels, copies = labels_and_copies(occ_ref, occupied)

    @pl.when(step == 0)
    def _():
        w1_ref[...] = win0_ref[...].astype(jnp.float32) + win1_ref[...].astype(jnp.float32)
        for i in range(occupied):
            for j in range(occupied):
                row = (labels[i] ^ labels[j]) * pairs + 2 * i + copies[j]
                w2_ref[pl.ds(row, 1), :] = w1_ref[i * occupied + j : i * occupied + j + 1, :]

    w2 = w2_ref[...].astype(jnp.bfloat16)
    u8 = u_ref[pl.ds(pl.multiple_of(step * 8, 8), 8), :]
    for a in range(8):
        ladder = contract_last(w2, lad_ref[a])
        ua = u8[a : a + 1, :]
        sel = ladder[0:pairs]
        for v in range(1, 4):
            sel = jnp.where(ua == v, ladder[v * pairs : (v + 1) * pairs], sel)
        ls_ref[:, a, :] = sel
    parts = (half0, half1, half2, half3)
    per = pairs // len(parts)
    for n, part in enumerate(parts):
        out_ref[n * per : (n + 1) * per] = part[...] + ls_ref[n * per : (n + 1) * per]


def cycle_kernel(dests, pos_ref, occ_ref, *refs):
    own_ref, mate_ref, cyc0, cyc1, cyc2, cyc3, half_ref, u_ref, out_ref = refs[:9]
    send_refs = refs[9 : 9 + dests]
    xs_ref, pay_ref = refs[9 + dests :]
    occupied = occ_ref.shape[0]
    pairs, per_device, virtuals = half_ref.shape
    labels, copies = labels_and_copies(occ_ref, occupied)
    pos = pos_ref[0]
    for r in range(dests):
        ref = mate_ref if r & 1 else own_ref
        block = ref[((r >> 1) & 1) * (dests // 4) + (r >> 2)].astype(jnp.float32)
        xs_ref[pl.ds((pos ^ r) * per_device, per_device)] = block
    u = u_ref[...]
    out_ref[...] = half_ref[...]
    left = jnp.concatenate([ref[...] for ref in (cyc0, cyc1, cyc2, cyc3)], axis=0)
    left = left.astype(jnp.float32).reshape(occupied * per_device, LANES).astype(jnp.bfloat16)
    for j in range(occupied):
        c = contract_last(left, xs_ref[:, j, :].astype(jnp.bfloat16))
        for i in range(occupied):
            e = 2 * i + copies[j]
            part = c[i * per_device : (i + 1) * per_device]
            out_ref[e] = out_ref[e] + jnp.where(u == (labels[i] ^ labels[j]), part, 0.0)

    pieces_of = payload_pieces(per_device, pairs, dests)
    lane = lax.broadcasted_iota(jnp.int32, (8, LANES), 1)

    def group(g, top):
        rows = pl.ds(pl.multiple_of(g * 8, 8), 8)
        tiles = {}
        for e in range(pairs):
            for v in range(virtuals // LANES):
                x = out_ref[e, rows, v * LANES : (v + 1) * LANES]
                top = jnp.maximum(top, jnp.abs(x))
                tiles[e, v] = x
        rolled = {}
        for (q, t), pieces in pieces_of.items():
            acc = None
            for first, e, v, shift in pieces:
                if (e, v, shift) not in rolled:
                    x = tiles[e, v]
                    rolled[e, v, shift] = pltpu.roll(x, shift, axis=1) if shift else x
                x = rolled[e, v, shift]
                acc = x if acc is None else jnp.where(lane >= first, x, acc)
            at = pl.ds(pl.multiple_of(t * per_device + g * 8, 8), 8)
            pay_ref[pos ^ q, at, :] = acc
        return top

    top = lax.fori_loop(0, per_device // 8, group, jnp.zeros((8, LANES), jnp.float32))
    top = jnp.max(jnp.max(top, axis=0, keepdims=True), axis=1, keepdims=True)
    k = jnp.floor(TOP_EXPONENT - jnp.log2(jnp.maximum(top, 1e-30)))
    scale = jnp.exp2(k)
    count = pay_ref.shape[1]
    row = lax.broadcasted_iota(jnp.int32, (count, LANES), 0)
    data_rows = (virtuals // LANES) * per_device
    for r in range(dests):
        z = pay_ref[r] * scale
        z2 = z * z
        z4 = z2 * z2
        y = jnp.where(row >= data_rows, k, z4 * z4 * z)
        send_refs[r][...] = y.astype(jnp.bfloat16)


def join_kernel(dests, pos_ref, occ_ref, half_ref, u_ref, *refs):
    recv_refs = refs[:dests]
    out_ref, dec_ref, mir_ref = refs[dests:]
    i = pl.program_id(0)
    occupied = occ_ref.shape[0]
    _, per_device, virtuals = half_ref.shape
    tiles = virtuals // LANES
    labels, copies = labels_and_copies(occ_ref, occupied)

    @pl.when(i == 0)
    def _():
        for r in range(dests):
            block = recv_refs[r][...].astype(jnp.float32)
            k = block[tiles * per_device : tiles * per_device + 1, 0:1]
            y = block[: tiles * per_device]
            size = jnp.exp2(jnp.log2(jnp.maximum(jnp.abs(y), 2.0**-126)) * (1.0 / POWER) - k)
            x = jnp.where(y < 0, -size, jnp.where(y > 0, size, 0.0))
            at = pl.ds(pl.multiple_of((pos_ref[0] ^ r) * per_device, 8), per_device)
            for t in range(tiles):
                dec_ref[t, at, :] = x[t * per_device : (t + 1) * per_device]
        for t in range(tiles):
            mir_ref[t * LANES : (t + 1) * LANES, :] = dec_ref[t].T

    own = occ_ref[i]
    copy = jnp.int32(0)
    for k in range(occupied):
        copy = copy + jnp.logical_and(labels[k] == own, k < i).astype(jnp.int32)
    u = u_ref[...]
    for j in range(occupied):
        at = pl.ds(pl.multiple_of((2 * j + copy) * per_device, 8), per_device)
        total = half_ref[copies[j]] + mir_ref[at, :]
        out_ref[0, j] = jnp.where(u == (own ^ labels[j]), total, 0.0)


def permute(x, flip, size):
    return lax.ppermute(x, "vir", [(n, n ^ flip) for n in range(size)])


def body(dests, amps, fock_vir, fock_occ, ladder_ints, cycle_ints, occ_irrep, vir_irrep):
    occupied, _, per_device, virtuals = amps.shape
    pairs = 2 * occupied
    tiles = virtuals // LANES
    rows = occupied * per_device
    kw = ladder_ints.shape[2]
    f32, bf16 = jnp.float32, jnp.bfloat16
    position = lax.axis_index("vir").astype(jnp.int32)
    pos = position.reshape(1)
    vir_local = lax.dynamic_slice_in_dim(vir_irrep, position * per_device, per_device)
    u = jnp.bitwise_xor(vir_local[:, None], vir_irrep[None, :])
    smem = pl.BlockSpec(memory_space=pltpu.SMEM)
    limit = 40 * 2**20

    def whole(shape):
        return pl.BlockSpec(shape, lambda n: (0,) * len(shape))

    def params():
        return pltpu.CompilerParams(vmem_limit_bytes=limit)

    def cost(flops, size):
        return pl.CostEstimate(flops=flops, bytes_accessed=size, transcendentals=0)

    anywhere = pl.BlockSpec(memory_space=pl.ANY)
    quarter = dests // 4
    x_z = [cycle_ints] + [permute(cycle_ints, m << 2, dests) for m in range(1, quarter)]
    x_y = [permute(cycle_ints, 2, dests)]
    corner = amps[:, :, :16, :LANES]
    win, mix = pl.pallas_call(
        prep_kernel,
        out_shape=(
            jax.ShapeDtypeStruct((occupied * occupied, LANES), bf16),
            jax.ShapeDtypeStruct((rows, rows), bf16),
        ),
        in_specs=[smem] + [pl.BlockSpec(memory_space=pltpu.VMEM)] * 2,
        compiler_params=params(),
        cost_estimate=cost(0, 500000),
    )(pos, fock_occ, corner)
    wins = [win] + [permute(win, m << 2, dests) for m in range(1, quarter)]

    flat_amps = amps.reshape(occupied, rows, virtuals)
    parts = 4
    per_part = occupied // parts

    def fock_part(n, after):
        first = n * per_part
        return pl.pallas_call(
            functools.partial(fock_kernel, first),
            grid=(per_part,),
            out_shape=(
                jax.ShapeDtypeStruct((2 * per_part, per_device, virtuals), f32),
                jax.ShapeDtypeStruct((per_part, per_device, LANES), bf16),
            ),
            in_specs=[
                smem,
                pl.BlockSpec((1, rows, virtuals), lambda i: (i + first, 0, 0)),
                whole(fock_vir.shape),
                whole(mix.shape),
                whole(u.shape),
                anywhere,
            ],
            out_specs=(
                pl.BlockSpec((2, per_device, virtuals), lambda i: (i, 0, 0)),
                pl.BlockSpec((1, per_device, LANES), lambda i: (i, 0, 0)),
            ),
            scratch_shapes=[pltpu.VMEM((occupied, per_device, virtuals), f32)],
            compiler_params=params(),
            cost_estimate=cost(3 * per_part * rows * virtuals * virtuals, 2 * 10**6),
        )(occ_irrep, flat_amps, fock_vir, mix, u, after)

    half0, cyc0 = fock_part(0, mix)
    (x_z[1],) = tie([x_z[1]], [], half0)
    x_y.append(permute(x_z[1], 2, dests))
    half1, cyc1 = fock_part(1, x_z[1])
    *x_z[2:], win = tie(x_z[2:], wins, half1)
    x_y.extend(permute(b, 2, dests) for b in x_z[2:])
    win_y = permute(win, 2, dests)
    half2, cyc2 = fock_part(2, x_z[2])
    *x_y, win = tie(x_y, [win, win_y], half2)
    own_blocks = jnp.stack(x_z + list(x_y))
    mate_blocks = permute(own_blocks, 1, dests)
    win_mate = permute(win, 1, dests)
    half3, cyc3 = fock_part(3, x_y[0])

    half = pl.pallas_call(
        ladder_kernel,
        grid=(per_device // 8,),
        out_shape=jax.ShapeDtypeStruct((pairs, per_device, virtuals), f32),
        in_specs=[smem, whole(win.shape), whole(win.shape)]
        + [pl.BlockSpec((2 * per_part, 8, virtuals), lambda n: (0, n, 0))] * parts
        + [whole(u.shape), pl.BlockSpec((8, virtuals, kw), lambda n: (n, 0, 0))],
        out_specs=pl.BlockSpec((pairs, 8, virtuals), lambda n: (0, n, 0)),
        scratch_shapes=[
            pltpu.VMEM((occupied * occupied, LANES), f32),
            pltpu.VMEM((occupied * occupied, LANES), f32),
            pltpu.VMEM((pairs, 8, virtuals), f32),
        ],
        compiler_params=params(),
        cost_estimate=cost(4 * occupied * rows * virtuals * LANES, 9 * 10**6),
    )(occ_irrep, win, win_mate, half0, half1, half2, half3, u, ladder_ints)

    send_rows = tiles * per_device + 8
    piece = jax.ShapeDtypeStruct((send_rows, LANES), bf16)
    vmem = pl.BlockSpec(memory_space=pltpu.VMEM)
    half, *sends = pl.pallas_call(
        functools.partial(cycle_kernel, dests),
        out_shape=(jax.ShapeDtypeStruct(half.shape, f32),) + (piece,) * dests,
        in_specs=[smem, smem] + [vmem] * 8,
        out_specs=(vmem,) * (1 + dests),
        scratch_shapes=[
            pltpu.VMEM((virtuals, occupied, LANES), f32),
            pltpu.VMEM((dests, send_rows, LANES), f32),
        ],
        compiler_params=params(),
        cost_estimate=cost(2 * occupied * rows * virtuals * LANES, 8 * 10**6),
    )(pos, occ_irrep, own_blocks, mate_blocks, cyc0, cyc1, cyc2, cyc3, half, u)

    recv = [None] * dests
    recv[0] = sends[0]
    for r in reversed(range(1, dests)):
        recv[r] = permute(sends[r], r, dests)

    return pl.pallas_call(
        functools.partial(join_kernel, dests),
        grid=(occupied,),
        out_shape=jax.ShapeDtypeStruct((occupied, occupied, per_device, virtuals), f32),
        in_specs=[
            smem,
            smem,
            pl.BlockSpec((2, per_device, virtuals), lambda n: (n, 0, 0)),
            whole(u.shape),
        ]
        + [whole(piece.shape)] * dests,
        out_specs=pl.BlockSpec((1, occupied, per_device, virtuals), lambda n: (n, 0, 0, 0)),
        scratch_shapes=[
            pltpu.VMEM((tiles, virtuals, LANES), f32),
            pltpu.VMEM((tiles * LANES, virtuals), f32),
        ],
        compiler_params=params(),
        cost_estimate=cost(10**6, 10**7),
    )(pos, occ_irrep, half, u, *recv)


def solution(mesh):
    dests = mesh.shape["vir"]

    def run(amps, *rest):
        occupied, _, per_device, virtuals = amps.shape
        tiled = (
            dests == 16
            and per_device % 8 == 0
            and virtuals % LANES == 0
            and 2 * occupied * per_device == virtuals
            and rest[2].shape[2] == LANES
            and rest[3].shape[2] == LANES
        )
        return body(dests, amps, *rest) if tiled else plain_body(amps, *rest)

    return jax.shard_map(
        run,
        mesh=mesh,
        in_specs=(
            P("groups", None, "vir", None),
            P("groups", None),
            P("groups", None),
            P("vir", "groups", None),
            P("vir", "groups", None),
            P("groups"),
            P("groups"),
        ),
        out_specs=P("groups", None, "vir", None),
        check_vma=False,
    )
```

```python
import functools

import jax
import jax.numpy as jnp
from jax import lax
from jax.experimental import pallas as pl
from jax.experimental.pallas import tpu as pltpu
from jax.sharding import PartitionSpec as P

DW = 8
CW = 16
LANES = 128
POWER = 9
TOP_EXPONENT = 13
LIMIT = 60 * 2**20


def contract_last(left_side, right_side):
    return lax.dot_general(
        left_side, right_side, (((1,), (1,)), ((), ())), preferred_element_type=jnp.float32
    )


def plain_body(amps, fock_vir, fock_occ, ladder_ints, cycle_ints, occ_irrep, vir_irrep):
    occupied = amps.shape[0]
    per_device = amps.shape[2]
    virtuals = amps.shape[3]
    pair_count = occupied * occupied
    position = lax.axis_index("vir")
    fock_term = jnp.dot(
        amps.reshape(pair_count * per_device, virtuals),
        fock_vir,
        preferred_element_type=jnp.float32,
    ).reshape(occupied, occupied, per_device, virtuals)
    occ_term = jnp.einsum("ikab,kj->ijab", amps, fock_occ, preferred_element_type=jnp.float32)
    flat_ints = ladder_ints.reshape(per_device * virtuals, ladder_ints.shape[2])
    local_window = amps[:, :, 0:1, :DW]
    local_cycle = amps[:, :, :, :CW]
    segment = lax.all_gather(local_window, "vir", axis=2, tiled=True)
    width = segment.shape[2] * DW
    ladder = contract_last(segment.reshape(pair_count, width), flat_ints)
    left_side = jnp.transpose(local_cycle, (0, 2, 1, 3)).reshape(
        occupied * per_device, occupied * CW
    )
    segment = lax.all_gather(cycle_ints, "vir", axis=0, tiled=True)
    right_side = segment.reshape(segment.shape[0] * occupied, occupied * CW)
    cycle_block = contract_last(left_side, right_side).reshape(
        occupied, per_device, segment.shape[0], occupied
    )
    cycle_part = jnp.transpose(cycle_block, (0, 3, 1, 2))
    half_sum = (
        fock_term - occ_term + ladder.reshape(occupied, occupied, per_device, virtuals) + cycle_part
    )
    vir_local = lax.dynamic_slice_in_dim(vir_irrep, position * per_device, per_device)
    occ_pair = jnp.bitwise_xor(occ_irrep[:, None], occ_irrep[None, :])
    vir_pair = jnp.bitwise_xor(vir_local[:, None], vir_irrep[None, :])
    received = lax.all_to_all(half_sum, "vir", split_axis=3, concat_axis=2, tiled=True)
    mirrored = jnp.transpose(received, (1, 0, 3, 2))
    product_irrep = jnp.bitwise_xor(occ_pair[:, :, None, None], vir_pair[None, None, :, :])
    allowed = jnp.where(product_irrep == 0, jnp.float32(1.0), jnp.float32(0.0))
    return allowed * (half_sum + mirrored)


def labels_and_copies(occ_ref, occupied):
    labels = [occ_ref[j] for j in range(occupied)]
    copies = []
    for j in range(occupied):
        s = jnp.int32(0)
        for k in range(j):
            s = s + (labels[k] == labels[j]).astype(jnp.int32)
        copies.append(s)
    return labels, copies


def prep_kernel(pos_ref, occ_vals_ref, cyc_ref, amps_ref, block_ref, mix_ref):
    occupied, _, _, _ = amps_ref.shape
    rows = mix_ref.shape[0]
    per_device = rows // occupied
    block_ref[:rows, :] = cyc_ref[...].astype(jnp.float32).reshape(rows, LANES).astype(jnp.bfloat16)
    lane = lax.broadcasted_iota(jnp.int32, (occupied, LANES), 1)
    packed = jnp.zeros((occupied, LANES), jnp.float32)
    for j in range(occupied):
        w = jnp.where(lane < DW, amps_ref[:, j, 0, :].astype(jnp.float32), 0.0)
        packed = packed + (pltpu.roll(w, j * DW, axis=1) if j else w)
    packed = jnp.concatenate([packed, jnp.zeros_like(packed)], axis=0)
    block_ref[rows:, :] = packed.astype(jnp.bfloat16)
    r = lax.broadcasted_iota(jnp.int32, (rows, rows), 0)
    c = lax.broadcasted_iota(jnp.int32, (rows, rows), 1)
    mix = jnp.zeros((rows, rows), jnp.float32)
    one = lax.broadcasted_iota(jnp.int32, (rows, occupied), 0)
    col = lax.broadcasted_iota(jnp.int32, (rows, occupied), 1) * per_device
    pick = jnp.logical_and(one >= col, one < col + per_device).astype(jnp.bfloat16)
    left = lax.dot_general(
        pick, occ_vals_ref[...], (((1,), (1,)), ((), ())), preferred_element_type=jnp.float32
    ).astype(jnp.bfloat16)
    mix = contract_last(left, pick)
    gap = r - c
    same = gap == 0
    for n in range(1, occupied):
        same = jnp.logical_or(same, jnp.abs(gap) == n * per_device)
    mix_ref[...] = jnp.where(same, mix, 0.0).astype(jnp.bfloat16)


def fock_kernel(first, occ_ref, amps_ref, fock_ref, mix_ref, u_ref, after_ref, half_ref, cyc_ref, hs_ref):
    i = pl.program_id(0) + first
    _, per_device, virtuals = half_ref.shape
    occupied = occ_ref.shape[0]
    labels, copies = labels_and_copies(occ_ref, occupied)
    a = amps_ref[0]
    h = jnp.dot(a, fock_ref[...], preferred_element_type=jnp.float32)
    h = h - jnp.dot(mix_ref[...], a, preferred_element_type=jnp.float32)
    hs_ref[...] = h.reshape(occupied, per_device, virtuals)
    own = occ_ref[i]
    u = u_ref[...]
    for j in range(occupied):
        s = copies[j]
        half_ref[s] = jnp.where(u == (own ^ labels[j]), hs_ref[j], half_ref[s])
    head = a[:, :LANES].astype(jnp.float32)
    lane = lax.broadcasted_iota(jnp.int32, (per_device, LANES), 1)
    acc = jnp.zeros((per_device, LANES), jnp.float32)
    for k in range(occupied):
        piece = jnp.where(lane < CW, head[k * per_device : (k + 1) * per_device], 0.0)
        acc = acc + (pltpu.roll(piece, k * CW, axis=1) if k else piece)
    cyc_ref[0] = acc.astype(jnp.bfloat16)


def stack(blocks, after):
    heads = [b.shape[0] for b in blocks]
    count = len(blocks)

    def kernel(*refs):
        out, sems = refs[count + 1], refs[count + 2]
        copies = []
        at = 0
        for n in range(count):
            copies.append(
                pltpu.make_async_copy(refs[n], out.at[at : at + heads[n]], sems.at[n])
            )
            at += heads[n]
        for copy in copies:
            copy.start()
        for copy in copies:
            copy.wait()

    anywhere = pl.BlockSpec(memory_space=pl.ANY)
    shape = (sum(heads),) + blocks[0].shape[1:]
    return pl.pallas_call(
        kernel,
        out_shape=jax.ShapeDtypeStruct(shape, blocks[0].dtype),
        in_specs=[anywhere] * (count + 1),
        out_specs=anywhere,
        scratch_shapes=[pltpu.SemaphoreType.DMA((count,))],
        compiler_params=pltpu.CompilerParams(vmem_limit_bytes=LIMIT),
        cost_estimate=pl.CostEstimate(flops=0, bytes_accessed=10**6, transcendentals=0),
    )(*blocks, after)


def unpack_kernel(pos_ref, blocks_ref, after_ref, win_ref):
    count, _, lanes = blocks_ref.shape
    occupied = win_ref.shape[0] // 8
    lane = lax.broadcasted_iota(jnp.int32, (8, lanes), 1)
    quarter = count // 2
    parts = []
    for j in range(occupied):
        total = jnp.zeros((8, lanes), jnp.float32)
        for n in range(count):
            flip = ((n // quarter) << 1) | ((n % quarter) << 2)
            p = pos_ref[0] ^ flip
            w = blocks_ref[n][:8].astype(jnp.float32)
            shift = lax.rem(p * DW - j * DW + lanes, lanes)
            w = jnp.where(jnp.logical_and(lane >= j * DW, lane < (j + 1) * DW), w, 0.0)
            total = total + pltpu.roll(w, shift, axis=1)
        parts.append(total)
    win_ref[...] = jnp.concatenate(parts, axis=0).astype(jnp.bfloat16)


def payload_pieces(per_device, pairs, dests):
    out = {}
    for q in range(dests):
        for e in range(pairs):
            start = 0
            while start < per_device:
                src = q * per_device + start
                dst = e * per_device + start
                length = min(LANES - src % LANES, LANES - dst % LANES, per_device - start)
                out.setdefault((q, dst // LANES), []).append(
                    (dst % LANES, e, src // LANES, (dst - src) % LANES)
                )
                start += length
    return out


def ladder_kernel(parts, occ_ref, win0_ref, win1_ref, *refs):
    halves = refs[: len(parts)]
    u_ref, lad_ref, out_ref, w1_ref, w2_ref, ls_ref = refs[len(parts) :]
    step = pl.program_id(0)
    occupied = occ_ref.shape[0]
    pairs, _, virtuals = out_ref.shape
    labels, copies = labels_and_copies(occ_ref, occupied)

    @pl.when(step == 0)
    def _():
        w1_ref[...] = win0_ref[...].astype(jnp.float32) + win1_ref[...].astype(jnp.float32)
        for i in range(occupied):
            for j in range(occupied):
                row = (labels[i] ^ labels[j]) * pairs + 2 * i + copies[j]
                w2_ref[pl.ds(row, 1), :] = w1_ref[j * occupied + i : j * occupied + i + 1, :]

    w2 = w2_ref[...].astype(jnp.bfloat16)
    u8 = u_ref[pl.ds(pl.multiple_of(step * 8, 8), 8), :]
    for a in range(8):
        ladder = contract_last(w2, lad_ref[a])
        ua = u8[a : a + 1, :]
        sel = ladder[0:pairs]
        for v in range(1, 4):
            sel = jnp.where(ua == v, ladder[v * pairs : (v + 1) * pairs], sel)
        ls_ref[:, a, :] = sel
    at = 0
    for part, count in zip(halves, parts):
        out_ref[at : at + 2 * count] = part[...] + ls_ref[at : at + 2 * count]
        at += 2 * count


def cycle_kernel(parts, pos_ref, occ_ref, own_ref, mate_ref, *refs):
    cycs = refs[: len(parts)]
    half_ref, u_ref, out_ref, send_ref, xs_ref, acc_ref, pay_ref, sems = refs[len(parts) :]
    occupied = occ_ref.shape[0]
    pairs, per_device, virtuals = acc_ref.shape
    dests = send_ref.shape[0]
    rows = occupied * per_device
    load = pltpu.make_async_copy(half_ref, acc_ref, sems.at[0])
    load.start()
    labels, copies = labels_and_copies(occ_ref, occupied)
    pos = pos_ref[0]
    for r in range(dests):
        ref = mate_ref if r & 1 else own_ref
        block = ref[((r >> 1) & 1) * (dests // 4) + (r >> 2)][:rows].astype(jnp.float32)
        xs_ref[pl.ds((pos ^ r) * per_device, per_device)] = block.reshape(
            per_device, occupied, LANES
        )
    u = u_ref[...]
    left = jnp.concatenate([ref[...].astype(jnp.float32) for ref in cycs], axis=0)
    left = left.reshape(rows, LANES).astype(jnp.bfloat16)
    load.wait()
    for j in range(occupied):
        c = contract_last(left, xs_ref[:, j, :].astype(jnp.bfloat16))
        for i in range(occupied):
            e = 2 * i + copies[j]
            part = c[i * per_device : (i + 1) * per_device]
            acc_ref[e] = acc_ref[e] + jnp.where(u == (labels[i] ^ labels[j]), part, 0.0)
    store = pltpu.make_async_copy(acc_ref, out_ref, sems.at[0])
    store.start()

    pieces_of = payload_pieces(per_device, pairs, dests)
    lane = lax.broadcasted_iota(jnp.int32, (8, LANES), 1)

    def group(g, top):
        rows = pl.ds(pl.multiple_of(g * 8, 8), 8)
        tiles = {}
        for e in range(pairs):
            for v in range(virtuals // LANES):
                x = acc_ref[e, rows, v * LANES : (v + 1) * LANES]
                top = jnp.maximum(top, jnp.abs(x))
                tiles[e, v] = x
        rolled = {}
        for (q, t), pieces in pieces_of.items():
            acc = None
            for first, e, v, shift in pieces:
                if (e, v, shift) not in rolled:
                    x = tiles[e, v]
                    rolled[e, v, shift] = pltpu.roll(x, shift, axis=1) if shift else x
                x = rolled[e, v, shift]
                acc = x if acc is None else jnp.where(lane >= first, x, acc)
            at = pl.ds(pl.multiple_of(t * per_device + g * 8, 8), 8)
            pay_ref[q, at, :] = acc
        return top

    top = lax.fori_loop(0, per_device // 8, group, jnp.zeros((8, LANES), jnp.float32))
    top = jnp.max(jnp.max(top, axis=0, keepdims=True), axis=1, keepdims=True)
    k = jnp.floor(TOP_EXPONENT - jnp.log2(jnp.maximum(top, 1e-30)))
    scale = jnp.exp2(k)
    count = pay_ref.shape[1]
    row = lax.broadcasted_iota(jnp.int32, (count, LANES), 0)
    data_rows = (virtuals // LANES) * per_device
    for q in range(dests):
        z = pay_ref[q] * scale
        z2 = z * z
        z4 = z2 * z2
        y = jnp.where(row >= data_rows, k, z4 * z4 * z)
        send_ref[q] = y.astype(jnp.bfloat16)
    store.wait()


def join_kernel(occ_ref, half_ref, recv_ref, u_ref, out_ref, dec_ref, mir_ref):
    i = pl.program_id(0)
    occupied = occ_ref.shape[0]
    _, per_device, virtuals = half_ref.shape
    dests = recv_ref.shape[0]
    tiles = virtuals // LANES
    labels, copies = labels_and_copies(occ_ref, occupied)

    @pl.when(i == 0)
    def _():
        for p in range(dests):
            block = recv_ref[p].astype(jnp.float32)
            k = block[tiles * per_device : tiles * per_device + 1, 0:1]
            y = block[: tiles * per_device]
            size = jnp.exp2(jnp.log2(jnp.maximum(jnp.abs(y), 2.0**-126)) * (1.0 / POWER) - k)
            x = jnp.where(y < 0, -size, jnp.where(y > 0, size, 0.0))
            for t in range(tiles):
                dec_ref[t, p * per_device : (p + 1) * per_device, :] = x[
                    t * per_device : (t + 1) * per_device
                ]
        for t in range(tiles):
            mir_ref[t * LANES : (t + 1) * LANES, :] = dec_ref[t].T

    own = occ_ref[i]
    copy = jnp.int32(0)
    for k in range(occupied):
        copy = copy + jnp.logical_and(labels[k] == own, k < i).astype(jnp.int32)
    u = u_ref[...]
    for j in range(occupied):
        at = pl.ds(pl.multiple_of((2 * j + copy) * per_device, 8), per_device)
        total = half_ref[copies[j]] + mir_ref[at, :]
        out_ref[0, j] = jnp.where(u == (own ^ labels[j]), total, 0.0)


def permute(x, flip, size):
    return lax.ppermute(x, "vir", [(n, n ^ flip) for n in range(size)])


def body(dests, amps, fock_vir, fock_occ, ladder_ints, cycle_ints, occ_irrep, vir_irrep):
    occupied, _, per_device, virtuals = amps.shape
    pairs = 2 * occupied
    tiles = virtuals // LANES
    rows = occupied * per_device
    kw = ladder_ints.shape[2]
    f32, bf16 = jnp.float32, jnp.bfloat16
    position = lax.axis_index("vir").astype(jnp.int32)
    pos = position.reshape(1)
    vir_local = lax.dynamic_slice_in_dim(vir_irrep, position * per_device, per_device)
    u = jnp.bitwise_xor(vir_local[:, None], vir_irrep[None, :])
    smem = pl.BlockSpec(memory_space=pltpu.SMEM)

    def whole(shape):
        return pl.BlockSpec(shape, lambda n: (0,) * len(shape))

    def params():
        return pltpu.CompilerParams(vmem_limit_bytes=LIMIT)

    def cost(flops, size):
        return pl.CostEstimate(flops=flops, bytes_accessed=size, transcendentals=0)

    anywhere = pl.BlockSpec(memory_space=pl.ANY)
    quarter = dests // 4
    block_rows = rows + 16
    block, mix = pl.pallas_call(
        prep_kernel,
        grid=(1,),
        out_shape=(
            jax.ShapeDtypeStruct((block_rows, LANES), bf16),
            jax.ShapeDtypeStruct((rows, rows), bf16),
        ),
        in_specs=[
            smem,
            whole(fock_occ.shape),
            whole(cycle_ints.shape),
            pl.BlockSpec((occupied, occupied, 16, LANES), lambda n: (0, 0, 0, 0)),
        ],
        out_specs=(whole((block_rows, LANES)), whole((rows, rows))),
        compiler_params=params(),
        cost_estimate=cost(0, 500000),
    )(pos, fock_occ, cycle_ints, amps)
    block = block.reshape(1, block_rows, LANES)

    flat_amps = amps.reshape(occupied, rows, virtuals)
    parts = (3, 3, 2)

    def fock_part(n, after):
        first, count = sum(parts[:n]), parts[n]
        return pl.pallas_call(
            functools.partial(fock_kernel, first),
            grid=(count,),
            out_shape=(
                jax.ShapeDtypeStruct((2 * count, per_device, virtuals), f32),
                jax.ShapeDtypeStruct((count, per_device, LANES), bf16),
            ),
            in_specs=[
                smem,
                pl.BlockSpec((1, rows, virtuals), lambda i: (i + first, 0, 0)),
                whole(fock_vir.shape),
                whole(mix.shape),
                whole(u.shape),
                anywhere,
            ],
            out_specs=(
                pl.BlockSpec((2, per_device, virtuals), lambda i: (i, 0, 0)),
                pl.BlockSpec((1, per_device, LANES), lambda i: (i, 0, 0)),
            ),
            scratch_shapes=[pltpu.VMEM((occupied, per_device, virtuals), f32)],
            compiler_params=params(),
            cost_estimate=cost(3 * count * rows * virtuals * virtuals, 2 * 10**6),
        )(occ_irrep, flat_amps, fock_vir, mix, u, after)

    z1, z2, z3 = [permute(block, m << 2, dests) for m in range(1, quarter)]
    half0, cyc0 = fock_part(0, mix)
    near = stack([block, z1], half0)
    near_y = permute(near, 2, dests)
    half1, cyc1 = fock_part(1, near)
    far = stack([z2, z3], half1)
    far_y = permute(far, 2, dests)
    half2, cyc2 = fock_part(2, far)
    own_blocks = stack([near, far, near_y, far_y], half2)
    win = pl.pallas_call(
        unpack_kernel,
        grid=(1,),
        out_shape=jax.ShapeDtypeStruct((occupied * occupied, LANES), bf16),
        in_specs=[
            smem,
            pl.BlockSpec((dests // 2, 16, LANES), lambda n: (0, rows // 16, 0)),
            anywhere,
        ],
        out_specs=whole((occupied * occupied, LANES)),
        compiler_params=params(),
        cost_estimate=cost(0, 10**5),
    )(pos, own_blocks, own_blocks)
    win_mate = permute(win, 1, dests)
    mate_blocks = permute(own_blocks, 1, dests)

    half = pl.pallas_call(
        functools.partial(ladder_kernel, parts),
        grid=(per_device // 8,),
        out_shape=jax.ShapeDtypeStruct((pairs, per_device, virtuals), f32),
        in_specs=[smem, whole(win.shape), whole(win.shape)]
        + [pl.BlockSpec((2 * count, 8, virtuals), lambda n: (0, n, 0)) for count in parts]
        + [whole(u.shape), pl.BlockSpec((8, virtuals, kw), lambda n: (n, 0, 0))],
        out_specs=pl.BlockSpec((pairs, 8, virtuals), lambda n: (0, n, 0)),
        scratch_shapes=[
            pltpu.VMEM((occupied * occupied, LANES), f32),
            pltpu.VMEM((occupied * occupied, LANES), f32),
            pltpu.VMEM((pairs, 8, virtuals), f32),
        ],
        compiler_params=params(),
        cost_estimate=cost(4 * occupied * rows * virtuals * LANES, 9 * 10**6),
    )(occ_irrep, win, win_mate, half0, half1, half2, u, ladder_ints)

    send_rows = tiles * per_device + 8
    vmem = pl.BlockSpec(memory_space=pltpu.VMEM)
    half, send = pl.pallas_call(
        functools.partial(cycle_kernel, parts),
        out_shape=(
            jax.ShapeDtypeStruct(half.shape, f32),
            jax.ShapeDtypeStruct((dests, send_rows, LANES), bf16),
        ),
        in_specs=[smem, smem] + [vmem] * 5 + [anywhere, vmem],
        out_specs=(anywhere, vmem),
        scratch_shapes=[
            pltpu.VMEM((virtuals, occupied, LANES), f32),
            pltpu.VMEM(half.shape, f32),
            pltpu.VMEM((dests, send_rows, LANES), f32),
            pltpu.SemaphoreType.DMA((1,)),
        ],
        compiler_params=params(),
        cost_estimate=cost(2 * occupied * rows * virtuals * LANES, 8 * 10**6),
    )(pos, occ_irrep, own_blocks, mate_blocks, cyc0, cyc1, cyc2, half, u)

    recv = lax.all_to_all(send, "vir", split_axis=0, concat_axis=0, tiled=True)

    return pl.pallas_call(
        join_kernel,
        grid=(occupied,),
        out_shape=jax.ShapeDtypeStruct((occupied, occupied, per_device, virtuals), f32),
        in_specs=[
            smem,
            pl.BlockSpec((2, per_device, virtuals), lambda n: (n, 0, 0)),
            whole(recv.shape),
            whole(u.shape),
        ],
        out_specs=pl.BlockSpec((1, occupied, per_device, virtuals), lambda n: (n, 0, 0, 0)),
        scratch_shapes=[
            pltpu.VMEM((tiles, virtuals, LANES), f32),
            pltpu.VMEM((tiles * LANES, virtuals), f32),
        ],
        compiler_params=params(),
        cost_estimate=cost(10**6, 10**7),
    )(occ_irrep, half, recv, u)


def solution(mesh):
    dests = mesh.shape["vir"]

    def run(amps, *rest):
        occupied, _, per_device, virtuals = amps.shape
        tiled = (
            dests == 16
            and per_device % 8 == 0
            and virtuals % LANES == 0
            and 2 * occupied * per_device == virtuals
            and rest[2].shape[2] == LANES
            and rest[3].shape[2] == LANES
        )
        return body(dests, amps, *rest) if tiled else plain_body(amps, *rest)

    return jax.shard_map(
        run,
        mesh=mesh,
        in_specs=(
            P("groups", None, "vir", None),
            P("groups", None),
            P("groups", None),
            P("vir", "groups", None),
            P("vir", "groups", None),
            P("groups"),
            P("groups"),
        ),
        out_specs=P("groups", None, "vir", None),
        check_vma=False,
    )
```

```python
import functools

import jax
import jax.numpy as jnp
from jax import lax
from jax.experimental import pallas as pl
from jax.experimental.pallas import tpu as pltpu
from jax.sharding import PartitionSpec as P

DW = 8
CW = 16
LANES = 128
POWER = 9
TOP_EXPONENT = 13


def contract_last(left_side, right_side):
    return lax.dot_general(
        left_side, right_side, (((1,), (1,)), ((), ())), preferred_element_type=jnp.float32
    )


def plain_body(amps, fock_vir, fock_occ, ladder_ints, cycle_ints, occ_irrep, vir_irrep):
    occupied = amps.shape[0]
    per_device = amps.shape[2]
    virtuals = amps.shape[3]
    pair_count = occupied * occupied
    position = lax.axis_index("vir")
    fock_term = jnp.dot(
        amps.reshape(pair_count * per_device, virtuals),
        fock_vir,
        preferred_element_type=jnp.float32,
    ).reshape(occupied, occupied, per_device, virtuals)
    occ_term = jnp.einsum("ikab,kj->ijab", amps, fock_occ, preferred_element_type=jnp.float32)
    flat_ints = ladder_ints.reshape(per_device * virtuals, ladder_ints.shape[2])
    local_window = amps[:, :, 0:1, :DW]
    local_cycle = amps[:, :, :, :CW]
    segment = lax.all_gather(local_window, "vir", axis=2, tiled=True)
    width = segment.shape[2] * DW
    ladder = contract_last(segment.reshape(pair_count, width), flat_ints)
    left_side = jnp.transpose(local_cycle, (0, 2, 1, 3)).reshape(
        occupied * per_device, occupied * CW
    )
    segment = lax.all_gather(cycle_ints, "vir", axis=0, tiled=True)
    right_side = segment.reshape(segment.shape[0] * occupied, occupied * CW)
    cycle_block = contract_last(left_side, right_side).reshape(
        occupied, per_device, segment.shape[0], occupied
    )
    cycle_part = jnp.transpose(cycle_block, (0, 3, 1, 2))
    half_sum = (
        fock_term - occ_term + ladder.reshape(occupied, occupied, per_device, virtuals) + cycle_part
    )
    vir_local = lax.dynamic_slice_in_dim(vir_irrep, position * per_device, per_device)
    occ_pair = jnp.bitwise_xor(occ_irrep[:, None], occ_irrep[None, :])
    vir_pair = jnp.bitwise_xor(vir_local[:, None], vir_irrep[None, :])
    received = lax.all_to_all(half_sum, "vir", split_axis=3, concat_axis=2, tiled=True)
    mirrored = jnp.transpose(received, (1, 0, 3, 2))
    product_irrep = jnp.bitwise_xor(occ_pair[:, :, None, None], vir_pair[None, None, :, :])
    allowed = jnp.where(product_irrep == 0, jnp.float32(1.0), jnp.float32(0.0))
    return allowed * (half_sum + mirrored)


def params(mib):
    return pltpu.CompilerParams(vmem_limit_bytes=mib * 2**20)


def labels_and_copies(occ_ref, occupied):
    labels = [occ_ref[j] for j in range(occupied)]
    copies = []
    for j in range(occupied):
        s = jnp.int32(0)
        for k in range(j):
            s = s + (labels[k] == labels[j]).astype(jnp.int32)
        copies.append(s)
    return labels, copies


def prep_kernel(pos_ref, occ_vals_ref, cyc_ref, amps_ref, block_ref, mix_ref):
    occupied, _, _, _ = amps_ref.shape
    rows = mix_ref.shape[0]
    per_device = rows // occupied
    block_ref[:rows, :] = cyc_ref[...].astype(jnp.float32).reshape(rows, LANES).astype(jnp.bfloat16)
    lane = lax.broadcasted_iota(jnp.int32, (occupied, LANES), 1)
    packed = jnp.zeros((occupied, LANES), jnp.float32)
    for j in range(occupied):
        w = jnp.where(lane < DW, amps_ref[:, j, 0, :].astype(jnp.float32), 0.0)
        packed = packed + (pltpu.roll(w, j * DW, axis=1) if j else w)
    packed = jnp.concatenate([packed, jnp.zeros_like(packed)], axis=0)
    block_ref[rows:, :] = packed.astype(jnp.bfloat16)
    r = lax.broadcasted_iota(jnp.int32, (rows, rows), 0)
    c = lax.broadcasted_iota(jnp.int32, (rows, rows), 1)
    mix = jnp.zeros((rows, rows), jnp.float32)
    one = lax.broadcasted_iota(jnp.int32, (rows, occupied), 0)
    col = lax.broadcasted_iota(jnp.int32, (rows, occupied), 1) * per_device
    pick = jnp.logical_and(one >= col, one < col + per_device).astype(jnp.bfloat16)
    left = lax.dot_general(
        pick, occ_vals_ref[...], (((1,), (1,)), ((), ())), preferred_element_type=jnp.float32
    ).astype(jnp.bfloat16)
    mix = contract_last(left, pick)
    gap = r - c
    same = gap == 0
    for n in range(1, occupied):
        same = jnp.logical_or(same, jnp.abs(gap) == n * per_device)
    mix_ref[...] = jnp.where(same, mix, 0.0).astype(jnp.bfloat16)


def fock_kernel(first, occ_ref, amps_ref, fock_ref, mix_ref, u_ref, after_ref, half_ref, cyc_ref, hs_ref):
    wide, rows, virtuals = amps_ref.shape
    _, per_device, _ = half_ref.shape
    occupied = occ_ref.shape[0]
    labels, copies = labels_and_copies(occ_ref, occupied)
    u = u_ref[...]
    h = jnp.dot(
        amps_ref[...].reshape(wide * rows, virtuals),
        fock_ref[...],
        preferred_element_type=jnp.float32,
    )
    for w in range(wide):
        a = amps_ref[w]
        mixed = jnp.dot(mix_ref[...], a, preferred_element_type=jnp.float32)
        hs_ref[...] = (h[w * rows : (w + 1) * rows] - mixed).reshape(hs_ref.shape)
        own = occ_ref[pl.program_id(0) * wide + w + first]
        for j in range(occupied):
            at = 2 * w + copies[j]
            half_ref[at] = jnp.where(u == (own ^ labels[j]), hs_ref[j], half_ref[at])
        head = a[:, :LANES].astype(jnp.float32)
        lane = lax.broadcasted_iota(jnp.int32, (per_device, LANES), 1)
        acc = jnp.zeros((per_device, LANES), jnp.float32)
        for k in range(occupied):
            piece = jnp.where(lane < CW, head[k * per_device : (k + 1) * per_device], 0.0)
            acc = acc + (pltpu.roll(piece, k * CW, axis=1) if k else piece)
        cyc_ref[w] = acc.astype(jnp.bfloat16)


def stack(blocks, after):
    count = len(blocks)

    def kernel(*refs):
        out = refs[count + 1]
        at = 0
        for n in range(count):
            head = blocks[n].shape[0]
            out[at : at + head] = refs[n][...]
            at += head

    vmem = pl.BlockSpec(memory_space=pltpu.VMEM)
    shape = (sum(b.shape[0] for b in blocks),) + blocks[0].shape[1:]
    return pl.pallas_call(
        kernel,
        out_shape=jax.ShapeDtypeStruct(shape, blocks[0].dtype),
        in_specs=[vmem] * count + [pl.BlockSpec(memory_space=pl.ANY)],
        out_specs=vmem,
        compiler_params=params(4),
        cost_estimate=pl.CostEstimate(flops=0, bytes_accessed=10**6, transcendentals=0),
    )(*blocks, after)


def unpack_kernel(pos_ref, blocks_ref, after_ref, win_ref):
    count, _, lanes = blocks_ref.shape
    occupied = win_ref.shape[0] // 8
    lane = lax.broadcasted_iota(jnp.int32, (8, lanes), 1)
    quarter = count // 2
    parts = []
    for j in range(occupied):
        total = jnp.zeros((8, lanes), jnp.float32)
        for n in range(count):
            flip = ((n // quarter) << 1) | ((n % quarter) << 2)
            p = pos_ref[0] ^ flip
            w = blocks_ref[n][:8].astype(jnp.float32)
            shift = lax.rem(p * DW - j * DW + lanes, lanes)
            w = jnp.where(jnp.logical_and(lane >= j * DW, lane < (j + 1) * DW), w, 0.0)
            total = total + pltpu.roll(w, shift, axis=1)
        parts.append(total)
    win_ref[...] = jnp.concatenate(parts, axis=0).astype(jnp.bfloat16)


def payload_pieces(per_device, pairs, dests):
    out = {}
    for q in range(dests):
        for e in range(pairs):
            start = 0
            while start < per_device:
                src = q * per_device + start
                dst = e * per_device + start
                length = min(LANES - src % LANES, LANES - dst % LANES, per_device - start)
                out.setdefault((q, dst // LANES), []).append(
                    (dst % LANES, e, src // LANES, (dst - src) % LANES)
                )
                start += length
    return out


def ladder_kernel(parts, occ_ref, win0_ref, win1_ref, *refs):
    halves = refs[: len(parts)]
    u_ref, lad_ref, out_ref, w1_ref, w2_ref, ls_ref = refs[len(parts) :]
    step = pl.program_id(0)
    occupied = occ_ref.shape[0]
    pairs, _, virtuals = out_ref.shape
    labels, copies = labels_and_copies(occ_ref, occupied)

    @pl.when(step == 0)
    def _():
        w1_ref[...] = win0_ref[...].astype(jnp.float32) + win1_ref[...].astype(jnp.float32)
        for i in range(occupied):
            for j in range(occupied):
                row = (labels[i] ^ labels[j]) * pairs + 2 * i + copies[j]
                w2_ref[pl.ds(row, 1), :] = w1_ref[j * occupied + i : j * occupied + i + 1, :]

    w2 = w2_ref[...].astype(jnp.bfloat16)
    u8 = u_ref[pl.ds(pl.multiple_of(step * 8, 8), 8), :]
    for a in range(8):
        ladder = contract_last(w2, lad_ref[a])
        ua = u8[a : a + 1, :]
        sel = ladder[0:pairs]
        for v in range(1, 4):
            sel = jnp.where(ua == v, ladder[v * pairs : (v + 1) * pairs], sel)
        ls_ref[:, a, :] = sel
    at = 0
    for part, count in zip(halves, parts):
        out_ref[at : at + 2 * count] = part[...] + ls_ref[at : at + 2 * count]
        at += 2 * count


def cycle_kernel(parts, pos_ref, occ_ref, own_ref, mate_ref, *refs):
    cycs = refs[: len(parts)]
    half_ref, u_ref, out_ref, send_ref, xs_ref, acc_ref, pay_ref, sems = refs[len(parts) :]
    occupied = occ_ref.shape[0]
    pairs, per_device, virtuals = acc_ref.shape
    dests = send_ref.shape[0]
    rows = occupied * per_device
    load = pltpu.make_async_copy(half_ref, acc_ref, sems.at[0])
    load.start()
    labels, copies = labels_and_copies(occ_ref, occupied)
    pos = pos_ref[0]
    for r in range(dests):
        ref = mate_ref if r & 1 else own_ref
        block = ref[((r >> 1) & 1) * (dests // 4) + (r >> 2)][:rows].astype(jnp.float32)
        xs_ref[pl.ds((pos ^ r) * per_device, per_device)] = block.reshape(
            per_device, occupied, LANES
        )
    u = u_ref[...]
    left = jnp.concatenate([ref[...].astype(jnp.float32) for ref in cycs], axis=0)
    left = left.reshape(rows, LANES).astype(jnp.bfloat16)
    load.wait()
    for j in range(occupied):
        c = contract_last(left, xs_ref[:, j, :].astype(jnp.bfloat16))
        for i in range(occupied):
            e = 2 * i + copies[j]
            part = c[i * per_device : (i + 1) * per_device]
            acc_ref[e] = acc_ref[e] + jnp.where(u == (labels[i] ^ labels[j]), part, 0.0)
    store = pltpu.make_async_copy(acc_ref, out_ref, sems.at[0])
    store.start()

    pieces_of = payload_pieces(per_device, pairs, dests)
    lane = lax.broadcasted_iota(jnp.int32, (8, LANES), 1)

    def group(g, top):
        rows = pl.ds(pl.multiple_of(g * 8, 8), 8)
        tiles = {}
        for e in range(pairs):
            for v in range(virtuals // LANES):
                x = acc_ref[e, rows, v * LANES : (v + 1) * LANES]
                top = jnp.maximum(top, jnp.abs(x))
                tiles[e, v] = x
        rolled = {}
        for (q, t), pieces in pieces_of.items():
            acc = None
            for first, e, v, shift in pieces:
                if (e, v, shift) not in rolled:
                    x = tiles[e, v]
                    rolled[e, v, shift] = pltpu.roll(x, shift, axis=1) if shift else x
                x = rolled[e, v, shift]
                acc = x if acc is None else jnp.where(lane >= first, x, acc)
            at = pl.ds(pl.multiple_of(t * per_device + g * 8, 8), 8)
            pay_ref[q, at, :] = acc
        return top

    top = lax.fori_loop(0, per_device // 8, group, jnp.zeros((8, LANES), jnp.float32))
    top = jnp.max(jnp.max(top, axis=0, keepdims=True), axis=1, keepdims=True)
    k = jnp.floor(TOP_EXPONENT - jnp.log2(jnp.maximum(top, 1e-30)))
    scale = jnp.exp2(k)
    count = pay_ref.shape[1]
    row = lax.broadcasted_iota(jnp.int32, (count, LANES), 0)
    data_rows = (virtuals // LANES) * per_device
    for q in range(dests):
        z = pay_ref[q] * scale
        z2 = z * z
        z4 = z2 * z2
        y = jnp.where(row >= data_rows, k, z4 * z4 * z)
        send_ref[q] = y.astype(jnp.bfloat16)
    store.wait()


def join_kernel(occ_ref, half_ref, recv_ref, u_ref, out_ref, dec_ref, mir_ref):
    i = pl.program_id(0)
    occupied = occ_ref.shape[0]
    _, per_device, virtuals = half_ref.shape
    dests = recv_ref.shape[0]
    tiles = virtuals // LANES
    labels, copies = labels_and_copies(occ_ref, occupied)

    @pl.when(i == 0)
    def _():
        for p in range(dests):
            block = recv_ref[p].astype(jnp.float32)
            k = block[tiles * per_device : tiles * per_device + 1, 0:1]
            y = block[: tiles * per_device]
            size = jnp.exp2(jnp.log2(jnp.maximum(jnp.abs(y), 2.0**-126)) * (1.0 / POWER) - k)
            x = jnp.where(y < 0, -size, jnp.where(y > 0, size, 0.0))
            for t in range(tiles):
                dec_ref[t, p * per_device : (p + 1) * per_device, :] = x[
                    t * per_device : (t + 1) * per_device
                ]
        for t in range(tiles):
            mir_ref[t * LANES : (t + 1) * LANES, :] = dec_ref[t].T

    own = occ_ref[i]
    copy = jnp.int32(0)
    for k in range(occupied):
        copy = copy + jnp.logical_and(labels[k] == own, k < i).astype(jnp.int32)
    u = u_ref[...]
    for j in range(occupied):
        at = pl.ds(pl.multiple_of((2 * j + copy) * per_device, 8), per_device)
        total = half_ref[copies[j]] + mir_ref[at, :]
        out_ref[0, j] = jnp.where(u == (own ^ labels[j]), total, 0.0)


def permute(x, flip, size):
    return lax.ppermute(x, "vir", [(n, n ^ flip) for n in range(size)])


def body(dests, amps, fock_vir, fock_occ, ladder_ints, cycle_ints, occ_irrep, vir_irrep):
    occupied, _, per_device, virtuals = amps.shape
    pairs = 2 * occupied
    tiles = virtuals // LANES
    rows = occupied * per_device
    kw = ladder_ints.shape[2]
    f32, bf16 = jnp.float32, jnp.bfloat16
    position = lax.axis_index("vir").astype(jnp.int32)
    pos = position.reshape(1)
    vir_local = lax.dynamic_slice_in_dim(vir_irrep, position * per_device, per_device)
    u = jnp.bitwise_xor(vir_local[:, None], vir_irrep[None, :])
    smem = pl.BlockSpec(memory_space=pltpu.SMEM)

    def whole(shape):
        return pl.BlockSpec(shape, lambda n: (0,) * len(shape))

    def cost(flops, size):
        return pl.CostEstimate(flops=flops, bytes_accessed=size, transcendentals=0)

    anywhere = pl.BlockSpec(memory_space=pl.ANY)
    quarter = dests // 4
    block_rows = rows + 16
    block, mix = pl.pallas_call(
        prep_kernel,
        grid=(1,),
        out_shape=(
            jax.ShapeDtypeStruct((block_rows, LANES), bf16),
            jax.ShapeDtypeStruct((rows, rows), bf16),
        ),
        in_specs=[
            smem,
            whole(fock_occ.shape),
            whole(cycle_ints.shape),
            pl.BlockSpec((occupied, occupied, 16, LANES), lambda n: (0, 0, 0, 0)),
        ],
        out_specs=(whole((block_rows, LANES)), whole((rows, rows))),
        compiler_params=params(8),
        cost_estimate=cost(0, 500000),
    )(pos, fock_occ, cycle_ints, amps)
    block = block.reshape(1, block_rows, LANES)

    flat_amps = amps.reshape(occupied, rows, virtuals)
    parts = (2, 4, 2)
    wide = 2

    def fock_part(n, after):
        first, count = sum(parts[:n]), parts[n]
        return pl.pallas_call(
            functools.partial(fock_kernel, first),
            grid=(count // wide,),
            out_shape=(
                jax.ShapeDtypeStruct((2 * count, per_device, virtuals), f32),
                jax.ShapeDtypeStruct((count, per_device, LANES), bf16),
            ),
            in_specs=[
                smem,
                pl.BlockSpec((wide, rows, virtuals), lambda i: (i + first // wide, 0, 0)),
                whole(fock_vir.shape),
                whole(mix.shape),
                whole(u.shape),
                anywhere,
            ],
            out_specs=(
                pl.BlockSpec((2 * wide, per_device, virtuals), lambda i: (i, 0, 0)),
                pl.BlockSpec((wide, per_device, LANES), lambda i: (i, 0, 0)),
            ),
            scratch_shapes=[pltpu.VMEM((occupied, per_device, virtuals), f32)],
            compiler_params=params(12),
            cost_estimate=cost(3 * count * rows * virtuals * virtuals, 2 * 10**6),
        )(occ_irrep, flat_amps, fock_vir, mix, u, after)

    z1, z2, z3 = [permute(block, m << 2, dests) for m in range(1, quarter)]
    half0, cyc0 = fock_part(0, mix)
    near = stack([block, z1], half0)
    near_y = permute(near, 2, dests)
    half1, cyc1 = fock_part(1, near)
    far = stack([z2, z3], half1)
    far_y = permute(far, 2, dests)
    half2, cyc2 = fock_part(2, far)
    own_blocks = stack([near, far, near_y, far_y], half2)
    win = pl.pallas_call(
        unpack_kernel,
        grid=(1,),
        out_shape=jax.ShapeDtypeStruct((occupied * occupied, LANES), bf16),
        in_specs=[
            smem,
            pl.BlockSpec((dests // 2, 16, LANES), lambda n: (0, rows // 16, 0)),
            anywhere,
        ],
        out_specs=whole((occupied * occupied, LANES)),
        compiler_params=params(4),
        cost_estimate=cost(0, 10**5),
    )(pos, own_blocks, own_blocks)
    win_mate = permute(win, 1, dests)
    mate_blocks = permute(own_blocks, 1, dests)

    half = pl.pallas_call(
        functools.partial(ladder_kernel, parts),
        grid=(per_device // 8,),
        out_shape=jax.ShapeDtypeStruct((pairs, per_device, virtuals), f32),
        in_specs=[smem, whole(win.shape), whole(win.shape)]
        + [pl.BlockSpec((2 * count, 8, virtuals), lambda n: (0, n, 0)) for count in parts]
        + [whole(u.shape), pl.BlockSpec((8, virtuals, kw), lambda n: (n, 0, 0))],
        out_specs=pl.BlockSpec((pairs, 8, virtuals), lambda n: (0, n, 0)),
        scratch_shapes=[
            pltpu.VMEM((occupied * occupied, LANES), f32),
            pltpu.VMEM((occupied * occupied, LANES), f32),
            pltpu.VMEM((pairs, 8, virtuals), f32),
        ],
        compiler_params=params(16),
        cost_estimate=cost(4 * occupied * rows * virtuals * LANES, 9 * 10**6),
    )(occ_irrep, win, win_mate, half0, half1, half2, u, ladder_ints)

    send_rows = tiles * per_device + 8
    vmem = pl.BlockSpec(memory_space=pltpu.VMEM)
    half, send = pl.pallas_call(
        functools.partial(cycle_kernel, parts),
        out_shape=(
            jax.ShapeDtypeStruct(half.shape, f32),
            jax.ShapeDtypeStruct((dests, send_rows, LANES), bf16),
        ),
        in_specs=[smem, smem] + [vmem] * 5 + [anywhere, vmem],
        out_specs=(anywhere, vmem),
        scratch_shapes=[
            pltpu.VMEM((virtuals, occupied, LANES), f32),
            pltpu.VMEM(half.shape, f32),
            pltpu.VMEM((dests, send_rows, LANES), f32),
            pltpu.SemaphoreType.DMA((1,)),
        ],
        compiler_params=params(24),
        cost_estimate=cost(2 * occupied * rows * virtuals * LANES, 8 * 10**6),
    )(pos, occ_irrep, own_blocks, mate_blocks, cyc0, cyc1, cyc2, half, u)

    recv = lax.all_to_all(send, "vir", split_axis=0, concat_axis=0, tiled=True)

    return pl.pallas_call(
        join_kernel,
        grid=(occupied,),
        out_shape=jax.ShapeDtypeStruct((occupied, occupied, per_device, virtuals), f32),
        in_specs=[
            smem,
            pl.BlockSpec((2, per_device, virtuals), lambda n: (n, 0, 0)),
            whole(recv.shape),
            whole(u.shape),
        ],
        out_specs=pl.BlockSpec((1, occupied, per_device, virtuals), lambda n: (n, 0, 0, 0)),
        scratch_shapes=[
            pltpu.VMEM((tiles, virtuals, LANES), f32),
            pltpu.VMEM((tiles * LANES, virtuals), f32),
        ],
        compiler_params=params(16),
        cost_estimate=cost(10**6, 10**7),
    )(occ_irrep, half, recv, u)


def solution(mesh):
    dests = mesh.shape["vir"]

    def run(amps, *rest):
        occupied, _, per_device, virtuals = amps.shape
        tiled = (
            dests == 16
            and per_device % 8 == 0
            and virtuals % LANES == 0
            and 2 * occupied * per_device == virtuals
            and rest[2].shape[2] == LANES
            and rest[3].shape[2] == LANES
        )
        return body(dests, amps, *rest) if tiled else plain_body(amps, *rest)

    return jax.shard_map(
        run,
        mesh=mesh,
        in_specs=(
            P("groups", None, "vir", None),
            P("groups", None),
            P("groups", None),
            P("vir", "groups", None),
            P("vir", "groups", None),
            P("groups"),
            P("groups"),
        ),
        out_specs=P("groups", None, "vir", None),
        check_vma=False,
    )
```

```python
import functools

import jax
import jax.numpy as jnp
from jax import lax
from jax.experimental import pallas as pl
from jax.experimental.pallas import tpu as pltpu
from jax.sharding import PartitionSpec as P

DW = 8
CW = 16
LANES = 128
POWER = 9
TOP_EXPONENT = 13


def contract_last(left_side, right_side):
    return lax.dot_general(
        left_side, right_side, (((1,), (1,)), ((), ())), preferred_element_type=jnp.float32
    )


def plain_body(amps, fock_vir, fock_occ, ladder_ints, cycle_ints, occ_irrep, vir_irrep):
    occupied = amps.shape[0]
    per_device = amps.shape[2]
    virtuals = amps.shape[3]
    pair_count = occupied * occupied
    position = lax.axis_index("vir")
    fock_term = jnp.dot(
        amps.reshape(pair_count * per_device, virtuals),
        fock_vir,
        preferred_element_type=jnp.float32,
    ).reshape(occupied, occupied, per_device, virtuals)
    occ_term = jnp.einsum("ikab,kj->ijab", amps, fock_occ, preferred_element_type=jnp.float32)
    flat_ints = ladder_ints.reshape(per_device * virtuals, ladder_ints.shape[2])
    local_window = amps[:, :, 0:1, :DW]
    local_cycle = amps[:, :, :, :CW]
    segment = lax.all_gather(local_window, "vir", axis=2, tiled=True)
    width = segment.shape[2] * DW
    ladder = contract_last(segment.reshape(pair_count, width), flat_ints)
    left_side = jnp.transpose(local_cycle, (0, 2, 1, 3)).reshape(
        occupied * per_device, occupied * CW
    )
    segment = lax.all_gather(cycle_ints, "vir", axis=0, tiled=True)
    right_side = segment.reshape(segment.shape[0] * occupied, occupied * CW)
    cycle_block = contract_last(left_side, right_side).reshape(
        occupied, per_device, segment.shape[0], occupied
    )
    cycle_part = jnp.transpose(cycle_block, (0, 3, 1, 2))
    half_sum = (
        fock_term - occ_term + ladder.reshape(occupied, occupied, per_device, virtuals) + cycle_part
    )
    vir_local = lax.dynamic_slice_in_dim(vir_irrep, position * per_device, per_device)
    occ_pair = jnp.bitwise_xor(occ_irrep[:, None], occ_irrep[None, :])
    vir_pair = jnp.bitwise_xor(vir_local[:, None], vir_irrep[None, :])
    received = lax.all_to_all(half_sum, "vir", split_axis=3, concat_axis=2, tiled=True)
    mirrored = jnp.transpose(received, (1, 0, 3, 2))
    product_irrep = jnp.bitwise_xor(occ_pair[:, :, None, None], vir_pair[None, None, :, :])
    allowed = jnp.where(product_irrep == 0, jnp.float32(1.0), jnp.float32(0.0))
    return allowed * (half_sum + mirrored)


def params(mib):
    return pltpu.CompilerParams(vmem_limit_bytes=mib * 2**20)


def labels_and_copies(occ_ref, occupied):
    labels = [occ_ref[j] for j in range(occupied)]
    copies = []
    for j in range(occupied):
        s = jnp.int32(0)
        for k in range(j):
            s = s + (labels[k] == labels[j]).astype(jnp.int32)
        copies.append(s)
    return labels, copies


def prep_kernel(cyc_ref, amps_ref, block_ref):
    occupied = amps_ref.shape[0]
    rows = cyc_ref.shape[0]
    block_ref[:rows, :] = cyc_ref[...]
    lane = lax.broadcasted_iota(jnp.int32, (occupied, LANES), 1)
    packed = jnp.zeros((occupied, LANES), jnp.float32)
    for j in range(occupied):
        w = jnp.where(lane < DW, amps_ref[:, j, 0, :].astype(jnp.float32), 0.0)
        packed = packed + (pltpu.roll(w, j * DW, axis=1) if j else w)
    packed = jnp.concatenate([packed, jnp.zeros_like(packed)], axis=0)
    block_ref[rows:, :] = packed.astype(jnp.bfloat16)


def mix_kernel(occ_vals_ref, after_ref, mix_ref):
    rows = mix_ref.shape[0]
    occupied = occ_vals_ref.shape[0]
    per_device = rows // occupied
    row = lax.broadcasted_iota(jnp.int32, (rows, occupied), 0)
    start = lax.broadcasted_iota(jnp.int32, (rows, occupied), 1) * per_device
    in_block = jnp.logical_and(row >= start, row < start + per_device).astype(jnp.bfloat16)
    row = lax.broadcasted_iota(jnp.int32, (rows, per_device), 0)
    at = lax.broadcasted_iota(jnp.int32, (rows, per_device), 1)
    same = row == at
    for n in range(1, occupied):
        same = jnp.logical_or(same, row == at + n * per_device)
    same = same.astype(jnp.bfloat16)
    left = contract_last(in_block, occ_vals_ref[...]).astype(jnp.bfloat16)
    mix = contract_last(left, in_block) * contract_last(same, same)
    mix_ref[...] = mix.astype(jnp.bfloat16)


def fock_kernel(first, occ_ref, amps_ref, fock_ref, mix_ref, u_ref, after_ref, half_ref, cyc_ref, hs_ref):
    wide, rows, virtuals = amps_ref.shape
    _, per_device, _ = half_ref.shape
    occupied = occ_ref.shape[0]
    labels, copies = labels_and_copies(occ_ref, occupied)
    u = u_ref[...]
    h = jnp.dot(
        amps_ref[...].reshape(wide * rows, virtuals),
        fock_ref[...],
        preferred_element_type=jnp.float32,
    )
    for w in range(wide):
        a = amps_ref[w]
        mixed = jnp.dot(mix_ref[...], a, preferred_element_type=jnp.float32)
        hs_ref[...] = (h[w * rows : (w + 1) * rows] - mixed).reshape(hs_ref.shape)
        own = occ_ref[pl.program_id(0) * wide + w + first]
        for j in range(occupied):
            at = 2 * w + copies[j]
            half_ref[at] = jnp.where(u == (own ^ labels[j]), hs_ref[j], half_ref[at])
        head = a[:, :LANES].astype(jnp.float32)
        lane = lax.broadcasted_iota(jnp.int32, (per_device, LANES), 1)
        acc = jnp.zeros((per_device, LANES), jnp.float32)
        for k in range(occupied):
            piece = jnp.where(lane < CW, head[k * per_device : (k + 1) * per_device], 0.0)
            acc = acc + (pltpu.roll(piece, k * CW, axis=1) if k else piece)
        cyc_ref[w] = acc.astype(jnp.bfloat16)


def stack(blocks, after):
    count = len(blocks)

    def kernel(*refs):
        out = refs[count + 1]
        at = 0
        for n in range(count):
            head = blocks[n].shape[0]
            out[at : at + head] = refs[n][...]
            at += head

    vmem = pl.BlockSpec(memory_space=pltpu.VMEM)
    shape = (sum(b.shape[0] for b in blocks),) + blocks[0].shape[1:]
    return pl.pallas_call(
        kernel,
        out_shape=jax.ShapeDtypeStruct(shape, blocks[0].dtype),
        in_specs=[vmem] * count + [pl.BlockSpec(memory_space=pl.ANY)],
        out_specs=vmem,
        compiler_params=params(4),
        cost_estimate=pl.CostEstimate(flops=0, bytes_accessed=10**6, transcendentals=0),
    )(*blocks, after)


def unpack_kernel(pos_ref, blocks_ref, after_ref, win_ref):
    count, _, lanes = blocks_ref.shape
    occupied = win_ref.shape[0] // 8
    lane = lax.broadcasted_iota(jnp.int32, (8, lanes), 1)
    quarter = count // 2
    parts = []
    for j in range(occupied):
        total = jnp.zeros((8, lanes), jnp.float32)
        for n in range(count):
            flip = ((n // quarter) << 1) | ((n % quarter) << 2)
            p = pos_ref[0] ^ flip
            w = blocks_ref[n][:8].astype(jnp.float32)
            shift = lax.rem(p * DW - j * DW + lanes, lanes)
            w = jnp.where(jnp.logical_and(lane >= j * DW, lane < (j + 1) * DW), w, 0.0)
            total = total + pltpu.roll(w, shift, axis=1)
        parts.append(total)
    win_ref[...] = jnp.concatenate(parts, axis=0).astype(jnp.bfloat16)


def payload_pieces(per_device, pairs, dests):
    out = {}
    for q in range(dests):
        for e in range(pairs):
            start = 0
            while start < per_device:
                src = q * per_device + start
                dst = e * per_device + start
                length = min(LANES - src % LANES, LANES - dst % LANES, per_device - start)
                out.setdefault((q, dst // LANES), []).append(
                    (dst % LANES, e, src // LANES, (dst - src) % LANES)
                )
                start += length
    return out


def ladder_kernel(parts, occ_ref, win0_ref, win1_ref, *refs):
    halves = refs[: len(parts)]
    u_ref, lad_ref, out_ref, w1_ref, w2_ref, ls_ref = refs[len(parts) :]
    step = pl.program_id(0)
    occupied = occ_ref.shape[0]
    pairs, _, virtuals = out_ref.shape
    labels, copies = labels_and_copies(occ_ref, occupied)

    @pl.when(step == 0)
    def _():
        w1_ref[...] = win0_ref[...].astype(jnp.float32) + win1_ref[...].astype(jnp.float32)
        for i in range(occupied):
            for j in range(occupied):
                row = (labels[i] ^ labels[j]) * pairs + 2 * i + copies[j]
                w2_ref[pl.ds(row, 1), :] = w1_ref[j * occupied + i : j * occupied + i + 1, :]

    w2 = w2_ref[...].astype(jnp.bfloat16)
    u8 = u_ref[pl.ds(pl.multiple_of(step * 8, 8), 8), :]
    for a in range(8):
        ladder = contract_last(w2, lad_ref[a])
        ua = u8[a : a + 1, :]
        sel = ladder[0:pairs]
        for v in range(1, 4):
            sel = jnp.where(ua == v, ladder[v * pairs : (v + 1) * pairs], sel)
        ls_ref[:, a, :] = sel
    at = 0
    for part, count in zip(halves, parts):
        out_ref[at : at + 2 * count] = part[...] + ls_ref[at : at + 2 * count]
        at += 2 * count


def cycle_kernel(chunk, before, parts, pos_ref, occ_ref, *refs):
    i0, i1, t0, t1 = chunk
    refs = list(refs)
    if before is None:
        own_ref, mate_ref = refs.pop(0), refs.pop(0)
    else:
        x_ref, prev_ref = refs.pop(0), refs.pop(0)
    cycs = [refs.pop(0) for _ in parts]
    half_ref, u_ref, out_ref, send_ref = (refs.pop(0) for _ in range(4))
    if before is None:
        x_ref = refs.pop(0)
    orb_ref, cs_ref, hin_ref, pay_ref, sems = (refs.pop(0) for _ in range(5))
    occupied = occ_ref.shape[0]
    pairs = 2 * occupied
    _, per_device, virtuals = hin_ref.shape
    dests = send_ref.shape[0]
    rows = occupied * per_device
    tiles = virtuals // LANES
    load = pltpu.make_async_copy(half_ref.at[2 * i0 : 2 * i1], hin_ref, sems.at[0])
    load.start()
    labels, copies = labels_and_copies(occ_ref, occupied)
    for j in range(occupied):
        orb_ref[2 * labels[j] + copies[j]] = jnp.int32(j)
    if before is None:
        (xs_ref,) = refs
        for r in range(dests):
            ref = mate_ref if r & 1 else own_ref
            block = ref[((r >> 1) & 1) * (dests // 4) + (r >> 2)][:rows].astype(jnp.float32)
            xs_ref[pl.ds((pos_ref[0] ^ r) * per_device, per_device)] = block.reshape(
                per_device, occupied, LANES
            )
        for j in range(occupied):
            x_ref[j] = xs_ref[:, j, :].astype(jnp.bfloat16)
    left = jnp.concatenate([ref[...].astype(jnp.float32) for ref in cycs], axis=0)[i0:i1]
    left = left.reshape((i1 - i0) * per_device, LANES).astype(jnp.bfloat16)
    for j in range(occupied):
        cs_ref[j] = contract_last(left, x_ref[j]).reshape(i1 - i0, per_device, virtuals)
    load.wait()

    pieces_of = payload_pieces(per_device, pairs, dests)
    lane = lax.broadcasted_iota(jnp.int32, (8, LANES), 1)
    choices = {
        (i, s): [orb_ref[2 * (labels[i] ^ n) + s] for n in range(4)]
        for i in range(i0, i1)
        for s in range(2)
    }

    def group(g, top):
        rows = pl.ds(pl.multiple_of(g * 8, 8), 8)
        found = {}

        def fill(e):
            nonlocal top
            for v in range(tiles):
                at = slice(v * LANES, (v + 1) * LANES)
                if e < 2 * i0:
                    x = prev_ref[e - 2 * before, rows, at]
                else:
                    js = choices[e // 2, e % 2]
                    uv = u_ref[rows, at]
                    x = cs_ref[js[0], e // 2 - i0, rows, at]
                    for n in range(1, 4):
                        x = jnp.where(uv == n, cs_ref[js[n], e // 2 - i0, rows, at], x)
                    x = x + hin_ref[e - 2 * i0, rows, at]
                    out_ref[e - 2 * i0, rows, at] = x
                top = jnp.maximum(top, jnp.abs(x))
                found[e, v] = x

        for t in range(t0, t1):
            first_e = t * LANES // per_device
            last_e = min(((t + 1) * LANES - 1) // per_device, pairs - 1)
            for e in range(first_e, last_e + 1):
                if (e, 0) not in found:
                    fill(e)
            for q in range(dests):
                acc = None
                for first, e, v, shift in pieces_of[q, t]:
                    x = pltpu.roll(found[e, v], shift, axis=1) if shift else found[e, v]
                    acc = x if acc is None else jnp.where(lane >= first, x, acc)
                at = pl.ds(pl.multiple_of((t - t0) * per_device + g * 8, 8), 8)
                pay_ref[q, at, :] = acc
        return top

    top = lax.fori_loop(0, per_device // 8, group, jnp.zeros((8, LANES), jnp.float32))
    top = jnp.max(jnp.max(top, axis=0, keepdims=True), axis=1, keepdims=True)
    k = jnp.floor(TOP_EXPONENT - jnp.log2(jnp.maximum(top, 1e-30)))
    scale = jnp.exp2(k)
    row = lax.broadcasted_iota(jnp.int32, pay_ref.shape[1:], 0)
    for q in range(dests):
        z = pay_ref[q] * scale
        z2 = z * z
        z4 = z2 * z2
        y = jnp.where(row >= (t1 - t0) * per_device, k, z4 * z4 * z)
        send_ref[q] = y.astype(jnp.bfloat16)


def join_kernel(chunks, first_j, occ_ref, u_ref, *refs):
    count = len(chunks)
    halves, recvs = refs[:count], refs[count : 2 * count]
    out_ref, dec_ref, mir_ref = refs[-3:]
    step = pl.program_id(0)
    j = step + first_j
    occupied = occ_ref.shape[0]
    per_device, virtuals = u_ref.shape
    labels, copies = labels_and_copies(occ_ref, occupied)
    spread = 2 * per_device
    for (_, _, t0, t1), recv_ref in zip(chunks, recvs):
        dests = recv_ref.shape[0]
        for t in range(t0, t1):
            if (t + 1) * LANES <= first_j * spread:
                continue
            need = max(t * LANES // spread - first_j, 0)

            @pl.when(step == need)
            def _(t=t, t0=t0, t1=t1, recv_ref=recv_ref, dests=dests):
                start = (t - t0) * per_device
                low, high = start // 16 * 16, (start + per_device + 15) // 16 * 16
                end = (t1 - t0) * per_device
                for p in range(dests):
                    tail = recv_ref[p, end // 16 * 16 : end // 16 * 16 + 16, :]
                    k = tail.astype(jnp.float32)[end % 16 : end % 16 + 1, 0:1]
                    y = recv_ref[p, low:high, :].astype(jnp.float32)
                    y = y[start - low : start - low + per_device]
                    size = jnp.log2(jnp.maximum(jnp.abs(y), 2.0**-126)) * (1.0 / POWER) - k
                    size = jnp.exp2(size)
                    x = jnp.where(y < 0, -size, jnp.where(y > 0, size, 0.0))
                    dec_ref[p * per_device : (p + 1) * per_device, :] = x
                mir_ref[t * LANES : (t + 1) * LANES, :] = dec_ref[...].T

    own = occ_ref[j]
    copy = jnp.int32(0)
    for k in range(occupied):
        copy = copy + jnp.logical_and(labels[k] == own, k < j).astype(jnp.int32)
    u = u_ref[...]
    for (i0, i1, _, _), half_ref in zip(chunks, halves):
        for i in range(i0, i1):
            at = pl.ds(pl.multiple_of((2 * j + copies[i]) * per_device, 8), per_device)
            total = half_ref[2 * (i - i0) + copy] + mir_ref[at, :]
            out_ref[i, 0] = jnp.where(u == (own ^ labels[i]), total, 0.0)


def permute(x, flip, size):
    return lax.ppermute(x, "vir", [(n, n ^ flip) for n in range(size)])


def body(dests, amps, fock_vir, fock_occ, ladder_ints, cycle_ints, occ_irrep, vir_irrep):
    occupied, _, per_device, virtuals = amps.shape
    pairs = 2 * occupied
    tiles = virtuals // LANES
    rows = occupied * per_device
    kw = ladder_ints.shape[2]
    f32, bf16 = jnp.float32, jnp.bfloat16
    position = lax.axis_index("vir").astype(jnp.int32)
    pos = position.reshape(1)
    vir_local = lax.dynamic_slice_in_dim(vir_irrep, position * per_device, per_device)
    u = jnp.bitwise_xor(vir_local[:, None], vir_irrep[None, :])
    smem = pl.BlockSpec(memory_space=pltpu.SMEM)

    def whole(shape):
        return pl.BlockSpec(shape, lambda n: (0,) * len(shape))

    def cost(flops, size):
        return pl.CostEstimate(flops=flops, bytes_accessed=size, transcendentals=0)

    anywhere = pl.BlockSpec(memory_space=pl.ANY)
    quarter = dests // 4
    block_rows = rows + 16
    block = pl.pallas_call(
        prep_kernel,
        grid=(1,),
        out_shape=jax.ShapeDtypeStruct((block_rows, LANES), bf16),
        in_specs=[
            whole((rows, LANES)),
            pl.BlockSpec((occupied, occupied, 16, LANES), lambda n: (0, 0, 0, 0)),
        ],
        out_specs=whole((block_rows, LANES)),
        compiler_params=params(60),
        cost_estimate=cost(0, 500000),
    )(cycle_ints.reshape(rows, LANES), amps)
    block = block.reshape(1, block_rows, LANES)
    vmem = pl.BlockSpec(memory_space=pltpu.VMEM)
    mix = pl.pallas_call(
        mix_kernel,
        out_shape=jax.ShapeDtypeStruct((rows, rows), bf16),
        in_specs=[vmem, anywhere],
        out_specs=vmem,
        compiler_params=params(4),
        cost_estimate=cost(10**7, 300000),
    )(fock_occ, block)

    flat_amps = amps.reshape(occupied, rows, virtuals)
    parts = (2, 4, 2)
    wide = 2

    def fock_part(n, after):
        first, count = sum(parts[:n]), parts[n]
        return pl.pallas_call(
            functools.partial(fock_kernel, first),
            grid=(count // wide,),
            out_shape=(
                jax.ShapeDtypeStruct((2 * count, per_device, virtuals), f32),
                jax.ShapeDtypeStruct((count, per_device, LANES), bf16),
            ),
            in_specs=[
                smem,
                pl.BlockSpec((wide, rows, virtuals), lambda i: (i + first // wide, 0, 0)),
                whole(fock_vir.shape),
                whole(mix.shape),
                whole(u.shape),
                anywhere,
            ],
            out_specs=(
                pl.BlockSpec((2 * wide, per_device, virtuals), lambda i: (i, 0, 0)),
                pl.BlockSpec((wide, per_device, LANES), lambda i: (i, 0, 0)),
            ),
            scratch_shapes=[pltpu.VMEM((occupied, per_device, virtuals), f32)],
            compiler_params=params(12),
            cost_estimate=cost(3 * count * rows * virtuals * virtuals, 2 * 10**6),
        )(occ_irrep, flat_amps, fock_vir, mix, u, after)

    z1, z2, z3 = [permute(block, m << 2, dests) for m in range(1, quarter)]
    half0, cyc0 = fock_part(0, mix)
    near = stack([block, z1], half0)
    near_y = permute(near, 2, dests)
    half1, cyc1 = fock_part(1, near)
    far = stack([z2, z3], half1)
    far_y = permute(far, 2, dests)
    half2, cyc2 = fock_part(2, far)
    own_blocks = stack([near, far, near_y, far_y], half2)
    win = pl.pallas_call(
        unpack_kernel,
        grid=(1,),
        out_shape=jax.ShapeDtypeStruct((occupied * occupied, LANES), bf16),
        in_specs=[
            smem,
            pl.BlockSpec((dests // 2, 16, LANES), lambda n: (0, rows // 16, 0)),
            anywhere,
        ],
        out_specs=whole((occupied * occupied, LANES)),
        compiler_params=params(4),
        cost_estimate=cost(0, 10**5),
    )(pos, own_blocks, own_blocks)
    win_mate = permute(win, 1, dests)
    mate_blocks = permute(own_blocks, 1, dests)

    half = pl.pallas_call(
        functools.partial(ladder_kernel, parts),
        grid=(per_device // 8,),
        out_shape=jax.ShapeDtypeStruct((pairs, per_device, virtuals), f32),
        in_specs=[smem, whole(win.shape), whole(win.shape)]
        + [pl.BlockSpec((2 * count, 8, virtuals), lambda n: (0, n, 0)) for count in parts]
        + [whole(u.shape), pl.BlockSpec((8, virtuals, kw), lambda n: (n, 0, 0))],
        out_specs=pl.BlockSpec((pairs, 8, virtuals), lambda n: (0, n, 0)),
        scratch_shapes=[
            pltpu.VMEM((occupied * occupied, LANES), f32),
            pltpu.VMEM((occupied * occupied, LANES), f32),
            pltpu.VMEM((pairs, 8, virtuals), f32),
        ],
        compiler_params=params(16),
        cost_estimate=cost(4 * occupied * rows * virtuals * LANES, 9 * 10**6),
    )(occ_irrep, win, win_mate, half0, half1, half2, u, ladder_ints)

    chunks = ((0, occupied, 0, tiles),)
    joins = ((0, occupied),)
    cycs = (cyc0, cyc1, cyc2)
    halves, recvs = [], []
    x_shape = (occupied, virtuals, LANES)
    for n, chunk in enumerate(chunks):
        i0, i1, t0, t1 = chunk
        wide_i = i1 - i0
        send_rows = ((t1 - t0) * per_device + 8 + 15) // 16 * 16
        half_shape = (2 * wide_i, per_device, virtuals)
        out_shape = [
            jax.ShapeDtypeStruct(half_shape, f32),
            jax.ShapeDtypeStruct((dests, send_rows, LANES), bf16),
        ]
        scratch = [
            pltpu.SMEM((occupied,), jnp.int32),
            pltpu.VMEM((occupied, wide_i, per_device, virtuals), f32),
            pltpu.VMEM(half_shape, f32),
            pltpu.VMEM((dests, send_rows, LANES), f32),
            pltpu.SemaphoreType.DMA((1,)),
        ]
        if n == 0:
            given = (own_blocks, mate_blocks)
            out_shape.append(jax.ShapeDtypeStruct(x_shape, bf16))
            scratch.append(pltpu.VMEM((virtuals, occupied, LANES), f32))
        else:
            given = (x_all, halves[-1])
        got = pl.pallas_call(
            functools.partial(cycle_kernel, chunk, chunks[n - 1][0] if n else None, parts),
            out_shape=out_shape,
            in_specs=[smem, smem] + [vmem] * 5 + [anywhere, vmem],
            out_specs=[vmem] * len(out_shape),
            scratch_shapes=scratch,
            compiler_params=params(28),
            cost_estimate=cost(2 * wide_i * rows * virtuals * LANES, 8 * 10**6),
        )(pos, occ_irrep, *given, *cycs, half, u)
        if n == 0:
            x_all = got[2]
        halves.append(got[0])
        recvs.append(
            lax.all_to_all(got[1], "vir", split_axis=0, concat_axis=0, tiled=True)
        )

    out = None
    for n, (j0, j1) in enumerate(joins):
        used = chunks if n + 1 == len(joins) else chunks
        extra = () if out is None else (out,)
        out = pl.pallas_call(
            functools.partial(join_kernel, used, j0),
            grid=(j1 - j0,),
            out_shape=jax.ShapeDtypeStruct((occupied, occupied, per_device, virtuals), f32),
            in_specs=[smem, whole(u.shape)]
            + [whole(x.shape) for x in halves]
            + [whole(x.shape) for x in recvs]
            + [anywhere] * len(extra),
            out_specs=pl.BlockSpec(
                (occupied, 1, per_device, virtuals), lambda n, j0=j0: (0, n + j0, 0, 0)
            ),
            scratch_shapes=[
                pltpu.VMEM((virtuals, LANES), f32),
                pltpu.VMEM((tiles * LANES, virtuals), f32),
            ],
            compiler_params=params(16),
            cost_estimate=cost(10**6, 10**7),
        )(occ_irrep, u, *halves, *recvs, *extra)
    return out


def solution(mesh):
    dests = mesh.shape["vir"]

    def run(amps, *rest):
        occupied, _, per_device, virtuals = amps.shape
        tiled = (
            dests == 16
            and per_device % 8 == 0
            and virtuals % LANES == 0
            and 2 * occupied * per_device == virtuals
            and rest[2].shape[2] == LANES
            and rest[3].shape[2] == LANES
        )
        return body(dests, amps, *rest) if tiled else plain_body(amps, *rest)

    return jax.shard_map(
        run,
        mesh=mesh,
        in_specs=(
            P("groups", None, "vir", None),
            P("groups", None),
            P("groups", None),
            P("vir", "groups", None),
            P("vir", "groups", None),
            P("groups"),
            P("groups"),
        ),
        out_specs=P("groups", None, "vir", None),
        check_vma=False,
    )
```

```python
import functools

import jax
import jax.numpy as jnp
from jax import lax
from jax.experimental import pallas as pl
from jax.experimental.pallas import tpu as pltpu
from jax.sharding import PartitionSpec as P

DW = 8
CW = 16
LANES = 128
POWER = 9
TOP_EXPONENT = 13


def contract_last(left_side, right_side):
    return lax.dot_general(
        left_side, right_side, (((1,), (1,)), ((), ())), preferred_element_type=jnp.float32
    )


def plain_body(amps, fock_vir, fock_occ, ladder_ints, cycle_ints, occ_irrep, vir_irrep):
    occupied = amps.shape[0]
    per_device = amps.shape[2]
    virtuals = amps.shape[3]
    pair_count = occupied * occupied
    position = lax.axis_index("vir")
    fock_term = jnp.dot(
        amps.reshape(pair_count * per_device, virtuals),
        fock_vir,
        preferred_element_type=jnp.float32,
    ).reshape(occupied, occupied, per_device, virtuals)
    occ_term = jnp.einsum("ikab,kj->ijab", amps, fock_occ, preferred_element_type=jnp.float32)
    flat_ints = ladder_ints.reshape(per_device * virtuals, ladder_ints.shape[2])
    local_window = amps[:, :, 0:1, :DW]
    local_cycle = amps[:, :, :, :CW]
    segment = lax.all_gather(local_window, "vir", axis=2, tiled=True)
    width = segment.shape[2] * DW
    ladder = contract_last(segment.reshape(pair_count, width), flat_ints)
    left_side = jnp.transpose(local_cycle, (0, 2, 1, 3)).reshape(
        occupied * per_device, occupied * CW
    )
    segment = lax.all_gather(cycle_ints, "vir", axis=0, tiled=True)
    right_side = segment.reshape(segment.shape[0] * occupied, occupied * CW)
    cycle_block = contract_last(left_side, right_side).reshape(
        occupied, per_device, segment.shape[0], occupied
    )
    cycle_part = jnp.transpose(cycle_block, (0, 3, 1, 2))
    half_sum = (
        fock_term - occ_term + ladder.reshape(occupied, occupied, per_device, virtuals) + cycle_part
    )
    vir_local = lax.dynamic_slice_in_dim(vir_irrep, position * per_device, per_device)
    occ_pair = jnp.bitwise_xor(occ_irrep[:, None], occ_irrep[None, :])
    vir_pair = jnp.bitwise_xor(vir_local[:, None], vir_irrep[None, :])
    received = lax.all_to_all(half_sum, "vir", split_axis=3, concat_axis=2, tiled=True)
    mirrored = jnp.transpose(received, (1, 0, 3, 2))
    product_irrep = jnp.bitwise_xor(occ_pair[:, :, None, None], vir_pair[None, None, :, :])
    allowed = jnp.where(product_irrep == 0, jnp.float32(1.0), jnp.float32(0.0))
    return allowed * (half_sum + mirrored)


def params(mib):
    return pltpu.CompilerParams(vmem_limit_bytes=mib * 2**20)


def labels_and_copies(occ_ref, occupied):
    labels = [occ_ref[j] for j in range(occupied)]
    copies = []
    for j in range(occupied):
        s = jnp.int32(0)
        for k in range(j):
            s = s + (labels[k] == labels[j]).astype(jnp.int32)
        copies.append(s)
    return labels, copies


def prep_kernel(cyc_ref, amps_ref, block_ref):
    occupied = amps_ref.shape[0]
    rows = cyc_ref.shape[0]
    block_ref[:rows, :] = cyc_ref[...]
    lane = lax.broadcasted_iota(jnp.int32, (occupied, LANES), 1)
    packed = jnp.zeros((occupied, LANES), jnp.float32)
    for j in range(occupied):
        w = jnp.where(lane < DW, amps_ref[:, j, 0, :].astype(jnp.float32), 0.0)
        packed = packed + (pltpu.roll(w, j * DW, axis=1) if j else w)
    packed = jnp.concatenate([packed, jnp.zeros_like(packed)], axis=0)
    block_ref[rows:, :] = packed.astype(jnp.bfloat16)


def mix_kernel(occ_vals_ref, after_ref, mix_ref):
    rows = mix_ref.shape[0]
    occupied = occ_vals_ref.shape[0]
    per_device = rows // occupied
    row = lax.broadcasted_iota(jnp.int32, (rows, occupied), 0)
    start = lax.broadcasted_iota(jnp.int32, (rows, occupied), 1) * per_device
    in_block = jnp.logical_and(row >= start, row < start + per_device).astype(jnp.bfloat16)
    row = lax.broadcasted_iota(jnp.int32, (rows, per_device), 0)
    at = lax.broadcasted_iota(jnp.int32, (rows, per_device), 1)
    same = row == at
    for n in range(1, occupied):
        same = jnp.logical_or(same, row == at + n * per_device)
    same = same.astype(jnp.bfloat16)
    left = contract_last(in_block, occ_vals_ref[...]).astype(jnp.bfloat16)
    mix = contract_last(left, in_block) * contract_last(same, same)
    mix_ref[...] = mix.astype(jnp.bfloat16)


def fock_kernel(first, occ_ref, amps_ref, fock_ref, mix_ref, u_ref, after_ref, half_ref, cyc_ref, hs_ref):
    wide, rows, virtuals = amps_ref.shape
    _, per_device, _ = half_ref.shape
    occupied = occ_ref.shape[0]
    labels, copies = labels_and_copies(occ_ref, occupied)
    u = u_ref[...]
    h = jnp.dot(
        amps_ref[...].reshape(wide * rows, virtuals),
        fock_ref[...],
        preferred_element_type=jnp.float32,
    )
    for w in range(wide):
        a = amps_ref[w]
        mixed = jnp.dot(mix_ref[...], a, preferred_element_type=jnp.float32)
        hs_ref[...] = (h[w * rows : (w + 1) * rows] - mixed).reshape(hs_ref.shape)
        own = occ_ref[pl.program_id(0) * wide + w + first]
        for j in range(occupied):
            at = 2 * w + copies[j]
            half_ref[at] = jnp.where(u == (own ^ labels[j]), hs_ref[j], half_ref[at])
        head = a[:, :LANES].astype(jnp.float32)
        lane = lax.broadcasted_iota(jnp.int32, (per_device, LANES), 1)
        acc = jnp.zeros((per_device, LANES), jnp.float32)
        for k in range(occupied):
            piece = jnp.where(lane < CW, head[k * per_device : (k + 1) * per_device], 0.0)
            acc = acc + (pltpu.roll(piece, k * CW, axis=1) if k else piece)
        cyc_ref[w] = acc.astype(jnp.bfloat16)


def stack(blocks, after):
    count = len(blocks)

    def kernel(*refs):
        out = refs[count + 1]
        at = 0
        for n in range(count):
            head = blocks[n].shape[0]
            out[at : at + head] = refs[n][...]
            at += head

    vmem = pl.BlockSpec(memory_space=pltpu.VMEM)
    shape = (sum(b.shape[0] for b in blocks),) + blocks[0].shape[1:]
    return pl.pallas_call(
        kernel,
        out_shape=jax.ShapeDtypeStruct(shape, blocks[0].dtype),
        in_specs=[vmem] * count + [pl.BlockSpec(memory_space=pl.ANY)],
        out_specs=vmem,
        compiler_params=params(4),
        cost_estimate=pl.CostEstimate(flops=0, bytes_accessed=10**6, transcendentals=0),
    )(*blocks, after)


def unpack_kernel(pos_ref, blocks_ref, after_ref, win_ref):
    count, _, lanes = blocks_ref.shape
    occupied = win_ref.shape[0] // 8
    lane = lax.broadcasted_iota(jnp.int32, (8, lanes), 1)
    quarter = count // 2
    parts = []
    for j in range(occupied):
        total = jnp.zeros((8, lanes), jnp.float32)
        for n in range(count):
            flip = ((n // quarter) << 1) | ((n % quarter) << 2)
            p = pos_ref[0] ^ flip
            w = blocks_ref[n][:8].astype(jnp.float32)
            shift = lax.rem(p * DW - j * DW + lanes, lanes)
            w = jnp.where(jnp.logical_and(lane >= j * DW, lane < (j + 1) * DW), w, 0.0)
            total = total + pltpu.roll(w, shift, axis=1)
        parts.append(total)
    win_ref[...] = jnp.concatenate(parts, axis=0).astype(jnp.bfloat16)


def payload_pieces(per_device, pairs, dests):
    out = {}
    for q in range(dests):
        for e in range(pairs):
            start = 0
            while start < per_device:
                src = q * per_device + start
                dst = e * per_device + start
                length = min(LANES - src % LANES, LANES - dst % LANES, per_device - start)
                out.setdefault((q, dst // LANES), []).append(
                    (dst % LANES, e, src // LANES, (dst - src) % LANES)
                )
                start += length
    return out


def ladder_kernel(parts, occ_ref, win0_ref, win1_ref, *refs):
    halves = refs[: len(parts)]
    u_ref, lad_ref, out_ref, w1_ref, w2_ref, ls_ref = refs[len(parts) :]
    step = pl.program_id(0)
    occupied = occ_ref.shape[0]
    pairs, _, virtuals = out_ref.shape
    labels, copies = labels_and_copies(occ_ref, occupied)

    @pl.when(step == 0)
    def _():
        w1_ref[...] = win0_ref[...].astype(jnp.float32) + win1_ref[...].astype(jnp.float32)
        for i in range(occupied):
            for j in range(occupied):
                row = (labels[i] ^ labels[j]) * pairs + 2 * i + copies[j]
                w2_ref[pl.ds(row, 1), :] = w1_ref[j * occupied + i : j * occupied + i + 1, :]

    w2 = w2_ref[...].astype(jnp.bfloat16)
    u8 = u_ref[pl.ds(pl.multiple_of(step * 8, 8), 8), :]
    for a in range(8):
        ladder = contract_last(w2, lad_ref[a])
        ua = u8[a : a + 1, :]
        sel = ladder[0:pairs]
        for v in range(1, 4):
            sel = jnp.where(ua == v, ladder[v * pairs : (v + 1) * pairs], sel)
        ls_ref[:, a, :] = sel
    at = 0
    for part, count in zip(halves, parts):
        out_ref[at : at + 2 * count] = part[...] + ls_ref[at : at + 2 * count]
        at += 2 * count


def cycle_kernel(chunk, before, parts, pos_ref, occ_ref, *refs):
    i0, i1, t0, t1 = chunk
    refs = list(refs)
    if before is None:
        own_ref, mate_ref = refs.pop(0), refs.pop(0)
    else:
        x_ref, prev_ref = refs.pop(0), refs.pop(0)
    cycs = [refs.pop(0) for _ in parts]
    half_ref, u_ref, out_ref, send_ref = (refs.pop(0) for _ in range(4))
    if before is None:
        x_ref = refs.pop(0)
    orb_ref, cs_ref, hin_ref, pay_ref, sems = (refs.pop(0) for _ in range(5))
    occupied = occ_ref.shape[0]
    pairs = 2 * occupied
    _, per_device, virtuals = hin_ref.shape
    dests = send_ref.shape[0]
    rows = occupied * per_device
    tiles = virtuals // LANES
    load = pltpu.make_async_copy(half_ref.at[2 * i0 : 2 * i1], hin_ref, sems.at[0])
    load.start()
    labels, copies = labels_and_copies(occ_ref, occupied)
    for j in range(occupied):
        orb_ref[2 * labels[j] + copies[j]] = jnp.int32(j)
    if before is None:
        (xs_ref,) = refs
        for r in range(dests):
            ref = mate_ref if r & 1 else own_ref
            block = ref[((r >> 1) & 1) * (dests // 4) + (r >> 2)][:rows].astype(jnp.float32)
            xs_ref[pl.ds((pos_ref[0] ^ r) * per_device, per_device)] = block.reshape(
                per_device, occupied, LANES
            )
        for j in range(occupied):
            x_ref[j] = xs_ref[:, j, :].astype(jnp.bfloat16)
    left = jnp.concatenate([ref[...].astype(jnp.float32) for ref in cycs], axis=0)[i0:i1]
    left = left.reshape((i1 - i0) * per_device, LANES).astype(jnp.bfloat16)
    for j in range(occupied):
        cs_ref[j] = contract_last(left, x_ref[j]).reshape(i1 - i0, per_device, virtuals)
    load.wait()

    pieces_of = payload_pieces(per_device, pairs, dests)
    lane = lax.broadcasted_iota(jnp.int32, (8, LANES), 1)
    choices = {
        (i, s): [orb_ref[2 * (labels[i] ^ n) + s] for n in range(4)]
        for i in range(i0, i1)
        for s in range(2)
    }

    def group(g, top):
        rows = pl.ds(pl.multiple_of(g * 8, 8), 8)
        found = {}

        def fill(e):
            nonlocal top
            for v in range(tiles):
                at = slice(v * LANES, (v + 1) * LANES)
                if e < 2 * i0:
                    x = prev_ref[e - 2 * before, rows, at]
                else:
                    js = choices[e // 2, e % 2]
                    uv = u_ref[rows, at]
                    x = cs_ref[js[0], e // 2 - i0, rows, at]
                    for n in range(1, 4):
                        x = jnp.where(uv == n, cs_ref[js[n], e // 2 - i0, rows, at], x)
                    x = x + hin_ref[e - 2 * i0, rows, at]
                    out_ref[e - 2 * i0, rows, at] = x
                top = jnp.maximum(top, jnp.abs(x))
                found[e, v] = x

        for t in range(t0, t1):
            first_e = t * LANES // per_device
            last_e = min(((t + 1) * LANES - 1) // per_device, pairs - 1)
            for e in range(first_e, last_e + 1):
                if (e, 0) not in found:
                    fill(e)
            for q in range(dests):
                acc = None
                for first, e, v, shift in pieces_of[q, t]:
                    x = pltpu.roll(found[e, v], shift, axis=1) if shift else found[e, v]
                    acc = x if acc is None else jnp.where(lane >= first, x, acc)
                at = pl.ds(pl.multiple_of((t - t0) * per_device + g * 8, 8), 8)
                pay_ref[q, at, :] = acc
        return top

    top = lax.fori_loop(0, per_device // 8, group, jnp.zeros((8, LANES), jnp.float32))
    top = jnp.max(jnp.max(top, axis=0, keepdims=True), axis=1, keepdims=True)
    k = jnp.floor(TOP_EXPONENT - jnp.log2(jnp.maximum(top, 1e-30)))
    scale = jnp.exp2(k)
    row = lax.broadcasted_iota(jnp.int32, pay_ref.shape[1:], 0)
    for q in range(dests):
        z = pay_ref[q] * scale
        z2 = z * z
        z4 = z2 * z2
        y = jnp.where(row >= (t1 - t0) * per_device, k, z4 * z4 * z)
        send_ref[q] = y.astype(jnp.bfloat16)


def join_kernel(chunks, some, j0, j1, occ_ref, u_ref, *refs):
    halves, recvs = refs[: len(chunks)], refs[len(chunks) : len(chunks) + some]
    out_ref, dec_ref, mir_ref, res_ref, sems = refs[-5:]
    occupied = occ_ref.shape[0]
    per_device, virtuals = u_ref.shape
    labels, copies = labels_and_copies(occ_ref, occupied)
    spread = 2 * per_device
    ready = set()

    def decode(t):
        ready.add(t)
        ((_, _, t0, t1), recv_ref), = [
            (c, r) for c, r in zip(chunks, recvs) if c[2] <= t < c[3]
        ]
        start = (t - t0) * per_device
        low, high = start // 16 * 16, (start + per_device + 15) // 16 * 16
        end = (t1 - t0) * per_device
        for p in range(recv_ref.shape[0]):
            tail = recv_ref[p, end // 16 * 16 : end // 16 * 16 + 16, :]
            k = tail.astype(jnp.float32)[end % 16 : end % 16 + 1, 0:1]
            y = recv_ref[p, low:high, :].astype(jnp.float32)
            y = y[start - low : start - low + per_device]
            size = jnp.log2(jnp.maximum(jnp.abs(y), 2.0**-126)) * (1.0 / POWER) - k
            size = jnp.exp2(size)
            x = jnp.where(y < 0, -size, jnp.where(y > 0, size, 0.0))
            dec_ref[p * per_device : (p + 1) * per_device, :] = x
        mir_ref[t * LANES : (t + 1) * LANES, :] = dec_ref[...].T

    stores = []
    for j in range(j0, j1):
        for t in range(j * spread // LANES, ((j + 1) * spread - 1) // LANES + 1):
            if t not in ready:
                decode(t)
        u = u_ref[...]
        for (i0, i1, _, _), half_ref in zip(chunks, halves):
            for i in range(i0, i1):
                at = pl.ds(pl.multiple_of((2 * j + copies[i]) * per_device, 8), per_device)
                total = half_ref[2 * (i - i0) + copies[j]] + mir_ref[at, :]
                n = (j - j0) * occupied + i
                res_ref[n] = jnp.where(u == (labels[j] ^ labels[i]), total, 0.0)
                store = pltpu.make_async_copy(res_ref.at[n], out_ref.at[i, j], sems.at[n])
                store.start()
                stores.append(store)
    for store in stores:
        store.wait()


def permute(x, flip, size):
    return lax.ppermute(x, "vir", [(n, n ^ flip) for n in range(size)])


def body(dests, amps, fock_vir, fock_occ, ladder_ints, cycle_ints, occ_irrep, vir_irrep):
    occupied, _, per_device, virtuals = amps.shape
    pairs = 2 * occupied
    tiles = virtuals // LANES
    rows = occupied * per_device
    kw = ladder_ints.shape[2]
    f32, bf16 = jnp.float32, jnp.bfloat16
    position = lax.axis_index("vir").astype(jnp.int32)
    pos = position.reshape(1)
    vir_local = lax.dynamic_slice_in_dim(vir_irrep, position * per_device, per_device)
    u = jnp.bitwise_xor(vir_local[:, None], vir_irrep[None, :])
    smem = pl.BlockSpec(memory_space=pltpu.SMEM)

    def whole(shape):
        return pl.BlockSpec(shape, lambda n: (0,) * len(shape))

    def cost(flops, size):
        return pl.CostEstimate(flops=flops, bytes_accessed=size, transcendentals=0)

    anywhere = pl.BlockSpec(memory_space=pl.ANY)
    quarter = dests // 4
    block_rows = rows + 16
    block = pl.pallas_call(
        prep_kernel,
        grid=(1,),
        out_shape=jax.ShapeDtypeStruct((block_rows, LANES), bf16),
        in_specs=[
            whole((rows, LANES)),
            pl.BlockSpec((occupied, occupied, 16, LANES), lambda n: (0, 0, 0, 0)),
        ],
        out_specs=whole((block_rows, LANES)),
        compiler_params=params(60),
        cost_estimate=cost(0, 500000),
    )(cycle_ints.reshape(rows, LANES), amps)
    block = block.reshape(1, block_rows, LANES)
    vmem = pl.BlockSpec(memory_space=pltpu.VMEM)
    mix = pl.pallas_call(
        mix_kernel,
        out_shape=jax.ShapeDtypeStruct((rows, rows), bf16),
        in_specs=[vmem, anywhere],
        out_specs=vmem,
        compiler_params=params(4),
        cost_estimate=cost(10**7, 300000),
    )(fock_occ, block)

    flat_amps = amps.reshape(occupied, rows, virtuals)
    parts = (2, 4, 2)
    wide = 2

    def fock_part(n, after):
        first, count = sum(parts[:n]), parts[n]
        return pl.pallas_call(
            functools.partial(fock_kernel, first),
            grid=(count // wide,),
            out_shape=(
                jax.ShapeDtypeStruct((2 * count, per_device, virtuals), f32),
                jax.ShapeDtypeStruct((count, per_device, LANES), bf16),
            ),
            in_specs=[
                smem,
                pl.BlockSpec((wide, rows, virtuals), lambda i: (i + first // wide, 0, 0)),
                whole(fock_vir.shape),
                whole(mix.shape),
                whole(u.shape),
                anywhere,
            ],
            out_specs=(
                pl.BlockSpec((2 * wide, per_device, virtuals), lambda i: (i, 0, 0)),
                pl.BlockSpec((wide, per_device, LANES), lambda i: (i, 0, 0)),
            ),
            scratch_shapes=[pltpu.VMEM((occupied, per_device, virtuals), f32)],
            compiler_params=params(12),
            cost_estimate=cost(3 * count * rows * virtuals * virtuals, 2 * 10**6),
        )(occ_irrep, flat_amps, fock_vir, mix, u, after)

    z1, z2, z3 = [permute(block, m << 2, dests) for m in range(1, quarter)]
    half0, cyc0 = fock_part(0, mix)
    near = stack([block, z1], half0)
    near_y = permute(near, 2, dests)
    half1, cyc1 = fock_part(1, near)
    far = stack([z2, z3], half1)
    far_y = permute(far, 2, dests)
    half2, cyc2 = fock_part(2, far)
    own_blocks = stack([near, far, near_y, far_y], half2)
    win = pl.pallas_call(
        unpack_kernel,
        grid=(1,),
        out_shape=jax.ShapeDtypeStruct((occupied * occupied, LANES), bf16),
        in_specs=[
            smem,
            pl.BlockSpec((dests // 2, 16, LANES), lambda n: (0, rows // 16, 0)),
            anywhere,
        ],
        out_specs=whole((occupied * occupied, LANES)),
        compiler_params=params(4),
        cost_estimate=cost(0, 10**5),
    )(pos, own_blocks, own_blocks)
    win_mate = permute(win, 1, dests)
    mate_blocks = permute(own_blocks, 1, dests)

    half = pl.pallas_call(
        functools.partial(ladder_kernel, parts),
        grid=(per_device // 8,),
        out_shape=jax.ShapeDtypeStruct((pairs, per_device, virtuals), f32),
        in_specs=[smem, whole(win.shape), whole(win.shape)]
        + [pl.BlockSpec((2 * count, 8, virtuals), lambda n: (0, n, 0)) for count in parts]
        + [whole(u.shape), pl.BlockSpec((8, virtuals, kw), lambda n: (n, 0, 0))],
        out_specs=pl.BlockSpec((pairs, 8, virtuals), lambda n: (0, n, 0)),
        scratch_shapes=[
            pltpu.VMEM((occupied * occupied, LANES), f32),
            pltpu.VMEM((occupied * occupied, LANES), f32),
            pltpu.VMEM((pairs, 8, virtuals), f32),
        ],
        compiler_params=params(16),
        cost_estimate=cost(4 * occupied * rows * virtuals * LANES, 9 * 10**6),
    )(occ_irrep, win, win_mate, half0, half1, half2, u, ladder_ints)

    spread = 2 * per_device
    t_mid = (3 * tiles + 4) // 5
    i_mid = -(-t_mid * LANES // spread)
    j_mid = t_mid * LANES // spread
    chunks = ((0, i_mid, 0, t_mid), (i_mid, occupied, t_mid, tiles))
    joins = ((0, j_mid), (j_mid, occupied))
    cycs = (cyc0, cyc1, cyc2)
    halves, recvs = [], []
    x_shape = (occupied, virtuals, LANES)
    for n, chunk in enumerate(chunks):
        i0, i1, t0, t1 = chunk
        wide_i = i1 - i0
        send_rows = ((t1 - t0) * per_device + 8 + 15) // 16 * 16
        half_shape = (2 * wide_i, per_device, virtuals)
        out_shape = [
            jax.ShapeDtypeStruct(half_shape, f32),
            jax.ShapeDtypeStruct((dests, send_rows, LANES), bf16),
        ]
        scratch = [
            pltpu.SMEM((occupied,), jnp.int32),
            pltpu.VMEM((occupied, wide_i, per_device, virtuals), f32),
            pltpu.VMEM(half_shape, f32),
            pltpu.VMEM((dests, send_rows, LANES), f32),
            pltpu.SemaphoreType.DMA((1,)),
        ]
        if n == 0:
            given = (own_blocks, mate_blocks)
            out_shape.append(jax.ShapeDtypeStruct(x_shape, bf16))
            scratch.append(pltpu.VMEM((virtuals, occupied, LANES), f32))
        else:
            given = (x_all, halves[-1])
        got = pl.pallas_call(
            functools.partial(cycle_kernel, chunk, chunks[n - 1][0] if n else None, parts),
            out_shape=out_shape,
            in_specs=[smem, smem] + [vmem] * 5 + [anywhere, vmem],
            out_specs=[vmem] * len(out_shape),
            scratch_shapes=scratch,
            compiler_params=params(28),
            cost_estimate=cost(2 * wide_i * rows * virtuals * LANES, 8 * 10**6),
        )(pos, occ_irrep, *given, *cycs, half, u)
        if n == 0:
            x_all = got[2]
        halves.append(got[0])
        recvs.append(
            lax.all_to_all(got[1], "vir", split_axis=0, concat_axis=0, tiled=True)
        )

    out = None
    for n, (j0, j1) in enumerate(joins):
        extra = () if out is None else (out,)
        some = n + 1
        count = (j1 - j0) * occupied
        out = pl.pallas_call(
            functools.partial(join_kernel, chunks, some, j0, j1),
            out_shape=jax.ShapeDtypeStruct((occupied, occupied, per_device, virtuals), f32),
            in_specs=[smem] + [vmem] * (1 + len(halves) + some) + [anywhere] * len(extra),
            out_specs=anywhere,
            input_output_aliases={2 + len(halves) + some: 0} if extra else {},
            scratch_shapes=[
                pltpu.VMEM((virtuals, LANES), f32),
                pltpu.VMEM((tiles * LANES, virtuals), f32),
                pltpu.VMEM((count, per_device, virtuals), f32),
                pltpu.SemaphoreType.DMA((count,)),
            ],
            compiler_params=params(16),
            cost_estimate=cost(10**6, 5 * 10**6),
        )(occ_irrep, u, *halves, *recvs[:some], *extra)
    return out


def solution(mesh):
    dests = mesh.shape["vir"]

    def run(amps, *rest):
        occupied, _, per_device, virtuals = amps.shape
        tiled = (
            dests == 16
            and per_device % 8 == 0
            and virtuals % LANES == 0
            and 2 * occupied * per_device == virtuals
            and rest[2].shape[2] == LANES
            and rest[3].shape[2] == LANES
        )
        return body(dests, amps, *rest) if tiled else plain_body(amps, *rest)

    return jax.shard_map(
        run,
        mesh=mesh,
        in_specs=(
            P("groups", None, "vir", None),
            P("groups", None),
            P("groups", None),
            P("vir", "groups", None),
            P("vir", "groups", None),
            P("groups"),
            P("groups"),
        ),
        out_specs=P("groups", None, "vir", None),
        check_vma=False,
    )
```

```python
import functools

import jax
import jax.numpy as jnp
from jax import lax
from jax.experimental import pallas as pl
from jax.experimental.pallas import tpu as pltpu
from jax.sharding import PartitionSpec as P

DW = 8
CW = 16
LANES = 128
POWER = 9
TOP_EXPONENT = 13


def contract_last(left_side, right_side):
    return lax.dot_general(
        left_side, right_side, (((1,), (1,)), ((), ())), preferred_element_type=jnp.float32
    )


def plain_body(amps, fock_vir, fock_occ, ladder_ints, cycle_ints, occ_irrep, vir_irrep):
    occupied = amps.shape[0]
    per_device = amps.shape[2]
    virtuals = amps.shape[3]
    pair_count = occupied * occupied
    position = lax.axis_index("vir")
    fock_term = jnp.dot(
        amps.reshape(pair_count * per_device, virtuals),
        fock_vir,
        preferred_element_type=jnp.float32,
    ).reshape(occupied, occupied, per_device, virtuals)
    occ_term = jnp.einsum("ikab,kj->ijab", amps, fock_occ, preferred_element_type=jnp.float32)
    flat_ints = ladder_ints.reshape(per_device * virtuals, ladder_ints.shape[2])
    local_window = amps[:, :, 0:1, :DW]
    local_cycle = amps[:, :, :, :CW]
    segment = lax.all_gather(local_window, "vir", axis=2, tiled=True)
    width = segment.shape[2] * DW
    ladder = contract_last(segment.reshape(pair_count, width), flat_ints)
    left_side = jnp.transpose(local_cycle, (0, 2, 1, 3)).reshape(
        occupied * per_device, occupied * CW
    )
    segment = lax.all_gather(cycle_ints, "vir", axis=0, tiled=True)
    right_side = segment.reshape(segment.shape[0] * occupied, occupied * CW)
    cycle_block = contract_last(left_side, right_side).reshape(
        occupied, per_device, segment.shape[0], occupied
    )
    cycle_part = jnp.transpose(cycle_block, (0, 3, 1, 2))
    half_sum = (
        fock_term - occ_term + ladder.reshape(occupied, occupied, per_device, virtuals) + cycle_part
    )
    vir_local = lax.dynamic_slice_in_dim(vir_irrep, position * per_device, per_device)
    occ_pair = jnp.bitwise_xor(occ_irrep[:, None], occ_irrep[None, :])
    vir_pair = jnp.bitwise_xor(vir_local[:, None], vir_irrep[None, :])
    received = lax.all_to_all(half_sum, "vir", split_axis=3, concat_axis=2, tiled=True)
    mirrored = jnp.transpose(received, (1, 0, 3, 2))
    product_irrep = jnp.bitwise_xor(occ_pair[:, :, None, None], vir_pair[None, None, :, :])
    allowed = jnp.where(product_irrep == 0, jnp.float32(1.0), jnp.float32(0.0))
    return allowed * (half_sum + mirrored)


def params(mib):
    return pltpu.CompilerParams(vmem_limit_bytes=mib * 2**20)


def labels_and_copies(occ_ref, occupied):
    labels = [occ_ref[j] for j in range(occupied)]
    copies = []
    for j in range(occupied):
        s = jnp.int32(0)
        for k in range(j):
            s = s + (labels[k] == labels[j]).astype(jnp.int32)
        copies.append(s)
    return labels, copies


def prep_kernel(cyc_ref, amps_ref, win_ref, xt_ref, t_ref):
    occupied, _, per_device, _ = amps_ref.shape
    xt_ref[0, 0] = cyc_ref[...]
    lane = lax.broadcasted_iota(jnp.int32, (occupied, LANES), 1)
    packed = jnp.zeros((occupied, LANES), jnp.float32)
    for j in range(occupied):
        w = jnp.where(lane < DW, amps_ref[:, j, 0, :].astype(jnp.float32), 0.0)
        packed = packed + (pltpu.roll(w, j * DW, axis=1) if j else w)
    packed = jnp.concatenate([packed, jnp.zeros_like(packed)], axis=0)
    win_ref[...] = packed.astype(jnp.bfloat16)
    lane = lax.broadcasted_iota(jnp.int32, (per_device, LANES), 1)
    for i in range(occupied):
        acc = jnp.zeros((per_device, LANES), jnp.float32)
        for k in range(occupied):
            piece = jnp.where(lane < CW, amps_ref[i, k].astype(jnp.float32), 0.0)
            acc = acc + (pltpu.roll(piece, k * CW, axis=1) if k else piece)
        t_ref[i * per_device : (i + 1) * per_device, :] = acc
    xt_ref[0, 1] = t_ref[...].astype(jnp.bfloat16)


def mix_kernel(occ_vals_ref, after_ref, mix_ref):
    rows = mix_ref.shape[0]
    occupied = occ_vals_ref.shape[0]
    per_device = rows // occupied
    row = lax.broadcasted_iota(jnp.int32, (rows, occupied), 0)
    start = lax.broadcasted_iota(jnp.int32, (rows, occupied), 1) * per_device
    in_block = jnp.logical_and(row >= start, row < start + per_device).astype(jnp.bfloat16)
    row = lax.broadcasted_iota(jnp.int32, (rows, per_device), 0)
    at = lax.broadcasted_iota(jnp.int32, (rows, per_device), 1)
    same = row == at
    for n in range(1, occupied):
        same = jnp.logical_or(same, row == at + n * per_device)
    same = same.astype(jnp.bfloat16)
    left = contract_last(in_block, occ_vals_ref[...]).astype(jnp.bfloat16)
    mix = contract_last(left, in_block) * contract_last(same, same)
    mix_ref[...] = mix.astype(jnp.bfloat16)


def fock_kernel(first, occ_ref, amps_ref, fock_ref, mix_ref, u_ref, after_ref, half_ref, hs_ref):
    wide, rows, virtuals = amps_ref.shape
    _, per_device, _ = half_ref.shape
    occupied = occ_ref.shape[0]
    labels, copies = labels_and_copies(occ_ref, occupied)
    u = u_ref[...]
    h = jnp.dot(
        amps_ref[...].reshape(wide * rows, virtuals),
        fock_ref[...],
        preferred_element_type=jnp.float32,
    )
    for w in range(wide):
        a = amps_ref[w]
        mixed = jnp.dot(mix_ref[...], a, preferred_element_type=jnp.float32)
        hs_ref[...] = (h[w * rows : (w + 1) * rows] - mixed).reshape(hs_ref.shape)
        own = occ_ref[pl.program_id(0) * wide + w + first]
        for j in range(occupied):
            at = 2 * w + copies[j]
            half_ref[at] = jnp.where(u == (own ^ labels[j]), hs_ref[j], half_ref[at])


def stack(blocks, after):
    count = len(blocks)

    def kernel(*refs):
        out = refs[count + 1]
        at = 0
        for n in range(count):
            head = blocks[n].shape[0]
            out[at : at + head] = refs[n][...]
            at += head

    vmem = pl.BlockSpec(memory_space=pltpu.VMEM)
    shape = (sum(b.shape[0] for b in blocks),) + blocks[0].shape[1:]
    return pl.pallas_call(
        kernel,
        out_shape=jax.ShapeDtypeStruct(shape, blocks[0].dtype),
        in_specs=[vmem] * count + [pl.BlockSpec(memory_space=pl.ANY)],
        out_specs=vmem,
        compiler_params=params(4),
        cost_estimate=pl.CostEstimate(flops=0, bytes_accessed=10**6, transcendentals=0),
    )(*blocks, after)


def unpack_kernel(pos_ref, *refs):
    blocks, win_ref = refs[:-2], refs[-1]
    occupied, _, lanes = win_ref.shape
    lane = lax.broadcasted_iota(jnp.int32, (8, lanes), 1)
    for j in range(occupied):
        total = jnp.zeros((8, lanes), jnp.float32)
        for m, block in enumerate(blocks):
            p = pos_ref[0] ^ (m << 2)
            w = block[...].astype(jnp.float32)[:8]
            w = jnp.where(jnp.logical_and(lane >= j * DW, lane < (j + 1) * DW), w, 0.0)
            total = total + pltpu.roll(w, lax.rem(p * DW - j * DW + lanes, lanes), axis=1)
        win_ref[j] = total


def add_kernel(a_ref, b_ref, after_ref, out_ref):
    out_ref[...] = a_ref[...] + b_ref[...]


def payload_pieces(per_device, pairs, dests):
    out = {}
    for q in range(dests):
        for e in range(pairs):
            start = 0
            while start < per_device:
                src = q * per_device + start
                dst = e * per_device + start
                length = min(LANES - src % LANES, LANES - dst % LANES, per_device - start)
                out.setdefault((q, dst // LANES), []).append(
                    (dst % LANES, e, src // LANES, (dst - src) % LANES)
                )
                start += length
    return out


def ladder_kernel(parts, occ_ref, win0_ref, win1_ref, *refs):
    halves = refs[: len(parts)]
    u_ref, lad_ref, out_ref, send_ref, w2_ref, ls_ref, pay_ref, max_ref = refs[len(parts) :]
    step = pl.program_id(0)
    occupied = occ_ref.shape[0]
    pairs, _, virtuals = out_ref.shape
    per_device = u_ref.shape[0]
    dests = send_ref.shape[0]
    tiles = virtuals // LANES
    labels, copies = labels_and_copies(occ_ref, occupied)

    @pl.when(step == 0)
    def _():
        for i in range(occupied):
            for j in range(occupied):
                row = (labels[i] ^ labels[j]) * pairs + 2 * i + copies[j]
                w = win0_ref[j, i : i + 1, :].astype(jnp.float32)
                w2_ref[pl.ds(row, 1), :] = w + win1_ref[j, i : i + 1, :].astype(jnp.float32)
        max_ref[...] = jnp.zeros_like(max_ref)

    w2 = w2_ref[...].astype(jnp.bfloat16)
    u8 = u_ref[pl.ds(pl.multiple_of(step * 8, 8), 8), :]
    for a in range(8):
        ladder = contract_last(w2, lad_ref[a])
        ua = u8[a : a + 1, :]
        sel = ladder[0:pairs]
        for v in range(1, 4):
            sel = jnp.where(ua == v, ladder[v * pairs : (v + 1) * pairs], sel)
        ls_ref[:, a, :] = sel
    sources = [(part, n) for part, count in zip(halves, parts) for n in range(2 * count)]
    pieces_of = payload_pieces(per_device, pairs, dests)
    lane = lax.broadcasted_iota(jnp.int32, (8, LANES), 1)
    top = max_ref[...]
    found = {}
    for t in range(tiles):
        last_e = min(((t + 1) * LANES - 1) // per_device, pairs - 1)
        for e in range(t * LANES // per_device, last_e + 1):
            if (e, 0) in found:
                continue
            part, n = sources[e]
            for v in range(tiles):
                at = slice(v * LANES, (v + 1) * LANES)
                x = part[n, :, at] + ls_ref[e, :, at]
                out_ref[e, :, at] = x
                top = jnp.maximum(top, jnp.abs(x))
                found[e, v] = x
        for q in range(dests):
            acc = None
            for first, e, v, shift in pieces_of[q, t]:
                x = pltpu.roll(found[e, v], shift, axis=1) if shift else found[e, v]
                acc = x if acc is None else jnp.where(lane >= first, x, acc)
            at = pl.ds(pl.multiple_of(t * per_device + step * 8, 8), 8)
            pay_ref[q, at, :] = acc
    max_ref[...] = top

    @pl.when(step == pl.num_programs(0) - 1)
    def _():
        most = jnp.max(jnp.max(max_ref[...], axis=0, keepdims=True), axis=1, keepdims=True)
        k = jnp.floor(TOP_EXPONENT - jnp.log2(jnp.maximum(most, 1e-30)))
        scale = jnp.exp2(k)
        row = lax.broadcasted_iota(jnp.int32, pay_ref.shape[1:], 0)
        for q in range(dests):
            z = pay_ref[q] * scale
            z2 = z * z
            z4 = z2 * z2
            y = jnp.where(row >= tiles * per_device, k, z4 * z4 * z)
            send_ref[q] = y.astype(jnp.bfloat16)


def cycle_kernel(pos_ref, occ_ref, own_ref, mate_ref, half_ref, u_ref, out_ref, orb_ref, cs_ref, xs_ref, ts_ref):
    occupied = occ_ref.shape[0]
    pairs, per_device, virtuals = half_ref.shape
    quads, _, rows, _ = own_ref.shape
    dests = 2 * quads
    tiles = virtuals // LANES
    labels, copies = labels_and_copies(occ_ref, occupied)
    for j in range(occupied):
        orb_ref[2 * labels[j] + copies[j]] = jnp.int32(j)
    for r in range(dests):
        ref = mate_ref if r & 1 else own_ref
        n = ((r >> 1) & 1) * (dests // 4) + (r >> 2)
        p = pos_ref[0] ^ r
        x = ref[n, 0].astype(jnp.float32).reshape(per_device, occupied, LANES)
        xs_ref[pl.ds(p * per_device, per_device)] = x
        t = ref[n, 1].astype(jnp.float32)
        at = pl.ds(pl.multiple_of(p * per_device, 8), per_device)
        for j in range(occupied):
            ts_ref[j, at, :] = t[j * per_device : (j + 1) * per_device]
    here = pl.ds(pos_ref[0] * per_device, per_device)
    x_left = jnp.concatenate([xs_ref[here, i, :] for i in range(occupied)], axis=0)
    left = jnp.concatenate([own_ref[0, 1], x_left.astype(jnp.bfloat16)], axis=1)
    for j in range(occupied):
        right = jnp.concatenate([xs_ref[:, j, :], ts_ref[j]], axis=1).astype(jnp.bfloat16)
        cs_ref[j] = contract_last(left, right).reshape(occupied, per_device, virtuals)
    choices = [
        [orb_ref[2 * (labels[e // 2] ^ n) + e % 2] for n in range(4)] for e in range(pairs)
    ]

    def group(g, carry):
        rows = pl.ds(pl.multiple_of(g * 8, 8), 8)
        for v in range(tiles):
            at = slice(v * LANES, (v + 1) * LANES)
            uv = u_ref[rows, at]
            masks = [uv == n for n in range(1, 4)]
            for e in range(pairs):
                x = cs_ref[choices[e][0], e // 2, rows, at]
                for n in range(1, 4):
                    x = jnp.where(masks[n - 1], cs_ref[choices[e][n], e // 2, rows, at], x)
                out_ref[e, rows, at] = half_ref[e, rows, at] + x
        return carry

    lax.fori_loop(0, per_device // 8, group, 0)


def join_kernel(occ_ref, u_ref, half_ref, recv_ref, out_ref, dec_ref, mir_ref, res_ref, sems):
    occupied = occ_ref.shape[0]
    per_device, virtuals = u_ref.shape
    labels, copies = labels_and_copies(occ_ref, occupied)
    spread = 2 * per_device
    ready = set()

    def decode(t):
        ready.add(t)
        start = t * per_device
        low, high = start // 16 * 16, (start + per_device + 15) // 16 * 16
        end = virtuals // LANES * per_device
        for p in range(recv_ref.shape[0]):
            tail = recv_ref[p, end // 16 * 16 : end // 16 * 16 + 16, :]
            k = tail.astype(jnp.float32)[end % 16 : end % 16 + 1, 0:1]
            y = recv_ref[p, low:high, :].astype(jnp.float32)
            y = y[start - low : start - low + per_device]
            size = jnp.log2(jnp.maximum(jnp.abs(y), 2.0**-126)) * (1.0 / POWER) - k
            size = jnp.exp2(size)
            x = jnp.where(y < 0, -size, jnp.where(y > 0, size, 0.0))
            dec_ref[p * per_device : (p + 1) * per_device, :] = x
        mir_ref[t * LANES : (t + 1) * LANES, :] = dec_ref[...].T

    stores = []
    for j in range(occupied):
        for t in range(j * spread // LANES, ((j + 1) * spread - 1) // LANES + 1):
            if t not in ready:
                decode(t)
        u = u_ref[...]
        for i in range(occupied):
            at = pl.ds(pl.multiple_of((2 * j + copies[i]) * per_device, 8), per_device)
            total = half_ref[2 * i + copies[j]] + mir_ref[at, :]
            n = j * occupied + i
            res_ref[n] = jnp.where(u == (labels[j] ^ labels[i]), total, 0.0)
            store = pltpu.make_async_copy(res_ref.at[n], out_ref.at[i, j], sems.at[n])
            store.start()
            stores.append(store)
    for store in stores:
        store.wait()


def permute(x, flip, size):
    return lax.ppermute(x, "vir", [(n, n ^ flip) for n in range(size)])


def body(dests, amps, fock_vir, fock_occ, ladder_ints, cycle_ints, occ_irrep, vir_irrep):
    occupied, _, per_device, virtuals = amps.shape
    pairs = 2 * occupied
    tiles = virtuals // LANES
    rows = occupied * per_device
    kw = ladder_ints.shape[2]
    f32, bf16 = jnp.float32, jnp.bfloat16
    position = lax.axis_index("vir").astype(jnp.int32)
    pos = position.reshape(1)
    vir_local = lax.dynamic_slice_in_dim(vir_irrep, position * per_device, per_device)
    u = jnp.bitwise_xor(vir_local[:, None], vir_irrep[None, :])
    smem = pl.BlockSpec(memory_space=pltpu.SMEM)

    def whole(shape):
        return pl.BlockSpec(shape, lambda n: (0,) * len(shape))

    def cost(flops, size):
        return pl.CostEstimate(flops=flops, bytes_accessed=size, transcendentals=0)

    anywhere = pl.BlockSpec(memory_space=pl.ANY)
    quarter = dests // 4
    win, xt = pl.pallas_call(
        prep_kernel,
        grid=(1,),
        out_shape=(
            jax.ShapeDtypeStruct((16, LANES), bf16),
            jax.ShapeDtypeStruct((1, 2, rows, LANES), bf16),
        ),
        in_specs=[
            whole((rows, LANES)),
            pl.BlockSpec((occupied, occupied, per_device, LANES), lambda n: (0, 0, 0, 0)),
        ],
        out_specs=(whole((16, LANES)), whole((1, 2, rows, LANES))),
        scratch_shapes=[pltpu.VMEM((rows, LANES), f32)],
        compiler_params=params(60),
        cost_estimate=cost(0, 500000),
    )(cycle_ints.reshape(rows, LANES), amps)
    vmem = pl.BlockSpec(memory_space=pltpu.VMEM)
    mix = pl.pallas_call(
        mix_kernel,
        out_shape=jax.ShapeDtypeStruct((rows, rows), bf16),
        in_specs=[vmem, anywhere],
        out_specs=vmem,
        compiler_params=params(4),
        cost_estimate=cost(10**7, 300000),
    )(fock_occ, win)

    flat_amps = amps.reshape(occupied, rows, virtuals)
    parts = (2, 2, 4)
    wide = 2

    def fock_part(n, after):
        first, count = sum(parts[:n]), parts[n]
        return pl.pallas_call(
            functools.partial(fock_kernel, first),
            grid=(count // wide,),
            out_shape=jax.ShapeDtypeStruct((2 * count, per_device, virtuals), f32),
            in_specs=[
                smem,
                pl.BlockSpec((wide, rows, virtuals), lambda i: (i + first // wide, 0, 0)),
                whole(fock_vir.shape),
                whole(mix.shape),
                whole(u.shape),
                anywhere,
            ],
            out_specs=pl.BlockSpec((2 * wide, per_device, virtuals), lambda i: (i, 0, 0)),
            scratch_shapes=[pltpu.VMEM((occupied, per_device, virtuals), f32)],
            compiler_params=params(12),
            cost_estimate=cost(3 * count * rows * virtuals * virtuals, 2 * 10**6),
        )(occ_irrep, flat_amps, fock_vir, mix, u, after)

    flips = [m << 2 for m in range(1, quarter)]
    win_shape = (occupied, occupied, LANES)
    wins = [win] + [permute(win, flip, dests) for flip in flips]
    blocks = [xt] + [permute(xt, flip, dests) for flip in flips]
    half0 = fock_part(0, mix)
    win = pl.pallas_call(
        unpack_kernel,
        out_shape=jax.ShapeDtypeStruct(win_shape, f32),
        in_specs=[smem] + [vmem] * quarter + [anywhere],
        out_specs=vmem,
        compiler_params=params(4),
        cost_estimate=cost(0, 10**5),
    )(pos, *wins, half0)

    def add(a, b, after):
        return pl.pallas_call(
            add_kernel,
            out_shape=jax.ShapeDtypeStruct(a.shape, a.dtype),
            in_specs=[vmem, vmem, anywhere],
            out_specs=vmem,
            compiler_params=params(4),
            cost_estimate=cost(0, 10**5),
        )(a, b, after)

    win_y = permute(win, 2, dests)
    half1 = fock_part(1, win)
    win = add(win, win_y, half1)
    win_mate = permute(win, 1, dests)
    half2 = fock_part(2, win)

    send_rows = tiles * per_device + 8
    half, send = pl.pallas_call(
        functools.partial(ladder_kernel, parts),
        grid=(per_device // 8,),
        out_shape=(
            jax.ShapeDtypeStruct((pairs, per_device, virtuals), f32),
            jax.ShapeDtypeStruct((dests, send_rows, LANES), bf16),
        ),
        in_specs=[smem, whole(win_shape), whole(win_shape)]
        + [pl.BlockSpec((2 * count, 8, virtuals), lambda n: (0, n, 0)) for count in parts]
        + [whole(u.shape), pl.BlockSpec((8, virtuals, kw), lambda n: (n, 0, 0))],
        out_specs=(
            pl.BlockSpec((pairs, 8, virtuals), lambda n: (0, n, 0)),
            whole((dests, send_rows, LANES)),
        ),
        scratch_shapes=[
            pltpu.VMEM((occupied * occupied, LANES), f32),
            pltpu.VMEM((pairs, 8, virtuals), f32),
            pltpu.VMEM((dests, send_rows, LANES), f32),
            pltpu.VMEM((8, LANES), f32),
        ],
        compiler_params=params(16),
        cost_estimate=cost(4 * occupied * rows * virtuals * LANES, 9 * 10**6),
    )(occ_irrep, win, win_mate, half0, half1, half2, u, ladder_ints)

    near = stack(blocks, half)
    near_y = permute(near, 2, dests)
    recv = lax.all_to_all(send, "vir", split_axis=0, concat_axis=0, tiled=True)
    own_blocks = stack([near, near_y], send)
    mate_blocks = permute(own_blocks, 1, dests)
    half = pl.pallas_call(
        cycle_kernel,
        out_shape=jax.ShapeDtypeStruct((pairs, per_device, virtuals), f32),
        in_specs=[smem, smem] + [vmem] * 4,
        out_specs=vmem,
        scratch_shapes=[
            pltpu.SMEM((occupied,), jnp.int32),
            pltpu.VMEM((occupied, occupied, per_device, virtuals), f32),
            pltpu.VMEM((virtuals, occupied, LANES), f32),
            pltpu.VMEM((occupied, virtuals, LANES), f32),
        ],
        compiler_params=params(28),
        cost_estimate=cost(1000, 1000),
    )(pos, occ_irrep, own_blocks, mate_blocks, half, u)

    return pl.pallas_call(
        join_kernel,
        out_shape=jax.ShapeDtypeStruct((occupied, occupied, per_device, virtuals), f32),
        in_specs=[smem, vmem, vmem, vmem],
        out_specs=anywhere,
        scratch_shapes=[
            pltpu.VMEM((virtuals, LANES), f32),
            pltpu.VMEM((tiles * LANES, virtuals), f32),
            pltpu.VMEM((occupied * occupied, per_device, virtuals), f32),
            pltpu.SemaphoreType.DMA((occupied * occupied,)),
        ],
        compiler_params=params(16),
        cost_estimate=cost(10**6, 5 * 10**6),
    )(occ_irrep, u, half, recv)


def solution(mesh):
    dests = mesh.shape["vir"]

    def run(amps, *rest):
        occupied, _, per_device, virtuals = amps.shape
        tiled = (
            dests == 16
            and per_device % 8 == 0
            and virtuals % LANES == 0
            and 2 * occupied * per_device == virtuals
            and rest[2].shape[2] == LANES
            and rest[3].shape[2] == LANES
        )
        return body(dests, amps, *rest) if tiled else plain_body(amps, *rest)

    return jax.shard_map(
        run,
        mesh=mesh,
        in_specs=(
            P("groups", None, "vir", None),
            P("groups", None),
            P("groups", None),
            P("vir", "groups", None),
            P("vir", "groups", None),
            P("groups"),
            P("groups"),
        ),
        out_specs=P("groups", None, "vir", None),
        check_vma=False,
    )
```

```python
import functools

import jax
import jax.numpy as jnp
from jax import lax
from jax.experimental import pallas as pl
from jax.experimental.pallas import tpu as pltpu
from jax.sharding import PartitionSpec as P

DW = 8
CW = 16
LANES = 128
POWER = 9
TOP_EXPONENT = 13


def contract_last(left_side, right_side):
    return lax.dot_general(
        left_side, right_side, (((1,), (1,)), ((), ())), preferred_element_type=jnp.float32
    )


def plain_body(amps, fock_vir, fock_occ, ladder_ints, cycle_ints, occ_irrep, vir_irrep):
    occupied = amps.shape[0]
    per_device = amps.shape[2]
    virtuals = amps.shape[3]
    pair_count = occupied * occupied
    position = lax.axis_index("vir")
    fock_term = jnp.dot(
        amps.reshape(pair_count * per_device, virtuals),
        fock_vir,
        preferred_element_type=jnp.float32,
    ).reshape(occupied, occupied, per_device, virtuals)
    occ_term = jnp.einsum("ikab,kj->ijab", amps, fock_occ, preferred_element_type=jnp.float32)
    flat_ints = ladder_ints.reshape(per_device * virtuals, ladder_ints.shape[2])
    local_window = amps[:, :, 0:1, :DW]
    local_cycle = amps[:, :, :, :CW]
    segment = lax.all_gather(local_window, "vir", axis=2, tiled=True)
    width = segment.shape[2] * DW
    ladder = contract_last(segment.reshape(pair_count, width), flat_ints)
    left_side = jnp.transpose(local_cycle, (0, 2, 1, 3)).reshape(
        occupied * per_device, occupied * CW
    )
    segment = lax.all_gather(cycle_ints, "vir", axis=0, tiled=True)
    right_side = segment.reshape(segment.shape[0] * occupied, occupied * CW)
    cycle_block = contract_last(left_side, right_side).reshape(
        occupied, per_device, segment.shape[0], occupied
    )
    cycle_part = jnp.transpose(cycle_block, (0, 3, 1, 2))
    half_sum = (
        fock_term - occ_term + ladder.reshape(occupied, occupied, per_device, virtuals) + cycle_part
    )
    vir_local = lax.dynamic_slice_in_dim(vir_irrep, position * per_device, per_device)
    occ_pair = jnp.bitwise_xor(occ_irrep[:, None], occ_irrep[None, :])
    vir_pair = jnp.bitwise_xor(vir_local[:, None], vir_irrep[None, :])
    received = lax.all_to_all(half_sum, "vir", split_axis=3, concat_axis=2, tiled=True)
    mirrored = jnp.transpose(received, (1, 0, 3, 2))
    product_irrep = jnp.bitwise_xor(occ_pair[:, :, None, None], vir_pair[None, None, :, :])
    allowed = jnp.where(product_irrep == 0, jnp.float32(1.0), jnp.float32(0.0))
    return allowed * (half_sum + mirrored)


def params(mib):
    return pltpu.CompilerParams(vmem_limit_bytes=mib * 2**20)


def labels_and_copies(occ_ref, occupied):
    labels = [occ_ref[j] for j in range(occupied)]
    copies = []
    for j in range(occupied):
        s = jnp.int32(0)
        for k in range(j):
            s = s + (labels[k] == labels[j]).astype(jnp.int32)
        copies.append(s)
    return labels, copies


def prep_kernel(cyc_ref, amps_ref, win_ref, xt_ref, t_ref):
    occupied, _, per_device, _ = amps_ref.shape
    xt_ref[0, 0] = cyc_ref[...]
    lane = lax.broadcasted_iota(jnp.int32, (occupied, LANES), 1)
    packed = jnp.zeros((occupied, LANES), jnp.float32)
    for j in range(occupied):
        w = jnp.where(lane < DW, amps_ref[:, j, 0, :].astype(jnp.float32), 0.0)
        packed = packed + (pltpu.roll(w, j * DW, axis=1) if j else w)
    packed = jnp.concatenate([packed, jnp.zeros_like(packed)], axis=0)
    win_ref[...] = packed.astype(jnp.bfloat16)
    lane = lax.broadcasted_iota(jnp.int32, (per_device, LANES), 1)
    for i in range(occupied):
        acc = jnp.zeros((per_device, LANES), jnp.float32)
        for k in range(occupied):
            piece = jnp.where(lane < CW, amps_ref[i, k].astype(jnp.float32), 0.0)
            acc = acc + (pltpu.roll(piece, k * CW, axis=1) if k else piece)
        t_ref[i * per_device : (i + 1) * per_device, :] = acc
    xt_ref[0, 1] = t_ref[...].astype(jnp.bfloat16)


def setup_kernel(pos_ref, vir_ref, occ_vals_ref, row_ref, mix_ref, u_ref):
    for a in range(u_ref.shape[0]):
        u_ref[a : a + 1, :] = row_ref[...] ^ vir_ref[pos_ref[0] * u_ref.shape[0] + a]
    rows = mix_ref.shape[0]
    occupied = occ_vals_ref.shape[0]
    per_device = rows // occupied
    row = lax.broadcasted_iota(jnp.int32, (rows, occupied), 0)
    start = lax.broadcasted_iota(jnp.int32, (rows, occupied), 1) * per_device
    in_block = jnp.logical_and(row >= start, row < start + per_device).astype(jnp.bfloat16)
    row = lax.broadcasted_iota(jnp.int32, (rows, per_device), 0)
    at = lax.broadcasted_iota(jnp.int32, (rows, per_device), 1)
    same = row == at
    for n in range(1, occupied):
        same = jnp.logical_or(same, row == at + n * per_device)
    same = same.astype(jnp.bfloat16)
    left = contract_last(in_block, occ_vals_ref[...]).astype(jnp.bfloat16)
    mix = contract_last(left, in_block) * contract_last(same, same)
    mix_ref[...] = mix.astype(jnp.bfloat16)


def fock_kernel(first, occ_ref, amps_ref, fock_ref, mix_ref, u_ref, after_ref, half_ref, hs_ref):
    wide, rows, virtuals = amps_ref.shape
    _, per_device, _ = half_ref.shape
    occupied = occ_ref.shape[0]
    labels, copies = labels_and_copies(occ_ref, occupied)
    u = u_ref[...]
    h = jnp.dot(
        amps_ref[...].reshape(wide * rows, virtuals),
        fock_ref[...],
        preferred_element_type=jnp.float32,
    )
    for w in range(wide):
        a = amps_ref[w]
        mixed = jnp.dot(mix_ref[...], a, preferred_element_type=jnp.float32)
        hs_ref[...] = (h[w * rows : (w + 1) * rows] - mixed).reshape(hs_ref.shape)
        own = occ_ref[pl.program_id(0) * wide + w + first]
        for j in range(occupied):
            at = 2 * w + copies[j]
            half_ref[at] = jnp.where(u == (own ^ labels[j]), hs_ref[j], half_ref[at])


def stack(blocks, after):
    count = len(blocks)

    def kernel(*refs):
        out = refs[count + 1]
        at = 0
        for n in range(count):
            head = blocks[n].shape[0]
            out[at : at + head] = refs[n][...]
            at += head

    vmem = pl.BlockSpec(memory_space=pltpu.VMEM)
    shape = (sum(b.shape[0] for b in blocks),) + blocks[0].shape[1:]
    return pl.pallas_call(
        kernel,
        out_shape=jax.ShapeDtypeStruct(shape, blocks[0].dtype),
        in_specs=[vmem] * count + [pl.BlockSpec(memory_space=pl.ANY)],
        out_specs=vmem,
        compiler_params=params(4),
        cost_estimate=pl.CostEstimate(flops=0, bytes_accessed=10**6, transcendentals=0),
    )(*blocks, after)


def unpack_kernel(pos_ref, *refs):
    blocks, win_ref = refs[:-2], refs[-1]
    occupied, _, lanes = win_ref.shape
    lane = lax.broadcasted_iota(jnp.int32, (8, lanes), 1)
    for j in range(occupied):
        total = jnp.zeros((8, lanes), jnp.float32)
        for m, block in enumerate(blocks):
            p = pos_ref[0] ^ (m << 2)
            w = block[...].astype(jnp.float32)[:8]
            w = jnp.where(jnp.logical_and(lane >= j * DW, lane < (j + 1) * DW), w, 0.0)
            total = total + pltpu.roll(w, lax.rem(p * DW - j * DW + lanes, lanes), axis=1)
        win_ref[j] = total


def add_kernel(a_ref, b_ref, after_ref, out_ref):
    out_ref[...] = a_ref[...] + b_ref[...]


def payload_pieces(per_device, pairs, dests):
    out = {}
    for q in range(dests):
        for e in range(pairs):
            start = 0
            while start < per_device:
                src = q * per_device + start
                dst = e * per_device + start
                length = min(LANES - src % LANES, LANES - dst % LANES, per_device - start)
                out.setdefault((q, dst // LANES), []).append(
                    (dst % LANES, e, src // LANES, (dst - src) % LANES)
                )
                start += length
    return out


def ladder_kernel(parts, occ_ref, win0_ref, win1_ref, *refs):
    halves = refs[: len(parts)]
    u_ref, lad_ref, _, out_ref, send_ref, w2_ref, ls_ref, pay_ref, max_ref = refs[len(parts) :]
    step = pl.program_id(0)
    occupied = occ_ref.shape[0]
    pairs, _, virtuals = out_ref.shape
    per_device = u_ref.shape[0]
    dests = send_ref.shape[0]
    tiles = virtuals // LANES
    labels, copies = labels_and_copies(occ_ref, occupied)

    @pl.when(step == 0)
    def _():
        for i in range(occupied):
            for j in range(occupied):
                row = (labels[i] ^ labels[j]) * pairs + 2 * i + copies[j]
                w = win0_ref[j, i : i + 1, :].astype(jnp.float32)
                w2_ref[pl.ds(row, 1), :] = w + win1_ref[j, i : i + 1, :].astype(jnp.float32)
        max_ref[...] = jnp.zeros_like(max_ref)

    w2 = w2_ref[...].astype(jnp.bfloat16)
    u8 = u_ref[pl.ds(pl.multiple_of(step * 8, 8), 8), :]
    for a in range(8):
        ladder = contract_last(w2, lad_ref[a])
        ua = u8[a : a + 1, :]
        sel = ladder[0:pairs]
        for v in range(1, 4):
            sel = jnp.where(ua == v, ladder[v * pairs : (v + 1) * pairs], sel)
        for v in range(tiles):
            ls_ref[v, pl.ds(a, pairs, stride=8), :] = sel[:, v * LANES : (v + 1) * LANES]
    sources = [(part, n) for part, count in zip(halves, parts) for n in range(2 * count)]
    pieces_of = payload_pieces(per_device, pairs, dests)
    lane = lax.broadcasted_iota(jnp.int32, (8, LANES), 1)
    top = max_ref[...]
    found = {}
    for t in range(tiles):
        last_e = min(((t + 1) * LANES - 1) // per_device, pairs - 1)
        for e in range(t * LANES // per_device, last_e + 1):
            if (e, 0) in found:
                continue
            part, n = sources[e]
            for v in range(tiles):
                at = slice(v * LANES, (v + 1) * LANES)
                x = part[n, :, at] + ls_ref[v, 8 * e : 8 * e + 8, :]
                out_ref[e, :, at] = x
                top = jnp.maximum(top, jnp.abs(x))
                found[e, v] = x
        for q in range(dests):
            acc = None
            for first, e, v, shift in pieces_of[q, t]:
                x = pltpu.roll(found[e, v], shift, axis=1) if shift else found[e, v]
                acc = x if acc is None else jnp.where(lane >= first, x, acc)
            at = pl.ds(pl.multiple_of(t * per_device + step * 8, 8), 8)
            pay_ref[q, at, :] = acc
    max_ref[...] = top

    @pl.when(step == pl.num_programs(0) - 1)
    def _():
        most = jnp.max(jnp.max(max_ref[...], axis=0, keepdims=True), axis=1, keepdims=True)
        k = jnp.floor(TOP_EXPONENT - jnp.log2(jnp.maximum(most, 1e-30)))
        scale = jnp.exp2(k)
        row = lax.broadcasted_iota(jnp.int32, pay_ref.shape[1:], 0)
        for q in range(dests):
            z = pay_ref[q] * scale
            z2 = z * z
            z4 = z2 * z2
            y = jnp.where(row >= tiles * per_device, k, z4 * z4 * z)
            send_ref[q] = y.astype(jnp.bfloat16)


def cycle_kernel(pos_ref, occ_ref, own_ref, mate_ref, half_ref, u_ref, out_ref, orb_ref, cs_ref, xs_ref, ts_ref):
    occupied = occ_ref.shape[0]
    pairs, per_device, virtuals = half_ref.shape
    quads, _, rows, _ = own_ref.shape
    dests = 2 * quads
    tiles = virtuals // LANES
    labels, copies = labels_and_copies(occ_ref, occupied)
    for j in range(occupied):
        orb_ref[2 * labels[j] + copies[j]] = jnp.int32(j)
    for r in range(dests):
        ref = mate_ref if r & 1 else own_ref
        n = ((r >> 1) & 1) * (dests // 4) + (r >> 2)
        p = pos_ref[0] ^ r
        x = ref[n, 0].astype(jnp.float32).reshape(per_device, occupied, LANES)
        xs_ref[pl.ds(p * per_device, per_device)] = x
        t = ref[n, 1].astype(jnp.float32)
        at = pl.ds(pl.multiple_of(p * per_device, 8), per_device)
        for j in range(occupied):
            ts_ref[j, at, :] = t[j * per_device : (j + 1) * per_device]
    here = pl.ds(pos_ref[0] * per_device, per_device)
    x_left = jnp.concatenate([xs_ref[here, i, :] for i in range(occupied)], axis=0)
    left = jnp.concatenate([own_ref[0, 1], x_left.astype(jnp.bfloat16)], axis=1)
    for j in range(occupied):
        right = jnp.concatenate([xs_ref[:, j, :], ts_ref[j]], axis=1).astype(jnp.bfloat16)
        cs_ref[j] = contract_last(left, right).reshape(occupied, per_device, virtuals)
    choices = [
        [orb_ref[2 * (labels[e // 2] ^ n) + e % 2] for n in range(4)] for e in range(pairs)
    ]

    def group(g, carry):
        rows = pl.ds(pl.multiple_of(g * 8, 8), 8)
        for v in range(tiles):
            at = slice(v * LANES, (v + 1) * LANES)
            uv = u_ref[rows, at]
            masks = [uv == n for n in range(1, 4)]
            for e in range(pairs):
                x = cs_ref[choices[e][0], e // 2, rows, at]
                for n in range(1, 4):
                    x = jnp.where(masks[n - 1], cs_ref[choices[e][n], e // 2, rows, at], x)
                out_ref[e, rows, at] = half_ref[e, rows, at] + x
        return carry

    lax.fori_loop(0, per_device // 8, group, 0)


def join_kernel(occ_ref, u_ref, half_ref, recv_ref, out_ref, dec_ref, mir_ref, res_ref, sems):
    occupied = occ_ref.shape[0]
    per_device, virtuals = u_ref.shape
    labels, copies = labels_and_copies(occ_ref, occupied)
    spread = 2 * per_device
    ready = set()

    def decode(t):
        ready.add(t)
        start = t * per_device
        low, high = start // 16 * 16, (start + per_device + 15) // 16 * 16
        end = virtuals // LANES * per_device
        for p in range(recv_ref.shape[0]):
            tail = recv_ref[p, end // 16 * 16 : end // 16 * 16 + 16, :]
            k = tail.astype(jnp.float32)[end % 16 : end % 16 + 1, 0:1]
            y = recv_ref[p, low:high, :].astype(jnp.float32)
            y = y[start - low : start - low + per_device]
            size = jnp.log2(jnp.maximum(jnp.abs(y), 2.0**-126)) * (1.0 / POWER) - k
            size = jnp.exp2(size)
            x = jnp.where(y < 0, -size, jnp.where(y > 0, size, 0.0))
            dec_ref[p * per_device : (p + 1) * per_device, :] = x
        mir_ref[t * LANES : (t + 1) * LANES, :] = dec_ref[...].T

    stores = []
    for j in range(occupied):
        for t in range(j * spread // LANES, ((j + 1) * spread - 1) // LANES + 1):
            if t not in ready:
                decode(t)
        u = u_ref[...]
        for i in range(occupied):
            at = pl.ds(pl.multiple_of((2 * j + copies[i]) * per_device, 8), per_device)
            total = half_ref[2 * i + copies[j]] + mir_ref[at, :]
            n = j * occupied + i
            res_ref[n] = jnp.where(u == (labels[j] ^ labels[i]), total, 0.0)
            store = pltpu.make_async_copy(res_ref.at[n], out_ref.at[i, j], sems.at[n])
            store.start()
            stores.append(store)
    for store in stores:
        store.wait()


def permute(x, flip, size):
    return lax.ppermute(x, "vir", [(n, n ^ flip) for n in range(size)])


def body(dests, amps, fock_vir, fock_occ, ladder_ints, cycle_ints, occ_irrep, vir_irrep):
    occupied, _, per_device, virtuals = amps.shape
    pairs = 2 * occupied
    tiles = virtuals // LANES
    rows = occupied * per_device
    kw = ladder_ints.shape[2]
    f32, bf16 = jnp.float32, jnp.bfloat16
    position = lax.axis_index("vir").astype(jnp.int32)
    pos = position.reshape(1)
    smem = pl.BlockSpec(memory_space=pltpu.SMEM)

    def whole(shape):
        return pl.BlockSpec(shape, lambda n: (0,) * len(shape))

    def cost(flops, size):
        return pl.CostEstimate(flops=flops, bytes_accessed=size, transcendentals=0)

    anywhere = pl.BlockSpec(memory_space=pl.ANY)
    quarter = dests // 4
    win, xt = pl.pallas_call(
        prep_kernel,
        grid=(1,),
        out_shape=(
            jax.ShapeDtypeStruct((16, LANES), bf16),
            jax.ShapeDtypeStruct((1, 2, rows, LANES), bf16),
        ),
        in_specs=[
            whole((rows, LANES)),
            pl.BlockSpec((occupied, occupied, per_device, LANES), lambda n: (0, 0, 0, 0)),
        ],
        out_specs=(whole((16, LANES)), whole((1, 2, rows, LANES))),
        scratch_shapes=[pltpu.VMEM((rows, LANES), f32)],
        compiler_params=params(60),
        cost_estimate=cost(0, 500000),
    )(cycle_ints.reshape(rows, LANES), amps)
    vmem = pl.BlockSpec(memory_space=pltpu.VMEM)
    mix, u = pl.pallas_call(
        setup_kernel,
        out_shape=(
            jax.ShapeDtypeStruct((rows, rows), bf16),
            jax.ShapeDtypeStruct((per_device, virtuals), jnp.int32),
        ),
        in_specs=[smem, smem, vmem, vmem],
        out_specs=(vmem, vmem),
        compiler_params=params(4),
        cost_estimate=cost(10**7, 300000),
    )(pos, vir_irrep, fock_occ, vir_irrep.reshape(1, virtuals))

    flat_amps = amps.reshape(occupied, rows, virtuals)
    parts = (4, 4)
    wide = 2

    def fock_part(n, after):
        first, count = sum(parts[:n]), parts[n]
        return pl.pallas_call(
            functools.partial(fock_kernel, first),
            grid=(count // wide,),
            out_shape=jax.ShapeDtypeStruct((2 * count, per_device, virtuals), f32),
            in_specs=[
                smem,
                pl.BlockSpec((wide, rows, virtuals), lambda i: (i + first // wide, 0, 0)),
                whole(fock_vir.shape),
                whole(mix.shape),
                whole((per_device, virtuals)),
                anywhere,
            ],
            out_specs=pl.BlockSpec((2 * wide, per_device, virtuals), lambda i: (i, 0, 0)),
            scratch_shapes=[pltpu.VMEM((occupied, per_device, virtuals), f32)],
            compiler_params=params(12),
            cost_estimate=cost(3 * count * rows * virtuals * virtuals, 2 * 10**6),
        )(occ_irrep, flat_amps, fock_vir, mix, u, after)

    flips = [m << 2 for m in range(1, quarter)]
    win_shape = (occupied, occupied, LANES)
    wins = [win] + [permute(win, flip, dests) for flip in flips]
    blocks = [xt] + [permute(xt, flip, dests) for flip in flips]
    half0 = fock_part(0, mix)
    win = pl.pallas_call(
        unpack_kernel,
        out_shape=jax.ShapeDtypeStruct(win_shape, f32),
        in_specs=[smem] + [vmem] * quarter + [anywhere],
        out_specs=vmem,
        compiler_params=params(4),
        cost_estimate=cost(0, 10**5),
    )(pos, *wins, half0)

    def add(a, b, after):
        return pl.pallas_call(
            add_kernel,
            out_shape=jax.ShapeDtypeStruct(a.shape, a.dtype),
            in_specs=[vmem, vmem, anywhere],
            out_specs=vmem,
            compiler_params=params(4),
            cost_estimate=cost(0, 10**5),
        )(a, b, after)

    win_y = permute(win, 2, dests)
    half1 = fock_part(1, win)
    win = add(win, win_y, half1)
    win_mate = permute(win, 1, dests)
    near = stack(blocks, win)
    near_y = permute(near, 2, dests)

    send_rows = tiles * per_device + 8
    half, send = pl.pallas_call(
        functools.partial(ladder_kernel, parts),
        grid=(per_device // 8,),
        out_shape=(
            jax.ShapeDtypeStruct((pairs, per_device, virtuals), f32),
            jax.ShapeDtypeStruct((dests, send_rows, LANES), bf16),
        ),
        in_specs=[smem, whole(win_shape), whole(win_shape)]
        + [pl.BlockSpec((2 * count, 8, virtuals), lambda n: (0, n, 0)) for count in parts]
        + [whole((per_device, virtuals)), pl.BlockSpec((8, virtuals, kw), lambda n: (n, 0, 0)), anywhere],
        out_specs=(
            pl.BlockSpec((pairs, 8, virtuals), lambda n: (0, n, 0)),
            whole((dests, send_rows, LANES)),
        ),
        scratch_shapes=[
            pltpu.VMEM((occupied * occupied, LANES), f32),
            pltpu.VMEM((tiles, 8 * pairs, LANES), f32),
            pltpu.VMEM((dests, send_rows, LANES), f32),
            pltpu.VMEM((8, LANES), f32),
        ],
        compiler_params=params(16),
        cost_estimate=cost(4 * occupied * rows * virtuals * LANES, 25 * 10**6),
    )(occ_irrep, win, win_mate, half0, half1, u, ladder_ints, near)

    recv = lax.all_to_all(send, "vir", split_axis=0, concat_axis=0, tiled=True)
    own_blocks = stack([near, near_y], send)
    mate_blocks = permute(own_blocks, 1, dests)
    half = pl.pallas_call(
        cycle_kernel,
        out_shape=jax.ShapeDtypeStruct((pairs, per_device, virtuals), f32),
        in_specs=[smem, smem] + [vmem] * 4,
        out_specs=vmem,
        scratch_shapes=[
            pltpu.SMEM((occupied,), jnp.int32),
            pltpu.VMEM((occupied, occupied, per_device, virtuals), f32),
            pltpu.VMEM((virtuals, occupied, LANES), f32),
            pltpu.VMEM((occupied, virtuals, LANES), f32),
        ],
        compiler_params=params(28),
        cost_estimate=cost(1000, 1000),
    )(pos, occ_irrep, own_blocks, mate_blocks, half, u)

    return pl.pallas_call(
        join_kernel,
        out_shape=jax.ShapeDtypeStruct((occupied, occupied, per_device, virtuals), f32),
        in_specs=[smem, vmem, vmem, vmem],
        out_specs=anywhere,
        scratch_shapes=[
            pltpu.VMEM((virtuals, LANES), f32),
            pltpu.VMEM((tiles * LANES, virtuals), f32),
            pltpu.VMEM((occupied * occupied, per_device, virtuals), f32),
            pltpu.SemaphoreType.DMA((occupied * occupied,)),
        ],
        compiler_params=params(16),
        cost_estimate=cost(10**6, 5 * 10**6),
    )(occ_irrep, u, half, recv)


def solution(mesh):
    dests = mesh.shape["vir"]

    def run(amps, *rest):
        occupied, _, per_device, virtuals = amps.shape
        tiled = (
            dests == 16
            and per_device % 8 == 0
            and virtuals % LANES == 0
            and 2 * occupied * per_device == virtuals
            and rest[2].shape[2] == LANES
            and rest[3].shape[2] == LANES
        )
        return body(dests, amps, *rest) if tiled else plain_body(amps, *rest)

    return jax.shard_map(
        run,
        mesh=mesh,
        in_specs=(
            P("groups", None, "vir", None),
            P("groups", None),
            P("groups", None),
            P("vir", "groups", None),
            P("vir", "groups", None),
            P("groups"),
            P("groups"),
        ),
        out_specs=P("groups", None, "vir", None),
        check_vma=False,
    )
```

```python
import functools

import jax
import jax.numpy as jnp
from jax import lax
from jax.experimental import pallas as pl
from jax.experimental.pallas import tpu as pltpu
from jax.sharding import PartitionSpec as P

DW = 8
CW = 16
LANES = 128
POWER = 9
TOP_EXPONENT = 13


def contract_last(left_side, right_side):
    return lax.dot_general(
        left_side, right_side, (((1,), (1,)), ((), ())), preferred_element_type=jnp.float32
    )


def plain_body(amps, fock_vir, fock_occ, ladder_ints, cycle_ints, occ_irrep, vir_irrep):
    occupied = amps.shape[0]
    per_device = amps.shape[2]
    virtuals = amps.shape[3]
    pair_count = occupied * occupied
    position = lax.axis_index("vir")
    fock_term = jnp.dot(
        amps.reshape(pair_count * per_device, virtuals),
        fock_vir,
        preferred_element_type=jnp.float32,
    ).reshape(occupied, occupied, per_device, virtuals)
    occ_term = jnp.einsum("ikab,kj->ijab", amps, fock_occ, preferred_element_type=jnp.float32)
    flat_ints = ladder_ints.reshape(per_device * virtuals, ladder_ints.shape[2])
    local_window = amps[:, :, 0:1, :DW]
    local_cycle = amps[:, :, :, :CW]
    segment = lax.all_gather(local_window, "vir", axis=2, tiled=True)
    width = segment.shape[2] * DW
    ladder = contract_last(segment.reshape(pair_count, width), flat_ints)
    left_side = jnp.transpose(local_cycle, (0, 2, 1, 3)).reshape(
        occupied * per_device, occupied * CW
    )
    segment = lax.all_gather(cycle_ints, "vir", axis=0, tiled=True)
    right_side = segment.reshape(segment.shape[0] * occupied, occupied * CW)
    cycle_block = contract_last(left_side, right_side).reshape(
        occupied, per_device, segment.shape[0], occupied
    )
    cycle_part = jnp.transpose(cycle_block, (0, 3, 1, 2))
    half_sum = (
        fock_term - occ_term + ladder.reshape(occupied, occupied, per_device, virtuals) + cycle_part
    )
    vir_local = lax.dynamic_slice_in_dim(vir_irrep, position * per_device, per_device)
    occ_pair = jnp.bitwise_xor(occ_irrep[:, None], occ_irrep[None, :])
    vir_pair = jnp.bitwise_xor(vir_local[:, None], vir_irrep[None, :])
    received = lax.all_to_all(half_sum, "vir", split_axis=3, concat_axis=2, tiled=True)
    mirrored = jnp.transpose(received, (1, 0, 3, 2))
    product_irrep = jnp.bitwise_xor(occ_pair[:, :, None, None], vir_pair[None, None, :, :])
    allowed = jnp.where(product_irrep == 0, jnp.float32(1.0), jnp.float32(0.0))
    return allowed * (half_sum + mirrored)


def params(mib):
    return pltpu.CompilerParams(vmem_limit_bytes=mib * 2**20)


def labels_and_copies(occ_ref, occupied):
    labels = [occ_ref[j] for j in range(occupied)]
    copies = []
    for j in range(occupied):
        s = jnp.int32(0)
        for k in range(j):
            s = s + (labels[k] == labels[j]).astype(jnp.int32)
        copies.append(s)
    return labels, copies


def prep_kernel(pos_ref, vir_ref, row_ref, occ_vals_ref, amps_ref, win_ref, mix_ref, u_ref, t_ref, acc_ref):
    dests = win_ref.shape[0]
    occupied, _, per_device, _ = amps_ref.shape
    rows = occupied * per_device
    row = row_ref[...]
    for a in range(per_device):
        u_ref[a : a + 1, :] = row ^ vir_ref[pos_ref[0] * per_device + a]
    at = lax.broadcasted_iota(jnp.int32, (rows, occupied), 0)
    start = lax.broadcasted_iota(jnp.int32, (rows, occupied), 1) * per_device
    in_block = jnp.logical_and(at >= start, at < start + per_device).astype(jnp.bfloat16)
    at = lax.broadcasted_iota(jnp.int32, (rows, per_device), 0)
    col = lax.broadcasted_iota(jnp.int32, (rows, per_device), 1)
    same = at == col
    for n in range(1, occupied):
        same = jnp.logical_or(same, at == col + n * per_device)
    same = same.astype(jnp.bfloat16)
    left = contract_last(in_block, occ_vals_ref[...]).astype(jnp.bfloat16)
    mix = contract_last(left, in_block) * contract_last(same, same)
    mix_ref[...] = mix.astype(jnp.bfloat16)
    lane = lax.broadcasted_iota(jnp.int32, (occupied, LANES), 1)
    packed = jnp.zeros((occupied, LANES), jnp.float32)
    for j in range(occupied):
        w = jnp.where(lane < DW, amps_ref[:, j, 0, :LANES].astype(jnp.float32), 0.0)
        packed = packed + (pltpu.roll(w, j * DW, axis=1) if j else w)
    packed = jnp.concatenate([packed, jnp.zeros_like(packed)], axis=0).astype(jnp.bfloat16)
    for q in range(dests):
        win_ref[q] = packed
    lane = lax.broadcasted_iota(jnp.int32, (per_device, LANES), 1)
    for i in range(occupied):
        acc = jnp.zeros((per_device, LANES), jnp.float32)
        for k in range(occupied):
            piece = jnp.where(lane < CW, amps_ref[i, k, :, :LANES].astype(jnp.float32), 0.0)
            acc = acc + (pltpu.roll(piece, k * CW, axis=1) if k else piece)
        acc_ref[i * per_device : (i + 1) * per_device, :] = acc
    t_ref[0] = acc_ref[...].astype(jnp.bfloat16)


def fock_kernel(occ_ref, amps_ref, fock_ref, mix_ref, u_ref, half_ref, hs_ref):
    wide, rows, virtuals = amps_ref.shape
    _, per_device, _ = half_ref.shape
    occupied = occ_ref.shape[0]
    labels, copies = labels_and_copies(occ_ref, occupied)
    u = u_ref[...]
    h = jnp.dot(
        amps_ref[...].reshape(wide * rows, virtuals),
        fock_ref[...],
        preferred_element_type=jnp.float32,
    )
    for w in range(wide):
        a = amps_ref[w]
        mixed = jnp.dot(mix_ref[...], a, preferred_element_type=jnp.float32)
        hs_ref[...] = (h[w * rows : (w + 1) * rows] - mixed).reshape(hs_ref.shape)
        own = occ_ref[pl.program_id(0) * wide + w]
        for j in range(occupied):
            at = 2 * w + copies[j]
            half_ref[at] = jnp.where(u == (own ^ labels[j]), hs_ref[j], half_ref[at])


def stack(blocks, after):
    count = len(blocks)

    def kernel(*refs):
        out = refs[count + 1]
        at = 0
        for n in range(count):
            head = blocks[n].shape[0]
            out[at : at + head] = refs[n][...]
            at += head

    vmem = pl.BlockSpec(memory_space=pltpu.VMEM)
    shape = (sum(b.shape[0] for b in blocks),) + blocks[0].shape[1:]
    return pl.pallas_call(
        kernel,
        out_shape=jax.ShapeDtypeStruct(shape, blocks[0].dtype),
        in_specs=[vmem] * count + [pl.BlockSpec(memory_space=pl.ANY)],
        out_specs=vmem,
        compiler_params=params(4),
        cost_estimate=pl.CostEstimate(flops=0, bytes_accessed=10**6, transcendentals=0),
    )(*blocks, after)


def payload_pieces(per_device, pairs, dests):
    out = {}
    for q in range(dests):
        for e in range(pairs):
            start = 0
            while start < per_device:
                src = q * per_device + start
                dst = e * per_device + start
                length = min(LANES - src % LANES, LANES - dst % LANES, per_device - start)
                out.setdefault((q, dst // LANES), []).append(
                    (dst % LANES, e, src // LANES, (dst - src) % LANES)
                )
                start += length
    return out


def ladder_kernel(
    groups, occ_ref, win_ref, half_ref, u_ref, lad_ref, _, out_ref, send_ref,
    w1_ref, w2_ref, hs_ref, pay_ref, code_ref, half_sems, send_sems, *ls_refs
):
    occupied = occ_ref.shape[0]
    pairs, per_device, virtuals = hs_ref.shape
    dests = pay_ref.shape[0]
    tiles = virtuals // LANES
    labels, copies = labels_and_copies(occ_ref, occupied)
    lane = lax.broadcasted_iota(jnp.int32, (8, LANES), 1)
    for j in range(occupied):
        total = jnp.zeros((8, LANES), jnp.float32)
        for p in range(dests):
            w = win_ref[p].astype(jnp.float32)[:8]
            w = jnp.where(jnp.logical_and(lane >= j * DW, lane < (j + 1) * DW), w, 0.0)
            shift = (p - j) * DW % LANES
            total = total + (pltpu.roll(w, shift, axis=1) if shift else w)
        w1_ref[j] = total
    for i in range(occupied):
        for j in range(occupied):
            row = (labels[i] ^ labels[j]) * pairs + 2 * i + copies[j]
            w2_ref[pl.ds(row, 1), :] = w1_ref[j, i : i + 1, :]
    w2 = w2_ref[...].astype(jnp.bfloat16)
    pieces_of = payload_pieces(per_device, pairs, dests)
    tops = [jnp.zeros((8, LANES), jnp.float32)]

    def ladder(g, a):
        product = contract_last(w2, lad_ref[8 * g + a])
        ua = u_ref[8 * g + a : 8 * g + a + 1, :]
        sel = product[0:pairs]
        for v in range(1, 4):
            sel = jnp.where(ua == v, product[v * pairs : (v + 1) * pairs], sel)
        for v in range(tiles):
            ls_refs[g][v, pl.ds(a, pairs, stride=8), :] = sel[:, v * LANES : (v + 1) * LANES]

    def payload(g):
        rows = slice(8 * g, 8 * g + 8)
        found = {}
        for t in range(tiles):
            last_e = min(((t + 1) * LANES - 1) // per_device, pairs - 1)
            for e in range(t * LANES // per_device, last_e + 1):
                if (e, 0) in found:
                    continue
                for v in range(tiles):
                    at = slice(v * LANES, (v + 1) * LANES)
                    x = half_ref[e, rows, at] + ls_refs[g][v, 8 * e : 8 * e + 8, :]
                    hs_ref[e, rows, at] = x
                    tops[0] = jnp.maximum(tops[0], jnp.abs(x))
                    found[e, v] = x
            for q in range(dests):
                acc = None
                for first, e, v, shift in pieces_of[q, t]:
                    x = pltpu.roll(found[e, v], shift, axis=1) if shift else found[e, v]
                    acc = x if acc is None else jnp.where(lane >= first, x, acc)
                start = t * per_device + 8 * g
                pay_ref[q, start : start + 8, :] = acc
                if q % 8 == 7:
                    yield

    stores = []
    for g in range(groups + 1):
        before = payload(g - 1) if g else iter(())
        for a in range(8):
            if g < groups:
                ladder(g, a)
            next(before, None)
        for _ in before:
            pass
        if g:
            rows = pl.ds(8 * (g - 1), 8)
            store = pltpu.make_async_copy(
                hs_ref.at[:, rows, :], out_ref.at[:, rows, :], half_sems.at[g - 1]
            )
            store.start()
            stores.append(store)
    most = jnp.max(jnp.max(tops[0], axis=0, keepdims=True), axis=1, keepdims=True)
    k = jnp.floor(TOP_EXPONENT - jnp.log2(jnp.maximum(most, 1e-30)))
    scale = jnp.exp2(k)
    row = lax.broadcasted_iota(jnp.int32, pay_ref.shape[1:], 0)
    for q in range(dests):
        z = pay_ref[q] * scale
        z2 = z * z
        z4 = z2 * z2
        y = jnp.where(row >= tiles * per_device, k, z4 * z4 * z)
        code_ref[q] = y.astype(jnp.bfloat16)
        store = pltpu.make_async_copy(code_ref.at[q], send_ref.at[q], send_sems.at[q])
        store.start()
        stores.append(store)
    for store in stores:
        store.wait()


def cycle_kernel(
    pos_ref, occ_ref, own_ref, mate_ref, half_hbm, u_ref, out_ref, orb_ref, cs_ref, xs_ref, ts_ref,
    half_ref, sems,
):
    occupied = occ_ref.shape[0]
    pairs, per_device, virtuals = half_ref.shape
    dests, rows, _ = own_ref.shape
    load = pltpu.make_async_copy(half_hbm, half_ref, sems.at[0])
    load.start()
    tiles = virtuals // LANES
    labels, copies = labels_and_copies(occ_ref, occupied)
    for j in range(occupied):
        orb_ref[2 * labels[j] + copies[j]] = jnp.int32(j)
    for r in range(dests):
        ref = mate_ref if r & 1 else own_ref
        n = ((r >> 1) & 1) * (dests // 2) + (r >> 2)
        p = pos_ref[0] ^ r
        x = ref[n].astype(jnp.float32).reshape(per_device, occupied, LANES)
        xs_ref[pl.ds(p * per_device, per_device)] = x
        t = ref[n + dests // 4].astype(jnp.float32)
        at = pl.ds(pl.multiple_of(p * per_device, 8), per_device)
        for j in range(occupied):
            ts_ref[j, at, :] = t[j * per_device : (j + 1) * per_device]
    here = pl.ds(pos_ref[0] * per_device, per_device)
    x_left = jnp.concatenate([xs_ref[here, i, :] for i in range(occupied)], axis=0)
    left = jnp.concatenate([own_ref[dests // 4], x_left.astype(jnp.bfloat16)], axis=1)
    for j in range(occupied):
        right = jnp.concatenate([xs_ref[:, j, :], ts_ref[j]], axis=1).astype(jnp.bfloat16)
        cs_ref[j] = contract_last(left, right).reshape(occupied, per_device, virtuals)
    load.wait()
    choices = [
        [orb_ref[2 * (labels[e // 2] ^ n) + e % 2] for n in range(4)] for e in range(pairs)
    ]

    def group(g, carry):
        rows = pl.ds(pl.multiple_of(g * 8, 8), 8)
        for v in range(tiles):
            at = slice(v * LANES, (v + 1) * LANES)
            uv = u_ref[rows, at]
            masks = [uv == n for n in range(1, 4)]
            for e in range(pairs):
                x = cs_ref[choices[e][0], e // 2, rows, at]
                for n in range(1, 4):
                    x = jnp.where(masks[n - 1], cs_ref[choices[e][n], e // 2, rows, at], x)
                out_ref[e, rows, at] = half_ref[e, rows, at] + x
        return carry

    lax.fori_loop(0, per_device // 8, group, 0)


def join_kernel(occ_ref, u_ref, half_ref, recv_ref, out_ref, dec_ref, mir_ref, res_ref, sems):
    occupied = occ_ref.shape[0]
    per_device, virtuals = u_ref.shape
    labels, copies = labels_and_copies(occ_ref, occupied)
    spread = 2 * per_device
    ready = set()

    def decode(t):
        ready.add(t)
        start = t * per_device
        low, high = start // 16 * 16, (start + per_device + 15) // 16 * 16
        end = virtuals // LANES * per_device
        for p in range(recv_ref.shape[0]):
            tail = recv_ref[p, end // 16 * 16 : end // 16 * 16 + 16, :]
            k = tail.astype(jnp.float32)[end % 16 : end % 16 + 1, 0:1]
            y = recv_ref[p, low:high, :].astype(jnp.float32)
            y = y[start - low : start - low + per_device]
            size = jnp.log2(jnp.maximum(jnp.abs(y), 2.0**-126)) * (1.0 / POWER) - k
            size = jnp.exp2(size)
            x = jnp.where(y < 0, -size, jnp.where(y > 0, size, 0.0))
            dec_ref[p * per_device : (p + 1) * per_device, :] = x
        mir_ref[t * LANES : (t + 1) * LANES, :] = dec_ref[...].T

    stores = []
    for j in range(occupied):
        for t in range(j * spread // LANES, ((j + 1) * spread - 1) // LANES + 1):
            if t not in ready:
                decode(t)
        u = u_ref[...]
        for i in range(occupied):
            at = pl.ds(pl.multiple_of((2 * j + copies[i]) * per_device, 8), per_device)
            total = half_ref[2 * i + copies[j]] + mir_ref[at, :]
            n = j * occupied + i
            res_ref[n] = jnp.where(u == (labels[j] ^ labels[i]), total, 0.0)
            store = pltpu.make_async_copy(res_ref.at[n], out_ref.at[i, j], sems.at[n])
            store.start()
            stores.append(store)
    for store in stores:
        store.wait()


def permute(x, flip, size):
    return lax.ppermute(x, "vir", [(n, n ^ flip) for n in range(size)])


def body(dests, amps, fock_vir, fock_occ, ladder_ints, cycle_ints, occ_irrep, vir_irrep):
    occupied, _, per_device, virtuals = amps.shape
    pairs = 2 * occupied
    tiles = virtuals // LANES
    rows = occupied * per_device
    kw = ladder_ints.shape[2]
    f32, bf16 = jnp.float32, jnp.bfloat16
    position = lax.axis_index("vir").astype(jnp.int32)
    pos = position.reshape(1)
    smem = pl.BlockSpec(memory_space=pltpu.SMEM)

    def whole(shape):
        return pl.BlockSpec(shape, lambda n: (0,) * len(shape))

    def cost(flops, size):
        return pl.CostEstimate(flops=flops, bytes_accessed=size, transcendentals=0)

    anywhere = pl.BlockSpec(memory_space=pl.ANY)
    quarter = dests // 4
    vmem = pl.BlockSpec(memory_space=pltpu.VMEM)
    hbm = pl.BlockSpec(memory_space=pltpu.HBM)
    x = cycle_ints.reshape(1, rows, LANES)
    flips = [m << 2 for m in range(1, quarter)]
    x_blocks = [x] + [permute(x, flip, dests) for flip in flips]
    win, mix, u, t = pl.pallas_call(
        prep_kernel,
        out_shape=(
            jax.ShapeDtypeStruct((dests, 16, LANES), bf16),
            jax.ShapeDtypeStruct((rows, rows), bf16),
            jax.ShapeDtypeStruct((per_device, virtuals), jnp.int32),
            jax.ShapeDtypeStruct((1, rows, LANES), bf16),
        ),
        in_specs=[smem, smem, vmem, vmem, vmem],
        out_specs=(vmem,) * 4,
        scratch_shapes=[pltpu.VMEM((rows, LANES), f32)],
        compiler_params=params(12),
        cost_estimate=cost(0, 10**6),
    )(pos, vir_irrep, vir_irrep.reshape(1, virtuals), fock_occ, amps)

    wins = lax.all_to_all(win, "vir", split_axis=0, concat_axis=0, tiled=True)
    t_blocks = [t] + [permute(t, flip, dests) for flip in flips]
    wide = 2
    half = pl.pallas_call(
        fock_kernel,
        grid=(occupied // wide,),
        out_shape=jax.ShapeDtypeStruct((pairs, per_device, virtuals), f32),
        in_specs=[
            smem,
            pl.BlockSpec((wide, rows, virtuals), lambda i: (i, 0, 0)),
            whole(fock_vir.shape),
            whole(mix.shape),
            whole(u.shape),
        ],
        out_specs=pl.BlockSpec((2 * wide, per_device, virtuals), lambda i: (i, 0, 0)),
        scratch_shapes=[pltpu.VMEM((occupied, per_device, virtuals), f32)],
        compiler_params=params(12),
        cost_estimate=cost(3 * occupied * rows * virtuals * virtuals, 8 * 10**6),
    )(occ_irrep, amps.reshape(occupied, rows, virtuals), fock_vir, mix, u)

    near = stack(x_blocks + t_blocks, half)
    near_y = permute(near, 2, dests)
    send_rows = tiles * per_device + 8
    groups = per_device // 8
    half, send = pl.pallas_call(
        functools.partial(ladder_kernel, groups),
        out_shape=(
            jax.ShapeDtypeStruct((pairs, per_device, virtuals), f32),
            jax.ShapeDtypeStruct((dests, send_rows, LANES), bf16),
        ),
        in_specs=[smem] + [vmem] * 4 + [anywhere],
        out_specs=(hbm, hbm),
        scratch_shapes=[
            pltpu.VMEM((occupied, occupied, LANES), f32),
            pltpu.VMEM((occupied * occupied, LANES), f32),
            pltpu.VMEM((pairs, per_device, virtuals), f32),
            pltpu.VMEM((dests, send_rows, LANES), f32),
            pltpu.VMEM((dests, send_rows, LANES), bf16),
            pltpu.SemaphoreType.DMA((groups,)),
            pltpu.SemaphoreType.DMA((dests,)),
        ]
        + [pltpu.VMEM((tiles, 8 * pairs, LANES), f32)] * groups,
        compiler_params=params(24),
        cost_estimate=cost(4 * occupied * rows * virtuals * LANES, 9 * 10**6),
    )(occ_irrep, wins, half, u, ladder_ints, near)

    recv = lax.all_to_all(send, "vir", split_axis=0, concat_axis=0, tiled=True)
    own_blocks = stack([near, near_y], send)
    mate_blocks = permute(own_blocks, 1, dests)
    half = pl.pallas_call(
        cycle_kernel,
        out_shape=jax.ShapeDtypeStruct((pairs, per_device, virtuals), f32),
        in_specs=[smem, smem, vmem, vmem, hbm, vmem],
        out_specs=vmem,
        scratch_shapes=[
            pltpu.SMEM((occupied,), jnp.int32),
            pltpu.VMEM((occupied, occupied, per_device, virtuals), f32),
            pltpu.VMEM((virtuals, occupied, LANES), f32),
            pltpu.VMEM((occupied, virtuals, LANES), f32),
            pltpu.VMEM((pairs, per_device, virtuals), f32),
            pltpu.SemaphoreType.DMA((1,)),
        ],
        compiler_params=params(28),
        cost_estimate=cost(1000, 1000),
    )(pos, occ_irrep, own_blocks, mate_blocks, half, u)

    return pl.pallas_call(
        join_kernel,
        out_shape=jax.ShapeDtypeStruct((occupied, occupied, per_device, virtuals), f32),
        in_specs=[smem, vmem, vmem, vmem],
        out_specs=anywhere,
        scratch_shapes=[
            pltpu.VMEM((virtuals, LANES), f32),
            pltpu.VMEM((tiles * LANES, virtuals), f32),
            pltpu.VMEM((occupied * occupied, per_device, virtuals), f32),
            pltpu.SemaphoreType.DMA((occupied * occupied,)),
        ],
        compiler_params=params(16),
        cost_estimate=cost(10**6, 5 * 10**6),
    )(occ_irrep, u, half, recv)


def solution(mesh):
    dests = mesh.shape["vir"]

    def run(amps, *rest):
        occupied, _, per_device, virtuals = amps.shape
        tiled = (
            dests == 16
            and per_device % 8 == 0
            and virtuals % LANES == 0
            and 2 * occupied * per_device == virtuals
            and rest[2].shape[2] == LANES
            and rest[3].shape[2] == LANES
        )
        return body(dests, amps, *rest) if tiled else plain_body(amps, *rest)

    return jax.shard_map(
        run,
        mesh=mesh,
        in_specs=(
            P("groups", None, "vir", None),
            P("groups", None),
            P("groups", None),
            P("vir", "groups", None),
            P("vir", "groups", None),
            P("groups"),
            P("groups"),
        ),
        out_specs=P("groups", None, "vir", None),
        check_vma=False,
    )
```

```python
import functools

import jax
import jax.numpy as jnp
from jax import lax
from jax.experimental import pallas as pl
from jax.experimental.pallas import tpu as pltpu
from jax.sharding import PartitionSpec as P

DW = 8
CW = 16
LANES = 128
POWER = 9
TOP_EXPONENT = 13


def contract_last(left_side, right_side):
    return lax.dot_general(
        left_side, right_side, (((1,), (1,)), ((), ())), preferred_element_type=jnp.float32
    )


def plain_body(amps, fock_vir, fock_occ, ladder_ints, cycle_ints, occ_irrep, vir_irrep):
    occupied = amps.shape[0]
    per_device = amps.shape[2]
    virtuals = amps.shape[3]
    pair_count = occupied * occupied
    position = lax.axis_index("vir")
    fock_term = jnp.dot(
        amps.reshape(pair_count * per_device, virtuals),
        fock_vir,
        preferred_element_type=jnp.float32,
    ).reshape(occupied, occupied, per_device, virtuals)
    occ_term = jnp.einsum("ikab,kj->ijab", amps, fock_occ, preferred_element_type=jnp.float32)
    flat_ints = ladder_ints.reshape(per_device * virtuals, ladder_ints.shape[2])
    local_window = amps[:, :, 0:1, :DW]
    local_cycle = amps[:, :, :, :CW]
    segment = lax.all_gather(local_window, "vir", axis=2, tiled=True)
    width = segment.shape[2] * DW
    ladder = contract_last(segment.reshape(pair_count, width), flat_ints)
    left_side = jnp.transpose(local_cycle, (0, 2, 1, 3)).reshape(
        occupied * per_device, occupied * CW
    )
    segment = lax.all_gather(cycle_ints, "vir", axis=0, tiled=True)
    right_side = segment.reshape(segment.shape[0] * occupied, occupied * CW)
    cycle_block = contract_last(left_side, right_side).reshape(
        occupied, per_device, segment.shape[0], occupied
    )
    cycle_part = jnp.transpose(cycle_block, (0, 3, 1, 2))
    half_sum = (
        fock_term - occ_term + ladder.reshape(occupied, occupied, per_device, virtuals) + cycle_part
    )
    vir_local = lax.dynamic_slice_in_dim(vir_irrep, position * per_device, per_device)
    occ_pair = jnp.bitwise_xor(occ_irrep[:, None], occ_irrep[None, :])
    vir_pair = jnp.bitwise_xor(vir_local[:, None], vir_irrep[None, :])
    received = lax.all_to_all(half_sum, "vir", split_axis=3, concat_axis=2, tiled=True)
    mirrored = jnp.transpose(received, (1, 0, 3, 2))
    product_irrep = jnp.bitwise_xor(occ_pair[:, :, None, None], vir_pair[None, None, :, :])
    allowed = jnp.where(product_irrep == 0, jnp.float32(1.0), jnp.float32(0.0))
    return allowed * (half_sum + mirrored)


def params(mib):
    return pltpu.CompilerParams(vmem_limit_bytes=mib * 2**20)


def labels_and_copies(occ_ref, occupied):
    labels = [occ_ref[j] for j in range(occupied)]
    copies = []
    for j in range(occupied):
        s = jnp.int32(0)
        for k in range(j):
            s = s + (labels[k] == labels[j]).astype(jnp.int32)
        copies.append(s)
    return labels, copies


def prep_kernel(
    pos_ref, cyc_ref, amps_ref, vir_ref, occ_vals_ref,
    win_ref, xt_ref, mix_ref, u_ref,
    corner_ref, acc_ref, vals_ref, row_ref, vir_smem, sems,
):
    occupied, _, per_device, _ = amps_ref.shape
    rows = occupied * per_device
    moves = [
        (amps_ref.at[:, :, :, :LANES], corner_ref),
        (occ_vals_ref, vals_ref),
        (vir_ref, row_ref),
        (vir_ref, vir_smem),
        (cyc_ref, xt_ref.at[0, 0]),
    ]
    copies = [pltpu.make_async_copy(s, d, sems.at[n]) for n, (s, d) in enumerate(moves)]
    for copy in copies:
        copy.start()
    for copy in copies[1:4]:
        copy.wait()
    row = row_ref[...].reshape(1, u_ref.shape[1])
    for a in range(per_device):
        u_ref[a : a + 1, :] = row ^ vir_smem[pos_ref[0] * per_device + a]
    at = lax.broadcasted_iota(jnp.int32, (rows, occupied), 0)
    start = lax.broadcasted_iota(jnp.int32, (rows, occupied), 1) * per_device
    in_block = jnp.logical_and(at >= start, at < start + per_device).astype(jnp.bfloat16)
    at = lax.broadcasted_iota(jnp.int32, (rows, per_device), 0)
    col = lax.broadcasted_iota(jnp.int32, (rows, per_device), 1)
    same = at == col
    for n in range(1, occupied):
        same = jnp.logical_or(same, at == col + n * per_device)
    same = same.astype(jnp.bfloat16)
    left = contract_last(in_block, vals_ref[...]).astype(jnp.bfloat16)
    mix = contract_last(left, in_block) * contract_last(same, same)
    mix_ref[...] = mix.astype(jnp.bfloat16)
    copies[0].wait()
    lane = lax.broadcasted_iota(jnp.int32, (occupied, LANES), 1)
    packed = jnp.zeros((occupied, LANES), jnp.float32)
    for j in range(occupied):
        w = jnp.where(lane < DW, corner_ref[:, j, 0, :].astype(jnp.float32), 0.0)
        packed = packed + (pltpu.roll(w, j * DW, axis=1) if j else w)
    packed = jnp.concatenate([packed, jnp.zeros_like(packed)], axis=0).astype(jnp.bfloat16)
    win_ref[...] = packed
    lane = lax.broadcasted_iota(jnp.int32, (per_device, LANES), 1)
    for i in range(occupied):
        acc = jnp.zeros((per_device, LANES), jnp.float32)
        for k in range(occupied):
            piece = jnp.where(lane < CW, corner_ref[i, k].astype(jnp.float32), 0.0)
            acc = acc + (pltpu.roll(piece, k * CW, axis=1) if k else piece)
        acc_ref[i * per_device : (i + 1) * per_device, :] = acc
    xt_ref[0, 1] = acc_ref[...].astype(jnp.bfloat16)
    copies[4].wait()


def fock_kernel(occ_ref, amps_ref, fock_ref, mix_ref, u_ref, _0, _1, _2, half_ref, hs_ref):
    wide, rows, virtuals = amps_ref.shape
    _, per_device, _ = half_ref.shape
    occupied = occ_ref.shape[0]
    labels, copies = labels_and_copies(occ_ref, occupied)
    u = u_ref[...]
    h = jnp.dot(
        amps_ref[...].reshape(wide * rows, virtuals),
        fock_ref[...],
        preferred_element_type=jnp.float32,
    )
    for w in range(wide):
        a = amps_ref[w]
        mixed = jnp.dot(mix_ref[...], a, preferred_element_type=jnp.float32)
        hs_ref[...] = (h[w * rows : (w + 1) * rows] - mixed).reshape(hs_ref.shape)
        own = occ_ref[pl.program_id(0) * wide + w]
        for j in range(occupied):
            at = 2 * w + copies[j]
            half_ref[at] = jnp.where(u == (own ^ labels[j]), hs_ref[j], half_ref[at])


def stack(blocks, after):
    count = len(blocks)

    def kernel(*refs):
        out = refs[count + 1]
        at = 0
        for n in range(count):
            head = blocks[n].shape[0]
            out[at : at + head] = refs[n][...]
            at += head

    vmem = pl.BlockSpec(memory_space=pltpu.VMEM)
    shape = (sum(b.shape[0] for b in blocks),) + blocks[0].shape[1:]
    return pl.pallas_call(
        kernel,
        out_shape=jax.ShapeDtypeStruct(shape, blocks[0].dtype),
        in_specs=[vmem] * count + [pl.BlockSpec(memory_space=pl.ANY)],
        out_specs=vmem,
        compiler_params=params(60),
        cost_estimate=pl.CostEstimate(flops=0, bytes_accessed=10**6, transcendentals=0),
    )(*blocks, after)


def unpack_kernel(pos_ref, *refs):
    blocks, win_ref = refs[:-1], refs[-1]
    occupied, _, lanes = win_ref.shape
    lane = lax.broadcasted_iota(jnp.int32, (8, lanes), 1)
    for j in range(occupied):
        total = jnp.zeros((8, lanes), jnp.float32)
        for m, block in enumerate(blocks):
            p = pos_ref[0] ^ (m << 2)
            w = block[...].astype(jnp.float32)[:8]
            w = jnp.where(jnp.logical_and(lane >= j * DW, lane < (j + 1) * DW), w, 0.0)
            total = total + pltpu.roll(w, lax.rem(p * DW - j * DW + lanes, lanes), axis=1)
        win_ref[j] = total


def payload_pieces(per_device, pairs, dests):
    out = {}
    for q in range(dests):
        for e in range(pairs):
            start = 0
            while start < per_device:
                src = q * per_device + start
                dst = e * per_device + start
                length = min(LANES - src % LANES, LANES - dst % LANES, per_device - start)
                out.setdefault((q, dst // LANES), []).append(
                    (dst % LANES, e, src // LANES, (dst - src) % LANES)
                )
                start += length
    return out


def ladder_kernel(
    groups, occ_ref, win0, win1, win2, win3, half_hbm, u_hbm, lad_hbm, _, out_ref, send_ref,
    win_ref, half_ref, u_ref, lad_ref, w2_ref, hs_ref, pay_ref, code_ref,
    in_sems, half_sems, send_sems, *ls_refs
):
    occupied = occ_ref.shape[0]
    pairs, per_device, virtuals = hs_ref.shape
    dests = pay_ref.shape[0]
    tiles = virtuals // LANES
    moves = [(w, win_ref.at[n]) for n, w in enumerate((win0, win1, win2, win3))]
    moves.append((u_hbm, u_ref))
    moves.extend((lad_hbm.at[pl.ds(8 * g, 8)], lad_ref.at[pl.ds(8 * g, 8)]) for g in range(groups))
    moves.append((half_hbm, half_ref))
    loads = [pltpu.make_async_copy(s, d, in_sems.at[n]) for n, (s, d) in enumerate(moves)]
    for load in loads:
        load.start()
    for load in loads[:5]:
        load.wait()
    labels, copies = labels_and_copies(occ_ref, occupied)
    lane = lax.broadcasted_iota(jnp.int32, (8, LANES), 1)
    for i in range(occupied):
        for j in range(occupied):
            row = (labels[i] ^ labels[j]) * pairs + 2 * i + copies[j]
            at = slice(i, i + 1)
            w = win_ref[0, j, at, :] + win_ref[1, j, at, :]
            w2_ref[pl.ds(row, 1), :] = w + (win_ref[2, j, at, :] + win_ref[3, j, at, :])
    w2 = w2_ref[...].astype(jnp.bfloat16)
    pieces_of = payload_pieces(per_device, pairs, dests)
    tops = [jnp.zeros((8, LANES), jnp.float32)]

    def ladder(g, a):
        product = contract_last(w2, lad_ref[8 * g + a])
        ua = u_ref[8 * g + a : 8 * g + a + 1, :]
        sel = product[0:pairs]
        for v in range(1, 4):
            sel = jnp.where(ua == v, product[v * pairs : (v + 1) * pairs], sel)
        for v in range(tiles):
            ls_refs[g][v, pl.ds(a, pairs, stride=8), :] = sel[:, v * LANES : (v + 1) * LANES]

    def payload(g):
        rows = slice(8 * g, 8 * g + 8)
        found = {}
        for t in range(tiles):
            last_e = min(((t + 1) * LANES - 1) // per_device, pairs - 1)
            for e in range(t * LANES // per_device, last_e + 1):
                if (e, 0) in found:
                    continue
                for v in range(tiles):
                    at = slice(v * LANES, (v + 1) * LANES)
                    x = half_ref[e, rows, at] + ls_refs[g][v, 8 * e : 8 * e + 8, :]
                    hs_ref[e, rows, at] = x
                    tops[0] = jnp.maximum(tops[0], jnp.abs(x))
                    found[e, v] = x
            for q in range(dests):
                acc = None
                for first, e, v, shift in pieces_of[q, t]:
                    x = pltpu.roll(found[e, v], shift, axis=1) if shift else found[e, v]
                    acc = x if acc is None else jnp.where(lane >= first, x, acc)
                start = t * per_device + 8 * g
                pay_ref[q, start : start + 8, :] = acc
                if q % 8 == 7:
                    yield

    stores = []
    for g in range(groups + 1):
        before = payload(g - 1) if g else iter(())
        if g < groups:
            loads[5 + g].wait()
        if g == 1:
            loads[-1].wait()
        for a in range(8):
            if g < groups:
                ladder(g, a)
            next(before, None)
        for _ in before:
            pass
        if g:
            rows = pl.ds(8 * (g - 1), 8)
            store = pltpu.make_async_copy(
                hs_ref.at[:, rows, :], out_ref.at[:, rows, :], half_sems.at[g - 1]
            )
            store.start()
            stores.append(store)
    most = jnp.max(jnp.max(tops[0], axis=0, keepdims=True), axis=1, keepdims=True)
    k = jnp.floor(TOP_EXPONENT - jnp.log2(jnp.maximum(most, 1e-30)))
    scale = jnp.exp2(k)
    row = lax.broadcasted_iota(jnp.int32, pay_ref.shape[1:], 0)
    for q in range(dests):
        z = pay_ref[q] * scale
        z2 = z * z
        z4 = z2 * z2
        y = jnp.where(row >= tiles * per_device, k, z4 * z4 * z)
        code_ref[q] = y.astype(jnp.bfloat16)
        store = pltpu.make_async_copy(code_ref.at[q], send_ref.at[q], send_sems.at[q])
        store.start()
        stores.append(store)
    for store in stores:
        store.wait()


def cycle_kernel(
    pos_ref, occ_ref, own_ref, mate_ref, half_hbm, u_ref, out_ref, orb_ref, cs_ref, xs_ref, ts_ref,
    half_ref, sems,
):
    occupied = occ_ref.shape[0]
    pairs, per_device, virtuals = half_ref.shape
    dests, rows = 2 * own_ref.shape[0], own_ref.shape[2]
    load = pltpu.make_async_copy(half_hbm, half_ref, sems.at[0])
    load.start()
    tiles = virtuals // LANES
    labels, copies = labels_and_copies(occ_ref, occupied)
    for j in range(occupied):
        orb_ref[2 * labels[j] + copies[j]] = jnp.int32(j)
    for r in range(dests):
        ref = mate_ref if r & 1 else own_ref
        n = ((r >> 1) & 1) * (dests // 4) + (r >> 2)
        p = pos_ref[0] ^ r
        x = ref[n, 0].astype(jnp.float32).reshape(per_device, occupied, LANES)
        xs_ref[pl.ds(p * per_device, per_device)] = x
        t = ref[n, 1].astype(jnp.float32)
        at = pl.ds(pl.multiple_of(p * per_device, 8), per_device)
        for j in range(occupied):
            ts_ref[j, at, :] = t[j * per_device : (j + 1) * per_device]
    here = pl.ds(pos_ref[0] * per_device, per_device)
    x_left = jnp.concatenate([xs_ref[here, i, :] for i in range(occupied)], axis=0)
    left = jnp.concatenate([own_ref[0, 1], x_left.astype(jnp.bfloat16)], axis=1)
    for j in range(occupied):
        right = jnp.concatenate([xs_ref[:, j, :], ts_ref[j]], axis=1).astype(jnp.bfloat16)
        cs_ref[j] = contract_last(left, right).reshape(occupied, per_device, virtuals)
    load.wait()
    choices = [
        [orb_ref[2 * (labels[e // 2] ^ n) + e % 2] for n in range(4)] for e in range(pairs)
    ]

    def group(g, carry):
        rows = pl.ds(pl.multiple_of(g * 8, 8), 8)
        for v in range(tiles):
            at = slice(v * LANES, (v + 1) * LANES)
            uv = u_ref[rows, at]
            masks = [uv == n for n in range(1, 4)]
            for e in range(pairs):
                x = cs_ref[choices[e][0], e // 2, rows, at]
                for n in range(1, 4):
                    x = jnp.where(masks[n - 1], cs_ref[choices[e][n], e // 2, rows, at], x)
                out_ref[e, rows, at] = half_ref[e, rows, at] + x
        return carry

    lax.fori_loop(0, per_device // 8, group, 0)


def join_kernel(occ_ref, u_ref, half_ref, recv_ref, out_ref, dec_ref, mir_ref, res_ref, sems):
    occupied = occ_ref.shape[0]
    per_device, virtuals = u_ref.shape
    labels, copies = labels_and_copies(occ_ref, occupied)
    spread = 2 * per_device
    ready = set()

    def decode(t):
        ready.add(t)
        start = t * per_device
        low, high = start // 16 * 16, (start + per_device + 15) // 16 * 16
        end = virtuals // LANES * per_device
        for p in range(recv_ref.shape[0]):
            tail = recv_ref[p, end // 16 * 16 : end // 16 * 16 + 16, :]
            k = tail.astype(jnp.float32)[end % 16 : end % 16 + 1, 0:1]
            y = recv_ref[p, low:high, :].astype(jnp.float32)
            y = y[start - low : start - low + per_device]
            size = jnp.log2(jnp.maximum(jnp.abs(y), 2.0**-126)) * (1.0 / POWER) - k
            size = jnp.exp2(size)
            x = jnp.where(y < 0, -size, jnp.where(y > 0, size, 0.0))
            dec_ref[p * per_device : (p + 1) * per_device, :] = x
        mir_ref[t * LANES : (t + 1) * LANES, :] = dec_ref[...].T

    stores = []
    for j in range(occupied):
        for t in range(j * spread // LANES, ((j + 1) * spread - 1) // LANES + 1):
            if t not in ready:
                decode(t)
        u = u_ref[...]
        for i in range(occupied):
            at = pl.ds(pl.multiple_of((2 * j + copies[i]) * per_device, 8), per_device)
            total = half_ref[2 * i + copies[j]] + mir_ref[at, :]
            n = j * occupied + i
            res_ref[n] = jnp.where(u == (labels[j] ^ labels[i]), total, 0.0)
            store = pltpu.make_async_copy(res_ref.at[n], out_ref.at[i, j], sems.at[n])
            store.start()
            stores.append(store)
    for store in stores:
        store.wait()


def permute(x, flip, size):
    return lax.ppermute(x, "vir", [(n, n ^ flip) for n in range(size)])


def body(dests, amps, fock_vir, fock_occ, ladder_ints, cycle_ints, occ_irrep, vir_irrep):
    occupied, _, per_device, virtuals = amps.shape
    pairs = 2 * occupied
    tiles = virtuals // LANES
    rows = occupied * per_device
    kw = ladder_ints.shape[2]
    f32, bf16 = jnp.float32, jnp.bfloat16
    position = lax.axis_index("vir").astype(jnp.int32)
    pos = position.reshape(1)
    smem = pl.BlockSpec(memory_space=pltpu.SMEM)

    def whole(shape):
        return pl.BlockSpec(shape, lambda n: (0,) * len(shape))

    def cost(flops, size):
        return pl.CostEstimate(flops=flops, bytes_accessed=size, transcendentals=0)

    anywhere = pl.BlockSpec(memory_space=pl.ANY)
    quarter = dests // 4
    vmem = pl.BlockSpec(memory_space=pltpu.VMEM)
    hbm = pl.BlockSpec(memory_space=pltpu.HBM)
    win, xt, mix, u = pl.pallas_call(
        prep_kernel,
        out_shape=(
            jax.ShapeDtypeStruct((16, LANES), bf16),
            jax.ShapeDtypeStruct((1, 2, rows, LANES), bf16),
            jax.ShapeDtypeStruct((rows, rows), bf16),
            jax.ShapeDtypeStruct((per_device, virtuals), jnp.int32),
        ),
        in_specs=[smem] + [anywhere] * 4,
        out_specs=(vmem,) * 4,
        scratch_shapes=[
            pltpu.VMEM((occupied, occupied, per_device, LANES), bf16),
            pltpu.VMEM((rows, LANES), f32),
            pltpu.VMEM(fock_occ.shape, bf16),
            pltpu.VMEM(vir_irrep.shape, jnp.int32),
            pltpu.SMEM(vir_irrep.shape, jnp.int32),
            pltpu.SemaphoreType.DMA((5,)),
        ],
        compiler_params=params(60),
        cost_estimate=cost(0, 10**6),
    )(pos, cycle_ints.reshape(rows, LANES), amps, vir_irrep, fock_occ)

    flips = [m << 2 for m in range(1, quarter)]
    wins = [win] + [permute(win, flip, dests) for flip in flips]
    blocks = [xt] + [permute(xt, flip, dests) for flip in flips]
    win = pl.pallas_call(
        unpack_kernel,
        out_shape=jax.ShapeDtypeStruct((occupied, occupied, LANES), f32),
        in_specs=[smem] + [vmem] * quarter,
        out_specs=vmem,
        compiler_params=params(60),
        cost_estimate=cost(0, 10**5),
    )(pos, *wins)
    wins = [win] + [permute(win, flip, dests) for flip in (1, 2, 3)]

    wide = 2
    half = pl.pallas_call(
        fock_kernel,
        grid=(occupied // wide,),
        out_shape=jax.ShapeDtypeStruct((pairs, per_device, virtuals), f32),
        in_specs=[
            smem,
            pl.BlockSpec((wide, rows, virtuals), lambda i: (i, 0, 0)),
            whole(fock_vir.shape),
            whole(mix.shape),
            whole(u.shape),
        ]
        + [anywhere] * 3,
        out_specs=pl.BlockSpec((2 * wide, per_device, virtuals), lambda i: (i, 0, 0)),
        scratch_shapes=[pltpu.VMEM((occupied, per_device, virtuals), f32)],
        compiler_params=params(60),
        cost_estimate=cost(3 * occupied * rows * virtuals * virtuals, 8 * 10**6),
    )(occ_irrep, amps.reshape(occupied, rows, virtuals), fock_vir, mix, u, *wins[1:])

    near = stack(blocks, half)
    near_y = permute(near, 2, dests)
    send_rows = tiles * per_device + 8
    groups = per_device // 8
    half, send = pl.pallas_call(
        functools.partial(ladder_kernel, groups),
        out_shape=(
            jax.ShapeDtypeStruct((pairs, per_device, virtuals), f32),
            jax.ShapeDtypeStruct((dests, send_rows, LANES), bf16),
        ),
        in_specs=[smem] + [anywhere] * 8,
        out_specs=(anywhere, anywhere),
        scratch_shapes=[
            pltpu.VMEM((4,) + win.shape, f32),
            pltpu.VMEM((pairs, per_device, virtuals), f32),
            pltpu.VMEM((per_device, virtuals), jnp.int32),
            pltpu.VMEM(ladder_ints.shape, bf16),
            pltpu.VMEM((occupied * occupied, LANES), f32),
            pltpu.VMEM((pairs, per_device, virtuals), f32),
            pltpu.VMEM((dests, send_rows, LANES), f32),
            pltpu.VMEM((dests, send_rows, LANES), bf16),
            pltpu.SemaphoreType.DMA((groups + 6,)),
            pltpu.SemaphoreType.DMA((groups,)),
            pltpu.SemaphoreType.DMA((dests,)),
        ]
        + [pltpu.VMEM((tiles, 8 * pairs, LANES), f32)] * groups,
        compiler_params=params(60),
        cost_estimate=cost(4 * occupied * rows * virtuals * LANES, 25 * 10**6),
    )(occ_irrep, *wins, half, u, ladder_ints, near)

    recv = lax.all_to_all(send, "vir", split_axis=0, concat_axis=0, tiled=True)
    own_blocks = stack([near, near_y], send)
    mate_blocks = permute(own_blocks, 1, dests)
    half = pl.pallas_call(
        cycle_kernel,
        out_shape=jax.ShapeDtypeStruct((pairs, per_device, virtuals), f32),
        in_specs=[smem, smem, vmem, vmem, hbm, vmem],
        out_specs=vmem,
        scratch_shapes=[
            pltpu.SMEM((occupied,), jnp.int32),
            pltpu.VMEM((occupied, occupied, per_device, virtuals), f32),
            pltpu.VMEM((virtuals, occupied, LANES), f32),
            pltpu.VMEM((occupied, virtuals, LANES), f32),
            pltpu.VMEM((pairs, per_device, virtuals), f32),
            pltpu.SemaphoreType.DMA((1,)),
        ],
        compiler_params=params(28),
        cost_estimate=cost(1000, 1000),
    )(pos, occ_irrep, own_blocks, mate_blocks, half, u)

    return pl.pallas_call(
        join_kernel,
        out_shape=jax.ShapeDtypeStruct((occupied, occupied, per_device, virtuals), f32),
        in_specs=[smem, vmem, vmem, vmem],
        out_specs=anywhere,
        scratch_shapes=[
            pltpu.VMEM((virtuals, LANES), f32),
            pltpu.VMEM((tiles * LANES, virtuals), f32),
            pltpu.VMEM((occupied * occupied, per_device, virtuals), f32),
            pltpu.SemaphoreType.DMA((occupied * occupied,)),
        ],
        compiler_params=params(16),
        cost_estimate=cost(10**6, 5 * 10**6),
    )(occ_irrep, u, half, recv)


def solution(mesh):
    dests = mesh.shape["vir"]

    def run(amps, *rest):
        occupied, _, per_device, virtuals = amps.shape
        tiled = (
            dests == 16
            and per_device % 8 == 0
            and virtuals % LANES == 0
            and 2 * occupied * per_device == virtuals
            and rest[2].shape[2] == LANES
            and rest[3].shape[2] == LANES
        )
        return body(dests, amps, *rest) if tiled else plain_body(amps, *rest)

    return jax.shard_map(
        run,
        mesh=mesh,
        in_specs=(
            P("groups", None, "vir", None),
            P("groups", None),
            P("groups", None),
            P("vir", "groups", None),
            P("vir", "groups", None),
            P("groups"),
            P("groups"),
        ),
        out_specs=P("groups", None, "vir", None),
        check_vma=False,
    )
```

```python
import functools

import jax
import jax.numpy as jnp
from jax import lax
from jax.experimental import pallas as pl
from jax.experimental.pallas import tpu as pltpu
from jax.sharding import PartitionSpec as P

DW = 8
CW = 16
LANES = 128
POWER = 9
TOP_EXPONENT = 13


def contract_last(left_side, right_side):
    return lax.dot_general(
        left_side, right_side, (((1,), (1,)), ((), ())), preferred_element_type=jnp.float32
    )


def plain_body(amps, fock_vir, fock_occ, ladder_ints, cycle_ints, occ_irrep, vir_irrep):
    occupied = amps.shape[0]
    per_device = amps.shape[2]
    virtuals = amps.shape[3]
    pair_count = occupied * occupied
    position = lax.axis_index("vir")
    fock_term = jnp.dot(
        amps.reshape(pair_count * per_device, virtuals),
        fock_vir,
        preferred_element_type=jnp.float32,
    ).reshape(occupied, occupied, per_device, virtuals)
    occ_term = jnp.einsum("ikab,kj->ijab", amps, fock_occ, preferred_element_type=jnp.float32)
    flat_ints = ladder_ints.reshape(per_device * virtuals, ladder_ints.shape[2])
    local_window = amps[:, :, 0:1, :DW]
    local_cycle = amps[:, :, :, :CW]
    segment = lax.all_gather(local_window, "vir", axis=2, tiled=True)
    width = segment.shape[2] * DW
    ladder = contract_last(segment.reshape(pair_count, width), flat_ints)
    left_side = jnp.transpose(local_cycle, (0, 2, 1, 3)).reshape(
        occupied * per_device, occupied * CW
    )
    segment = lax.all_gather(cycle_ints, "vir", axis=0, tiled=True)
    right_side = segment.reshape(segment.shape[0] * occupied, occupied * CW)
    cycle_block = contract_last(left_side, right_side).reshape(
        occupied, per_device, segment.shape[0], occupied
    )
    cycle_part = jnp.transpose(cycle_block, (0, 3, 1, 2))
    half_sum = (
        fock_term - occ_term + ladder.reshape(occupied, occupied, per_device, virtuals) + cycle_part
    )
    vir_local = lax.dynamic_slice_in_dim(vir_irrep, position * per_device, per_device)
    occ_pair = jnp.bitwise_xor(occ_irrep[:, None], occ_irrep[None, :])
    vir_pair = jnp.bitwise_xor(vir_local[:, None], vir_irrep[None, :])
    received = lax.all_to_all(half_sum, "vir", split_axis=3, concat_axis=2, tiled=True)
    mirrored = jnp.transpose(received, (1, 0, 3, 2))
    product_irrep = jnp.bitwise_xor(occ_pair[:, :, None, None], vir_pair[None, None, :, :])
    allowed = jnp.where(product_irrep == 0, jnp.float32(1.0), jnp.float32(0.0))
    return allowed * (half_sum + mirrored)


def params(mib):
    return pltpu.CompilerParams(vmem_limit_bytes=mib * 2**20)


def labels_and_copies(occ_ref, occupied):
    labels = [occ_ref[j] for j in range(occupied)]
    copies = []
    for j in range(occupied):
        s = jnp.int32(0)
        for k in range(j):
            s = s + (labels[k] == labels[j]).astype(jnp.int32)
        copies.append(s)
    return labels, copies


def prep_kernel(cyc_ref, amps_ref, win_ref, xt_ref, t_ref):
    occupied, _, per_device, _ = amps_ref.shape
    xt_ref[0, 0] = cyc_ref[...]
    lane = lax.broadcasted_iota(jnp.int32, (occupied, LANES), 1)
    packed = jnp.zeros((occupied, LANES), jnp.float32)
    for j in range(occupied):
        w = jnp.where(lane < DW, amps_ref[:, j, 0, :].astype(jnp.float32), 0.0)
        packed = packed + (pltpu.roll(w, j * DW, axis=1) if j else w)
    packed = jnp.concatenate([packed, jnp.zeros_like(packed)], axis=0)
    win_ref[...] = packed.astype(jnp.bfloat16)
    lane = lax.broadcasted_iota(jnp.int32, (per_device, LANES), 1)
    for i in range(occupied):
        acc = jnp.zeros((per_device, LANES), jnp.float32)
        for k in range(occupied):
            piece = jnp.where(lane < CW, amps_ref[i, k].astype(jnp.float32), 0.0)
            acc = acc + (pltpu.roll(piece, k * CW, axis=1) if k else piece)
        t_ref[i * per_device : (i + 1) * per_device, :] = acc
    xt_ref[0, 1] = t_ref[...].astype(jnp.bfloat16)


def setup_kernel(pos_ref, vir_ref, occ_vals_ref, row_ref, mix_ref, u_ref):
    for a in range(u_ref.shape[0]):
        u_ref[a : a + 1, :] = row_ref[...] ^ vir_ref[pos_ref[0] * u_ref.shape[0] + a]
    rows = mix_ref.shape[0]
    occupied = occ_vals_ref.shape[0]
    per_device = rows // occupied
    row = lax.broadcasted_iota(jnp.int32, (rows, occupied), 0)
    start = lax.broadcasted_iota(jnp.int32, (rows, occupied), 1) * per_device
    in_block = jnp.logical_and(row >= start, row < start + per_device).astype(jnp.bfloat16)
    row = lax.broadcasted_iota(jnp.int32, (rows, per_device), 0)
    at = lax.broadcasted_iota(jnp.int32, (rows, per_device), 1)
    same = row == at
    for n in range(1, occupied):
        same = jnp.logical_or(same, row == at + n * per_device)
    same = same.astype(jnp.bfloat16)
    left = contract_last(in_block, occ_vals_ref[...]).astype(jnp.bfloat16)
    mix = contract_last(left, in_block) * contract_last(same, same)
    mix_ref[...] = mix.astype(jnp.bfloat16)


def fock_kernel(first, occ_ref, amps_ref, fock_ref, mix_ref, u_ref, after_ref, half_ref, hs_ref):
    wide, rows, virtuals = amps_ref.shape
    _, per_device, _ = half_ref.shape
    occupied = occ_ref.shape[0]
    labels, copies = labels_and_copies(occ_ref, occupied)
    u = u_ref[...]
    h = jnp.dot(
        amps_ref[...].reshape(wide * rows, virtuals),
        fock_ref[...],
        preferred_element_type=jnp.float32,
    )
    for w in range(wide):
        a = amps_ref[w]
        mixed = jnp.dot(mix_ref[...], a, preferred_element_type=jnp.float32)
        hs_ref[...] = (h[w * rows : (w + 1) * rows] - mixed).reshape(hs_ref.shape)
        own = occ_ref[pl.program_id(0) * wide + w + first]
        for j in range(occupied):
            at = 2 * w + copies[j]
            half_ref[at] = jnp.where(u == (own ^ labels[j]), hs_ref[j], half_ref[at])


def stack(blocks, *after):
    count = len(blocks)

    def kernel(*refs):
        out = refs[-1]
        at = 0
        for n in range(count):
            head = blocks[n].shape[0]
            out[at : at + head] = refs[n][...]
            at += head

    vmem = pl.BlockSpec(memory_space=pltpu.VMEM)
    shape = (sum(b.shape[0] for b in blocks),) + blocks[0].shape[1:]
    return pl.pallas_call(
        kernel,
        out_shape=jax.ShapeDtypeStruct(shape, blocks[0].dtype),
        in_specs=[vmem] * count + [pl.BlockSpec(memory_space=pl.ANY)] * len(after),
        out_specs=vmem,
        compiler_params=params(4),
        cost_estimate=pl.CostEstimate(flops=0, bytes_accessed=10**6, transcendentals=0),
    )(*blocks, *after)


def unpack_kernel(pos_ref, *refs):
    blocks, win_ref = refs[:-2], refs[-1]
    occupied, _, lanes = win_ref.shape
    lane = lax.broadcasted_iota(jnp.int32, (8, lanes), 1)
    for j in range(occupied):
        total = jnp.zeros((8, lanes), jnp.float32)
        for m, block in enumerate(blocks):
            p = pos_ref[0] ^ (m << 2)
            w = block[...].astype(jnp.float32)[:8]
            w = jnp.where(jnp.logical_and(lane >= j * DW, lane < (j + 1) * DW), w, 0.0)
            total = total + pltpu.roll(w, lax.rem(p * DW - j * DW + lanes, lanes), axis=1)
        win_ref[j] = total


def payload_pieces(per_device, pairs, dests):
    out = {}
    for q in range(dests):
        for e in range(pairs):
            start = 0
            while start < per_device:
                src = q * per_device + start
                dst = e * per_device + start
                length = min(LANES - src % LANES, LANES - dst % LANES, per_device - start)
                out.setdefault((q, dst // LANES), []).append(
                    (dst % LANES, e, src // LANES, (dst - src) % LANES)
                )
                start += length
    return out


def ladder_kernel(
    groups, occ_ref, win0, win1, win2, win3, part0, part1, u_ref, lad_ref, _, out_ref, send_ref,
    w2_ref, hs_ref, pay_ref, code_ref, half_sems, send_sems, *ls_refs
):
    occupied = occ_ref.shape[0]
    pairs, per_device, virtuals = hs_ref.shape
    dests = pay_ref.shape[0]
    tiles = virtuals // LANES
    labels, copies = labels_and_copies(occ_ref, occupied)
    lane = lax.broadcasted_iota(jnp.int32, (8, LANES), 1)
    for i in range(occupied):
        for j in range(occupied):
            row = (labels[i] ^ labels[j]) * pairs + 2 * i + copies[j]
            at = slice(i, i + 1)
            w = (win0[j, at, :] + win1[j, at, :]) + (win2[j, at, :] + win3[j, at, :])
            w2_ref[pl.ds(row, 1), :] = w
    w2 = w2_ref[...].astype(jnp.bfloat16)
    sources = [(part, n) for part in (part0, part1) for n in range(part.shape[0])]
    pieces_of = payload_pieces(per_device, pairs, dests)
    tops = [jnp.zeros((8, LANES), jnp.float32)]

    def ladder(g, a):
        product = contract_last(w2, lad_ref[8 * g + a])
        ua = u_ref[8 * g + a : 8 * g + a + 1, :]
        sel = product[0:pairs]
        for v in range(1, 4):
            sel = jnp.where(ua == v, product[v * pairs : (v + 1) * pairs], sel)
        for v in range(tiles):
            ls_refs[g][v, pl.ds(a, pairs, stride=8), :] = sel[:, v * LANES : (v + 1) * LANES]

    def payload(g):
        rows = slice(8 * g, 8 * g + 8)
        found = {}
        for t in range(tiles):
            last_e = min(((t + 1) * LANES - 1) // per_device, pairs - 1)
            for e in range(t * LANES // per_device, last_e + 1):
                if (e, 0) in found:
                    continue
                for v in range(tiles):
                    at = slice(v * LANES, (v + 1) * LANES)
                    x = sources[e][0][sources[e][1], rows, at] + ls_refs[g][v, 8 * e : 8 * e + 8, :]
                    hs_ref[e, rows, at] = x
                    tops[0] = jnp.maximum(tops[0], jnp.abs(x))
                    found[e, v] = x
            for q in range(dests):
                acc = None
                for first, e, v, shift in pieces_of[q, t]:
                    x = pltpu.roll(found[e, v], shift, axis=1) if shift else found[e, v]
                    acc = x if acc is None else jnp.where(lane >= first, x, acc)
                start = t * per_device + 8 * g
                pay_ref[q, start : start + 8, :] = acc
                if q % 8 == 7:
                    yield

    stores = []
    for g in range(groups + 1):
        before = payload(g - 1) if g else iter(())
        for a in range(8):
            if g < groups:
                ladder(g, a)
            next(before, None)
        for _ in before:
            pass
        if g:
            rows = pl.ds(8 * (g - 1), 8)
            store = pltpu.make_async_copy(
                hs_ref.at[:, rows, :], out_ref.at[:, rows, :], half_sems.at[g - 1]
            )
            store.start()
            stores.append(store)
    most = jnp.max(jnp.max(tops[0], axis=0, keepdims=True), axis=1, keepdims=True)
    k = jnp.floor(TOP_EXPONENT - jnp.log2(jnp.maximum(most, 1e-30)))
    scale = jnp.exp2(k)
    row = lax.broadcasted_iota(jnp.int32, pay_ref.shape[1:], 0)
    for q in range(dests):
        z = pay_ref[q] * scale
        z2 = z * z
        z4 = z2 * z2
        y = jnp.where(row >= tiles * per_device, k, z4 * z4 * z)
        code_ref[q] = y.astype(jnp.bfloat16)
        store = pltpu.make_async_copy(code_ref.at[q], send_ref.at[q], send_sems.at[q])
        store.start()
        stores.append(store)
    for store in stores:
        store.wait()


def cycle_kernel(pos_ref, occ_ref, own_ref, mate_ref, half_ref, u_ref, out_ref, orb_ref, cs_ref, xs_ref, ts_ref):
    occupied = occ_ref.shape[0]
    pairs, per_device, virtuals = half_ref.shape
    quads, _, rows, _ = own_ref.shape
    dests = 2 * quads
    tiles = virtuals // LANES
    labels, copies = labels_and_copies(occ_ref, occupied)
    for j in range(occupied):
        orb_ref[2 * labels[j] + copies[j]] = jnp.int32(j)
    for r in range(dests):
        ref = mate_ref if r & 1 else own_ref
        n = ((r >> 1) & 1) * (dests // 4) + (r >> 2)
        p = pos_ref[0] ^ r
        x = ref[n, 0].astype(jnp.float32).reshape(per_device, occupied, LANES)
        xs_ref[pl.ds(p * per_device, per_device)] = x
        t = ref[n, 1].astype(jnp.float32)
        at = pl.ds(pl.multiple_of(p * per_device, 8), per_device)
        for j in range(occupied):
            ts_ref[j, at, :] = t[j * per_device : (j + 1) * per_device]
    here = pl.ds(pos_ref[0] * per_device, per_device)
    x_left = jnp.concatenate([xs_ref[here, i, :] for i in range(occupied)], axis=0)
    left = jnp.concatenate([own_ref[0, 1], x_left.astype(jnp.bfloat16)], axis=1)
    for j in range(occupied):
        right = jnp.concatenate([xs_ref[:, j, :], ts_ref[j]], axis=1).astype(jnp.bfloat16)
        cs_ref[j] = contract_last(left, right).reshape(occupied, per_device, virtuals)
    choices = [
        [orb_ref[2 * (labels[e // 2] ^ n) + e % 2] for n in range(4)] for e in range(pairs)
    ]

    def group(g, carry):
        rows = pl.ds(pl.multiple_of(g * 8, 8), 8)
        for v in range(tiles):
            at = slice(v * LANES, (v + 1) * LANES)
            uv = u_ref[rows, at]
            masks = [uv == n for n in range(1, 4)]
            for e in range(pairs):
                x = cs_ref[choices[e][0], e // 2, rows, at]
                for n in range(1, 4):
                    x = jnp.where(masks[n - 1], cs_ref[choices[e][n], e // 2, rows, at], x)
                out_ref[e, rows, at] = half_ref[e, rows, at] + x
        return carry

    lax.fori_loop(0, per_device // 8, group, 0)


def join_kernel(occ_ref, u_ref, half_ref, recv_ref, out_ref, dec_ref, mir_ref, res_ref, sems):
    occupied = occ_ref.shape[0]
    per_device, virtuals = u_ref.shape
    labels, copies = labels_and_copies(occ_ref, occupied)
    spread = 2 * per_device
    ready = set()

    def decode(t):
        ready.add(t)
        start = t * per_device
        low, high = start // 16 * 16, (start + per_device + 15) // 16 * 16
        end = virtuals // LANES * per_device
        for p in range(recv_ref.shape[0]):
            tail = recv_ref[p, end // 16 * 16 : end // 16 * 16 + 16, :]
            k = tail.astype(jnp.float32)[end % 16 : end % 16 + 1, 0:1]
            y = recv_ref[p, low:high, :].astype(jnp.float32)
            y = y[start - low : start - low + per_device]
            size = jnp.log2(jnp.maximum(jnp.abs(y), 2.0**-126)) * (1.0 / POWER) - k
            size = jnp.exp2(size)
            x = jnp.where(y < 0, -size, jnp.where(y > 0, size, 0.0))
            dec_ref[p * per_device : (p + 1) * per_device, :] = x
        mir_ref[t * LANES : (t + 1) * LANES, :] = dec_ref[...].T

    stores = []
    for j in range(occupied):
        for t in range(j * spread // LANES, ((j + 1) * spread - 1) // LANES + 1):
            if t not in ready:
                decode(t)
        u = u_ref[...]
        for i in range(occupied):
            at = pl.ds(pl.multiple_of((2 * j + copies[i]) * per_device, 8), per_device)
            total = half_ref[2 * i + copies[j]] + mir_ref[at, :]
            n = j * occupied + i
            res_ref[n] = jnp.where(u == (labels[j] ^ labels[i]), total, 0.0)
            store = pltpu.make_async_copy(res_ref.at[n], out_ref.at[i, j], sems.at[n])
            store.start()
            stores.append(store)
    for store in stores:
        store.wait()


def permute(x, flip, size):
    return lax.ppermute(x, "vir", [(n, n ^ flip) for n in range(size)])


def body(dests, amps, fock_vir, fock_occ, ladder_ints, cycle_ints, occ_irrep, vir_irrep):
    occupied, _, per_device, virtuals = amps.shape
    pairs = 2 * occupied
    tiles = virtuals // LANES
    rows = occupied * per_device
    kw = ladder_ints.shape[2]
    f32, bf16 = jnp.float32, jnp.bfloat16
    position = lax.axis_index("vir").astype(jnp.int32)
    pos = position.reshape(1)
    smem = pl.BlockSpec(memory_space=pltpu.SMEM)

    def whole(shape):
        return pl.BlockSpec(shape, lambda n: (0,) * len(shape))

    def cost(flops, size):
        return pl.CostEstimate(flops=flops, bytes_accessed=size, transcendentals=0)

    anywhere = pl.BlockSpec(memory_space=pl.ANY)
    quarter = dests // 4
    win, xt = pl.pallas_call(
        prep_kernel,
        grid=(1,),
        out_shape=(
            jax.ShapeDtypeStruct((16, LANES), bf16),
            jax.ShapeDtypeStruct((1, 2, rows, LANES), bf16),
        ),
        in_specs=[
            whole((rows, LANES)),
            pl.BlockSpec((occupied, occupied, per_device, LANES), lambda n: (0, 0, 0, 0)),
        ],
        out_specs=(whole((16, LANES)), whole((1, 2, rows, LANES))),
        scratch_shapes=[pltpu.VMEM((rows, LANES), f32)],
        compiler_params=params(58),
        cost_estimate=cost(0, 500000),
    )(cycle_ints.reshape(rows, LANES), amps)
    vmem = pl.BlockSpec(memory_space=pltpu.VMEM)
    mix, u = pl.pallas_call(
        setup_kernel,
        out_shape=(
            jax.ShapeDtypeStruct((rows, rows), bf16),
            jax.ShapeDtypeStruct((per_device, virtuals), jnp.int32),
        ),
        in_specs=[smem, smem, vmem, vmem],
        out_specs=(vmem, vmem),
        compiler_params=params(4),
        cost_estimate=cost(10**7, 300000),
    )(pos, vir_irrep, fock_occ, vir_irrep.reshape(1, virtuals))

    flat_amps = amps.reshape(occupied, rows, virtuals)
    parts = (4, 4)
    wide = 2

    def fock_part(n, after):
        first, count = sum(parts[:n]), parts[n]
        return pl.pallas_call(
            functools.partial(fock_kernel, first),
            grid=(count // wide,),
            out_shape=jax.ShapeDtypeStruct((2 * count, per_device, virtuals), f32),
            in_specs=[
                smem,
                pl.BlockSpec((wide, rows, virtuals), lambda i: (i + first // wide, 0, 0)),
                whole(fock_vir.shape),
                whole(mix.shape),
                whole((per_device, virtuals)),
                anywhere,
            ],
            out_specs=pl.BlockSpec((2 * wide, per_device, virtuals), lambda i: (i, 0, 0)),
            scratch_shapes=[pltpu.VMEM((occupied, per_device, virtuals), f32)],
            compiler_params=params(12),
            cost_estimate=cost(3 * count * rows * virtuals * virtuals, 2 * 10**6),
        )(occ_irrep, flat_amps, fock_vir, mix, u, after)

    flips = [m << 2 for m in range(1, quarter)]
    win_shape = (occupied, occupied, LANES)
    wins = [win] + [permute(win, flip, dests) for flip in flips]
    blocks = [xt] + [permute(xt, flip, dests) for flip in flips]
    half0 = fock_part(0, mix)
    win = pl.pallas_call(
        unpack_kernel,
        out_shape=jax.ShapeDtypeStruct(win_shape, f32),
        in_specs=[smem] + [vmem] * quarter + [anywhere],
        out_specs=vmem,
        compiler_params=params(4),
        cost_estimate=cost(0, 10**5),
    )(pos, *wins, half0)

    wins = [win] + [permute(win, flip, dests) for flip in (1, 2, 3)]
    half1 = fock_part(1, win)
    near = stack(blocks, half1)
    near_y = permute(near, 2, dests)

    send_rows = tiles * per_device + 8
    groups = per_device // 8
    half, send = pl.pallas_call(
        functools.partial(ladder_kernel, groups),
        out_shape=(
            jax.ShapeDtypeStruct((pairs, per_device, virtuals), f32),
            jax.ShapeDtypeStruct((dests, send_rows, LANES), bf16),
        ),
        in_specs=[smem] + [vmem] * 8 + [anywhere],
        out_specs=(anywhere, anywhere),
        scratch_shapes=[
            pltpu.VMEM((occupied * occupied, LANES), f32),
            pltpu.VMEM((pairs, per_device, virtuals), f32),
            pltpu.VMEM((dests, send_rows, LANES), f32),
            pltpu.VMEM((dests, send_rows, LANES), bf16),
            pltpu.SemaphoreType.DMA((groups,)),
            pltpu.SemaphoreType.DMA((dests,)),
        ]
        + [pltpu.VMEM((tiles, 8 * pairs, LANES), f32)] * groups,
        compiler_params=params(24),
        cost_estimate=cost(4 * occupied * rows * virtuals * LANES, 25 * 10**6),
    )(occ_irrep, *wins, half0, half1, u, ladder_ints, near)

    recv = lax.all_to_all(send, "vir", split_axis=0, concat_axis=0, tiled=True)
    own_blocks = stack([near, near_y], send)
    mate_blocks = permute(own_blocks, 1, dests)
    half = pl.pallas_call(
        cycle_kernel,
        out_shape=jax.ShapeDtypeStruct((pairs, per_device, virtuals), f32),
        in_specs=[smem, smem] + [vmem] * 4,
        out_specs=vmem,
        scratch_shapes=[
            pltpu.SMEM((occupied,), jnp.int32),
            pltpu.VMEM((occupied, occupied, per_device, virtuals), f32),
            pltpu.VMEM((virtuals, occupied, LANES), f32),
            pltpu.VMEM((occupied, virtuals, LANES), f32),
        ],
        compiler_params=params(28),
        cost_estimate=cost(1000, 1000),
    )(pos, occ_irrep, own_blocks, mate_blocks, half, u)

    return pl.pallas_call(
        join_kernel,
        out_shape=jax.ShapeDtypeStruct((occupied, occupied, per_device, virtuals), f32),
        in_specs=[smem, vmem, vmem, vmem],
        out_specs=anywhere,
        scratch_shapes=[
            pltpu.VMEM((virtuals, LANES), f32),
            pltpu.VMEM((tiles * LANES, virtuals), f32),
            pltpu.VMEM((occupied * occupied, per_device, virtuals), f32),
            pltpu.SemaphoreType.DMA((occupied * occupied,)),
        ],
        compiler_params=params(16),
        cost_estimate=cost(10**6, 5 * 10**6),
    )(occ_irrep, u, half, recv)


def solution(mesh):
    dests = mesh.shape["vir"]

    def run(amps, *rest):
        occupied, _, per_device, virtuals = amps.shape
        tiled = (
            dests == 16
            and per_device % 8 == 0
            and virtuals % LANES == 0
            and 2 * occupied * per_device == virtuals
            and rest[2].shape[2] == LANES
            and rest[3].shape[2] == LANES
        )
        return body(dests, amps, *rest) if tiled else plain_body(amps, *rest)

    return jax.shard_map(
        run,
        mesh=mesh,
        in_specs=(
            P("groups", None, "vir", None),
            P("groups", None),
            P("groups", None),
            P("vir", "groups", None),
            P("vir", "groups", None),
            P("groups"),
            P("groups"),
        ),
        out_specs=P("groups", None, "vir", None),
        check_vma=False,
    )
```

```python
import functools

import jax
import jax.numpy as jnp
from jax import lax
from jax.experimental import pallas as pl
from jax.experimental.pallas import tpu as pltpu
from jax.sharding import PartitionSpec as P

DW = 8
CW = 16
LANES = 128
POWER = 9
TOP_EXPONENT = 13


def contract_last(left_side, right_side):
    return lax.dot_general(
        left_side, right_side, (((1,), (1,)), ((), ())), preferred_element_type=jnp.float32
    )


def plain_body(amps, fock_vir, fock_occ, ladder_ints, cycle_ints, occ_irrep, vir_irrep):
    occupied = amps.shape[0]
    per_device = amps.shape[2]
    virtuals = amps.shape[3]
    pair_count = occupied * occupied
    position = lax.axis_index("vir")
    fock_term = jnp.dot(
        amps.reshape(pair_count * per_device, virtuals),
        fock_vir,
        preferred_element_type=jnp.float32,
    ).reshape(occupied, occupied, per_device, virtuals)
    occ_term = jnp.einsum("ikab,kj->ijab", amps, fock_occ, preferred_element_type=jnp.float32)
    flat_ints = ladder_ints.reshape(per_device * virtuals, ladder_ints.shape[2])
    local_window = amps[:, :, 0:1, :DW]
    local_cycle = amps[:, :, :, :CW]
    segment = lax.all_gather(local_window, "vir", axis=2, tiled=True)
    width = segment.shape[2] * DW
    ladder = contract_last(segment.reshape(pair_count, width), flat_ints)
    left_side = jnp.transpose(local_cycle, (0, 2, 1, 3)).reshape(
        occupied * per_device, occupied * CW
    )
    segment = lax.all_gather(cycle_ints, "vir", axis=0, tiled=True)
    right_side = segment.reshape(segment.shape[0] * occupied, occupied * CW)
    cycle_block = contract_last(left_side, right_side).reshape(
        occupied, per_device, segment.shape[0], occupied
    )
    cycle_part = jnp.transpose(cycle_block, (0, 3, 1, 2))
    half_sum = (
        fock_term - occ_term + ladder.reshape(occupied, occupied, per_device, virtuals) + cycle_part
    )
    vir_local = lax.dynamic_slice_in_dim(vir_irrep, position * per_device, per_device)
    occ_pair = jnp.bitwise_xor(occ_irrep[:, None], occ_irrep[None, :])
    vir_pair = jnp.bitwise_xor(vir_local[:, None], vir_irrep[None, :])
    received = lax.all_to_all(half_sum, "vir", split_axis=3, concat_axis=2, tiled=True)
    mirrored = jnp.transpose(received, (1, 0, 3, 2))
    product_irrep = jnp.bitwise_xor(occ_pair[:, :, None, None], vir_pair[None, None, :, :])
    allowed = jnp.where(product_irrep == 0, jnp.float32(1.0), jnp.float32(0.0))
    return allowed * (half_sum + mirrored)


def params(mib):
    return pltpu.CompilerParams(vmem_limit_bytes=mib * 2**20)


def labels_and_copies(occ_ref, occupied):
    labels = [occ_ref[j] for j in range(occupied)]
    copies = []
    for j in range(occupied):
        s = jnp.int32(0)
        for k in range(j):
            s = s + (labels[k] == labels[j]).astype(jnp.int32)
        copies.append(s)
    return labels, copies


def prep_kernel(cyc_ref, amps_ref, block_ref):
    occupied = amps_ref.shape[0]
    rows = cyc_ref.shape[0]
    block_ref[:rows, :] = cyc_ref[...]
    lane = lax.broadcasted_iota(jnp.int32, (occupied, LANES), 1)
    packed = jnp.zeros((occupied, LANES), jnp.float32)
    for j in range(occupied):
        w = jnp.where(lane < DW, amps_ref[:, j, 0, :].astype(jnp.float32), 0.0)
        packed = packed + (pltpu.roll(w, j * DW, axis=1) if j else w)
    packed = jnp.concatenate([packed, jnp.zeros_like(packed)], axis=0)
    block_ref[rows:, :] = packed.astype(jnp.bfloat16)


def mix_kernel(occ_vals_ref, mix_ref):
    rows = mix_ref.shape[0]
    occupied = occ_vals_ref.shape[0]
    per_device = rows // occupied
    row = lax.broadcasted_iota(jnp.int32, (rows, occupied), 0)
    start = lax.broadcasted_iota(jnp.int32, (rows, occupied), 1) * per_device
    in_block = jnp.logical_and(row >= start, row < start + per_device).astype(jnp.bfloat16)
    row = lax.broadcasted_iota(jnp.int32, (rows, per_device), 0)
    at = lax.broadcasted_iota(jnp.int32, (rows, per_device), 1)
    same = row == at
    for n in range(1, occupied):
        same = jnp.logical_or(same, row == at + n * per_device)
    same = same.astype(jnp.bfloat16)
    left = contract_last(in_block, occ_vals_ref[...]).astype(jnp.bfloat16)
    mix = contract_last(left, in_block) * contract_last(same, same)
    mix_ref[...] = mix.astype(jnp.bfloat16)


def fock_kernel(first, occ_ref, amps_ref, fock_ref, mix_ref, u_ref, after_ref, half_ref, cyc_ref, hs_ref):
    wide, rows, virtuals = amps_ref.shape
    _, per_device, _ = half_ref.shape
    occupied = occ_ref.shape[0]
    labels, copies = labels_and_copies(occ_ref, occupied)
    u = u_ref[...]
    h = jnp.dot(
        amps_ref[...].reshape(wide * rows, virtuals),
        fock_ref[...],
        preferred_element_type=jnp.float32,
    )
    for w in range(wide):
        a = amps_ref[w]
        mixed = jnp.dot(mix_ref[...], a, preferred_element_type=jnp.float32)
        hs_ref[...] = (h[w * rows : (w + 1) * rows] - mixed).reshape(hs_ref.shape)
        own = occ_ref[pl.program_id(0) * wide + w + first]
        for j in range(occupied):
            at = 2 * w + copies[j]
            half_ref[at] = jnp.where(u == (own ^ labels[j]), hs_ref[j], half_ref[at])
        head = a[:, :LANES].astype(jnp.float32)
        lane = lax.broadcasted_iota(jnp.int32, (per_device, LANES), 1)
        acc = jnp.zeros((per_device, LANES), jnp.float32)
        for k in range(occupied):
            piece = jnp.where(lane < CW, head[k * per_device : (k + 1) * per_device], 0.0)
            acc = acc + (pltpu.roll(piece, k * CW, axis=1) if k else piece)
        cyc_ref[w] = acc.astype(jnp.bfloat16)


def stack(blocks, after):
    count = len(blocks)

    def kernel(*refs):
        out = refs[count + 1]
        at = 0
        for n in range(count):
            head = blocks[n].shape[0]
            out[at : at + head] = refs[n][...]
            at += head

    vmem = pl.BlockSpec(memory_space=pltpu.VMEM)
    shape = (sum(b.shape[0] for b in blocks),) + blocks[0].shape[1:]
    return pl.pallas_call(
        kernel,
        out_shape=jax.ShapeDtypeStruct(shape, blocks[0].dtype),
        in_specs=[vmem] * count + [pl.BlockSpec(memory_space=pl.ANY)],
        out_specs=vmem,
        compiler_params=params(4),
        cost_estimate=pl.CostEstimate(flops=0, bytes_accessed=10**6, transcendentals=0),
    )(*blocks, after)


def payload_pieces(per_device, pairs, dests):
    out = {}
    for q in range(dests):
        for e in range(pairs):
            start = 0
            while start < per_device:
                src = q * per_device + start
                dst = e * per_device + start
                length = min(LANES - src % LANES, LANES - dst % LANES, per_device - start)
                out.setdefault((q, dst // LANES), []).append(
                    (dst % LANES, e, src // LANES, (dst - src) % LANES)
                )
                start += length
    return out


def half_kernel(groups, parts, pos_ref, occ_ref, own_ref, mate_ref, *refs):
    halves, refs = refs[: len(parts)], refs[len(parts) :]
    cycs, refs = refs[: len(parts)], refs[len(parts) :]
    u_ref, lad_ref, out_ref, send_ref, orb_ref, w2_ref, xs_ref, cs_ref, pay_ref = refs[:9]
    ls_refs = refs[9:]
    occupied = occ_ref.shape[0]
    pairs, per_device, virtuals = out_ref.shape
    dests = pay_ref.shape[0]
    tiles = virtuals // LANES
    rows = occupied * per_device
    labels, copies = labels_and_copies(occ_ref, occupied)
    lane = lax.broadcasted_iota(jnp.int32, (8, LANES), 1)

    def block_of(r):
        ref = mate_ref if r & 1 else own_ref
        return ref[((r >> 1) & 1) * (dests // 4) + (r >> 2)]

    packed = [block_of(r)[rows:].astype(jnp.float32)[:8] for r in range(dests)]
    for j in range(occupied):
        orb_ref[2 * labels[j] + copies[j]] = jnp.int32(j)
        window = jnp.zeros((8, LANES), jnp.float32)
        for r in range(dests):
            w = jnp.where(jnp.logical_and(lane >= j * DW, lane < (j + 1) * DW), packed[r], 0.0)
            shift = lax.rem((pos_ref[0] ^ r) * DW - j * DW + LANES, LANES)
            window = window + pltpu.roll(w, shift, axis=1)
        for i in range(occupied):
            row = (labels[i] ^ labels[j]) * pairs + 2 * i + copies[j]
            w2_ref[pl.ds(row, 1), :] = window[i : i + 1, :]
    w2 = w2_ref[...].astype(jnp.bfloat16)
    left = jnp.concatenate([ref[...].astype(jnp.float32) for ref in cycs], axis=0)
    left = left.reshape(rows, LANES).astype(jnp.bfloat16)
    choices = [
        [orb_ref[2 * (labels[e // 2] ^ n) + e % 2] for n in range(4)] for e in range(pairs)
    ]
    sources = [(part, n) for part in halves for n in range(part.shape[0])]
    pieces_of = payload_pieces(per_device, pairs, dests)
    tops = [jnp.zeros((8, LANES), jnp.float32)]

    def ladder(g, a):
        product = contract_last(w2, lad_ref[8 * g + a])
        ua = u_ref[8 * g + a : 8 * g + a + 1, :]
        sel = product[0:pairs]
        for v in range(1, 4):
            sel = jnp.where(ua == v, product[v * pairs : (v + 1) * pairs], sel)
        for v in range(tiles):
            ls_refs[g][v, pl.ds(a, pairs, stride=8), :] = sel[:, v * LANES : (v + 1) * LANES]

    def gathered():
        for r in range(dests):
            x = block_of(r)[:rows].astype(jnp.float32).reshape(per_device, occupied, LANES)
            xs_ref[pl.ds((pos_ref[0] ^ r) * per_device, per_device)] = x
            if r % 2:
                yield

    def cycle():
        for j in range(occupied):
            c = contract_last(left, xs_ref[:, j, :].astype(jnp.bfloat16))
            cs_ref[j] = c.reshape(occupied, per_device, virtuals)
            yield

    def payload(g):
        group = slice(8 * g, 8 * g + 8)
        found = {}
        for t in range(tiles):
            last_e = min(((t + 1) * LANES - 1) // per_device, pairs - 1)
            for e in range(t * LANES // per_device, last_e + 1):
                if (e, 0) in found:
                    continue
                part, n = sources[e]
                for v in range(tiles):
                    at = slice(v * LANES, (v + 1) * LANES)
                    uv = u_ref[group, at]
                    x = cs_ref[choices[e][0], e // 2, group, at]
                    for m in range(1, 4):
                        x = jnp.where(uv == m, cs_ref[choices[e][m], e // 2, group, at], x)
                    x = x + (part[n, group, at] + ls_refs[g][v, 8 * e : 8 * e + 8, :])
                    out_ref[e, group, at] = x
                    tops[0] = jnp.maximum(tops[0], jnp.abs(x))
                    found[e, v] = x
            for q in range(dests):
                acc = None
                for first, e, v, shift in pieces_of[q, t]:
                    x = pltpu.roll(found[e, v], shift, axis=1) if shift else found[e, v]
                    acc = x if acc is None else jnp.where(lane >= first, x, acc)
                start = t * per_device + 8 * g
                pay_ref[q, start : start + 8, :] = acc
                if q % 8 == 7:
                    yield

    others = [gathered(), cycle()] + [payload(g) for g in range(groups)]
    for g, other in enumerate(others):
        for a in range(8):
            if g < groups:
                ladder(g, a)
            next(other, None)
        for _ in other:
            pass
    most = jnp.max(jnp.max(tops[0], axis=0, keepdims=True), axis=1, keepdims=True)
    k = jnp.floor(TOP_EXPONENT - jnp.log2(jnp.maximum(most, 1e-30)))
    scale = jnp.exp2(k)
    row = lax.broadcasted_iota(jnp.int32, pay_ref.shape[1:], 0)
    for q in range(dests):
        z = pay_ref[q] * scale
        z2 = z * z
        z4 = z2 * z2
        y = jnp.where(row >= tiles * per_device, k, z4 * z4 * z)
        send_ref[q] = y.astype(jnp.bfloat16)


def join_kernel(occ_ref, u_ref, half_ref, recv_ref, out_ref, dec_ref, mir_ref, res_ref, sems):
    occupied = occ_ref.shape[0]
    per_device, virtuals = u_ref.shape
    labels, copies = labels_and_copies(occ_ref, occupied)
    spread = 2 * per_device
    ready = set()

    def decode(t):
        ready.add(t)
        start = t * per_device
        low, high = start // 16 * 16, (start + per_device + 15) // 16 * 16
        end = virtuals // LANES * per_device
        for p in range(recv_ref.shape[0]):
            tail = recv_ref[p, end // 16 * 16 : end // 16 * 16 + 16, :]
            k = tail.astype(jnp.float32)[end % 16 : end % 16 + 1, 0:1]
            y = recv_ref[p, low:high, :].astype(jnp.float32)
            y = y[start - low : start - low + per_device]
            size = jnp.log2(jnp.maximum(jnp.abs(y), 2.0**-126)) * (1.0 / POWER) - k
            size = jnp.exp2(size)
            x = jnp.where(y < 0, -size, jnp.where(y > 0, size, 0.0))
            dec_ref[p * per_device : (p + 1) * per_device, :] = x
        mir_ref[t * LANES : (t + 1) * LANES, :] = dec_ref[...].T

    stores = []
    for j in range(occupied):
        for t in range(j * spread // LANES, ((j + 1) * spread - 1) // LANES + 1):
            if t not in ready:
                decode(t)
        u = u_ref[...]
        for i in range(occupied):
            at = pl.ds(pl.multiple_of((2 * j + copies[i]) * per_device, 8), per_device)
            total = half_ref[2 * i + copies[j]] + mir_ref[at, :]
            n = j * occupied + i
            res_ref[n] = jnp.where(u == (labels[j] ^ labels[i]), total, 0.0)
            store = pltpu.make_async_copy(res_ref.at[n], out_ref.at[i, j], sems.at[n])
            store.start()
            stores.append(store)
    for store in stores:
        store.wait()


def permute(x, flip, size):
    return lax.ppermute(x, "vir", [(n, n ^ flip) for n in range(size)])


def body(dests, amps, fock_vir, fock_occ, ladder_ints, cycle_ints, occ_irrep, vir_irrep):
    occupied, _, per_device, virtuals = amps.shape
    pairs = 2 * occupied
    tiles = virtuals // LANES
    rows = occupied * per_device
    kw = ladder_ints.shape[2]
    f32, bf16 = jnp.float32, jnp.bfloat16
    position = lax.axis_index("vir").astype(jnp.int32)
    pos = position.reshape(1)
    vir_local = lax.dynamic_slice_in_dim(vir_irrep, position * per_device, per_device)
    u = jnp.bitwise_xor(vir_local[:, None], vir_irrep[None, :])
    smem = pl.BlockSpec(memory_space=pltpu.SMEM)

    def whole(shape):
        return pl.BlockSpec(shape, lambda n: (0,) * len(shape))

    def cost(flops, size):
        return pl.CostEstimate(flops=flops, bytes_accessed=size, transcendentals=0)

    anywhere = pl.BlockSpec(memory_space=pl.ANY)
    quarter = dests // 4
    block_rows = rows + 16
    block = pl.pallas_call(
        prep_kernel,
        grid=(1,),
        out_shape=jax.ShapeDtypeStruct((block_rows, LANES), bf16),
        in_specs=[
            whole((rows, LANES)),
            pl.BlockSpec((occupied, occupied, 16, LANES), lambda n: (0, 0, 0, 0)),
        ],
        out_specs=whole((block_rows, LANES)),
        compiler_params=params(60),
        cost_estimate=cost(0, 500000),
    )(cycle_ints.reshape(rows, LANES), amps)
    block = block.reshape(1, block_rows, LANES)
    vmem = pl.BlockSpec(memory_space=pltpu.VMEM)
    mix = pl.pallas_call(
        mix_kernel,
        out_shape=jax.ShapeDtypeStruct((rows, rows), bf16),
        in_specs=[vmem],
        out_specs=vmem,
        compiler_params=params(4),
        cost_estimate=cost(10**7, 300000),
    )(fock_occ)

    flat_amps = amps.reshape(occupied, rows, virtuals)
    parts = (2, 2, 2, 2)
    wide = 2

    def fock_part(n, after):
        first, count = sum(parts[:n]), parts[n]
        return pl.pallas_call(
            functools.partial(fock_kernel, first),
            grid=(count // wide,),
            out_shape=(
                jax.ShapeDtypeStruct((2 * count, per_device, virtuals), f32),
                jax.ShapeDtypeStruct((count, per_device, LANES), bf16),
            ),
            in_specs=[
                smem,
                pl.BlockSpec((wide, rows, virtuals), lambda i: (i + first // wide, 0, 0)),
                whole(fock_vir.shape),
                whole(mix.shape),
                whole(u.shape),
                anywhere,
            ],
            out_specs=(
                pl.BlockSpec((2 * wide, per_device, virtuals), lambda i: (i, 0, 0)),
                pl.BlockSpec((wide, per_device, LANES), lambda i: (i, 0, 0)),
            ),
            scratch_shapes=[pltpu.VMEM((occupied, per_device, virtuals), f32)],
            compiler_params=params(12),
            cost_estimate=cost(3 * count * rows * virtuals * virtuals, 2 * 10**6),
        )(occ_irrep, flat_amps, fock_vir, mix, u, after)

    z1, z2, z3 = [permute(block, m << 2, dests) for m in range(1, quarter)]
    half0, cyc0 = fock_part(0, mix)
    near = stack([block, z1], half0)
    near_y = permute(near, 2, dests)
    half1, cyc1 = fock_part(1, near)
    far = stack([z2, z3], half1)
    far_y = permute(far, 2, dests)
    half2, cyc2 = fock_part(2, far)
    own_blocks = stack([near, far, near_y, far_y], half2)
    mate_blocks = permute(own_blocks, 1, dests)
    half3, cyc3 = fock_part(3, own_blocks)

    send_rows = tiles * per_device + 8
    groups = per_device // 8
    half, send = pl.pallas_call(
        functools.partial(half_kernel, groups, parts),
        out_shape=(
            jax.ShapeDtypeStruct((pairs, per_device, virtuals), f32),
            jax.ShapeDtypeStruct((dests, send_rows, LANES), bf16),
        ),
        in_specs=[smem, smem] + [vmem] * (4 + 2 * len(parts)),
        out_specs=(vmem, vmem),
        scratch_shapes=[
            pltpu.SMEM((occupied,), jnp.int32),
            pltpu.VMEM((occupied * occupied, LANES), f32),
            pltpu.VMEM((virtuals, occupied, LANES), f32),
            pltpu.VMEM((occupied, occupied, per_device, virtuals), f32),
            pltpu.VMEM((dests, send_rows, LANES), f32),
        ]
        + [pltpu.VMEM((tiles, 8 * pairs, LANES), f32)] * groups,
        compiler_params=params(28),
        cost_estimate=cost(6 * occupied * rows * virtuals * LANES, 15 * 10**6),
    )(
        pos, occ_irrep, own_blocks, mate_blocks, half0, half1, half2, half3,
        cyc0, cyc1, cyc2, cyc3, u, ladder_ints,
    )

    recv = lax.all_to_all(send, "vir", split_axis=0, concat_axis=0, tiled=True)

    return pl.pallas_call(
        join_kernel,
        out_shape=jax.ShapeDtypeStruct((occupied, occupied, per_device, virtuals), f32),
        in_specs=[smem, vmem, vmem, vmem],
        out_specs=anywhere,
        scratch_shapes=[
            pltpu.VMEM((virtuals, LANES), f32),
            pltpu.VMEM((tiles * LANES, virtuals), f32),
            pltpu.VMEM((occupied * occupied, per_device, virtuals), f32),
            pltpu.SemaphoreType.DMA((occupied * occupied,)),
        ],
        compiler_params=params(16),
        cost_estimate=cost(10**6, 5 * 10**6),
    )(occ_irrep, u, half, recv)


def solution(mesh):
    dests = mesh.shape["vir"]

    def run(amps, *rest):
        occupied, _, per_device, virtuals = amps.shape
        tiled = (
            dests == 16
            and per_device % 8 == 0
            and virtuals % LANES == 0
            and 2 * occupied * per_device == virtuals
            and rest[2].shape[2] == LANES
            and rest[3].shape[2] == LANES
        )
        return body(dests, amps, *rest) if tiled else plain_body(amps, *rest)

    return jax.shard_map(
        run,
        mesh=mesh,
        in_specs=(
            P("groups", None, "vir", None),
            P("groups", None),
            P("groups", None),
            P("vir", "groups", None),
            P("vir", "groups", None),
            P("groups"),
            P("groups"),
        ),
        out_specs=P("groups", None, "vir", None),
        check_vma=False,
    )
```

```python
import functools

import jax
import jax.numpy as jnp
from jax import lax
from jax.experimental import pallas as pl
from jax.experimental.pallas import tpu as pltpu
from jax.sharding import PartitionSpec as P

DW = 8
CW = 16
LANES = 128
POWER = 9
TOP_EXPONENT = 13


def contract_last(left_side, right_side):
    return lax.dot_general(
        left_side, right_side, (((1,), (1,)), ((), ())), preferred_element_type=jnp.float32
    )


def plain_body(amps, fock_vir, fock_occ, ladder_ints, cycle_ints, occ_irrep, vir_irrep):
    occupied = amps.shape[0]
    per_device = amps.shape[2]
    virtuals = amps.shape[3]
    pair_count = occupied * occupied
    position = lax.axis_index("vir")
    fock_term = jnp.dot(
        amps.reshape(pair_count * per_device, virtuals),
        fock_vir,
        preferred_element_type=jnp.float32,
    ).reshape(occupied, occupied, per_device, virtuals)
    occ_term = jnp.einsum("ikab,kj->ijab", amps, fock_occ, preferred_element_type=jnp.float32)
    flat_ints = ladder_ints.reshape(per_device * virtuals, ladder_ints.shape[2])
    local_window = amps[:, :, 0:1, :DW]
    local_cycle = amps[:, :, :, :CW]
    segment = lax.all_gather(local_window, "vir", axis=2, tiled=True)
    width = segment.shape[2] * DW
    ladder = contract_last(segment.reshape(pair_count, width), flat_ints)
    left_side = jnp.transpose(local_cycle, (0, 2, 1, 3)).reshape(
        occupied * per_device, occupied * CW
    )
    segment = lax.all_gather(cycle_ints, "vir", axis=0, tiled=True)
    right_side = segment.reshape(segment.shape[0] * occupied, occupied * CW)
    cycle_block = contract_last(left_side, right_side).reshape(
        occupied, per_device, segment.shape[0], occupied
    )
    cycle_part = jnp.transpose(cycle_block, (0, 3, 1, 2))
    half_sum = (
        fock_term - occ_term + ladder.reshape(occupied, occupied, per_device, virtuals) + cycle_part
    )
    vir_local = lax.dynamic_slice_in_dim(vir_irrep, position * per_device, per_device)
    occ_pair = jnp.bitwise_xor(occ_irrep[:, None], occ_irrep[None, :])
    vir_pair = jnp.bitwise_xor(vir_local[:, None], vir_irrep[None, :])
    received = lax.all_to_all(half_sum, "vir", split_axis=3, concat_axis=2, tiled=True)
    mirrored = jnp.transpose(received, (1, 0, 3, 2))
    product_irrep = jnp.bitwise_xor(occ_pair[:, :, None, None], vir_pair[None, None, :, :])
    allowed = jnp.where(product_irrep == 0, jnp.float32(1.0), jnp.float32(0.0))
    return allowed * (half_sum + mirrored)


def params(mib):
    return pltpu.CompilerParams(vmem_limit_bytes=mib * 2**20)


def labels_and_copies(occ_ref, occupied):
    labels = [occ_ref[j] for j in range(occupied)]
    copies = []
    for j in range(occupied):
        s = jnp.int32(0)
        for k in range(j):
            s = s + (labels[k] == labels[j]).astype(jnp.int32)
        copies.append(s)
    return labels, copies


def prep_kernel(cyc_ref, amps_ref, block_ref):
    occupied = amps_ref.shape[0]
    rows = cyc_ref.shape[0]
    block_ref[:rows, :] = cyc_ref[...]
    lane = lax.broadcasted_iota(jnp.int32, (occupied, LANES), 1)
    packed = jnp.zeros((occupied, LANES), jnp.float32)
    for j in range(occupied):
        w = jnp.where(lane < DW, amps_ref[:, j, 0, :].astype(jnp.float32), 0.0)
        packed = packed + (pltpu.roll(w, j * DW, axis=1) if j else w)
    packed = jnp.concatenate([packed, jnp.zeros_like(packed)], axis=0)
    block_ref[rows:, :] = packed.astype(jnp.bfloat16)


def mix_kernel(occ_vals_ref, after_ref, mix_ref):
    rows = mix_ref.shape[0]
    occupied = occ_vals_ref.shape[0]
    per_device = rows // occupied
    row = lax.broadcasted_iota(jnp.int32, (rows, occupied), 0)
    start = lax.broadcasted_iota(jnp.int32, (rows, occupied), 1) * per_device
    in_block = jnp.logical_and(row >= start, row < start + per_device).astype(jnp.bfloat16)
    row = lax.broadcasted_iota(jnp.int32, (rows, per_device), 0)
    at = lax.broadcasted_iota(jnp.int32, (rows, per_device), 1)
    same = row == at
    for n in range(1, occupied):
        same = jnp.logical_or(same, row == at + n * per_device)
    same = same.astype(jnp.bfloat16)
    left = contract_last(in_block, occ_vals_ref[...]).astype(jnp.bfloat16)
    mix = contract_last(left, in_block) * contract_last(same, same)
    mix_ref[...] = mix.astype(jnp.bfloat16)


def fock_kernel(first, occ_ref, amps_ref, fock_ref, mix_ref, u_ref, after_ref, half_ref, cyc_ref, hs_ref):
    wide, rows, virtuals = amps_ref.shape
    _, per_device, _ = half_ref.shape
    occupied = occ_ref.shape[0]
    labels, copies = labels_and_copies(occ_ref, occupied)
    u = u_ref[...]
    h = jnp.dot(
        amps_ref[...].reshape(wide * rows, virtuals),
        fock_ref[...],
        preferred_element_type=jnp.float32,
    )
    for w in range(wide):
        a = amps_ref[w]
        mixed = jnp.dot(mix_ref[...], a, preferred_element_type=jnp.float32)
        hs_ref[...] = (h[w * rows : (w + 1) * rows] - mixed).reshape(hs_ref.shape)
        own = occ_ref[pl.program_id(0) * wide + w + first]
        for j in range(occupied):
            at = 2 * w + copies[j]
            half_ref[at] = jnp.where(u == (own ^ labels[j]), hs_ref[j], half_ref[at])
        head = a[:, :LANES].astype(jnp.float32)
        lane = lax.broadcasted_iota(jnp.int32, (per_device, LANES), 1)
        acc = jnp.zeros((per_device, LANES), jnp.float32)
        for k in range(occupied):
            piece = jnp.where(lane < CW, head[k * per_device : (k + 1) * per_device], 0.0)
            acc = acc + (pltpu.roll(piece, k * CW, axis=1) if k else piece)
        cyc_ref[w] = acc.astype(jnp.bfloat16)


def stack(blocks, after):
    count = len(blocks)

    def kernel(*refs):
        out = refs[count + 1]
        at = 0
        for n in range(count):
            head = blocks[n].shape[0]
            out[at : at + head] = refs[n][...]
            at += head

    vmem = pl.BlockSpec(memory_space=pltpu.VMEM)
    shape = (sum(b.shape[0] for b in blocks),) + blocks[0].shape[1:]
    return pl.pallas_call(
        kernel,
        out_shape=jax.ShapeDtypeStruct(shape, blocks[0].dtype),
        in_specs=[vmem] * count + [pl.BlockSpec(memory_space=pl.ANY)],
        out_specs=vmem,
        compiler_params=params(4),
        cost_estimate=pl.CostEstimate(flops=0, bytes_accessed=10**6, transcendentals=0),
    )(*blocks, after)


def payload_pieces(per_device, pairs, dests):
    out = {}
    for q in range(dests):
        for e in range(pairs):
            start = 0
            while start < per_device:
                src = q * per_device + start
                dst = e * per_device + start
                length = min(LANES - src % LANES, LANES - dst % LANES, per_device - start)
                out.setdefault((q, dst // LANES), []).append(
                    (dst % LANES, e, src // LANES, (dst - src) % LANES)
                )
                start += length
    return out


def half_kernel(groups, parts, pos_ref, occ_ref, own_ref, mate_ref, *refs):
    halves, refs = refs[: len(parts)], refs[len(parts) :]
    cycs, refs = refs[: len(parts)], refs[len(parts) :]
    u_ref, lad_ref, out_ref, send_ref, orb_ref, w2_ref, xs_ref, cs_ref, pay_ref = refs[:9]
    ls_refs = refs[9:]
    occupied = occ_ref.shape[0]
    pairs, per_device, virtuals = out_ref.shape
    dests = pay_ref.shape[0]
    tiles = virtuals // LANES
    rows = occupied * per_device
    labels, copies = labels_and_copies(occ_ref, occupied)
    lane = lax.broadcasted_iota(jnp.int32, (8, LANES), 1)

    def block_of(r):
        ref = mate_ref if r & 1 else own_ref
        return ref[((r >> 1) & 1) * (dests // 4) + (r >> 2)]

    packed = [block_of(r)[rows:].astype(jnp.float32)[:8] for r in range(dests)]
    for j in range(occupied):
        orb_ref[2 * labels[j] + copies[j]] = jnp.int32(j)
        window = jnp.zeros((8, LANES), jnp.float32)
        for r in range(dests):
            w = jnp.where(jnp.logical_and(lane >= j * DW, lane < (j + 1) * DW), packed[r], 0.0)
            shift = lax.rem((pos_ref[0] ^ r) * DW - j * DW + LANES, LANES)
            window = window + pltpu.roll(w, shift, axis=1)
        for i in range(occupied):
            row = (labels[i] ^ labels[j]) * pairs + 2 * i + copies[j]
            w2_ref[pl.ds(row, 1), :] = window[i : i + 1, :]
    w2 = w2_ref[...].astype(jnp.bfloat16)
    left = jnp.concatenate([ref[...].astype(jnp.float32) for ref in cycs], axis=0)
    left = left.reshape(rows, LANES).astype(jnp.bfloat16)
    choices = [
        [orb_ref[2 * (labels[e // 2] ^ n) + e % 2] for n in range(4)] for e in range(pairs)
    ]
    sources = [(part, n) for part in halves for n in range(part.shape[0])]
    pieces_of = payload_pieces(per_device, pairs, dests)
    tops = [jnp.zeros((8, LANES), jnp.float32)]

    def ladder(g, a):
        product = contract_last(w2, lad_ref[8 * g + a])
        ua = u_ref[8 * g + a : 8 * g + a + 1, :]
        sel = product[0:pairs]
        for v in range(1, 4):
            sel = jnp.where(ua == v, product[v * pairs : (v + 1) * pairs], sel)
        for v in range(tiles):
            ls_refs[g][v, pl.ds(a, pairs, stride=8), :] = sel[:, v * LANES : (v + 1) * LANES]

    def gathered():
        for r in range(dests):
            x = block_of(r)[:rows].astype(jnp.float32).reshape(per_device, occupied, LANES)
            xs_ref[pl.ds((pos_ref[0] ^ r) * per_device, per_device)] = x
            if r % 2:
                yield

    def cycle():
        for j in range(occupied):
            c = contract_last(left, xs_ref[:, j, :].astype(jnp.bfloat16))
            cs_ref[j] = c.reshape(occupied, per_device, virtuals)
            yield

    def payload(g):
        group = slice(8 * g, 8 * g + 8)
        found = {}
        for t in range(tiles):
            last_e = min(((t + 1) * LANES - 1) // per_device, pairs - 1)
            for e in range(t * LANES // per_device, last_e + 1):
                if (e, 0) in found:
                    continue
                part, n = sources[e]
                for v in range(tiles):
                    at = slice(v * LANES, (v + 1) * LANES)
                    uv = u_ref[group, at]
                    x = cs_ref[choices[e][0], e // 2, group, at]
                    for m in range(1, 4):
                        x = jnp.where(uv == m, cs_ref[choices[e][m], e // 2, group, at], x)
                    x = x + (part[n, group, at] + ls_refs[g][v, 8 * e : 8 * e + 8, :])
                    out_ref[e, group, at] = x
                    tops[0] = jnp.maximum(tops[0], jnp.abs(x))
                    found[e, v] = x
            for q in range(dests):
                acc = None
                for first, e, v, shift in pieces_of[q, t]:
                    x = pltpu.roll(found[e, v], shift, axis=1) if shift else found[e, v]
                    acc = x if acc is None else jnp.where(lane >= first, x, acc)
                start = t * per_device + 8 * g
                pay_ref[q, start : start + 8, :] = acc
                if q % 8 == 7:
                    yield

    others = [gathered(), cycle()] + [payload(g) for g in range(groups)]
    for g, other in enumerate(others):
        for a in range(8):
            if g < groups:
                ladder(g, a)
            next(other, None)
        for _ in other:
            pass
    most = jnp.max(jnp.max(tops[0], axis=0, keepdims=True), axis=1, keepdims=True)
    k = jnp.floor(TOP_EXPONENT - jnp.log2(jnp.maximum(most, 1e-30)))
    scale = jnp.exp2(k)
    row = lax.broadcasted_iota(jnp.int32, pay_ref.shape[1:], 0)
    for q in range(dests):
        z = pay_ref[q] * scale
        z2 = z * z
        z4 = z2 * z2
        y = jnp.where(row >= tiles * per_device, k, z4 * z4 * z)
        send_ref[q] = y.astype(jnp.bfloat16)


def join_kernel(occ_ref, u_ref, half_ref, recv_ref, out_ref, dec_ref, mir_ref, res_ref, sems):
    occupied = occ_ref.shape[0]
    per_device, virtuals = u_ref.shape
    labels, copies = labels_and_copies(occ_ref, occupied)
    spread = 2 * per_device
    ready = set()

    def decode(t):
        ready.add(t)
        start = t * per_device
        low, high = start // 16 * 16, (start + per_device + 15) // 16 * 16
        end = virtuals // LANES * per_device
        for p in range(recv_ref.shape[0]):
            tail = recv_ref[p, end // 16 * 16 : end // 16 * 16 + 16, :]
            k = tail.astype(jnp.float32)[end % 16 : end % 16 + 1, 0:1]
            y = recv_ref[p, low:high, :].astype(jnp.float32)
            y = y[start - low : start - low + per_device]
            size = jnp.log2(jnp.maximum(jnp.abs(y), 2.0**-126)) * (1.0 / POWER) - k
            size = jnp.exp2(size)
            x = jnp.where(y < 0, -size, jnp.where(y > 0, size, 0.0))
            dec_ref[p * per_device : (p + 1) * per_device, :] = x
        mir_ref[t * LANES : (t + 1) * LANES, :] = dec_ref[...].T

    stores = []
    for j in range(occupied):
        for t in range(j * spread // LANES, ((j + 1) * spread - 1) // LANES + 1):
            if t not in ready:
                decode(t)
        u = u_ref[...]
        for i in range(occupied):
            at = pl.ds(pl.multiple_of((2 * j + copies[i]) * per_device, 8), per_device)
            total = half_ref[2 * i + copies[j]] + mir_ref[at, :]
            n = j * occupied + i
            res_ref[n] = jnp.where(u == (labels[j] ^ labels[i]), total, 0.0)
            store = pltpu.make_async_copy(res_ref.at[n], out_ref.at[i, j], sems.at[n])
            store.start()
            stores.append(store)
    for store in stores:
        store.wait()


def permute(x, flip, size):
    return lax.ppermute(x, "vir", [(n, n ^ flip) for n in range(size)])


def body(dests, amps, fock_vir, fock_occ, ladder_ints, cycle_ints, occ_irrep, vir_irrep):
    occupied, _, per_device, virtuals = amps.shape
    pairs = 2 * occupied
    tiles = virtuals // LANES
    rows = occupied * per_device
    kw = ladder_ints.shape[2]
    f32, bf16 = jnp.float32, jnp.bfloat16
    position = lax.axis_index("vir").astype(jnp.int32)
    pos = position.reshape(1)
    vir_local = lax.dynamic_slice_in_dim(vir_irrep, position * per_device, per_device)
    u = jnp.bitwise_xor(vir_local[:, None], vir_irrep[None, :])
    smem = pl.BlockSpec(memory_space=pltpu.SMEM)

    def whole(shape):
        return pl.BlockSpec(shape, lambda n: (0,) * len(shape))

    def cost(flops, size):
        return pl.CostEstimate(flops=flops, bytes_accessed=size, transcendentals=0)

    anywhere = pl.BlockSpec(memory_space=pl.ANY)
    quarter = dests // 4
    block_rows = rows + 16
    block = pl.pallas_call(
        prep_kernel,
        grid=(1,),
        out_shape=jax.ShapeDtypeStruct((block_rows, LANES), bf16),
        in_specs=[
            whole((rows, LANES)),
            pl.BlockSpec((occupied, occupied, 16, LANES), lambda n: (0, 0, 0, 0)),
        ],
        out_specs=whole((block_rows, LANES)),
        compiler_params=params(60),
        cost_estimate=cost(0, 500000),
    )(cycle_ints.reshape(rows, LANES), amps)
    block = block.reshape(1, block_rows, LANES)
    vmem = pl.BlockSpec(memory_space=pltpu.VMEM)
    mix = pl.pallas_call(
        mix_kernel,
        out_shape=jax.ShapeDtypeStruct((rows, rows), bf16),
        in_specs=[vmem, anywhere],
        out_specs=vmem,
        compiler_params=params(4),
        cost_estimate=cost(10**7, 300000),
    )(fock_occ, block)

    flat_amps = amps.reshape(occupied, rows, virtuals)
    parts = (2, 2, 2, 2)
    wide = 2

    def fock_part(n, after):
        first, count = sum(parts[:n]), parts[n]
        return pl.pallas_call(
            functools.partial(fock_kernel, first),
            grid=(count // wide,),
            out_shape=(
                jax.ShapeDtypeStruct((2 * count, per_device, virtuals), f32),
                jax.ShapeDtypeStruct((count, per_device, LANES), bf16),
            ),
            in_specs=[
                smem,
                pl.BlockSpec((wide, rows, virtuals), lambda i: (i + first // wide, 0, 0)),
                whole(fock_vir.shape),
                whole(mix.shape),
                whole(u.shape),
                anywhere,
            ],
            out_specs=(
                pl.BlockSpec((2 * wide, per_device, virtuals), lambda i: (i, 0, 0)),
                pl.BlockSpec((wide, per_device, LANES), lambda i: (i, 0, 0)),
            ),
            scratch_shapes=[pltpu.VMEM((occupied, per_device, virtuals), f32)],
            compiler_params=params(12),
            cost_estimate=cost(3 * count * rows * virtuals * virtuals, 2 * 10**6),
        )(occ_irrep, flat_amps, fock_vir, mix, u, after)

    z1, z2, z3 = [permute(block, m << 2, dests) for m in range(1, quarter)]
    half0, cyc0 = fock_part(0, mix)
    near = stack([block, z1], half0)
    near_y = permute(near, 2, dests)
    half1, cyc1 = fock_part(1, near)
    far = stack([z2, z3], half1)
    far_y = permute(far, 2, dests)
    half2, cyc2 = fock_part(2, far)
    own_blocks = stack([near, far, near_y, far_y], half2)
    mate_blocks = permute(own_blocks, 1, dests)
    half3, cyc3 = fock_part(3, own_blocks)

    send_rows = tiles * per_device + 8
    groups = per_device // 8
    half, send = pl.pallas_call(
        functools.partial(half_kernel, groups, parts),
        out_shape=(
            jax.ShapeDtypeStruct((pairs, per_device, virtuals), f32),
            jax.ShapeDtypeStruct((dests, send_rows, LANES), bf16),
        ),
        in_specs=[smem, smem] + [vmem] * (4 + 2 * len(parts)),
        out_specs=(vmem, vmem),
        scratch_shapes=[
            pltpu.SMEM((occupied,), jnp.int32),
            pltpu.VMEM((occupied * occupied, LANES), f32),
            pltpu.VMEM((virtuals, occupied, LANES), f32),
            pltpu.VMEM((occupied, occupied, per_device, virtuals), f32),
            pltpu.VMEM((dests, send_rows, LANES), f32),
        ]
        + [pltpu.VMEM((tiles, 8 * pairs, LANES), f32)] * groups,
        compiler_params=params(28),
        cost_estimate=cost(6 * occupied * rows * virtuals * LANES, 15 * 10**6),
    )(
        pos, occ_irrep, own_blocks, mate_blocks, half0, half1, half2, half3,
        cyc0, cyc1, cyc2, cyc3, u, ladder_ints,
    )

    recv = lax.all_to_all(send, "vir", split_axis=0, concat_axis=0, tiled=True)

    return pl.pallas_call(
        join_kernel,
        out_shape=jax.ShapeDtypeStruct((occupied, occupied, per_device, virtuals), f32),
        in_specs=[smem, vmem, vmem, vmem],
        out_specs=anywhere,
        scratch_shapes=[
            pltpu.VMEM((virtuals, LANES), f32),
            pltpu.VMEM((tiles * LANES, virtuals), f32),
            pltpu.VMEM((occupied * occupied, per_device, virtuals), f32),
            pltpu.SemaphoreType.DMA((occupied * occupied,)),
        ],
        compiler_params=params(16),
        cost_estimate=cost(10**6, 5 * 10**6),
    )(occ_irrep, u, half, recv)


def solution(mesh):
    dests = mesh.shape["vir"]

    def run(amps, *rest):
        occupied, _, per_device, virtuals = amps.shape
        tiled = (
            dests == 16
            and per_device % 8 == 0
            and virtuals % LANES == 0
            and 2 * occupied * per_device == virtuals
            and rest[2].shape[2] == LANES
            and rest[3].shape[2] == LANES
        )
        return body(dests, amps, *rest) if tiled else plain_body(amps, *rest)

    return jax.shard_map(
        run,
        mesh=mesh,
        in_specs=(
            P("groups", None, "vir", None),
            P("groups", None),
            P("groups", None),
            P("vir", "groups", None),
            P("vir", "groups", None),
            P("groups"),
            P("groups"),
        ),
        out_specs=P("groups", None, "vir", None),
        check_vma=False,
    )
```

```python
import functools

import jax
import jax.numpy as jnp
from jax import lax
from jax.experimental import pallas as pl
from jax.experimental.pallas import tpu as pltpu
from jax.sharding import PartitionSpec as P

DW = 8
CW = 16
LANES = 128
POWER = 9
TOP_EXPONENT = 13


def contract_last(left_side, right_side):
    return lax.dot_general(
        left_side, right_side, (((1,), (1,)), ((), ())), preferred_element_type=jnp.float32
    )


def plain_body(amps, fock_vir, fock_occ, ladder_ints, cycle_ints, occ_irrep, vir_irrep):
    occupied = amps.shape[0]
    per_device = amps.shape[2]
    virtuals = amps.shape[3]
    pair_count = occupied * occupied
    position = lax.axis_index("vir")
    fock_term = jnp.dot(
        amps.reshape(pair_count * per_device, virtuals),
        fock_vir,
        preferred_element_type=jnp.float32,
    ).reshape(occupied, occupied, per_device, virtuals)
    occ_term = jnp.einsum("ikab,kj->ijab", amps, fock_occ, preferred_element_type=jnp.float32)
    flat_ints = ladder_ints.reshape(per_device * virtuals, ladder_ints.shape[2])
    local_window = amps[:, :, 0:1, :DW]
    local_cycle = amps[:, :, :, :CW]
    segment = lax.all_gather(local_window, "vir", axis=2, tiled=True)
    width = segment.shape[2] * DW
    ladder = contract_last(segment.reshape(pair_count, width), flat_ints)
    left_side = jnp.transpose(local_cycle, (0, 2, 1, 3)).reshape(
        occupied * per_device, occupied * CW
    )
    segment = lax.all_gather(cycle_ints, "vir", axis=0, tiled=True)
    right_side = segment.reshape(segment.shape[0] * occupied, occupied * CW)
    cycle_block = contract_last(left_side, right_side).reshape(
        occupied, per_device, segment.shape[0], occupied
    )
    cycle_part = jnp.transpose(cycle_block, (0, 3, 1, 2))
    half_sum = (
        fock_term - occ_term + ladder.reshape(occupied, occupied, per_device, virtuals) + cycle_part
    )
    vir_local = lax.dynamic_slice_in_dim(vir_irrep, position * per_device, per_device)
    occ_pair = jnp.bitwise_xor(occ_irrep[:, None], occ_irrep[None, :])
    vir_pair = jnp.bitwise_xor(vir_local[:, None], vir_irrep[None, :])
    received = lax.all_to_all(half_sum, "vir", split_axis=3, concat_axis=2, tiled=True)
    mirrored = jnp.transpose(received, (1, 0, 3, 2))
    product_irrep = jnp.bitwise_xor(occ_pair[:, :, None, None], vir_pair[None, None, :, :])
    allowed = jnp.where(product_irrep == 0, jnp.float32(1.0), jnp.float32(0.0))
    return allowed * (half_sum + mirrored)


def params(mib):
    return pltpu.CompilerParams(vmem_limit_bytes=mib * 2**20)


def labels_and_copies(occ_ref, occupied):
    labels = [occ_ref[j] for j in range(occupied)]
    copies = []
    for j in range(occupied):
        s = jnp.int32(0)
        for k in range(j):
            s = s + (labels[k] == labels[j]).astype(jnp.int32)
        copies.append(s)
    return labels, copies


def prep_kernel(cyc_ref, amps_ref, block_ref):
    occupied = amps_ref.shape[0]
    rows = cyc_ref.shape[0]
    block_ref[:rows, :] = cyc_ref[...]
    lane = lax.broadcasted_iota(jnp.int32, (occupied, LANES), 1)
    packed = jnp.zeros((occupied, LANES), jnp.float32)
    for j in range(occupied):
        w = jnp.where(lane < DW, amps_ref[:, j, 0, :].astype(jnp.float32), 0.0)
        packed = packed + (pltpu.roll(w, j * DW, axis=1) if j else w)
    packed = jnp.concatenate([packed, jnp.zeros_like(packed)], axis=0)
    block_ref[rows:, :] = packed.astype(jnp.bfloat16)


def mix_kernel(occ_vals_ref, mix_ref):
    rows = mix_ref.shape[0]
    occupied = occ_vals_ref.shape[0]
    per_device = rows // occupied
    row = lax.broadcasted_iota(jnp.int32, (rows, occupied), 0)
    start = lax.broadcasted_iota(jnp.int32, (rows, occupied), 1) * per_device
    in_block = jnp.logical_and(row >= start, row < start + per_device).astype(jnp.bfloat16)
    row = lax.broadcasted_iota(jnp.int32, (rows, per_device), 0)
    at = lax.broadcasted_iota(jnp.int32, (rows, per_device), 1)
    same = row == at
    for n in range(1, occupied):
        same = jnp.logical_or(same, row == at + n * per_device)
    same = same.astype(jnp.bfloat16)
    left = contract_last(in_block, occ_vals_ref[...]).astype(jnp.bfloat16)
    mix = contract_last(left, in_block) * contract_last(same, same)
    mix_ref[...] = mix.astype(jnp.bfloat16)


def fock_kernel(first, occ_ref, amps_ref, fock_ref, mix_ref, u_ref, after_ref, half_ref, cyc_ref, hs_ref):
    wide, rows, virtuals = amps_ref.shape
    _, per_device, _ = half_ref.shape
    occupied = occ_ref.shape[0]
    labels, copies = labels_and_copies(occ_ref, occupied)
    u = u_ref[...]
    h = jnp.dot(
        amps_ref[...].reshape(wide * rows, virtuals),
        fock_ref[...],
        preferred_element_type=jnp.float32,
    )
    for w in range(wide):
        a = amps_ref[w]
        mixed = jnp.dot(mix_ref[...], a, preferred_element_type=jnp.float32)
        hs_ref[...] = (h[w * rows : (w + 1) * rows] - mixed).reshape(hs_ref.shape)
        own = occ_ref[pl.program_id(0) * wide + w + first]
        for j in range(occupied):
            at = 2 * w + copies[j]
            half_ref[at] = jnp.where(u == (own ^ labels[j]), hs_ref[j], half_ref[at])
        head = a[:, :LANES].astype(jnp.float32)
        lane = lax.broadcasted_iota(jnp.int32, (per_device, LANES), 1)
        acc = jnp.zeros((per_device, LANES), jnp.float32)
        for k in range(occupied):
            piece = jnp.where(lane < CW, head[k * per_device : (k + 1) * per_device], 0.0)
            acc = acc + (pltpu.roll(piece, k * CW, axis=1) if k else piece)
        cyc_ref[w] = acc.astype(jnp.bfloat16)


def stack(blocks, after):
    count = len(blocks)

    def kernel(*refs):
        out = refs[count + 1]
        at = 0
        for n in range(count):
            head = blocks[n].shape[0]
            out[at : at + head] = refs[n][...]
            at += head

    vmem = pl.BlockSpec(memory_space=pltpu.VMEM)
    shape = (sum(b.shape[0] for b in blocks),) + blocks[0].shape[1:]
    return pl.pallas_call(
        kernel,
        out_shape=jax.ShapeDtypeStruct(shape, blocks[0].dtype),
        in_specs=[vmem] * count + [pl.BlockSpec(memory_space=pl.ANY)],
        out_specs=vmem,
        compiler_params=params(4),
        cost_estimate=pl.CostEstimate(flops=0, bytes_accessed=10**6, transcendentals=0),
    )(*blocks, after)


def payload_pieces(per_device, pairs, dests):
    out = {}
    for q in range(dests):
        for e in range(pairs):
            start = 0
            while start < per_device:
                src = q * per_device + start
                dst = e * per_device + start
                length = min(LANES - src % LANES, LANES - dst % LANES, per_device - start)
                out.setdefault((q, dst // LANES), []).append(
                    (dst % LANES, e, src // LANES, (dst - src) % LANES)
                )
                start += length
    return out


def half_kernel(groups, parts, pos_ref, occ_ref, own_ref, mate_ref, *refs):
    halves, refs = refs[: len(parts)], refs[len(parts) :]
    cycs, refs = refs[: len(parts)], refs[len(parts) :]
    u_ref, lad_ref, out_ref, send_ref, orb_ref, w2_ref, xs_ref, cs_ref, pay_ref = refs[:9]
    ls_refs = refs[9:]
    occupied = occ_ref.shape[0]
    pairs, per_device, virtuals = out_ref.shape
    dests = pay_ref.shape[0]
    tiles = virtuals // LANES
    rows = occupied * per_device
    labels, copies = labels_and_copies(occ_ref, occupied)
    lane = lax.broadcasted_iota(jnp.int32, (8, LANES), 1)

    def block_of(r):
        ref = mate_ref if r & 1 else own_ref
        return ref[((r >> 1) & 1) * (dests // 4) + (r >> 2)]

    packed = [block_of(r)[rows:].astype(jnp.float32)[:8] for r in range(dests)]
    for j in range(occupied):
        orb_ref[2 * labels[j] + copies[j]] = jnp.int32(j)
        window = jnp.zeros((8, LANES), jnp.float32)
        for r in range(dests):
            w = jnp.where(jnp.logical_and(lane >= j * DW, lane < (j + 1) * DW), packed[r], 0.0)
            shift = lax.rem((pos_ref[0] ^ r) * DW - j * DW + LANES, LANES)
            window = window + pltpu.roll(w, shift, axis=1)
        for i in range(occupied):
            row = (labels[i] ^ labels[j]) * pairs + 2 * i + copies[j]
            w2_ref[pl.ds(row, 1), :] = window[i : i + 1, :]
    w2 = w2_ref[...].astype(jnp.bfloat16)
    left = jnp.concatenate([ref[...].astype(jnp.float32) for ref in cycs], axis=0)
    left = left.reshape(rows, LANES).astype(jnp.bfloat16)
    choices = [
        [orb_ref[2 * (labels[e // 2] ^ n) + e % 2] for n in range(4)] for e in range(pairs)
    ]
    sources = [(part, n) for part in halves for n in range(part.shape[0])]
    pieces_of = payload_pieces(per_device, pairs, dests)
    tops = [jnp.zeros((8, LANES), jnp.float32)]

    def ladder(g, a):
        product = contract_last(w2, lad_ref[8 * g + a])
        ua = u_ref[8 * g + a : 8 * g + a + 1, :]
        sel = product[0:pairs]
        for v in range(1, 4):
            sel = jnp.where(ua == v, product[v * pairs : (v + 1) * pairs], sel)
        for v in range(tiles):
            ls_refs[g][v, pl.ds(a, pairs, stride=8), :] = sel[:, v * LANES : (v + 1) * LANES]

    def gathered():
        for r in range(dests):
            x = block_of(r)[:rows].astype(jnp.float32).reshape(per_device, occupied, LANES)
            xs_ref[pl.ds((pos_ref[0] ^ r) * per_device, per_device)] = x
            if r % 2:
                yield

    def cycle():
        for j in range(occupied):
            c = contract_last(left, xs_ref[:, j, :].astype(jnp.bfloat16))
            cs_ref[j] = c.reshape(occupied, per_device, virtuals)
            yield

    def payload(g):
        group = slice(8 * g, 8 * g + 8)
        found = {}
        for t in range(tiles):
            last_e = min(((t + 1) * LANES - 1) // per_device, pairs - 1)
            for e in range(t * LANES // per_device, last_e + 1):
                if (e, 0) in found:
                    continue
                part, n = sources[e]
                for v in range(tiles):
                    at = slice(v * LANES, (v + 1) * LANES)
                    uv = u_ref[group, at]
                    x = cs_ref[choices[e][0], e // 2, group, at]
                    for m in range(1, 4):
                        x = jnp.where(uv == m, cs_ref[choices[e][m], e // 2, group, at], x)
                    x = x + (part[n, group, at] + ls_refs[g][v, 8 * e : 8 * e + 8, :])
                    out_ref[e, group, at] = x
                    tops[0] = jnp.maximum(tops[0], jnp.abs(x))
                    found[e, v] = x
            for q in range(dests):
                acc = None
                for first, e, v, shift in pieces_of[q, t]:
                    x = pltpu.roll(found[e, v], shift, axis=1) if shift else found[e, v]
                    acc = x if acc is None else jnp.where(lane >= first, x, acc)
                start = t * per_device + 8 * g
                pay_ref[q, start : start + 8, :] = acc
                if q % 8 == 7:
                    yield

    others = [gathered(), cycle()] + [payload(g) for g in range(groups)]
    for g, other in enumerate(others):
        for a in range(8):
            if g < groups:
                ladder(g, a)
            next(other, None)
        for _ in other:
            pass
    most = jnp.max(jnp.max(tops[0], axis=0, keepdims=True), axis=1, keepdims=True)
    k = jnp.floor(TOP_EXPONENT - jnp.log2(jnp.maximum(most, 1e-30)))
    scale = jnp.exp2(k)
    row = lax.broadcasted_iota(jnp.int32, pay_ref.shape[1:], 0)
    for q in range(dests):
        z = pay_ref[q] * scale
        z2 = z * z
        z4 = z2 * z2
        y = jnp.where(row >= tiles * per_device, k, z4 * z4 * z)
        send_ref[q] = y.astype(jnp.bfloat16)


def join_kernel(occ_ref, u_ref, half_ref, recv_ref, out_ref, dec_ref, mir_ref, res_ref, sems):
    occupied = occ_ref.shape[0]
    per_device, virtuals = u_ref.shape
    labels, copies = labels_and_copies(occ_ref, occupied)
    spread = 2 * per_device
    ready = set()

    def decode(t):
        ready.add(t)
        start = t * per_device
        low, high = start // 16 * 16, (start + per_device + 15) // 16 * 16
        end = virtuals // LANES * per_device
        for p in range(recv_ref.shape[0]):
            tail = recv_ref[p, end // 16 * 16 : end // 16 * 16 + 16, :]
            k = tail.astype(jnp.float32)[end % 16 : end % 16 + 1, 0:1]
            y = recv_ref[p, low:high, :].astype(jnp.float32)
            y = y[start - low : start - low + per_device]
            size = jnp.log2(jnp.maximum(jnp.abs(y), 2.0**-126)) * (1.0 / POWER) - k
            size = jnp.exp2(size)
            x = jnp.where(y < 0, -size, jnp.where(y > 0, size, 0.0))
            dec_ref[p * per_device : (p + 1) * per_device, :] = x
        mir_ref[t * LANES : (t + 1) * LANES, :] = dec_ref[...].T

    stores = []
    for j in range(occupied):
        for t in range(j * spread // LANES, ((j + 1) * spread - 1) // LANES + 1):
            if t not in ready:
                decode(t)
        u = u_ref[...]
        for i in range(occupied):
            at = pl.ds(pl.multiple_of((2 * j + copies[i]) * per_device, 8), per_device)
            total = half_ref[2 * i + copies[j]] + mir_ref[at, :]
            n = j * occupied + i
            res_ref[n] = jnp.where(u == (labels[j] ^ labels[i]), total, 0.0)
            store = pltpu.make_async_copy(res_ref.at[n], out_ref.at[i, j], sems.at[n])
            store.start()
            stores.append(store)
    for store in stores:
        store.wait()


def permute(x, flip, size):
    return lax.ppermute(x, "vir", [(n, n ^ flip) for n in range(size)])


def body(dests, amps, fock_vir, fock_occ, ladder_ints, cycle_ints, occ_irrep, vir_irrep):
    occupied, _, per_device, virtuals = amps.shape
    pairs = 2 * occupied
    tiles = virtuals // LANES
    rows = occupied * per_device
    kw = ladder_ints.shape[2]
    f32, bf16 = jnp.float32, jnp.bfloat16
    position = lax.axis_index("vir").astype(jnp.int32)
    pos = position.reshape(1)
    vir_local = lax.dynamic_slice_in_dim(vir_irrep, position * per_device, per_device)
    u = jnp.bitwise_xor(vir_local[:, None], vir_irrep[None, :])
    smem = pl.BlockSpec(memory_space=pltpu.SMEM)

    def whole(shape):
        return pl.BlockSpec(shape, lambda n: (0,) * len(shape))

    def cost(flops, size):
        return pl.CostEstimate(flops=flops, bytes_accessed=size, transcendentals=0)

    anywhere = pl.BlockSpec(memory_space=pl.ANY)
    quarter = dests // 4
    block_rows = rows + 16
    block = pl.pallas_call(
        prep_kernel,
        grid=(1,),
        out_shape=jax.ShapeDtypeStruct((block_rows, LANES), bf16),
        in_specs=[
            whole((rows, LANES)),
            pl.BlockSpec((occupied, occupied, 16, LANES), lambda n: (0, 0, 0, 0)),
        ],
        out_specs=whole((block_rows, LANES)),
        compiler_params=params(60),
        cost_estimate=cost(0, 500000),
    )(cycle_ints.reshape(rows, LANES), amps)
    block = block.reshape(1, block_rows, LANES)
    vmem = pl.BlockSpec(memory_space=pltpu.VMEM)
    mix = pl.pallas_call(
        mix_kernel,
        out_shape=jax.ShapeDtypeStruct((rows, rows), bf16),
        in_specs=[vmem],
        out_specs=vmem,
        compiler_params=params(4),
        cost_estimate=cost(10**7, 300000),
    )(fock_occ)

    flat_amps = amps.reshape(occupied, rows, virtuals)
    parts = (6, 2)
    wide = 2

    def fock_part(n, after):
        first, count = sum(parts[:n]), parts[n]
        return pl.pallas_call(
            functools.partial(fock_kernel, first),
            grid=(count // wide,),
            out_shape=(
                jax.ShapeDtypeStruct((2 * count, per_device, virtuals), f32),
                jax.ShapeDtypeStruct((count, per_device, LANES), bf16),
            ),
            in_specs=[
                smem,
                pl.BlockSpec((wide, rows, virtuals), lambda i: (i + first // wide, 0, 0)),
                whole(fock_vir.shape),
                whole(mix.shape),
                whole(u.shape),
                anywhere,
            ],
            out_specs=(
                pl.BlockSpec((2 * wide, per_device, virtuals), lambda i: (i, 0, 0)),
                pl.BlockSpec((wide, per_device, LANES), lambda i: (i, 0, 0)),
            ),
            scratch_shapes=[pltpu.VMEM((occupied, per_device, virtuals), f32)],
            compiler_params=params(12),
            cost_estimate=cost(3 * count * rows * virtuals * virtuals, 2 * 10**6),
        )(occ_irrep, flat_amps, fock_vir, mix, u, after)

    z1, z2, z3 = [permute(block, m << 2, dests) for m in range(1, quarter)]
    column = stack([block, z1, z2, z3], mix)
    column_y = permute(column, 2, dests)
    half0, cyc0 = fock_part(0, column)
    own_blocks = stack([column, column_y], half0)
    mate_blocks = permute(own_blocks, 1, dests)
    half1, cyc1 = fock_part(1, own_blocks)

    send_rows = tiles * per_device + 8
    groups = per_device // 8
    half, send = pl.pallas_call(
        functools.partial(half_kernel, groups, parts),
        out_shape=(
            jax.ShapeDtypeStruct((pairs, per_device, virtuals), f32),
            jax.ShapeDtypeStruct((dests, send_rows, LANES), bf16),
        ),
        in_specs=[smem, smem] + [vmem] * (4 + 2 * len(parts)),
        out_specs=(vmem, vmem),
        scratch_shapes=[
            pltpu.SMEM((occupied,), jnp.int32),
            pltpu.VMEM((occupied * occupied, LANES), f32),
            pltpu.VMEM((virtuals, occupied, LANES), f32),
            pltpu.VMEM((occupied, occupied, per_device, virtuals), f32),
            pltpu.VMEM((dests, send_rows, LANES), f32),
        ]
        + [pltpu.VMEM((tiles, 8 * pairs, LANES), f32)] * groups,
        compiler_params=params(28),
        cost_estimate=cost(6 * occupied * rows * virtuals * LANES, 15 * 10**6),
    )(
        pos, occ_irrep, own_blocks, mate_blocks, half0, half1, cyc0, cyc1, u, ladder_ints,
    )

    recv = lax.all_to_all(send, "vir", split_axis=0, concat_axis=0, tiled=True)

    return pl.pallas_call(
        join_kernel,
        out_shape=jax.ShapeDtypeStruct((occupied, occupied, per_device, virtuals), f32),
        in_specs=[smem, vmem, vmem, vmem],
        out_specs=anywhere,
        scratch_shapes=[
            pltpu.VMEM((virtuals, LANES), f32),
            pltpu.VMEM((tiles * LANES, virtuals), f32),
            pltpu.VMEM((occupied * occupied, per_device, virtuals), f32),
            pltpu.SemaphoreType.DMA((occupied * occupied,)),
        ],
        compiler_params=params(16),
        cost_estimate=cost(10**6, 5 * 10**6),
    )(occ_irrep, u, half, recv)


def solution(mesh):
    dests = mesh.shape["vir"]

    def run(amps, *rest):
        occupied, _, per_device, virtuals = amps.shape
        tiled = (
            dests == 16
            and per_device % 8 == 0
            and virtuals % LANES == 0
            and 2 * occupied * per_device == virtuals
            and rest[2].shape[2] == LANES
            and rest[3].shape[2] == LANES
        )
        return body(dests, amps, *rest) if tiled else plain_body(amps, *rest)

    return jax.shard_map(
        run,
        mesh=mesh,
        in_specs=(
            P("groups", None, "vir", None),
            P("groups", None),
            P("groups", None),
            P("vir", "groups", None),
            P("vir", "groups", None),
            P("groups"),
            P("groups"),
        ),
        out_specs=P("groups", None, "vir", None),
        check_vma=False,
    )
```

```python
import functools

import jax
import jax.numpy as jnp
from jax import lax
from jax.experimental import pallas as pl
from jax.experimental.pallas import tpu as pltpu
from jax.sharding import PartitionSpec as P

DW = 8
CW = 16
LANES = 128
POWER = 9
TOP_EXPONENT = 13


def contract_last(left_side, right_side):
    return lax.dot_general(
        left_side, right_side, (((1,), (1,)), ((), ())), preferred_element_type=jnp.float32
    )


def plain_body(amps, fock_vir, fock_occ, ladder_ints, cycle_ints, occ_irrep, vir_irrep):
    occupied = amps.shape[0]
    per_device = amps.shape[2]
    virtuals = amps.shape[3]
    pair_count = occupied * occupied
    position = lax.axis_index("vir")
    fock_term = jnp.dot(
        amps.reshape(pair_count * per_device, virtuals),
        fock_vir,
        preferred_element_type=jnp.float32,
    ).reshape(occupied, occupied, per_device, virtuals)
    occ_term = jnp.einsum("ikab,kj->ijab", amps, fock_occ, preferred_element_type=jnp.float32)
    flat_ints = ladder_ints.reshape(per_device * virtuals, ladder_ints.shape[2])
    local_window = amps[:, :, 0:1, :DW]
    local_cycle = amps[:, :, :, :CW]
    segment = lax.all_gather(local_window, "vir", axis=2, tiled=True)
    width = segment.shape[2] * DW
    ladder = contract_last(segment.reshape(pair_count, width), flat_ints)
    left_side = jnp.transpose(local_cycle, (0, 2, 1, 3)).reshape(
        occupied * per_device, occupied * CW
    )
    segment = lax.all_gather(cycle_ints, "vir", axis=0, tiled=True)
    right_side = segment.reshape(segment.shape[0] * occupied, occupied * CW)
    cycle_block = contract_last(left_side, right_side).reshape(
        occupied, per_device, segment.shape[0], occupied
    )
    cycle_part = jnp.transpose(cycle_block, (0, 3, 1, 2))
    half_sum = (
        fock_term - occ_term + ladder.reshape(occupied, occupied, per_device, virtuals) + cycle_part
    )
    vir_local = lax.dynamic_slice_in_dim(vir_irrep, position * per_device, per_device)
    occ_pair = jnp.bitwise_xor(occ_irrep[:, None], occ_irrep[None, :])
    vir_pair = jnp.bitwise_xor(vir_local[:, None], vir_irrep[None, :])
    received = lax.all_to_all(half_sum, "vir", split_axis=3, concat_axis=2, tiled=True)
    mirrored = jnp.transpose(received, (1, 0, 3, 2))
    product_irrep = jnp.bitwise_xor(occ_pair[:, :, None, None], vir_pair[None, None, :, :])
    allowed = jnp.where(product_irrep == 0, jnp.float32(1.0), jnp.float32(0.0))
    return allowed * (half_sum + mirrored)


def params(mib):
    return pltpu.CompilerParams(vmem_limit_bytes=mib * 2**20)


def labels_and_copies(occ_ref, occupied):
    labels = [occ_ref[j] for j in range(occupied)]
    copies = []
    for j in range(occupied):
        s = jnp.int32(0)
        for k in range(j):
            s = s + (labels[k] == labels[j]).astype(jnp.int32)
        copies.append(s)
    return labels, copies


def prep_kernel(cyc_ref, amps_ref, block_ref):
    occupied = amps_ref.shape[0]
    rows = cyc_ref.shape[0]
    block_ref[:rows, :] = cyc_ref[...]
    lane = lax.broadcasted_iota(jnp.int32, (occupied, LANES), 1)
    packed = jnp.zeros((occupied, LANES), jnp.float32)
    for j in range(occupied):
        w = jnp.where(lane < DW, amps_ref[:, j, 0, :].astype(jnp.float32), 0.0)
        packed = packed + (pltpu.roll(w, j * DW, axis=1) if j else w)
    packed = jnp.concatenate([packed, jnp.zeros_like(packed)], axis=0)
    block_ref[rows:, :] = packed.astype(jnp.bfloat16)


def mix_kernel(occ_vals_ref, fock_ref, mix_ref, fock_out_ref):
    fock_out_ref[...] = fock_ref[...]
    rows = mix_ref.shape[0]
    occupied = occ_vals_ref.shape[0]
    per_device = rows // occupied
    row = lax.broadcasted_iota(jnp.int32, (rows, occupied), 0)
    start = lax.broadcasted_iota(jnp.int32, (rows, occupied), 1) * per_device
    in_block = jnp.logical_and(row >= start, row < start + per_device).astype(jnp.bfloat16)
    row = lax.broadcasted_iota(jnp.int32, (rows, per_device), 0)
    at = lax.broadcasted_iota(jnp.int32, (rows, per_device), 1)
    same = row == at
    for n in range(1, occupied):
        same = jnp.logical_or(same, row == at + n * per_device)
    same = same.astype(jnp.bfloat16)
    left = contract_last(in_block, occ_vals_ref[...]).astype(jnp.bfloat16)
    mix = contract_last(left, in_block) * contract_last(same, same)
    mix_ref[...] = mix.astype(jnp.bfloat16)


def fock_kernel(first, occ_ref, amps_ref, fock_ref, mix_ref, u_ref, after_ref, half_ref, cyc_ref, hs_ref):
    wide, rows, virtuals = amps_ref.shape
    _, per_device, _ = half_ref.shape
    occupied = occ_ref.shape[0]
    labels, copies = labels_and_copies(occ_ref, occupied)
    u = u_ref[...]
    h = jnp.dot(
        amps_ref[...].reshape(wide * rows, virtuals),
        fock_ref[...],
        preferred_element_type=jnp.float32,
    )
    for w in range(wide):
        a = amps_ref[w]
        mixed = jnp.dot(mix_ref[...], a, preferred_element_type=jnp.float32)
        hs_ref[...] = (h[w * rows : (w + 1) * rows] - mixed).reshape(hs_ref.shape)
        own = occ_ref[pl.program_id(0) * wide + w + first]
        for j in range(occupied):
            at = 2 * w + copies[j]
            half_ref[at] = jnp.where(u == (own ^ labels[j]), hs_ref[j], half_ref[at])
        head = a[:, :LANES].astype(jnp.float32)
        lane = lax.broadcasted_iota(jnp.int32, (per_device, LANES), 1)
        acc = jnp.zeros((per_device, LANES), jnp.float32)
        for k in range(occupied):
            piece = jnp.where(lane < CW, head[k * per_device : (k + 1) * per_device], 0.0)
            acc = acc + (pltpu.roll(piece, k * CW, axis=1) if k else piece)
        cyc_ref[w] = acc.astype(jnp.bfloat16)


def stack(blocks, after):
    count = len(blocks)

    def kernel(*refs):
        out = refs[count + 1]
        at = 0
        for n in range(count):
            head = blocks[n].shape[0]
            out[at : at + head] = refs[n][...]
            at += head

    vmem = pl.BlockSpec(memory_space=pltpu.VMEM)
    shape = (sum(b.shape[0] for b in blocks),) + blocks[0].shape[1:]
    return pl.pallas_call(
        kernel,
        out_shape=jax.ShapeDtypeStruct(shape, blocks[0].dtype),
        in_specs=[vmem] * count + [pl.BlockSpec(memory_space=pl.ANY)],
        out_specs=vmem,
        compiler_params=params(4),
        cost_estimate=pl.CostEstimate(flops=0, bytes_accessed=10**6, transcendentals=0),
    )(*blocks, after)


def payload_pieces(per_device, pairs, dests):
    out = {}
    for q in range(dests):
        for e in range(pairs):
            start = 0
            while start < per_device:
                src = q * per_device + start
                dst = e * per_device + start
                length = min(LANES - src % LANES, LANES - dst % LANES, per_device - start)
                out.setdefault((q, dst // LANES), []).append(
                    (dst % LANES, e, src // LANES, (dst - src) % LANES)
                )
                start += length
    return out


def half_kernel(groups, parts, pos_ref, occ_ref, own_ref, mate_ref, *refs):
    halves, refs = refs[: len(parts)], refs[len(parts) :]
    cycs, refs = refs[: len(parts)], refs[len(parts) :]
    u_ref, lad_ref, out_ref, send_ref, orb_ref, w2_ref, xs_ref, cs_ref, pay_ref = refs[:9]
    ls_refs = refs[9:]
    occupied = occ_ref.shape[0]
    pairs, per_device, virtuals = out_ref.shape
    dests = pay_ref.shape[0]
    tiles = virtuals // LANES
    rows = occupied * per_device
    labels, copies = labels_and_copies(occ_ref, occupied)
    lane = lax.broadcasted_iota(jnp.int32, (8, LANES), 1)

    def block_of(r):
        ref = mate_ref if r & 1 else own_ref
        return ref[((r >> 1) & 1) * (dests // 4) + (r >> 2)]

    packed = [block_of(r)[rows:].astype(jnp.float32)[:8] for r in range(dests)]
    for j in range(occupied):
        orb_ref[2 * labels[j] + copies[j]] = jnp.int32(j)
        window = jnp.zeros((8, LANES), jnp.float32)
        for r in range(dests):
            w = jnp.where(jnp.logical_and(lane >= j * DW, lane < (j + 1) * DW), packed[r], 0.0)
            shift = lax.rem((pos_ref[0] ^ r) * DW - j * DW + LANES, LANES)
            window = window + pltpu.roll(w, shift, axis=1)
        for i in range(occupied):
            row = (labels[i] ^ labels[j]) * pairs + 2 * i + copies[j]
            w2_ref[pl.ds(row, 1), :] = window[i : i + 1, :]
    w2 = w2_ref[...].astype(jnp.bfloat16)
    left = jnp.concatenate([ref[...].astype(jnp.float32) for ref in cycs], axis=0)
    left = left.reshape(rows, LANES).astype(jnp.bfloat16)
    choices = [
        [orb_ref[2 * (labels[e // 2] ^ n) + e % 2] for n in range(4)] for e in range(pairs)
    ]
    sources = [(part, n) for part in halves for n in range(part.shape[0])]
    pieces_of = payload_pieces(per_device, pairs, dests)
    tops = [jnp.zeros((8, LANES), jnp.float32)]

    def ladder(g, a):
        product = contract_last(w2, lad_ref[8 * g + a])
        ua = u_ref[8 * g + a : 8 * g + a + 1, :]
        sel = product[0:pairs]
        for v in range(1, 4):
            sel = jnp.where(ua == v, product[v * pairs : (v + 1) * pairs], sel)
        for v in range(tiles):
            ls_refs[g][v, pl.ds(a, pairs, stride=8), :] = sel[:, v * LANES : (v + 1) * LANES]

    def gathered():
        for r in range(dests):
            x = block_of(r)[:rows].astype(jnp.float32).reshape(per_device, occupied, LANES)
            xs_ref[pl.ds((pos_ref[0] ^ r) * per_device, per_device)] = x
            if r % 2:
                yield

    def cycle():
        for j in range(occupied):
            c = contract_last(left, xs_ref[:, j, :].astype(jnp.bfloat16))
            cs_ref[j] = c.reshape(occupied, per_device, virtuals)
            yield

    def payload(g):
        group = slice(8 * g, 8 * g + 8)
        found = {}
        for t in range(tiles):
            last_e = min(((t + 1) * LANES - 1) // per_device, pairs - 1)
            for e in range(t * LANES // per_device, last_e + 1):
                if (e, 0) in found:
                    continue
                part, n = sources[e]
                for v in range(tiles):
                    at = slice(v * LANES, (v + 1) * LANES)
                    uv = u_ref[group, at]
                    x = cs_ref[choices[e][0], e // 2, group, at]
                    for m in range(1, 4):
                        x = jnp.where(uv == m, cs_ref[choices[e][m], e // 2, group, at], x)
                    x = x + (part[n, group, at] + ls_refs[g][v, 8 * e : 8 * e + 8, :])
                    out_ref[e, group, at] = x
                    tops[0] = jnp.maximum(tops[0], jnp.abs(x))
                    found[e, v] = x
            for q in range(dests):
                acc = None
                for first, e, v, shift in pieces_of[q, t]:
                    x = pltpu.roll(found[e, v], shift, axis=1) if shift else found[e, v]
                    acc = x if acc is None else jnp.where(lane >= first, x, acc)
                start = t * per_device + 8 * g
                pay_ref[q, start : start + 8, :] = acc
                if q % 8 == 7:
                    yield

    others = [gathered(), cycle()] + [payload(g) for g in range(groups)]
    for g, other in enumerate(others):
        for a in range(8):
            if g < groups:
                ladder(g, a)
            next(other, None)
        for _ in other:
            pass
    most = jnp.max(jnp.max(tops[0], axis=0, keepdims=True), axis=1, keepdims=True)
    k = jnp.floor(TOP_EXPONENT - jnp.log2(jnp.maximum(most, 1e-30)))
    scale = jnp.exp2(k)
    row = lax.broadcasted_iota(jnp.int32, pay_ref.shape[1:], 0)
    for q in range(dests):
        z = pay_ref[q] * scale
        z2 = z * z
        z4 = z2 * z2
        y = jnp.where(row >= tiles * per_device, k, z4 * z4 * z)
        send_ref[q] = y.astype(jnp.bfloat16)


def join_kernel(occ_ref, u_ref, half_ref, recv_ref, out_ref, dec_ref, mir_ref, res_ref, sems):
    occupied = occ_ref.shape[0]
    per_device, virtuals = u_ref.shape
    labels, copies = labels_and_copies(occ_ref, occupied)
    spread = 2 * per_device
    ready = set()

    def decode(t):
        ready.add(t)
        start = t * per_device
        low, high = start // 16 * 16, (start + per_device + 15) // 16 * 16
        end = virtuals // LANES * per_device
        for p in range(recv_ref.shape[0]):
            tail = recv_ref[p, end // 16 * 16 : end // 16 * 16 + 16, :]
            k = tail.astype(jnp.float32)[end % 16 : end % 16 + 1, 0:1]
            y = recv_ref[p, low:high, :].astype(jnp.float32)
            y = y[start - low : start - low + per_device]
            size = jnp.log2(jnp.maximum(jnp.abs(y), 2.0**-126)) * (1.0 / POWER) - k
            size = jnp.exp2(size)
            x = jnp.where(y < 0, -size, jnp.where(y > 0, size, 0.0))
            dec_ref[p * per_device : (p + 1) * per_device, :] = x
        mir_ref[t * LANES : (t + 1) * LANES, :] = dec_ref[...].T

    stores = []
    for j in range(occupied):
        for t in range(j * spread // LANES, ((j + 1) * spread - 1) // LANES + 1):
            if t not in ready:
                decode(t)
        u = u_ref[...]
        for i in range(occupied):
            at = pl.ds(pl.multiple_of((2 * j + copies[i]) * per_device, 8), per_device)
            total = half_ref[2 * i + copies[j]] + mir_ref[at, :]
            n = j * occupied + i
            res_ref[n] = jnp.where(u == (labels[j] ^ labels[i]), total, 0.0)
            store = pltpu.make_async_copy(res_ref.at[n], out_ref.at[i, j], sems.at[n])
            store.start()
            stores.append(store)
    for store in stores:
        store.wait()


def permute(x, flip, size):
    return lax.ppermute(x, "vir", [(n, n ^ flip) for n in range(size)])


def body(dests, amps, fock_vir, fock_occ, ladder_ints, cycle_ints, occ_irrep, vir_irrep):
    occupied, _, per_device, virtuals = amps.shape
    pairs = 2 * occupied
    tiles = virtuals // LANES
    rows = occupied * per_device
    kw = ladder_ints.shape[2]
    f32, bf16 = jnp.float32, jnp.bfloat16
    position = lax.axis_index("vir").astype(jnp.int32)
    pos = position.reshape(1)
    vir_local = lax.dynamic_slice_in_dim(vir_irrep, position * per_device, per_device)
    u = jnp.bitwise_xor(vir_local[:, None], vir_irrep[None, :])
    smem = pl.BlockSpec(memory_space=pltpu.SMEM)

    def whole(shape):
        return pl.BlockSpec(shape, lambda n: (0,) * len(shape))

    def cost(flops, size):
        return pl.CostEstimate(flops=flops, bytes_accessed=size, transcendentals=0)

    anywhere = pl.BlockSpec(memory_space=pl.ANY)
    quarter = dests // 4
    block_rows = rows + 16
    block = pl.pallas_call(
        prep_kernel,
        grid=(1,),
        out_shape=jax.ShapeDtypeStruct((block_rows, LANES), bf16),
        in_specs=[
            whole((rows, LANES)),
            pl.BlockSpec((occupied, occupied, 16, LANES), lambda n: (0, 0, 0, 0)),
        ],
        out_specs=whole((block_rows, LANES)),
        compiler_params=params(60),
        cost_estimate=cost(0, 500000),
    )(cycle_ints.reshape(rows, LANES), amps)
    block = block.reshape(1, block_rows, LANES)
    vmem = pl.BlockSpec(memory_space=pltpu.VMEM)
    mix, fock = pl.pallas_call(
        mix_kernel,
        out_shape=(
            jax.ShapeDtypeStruct((rows, rows), bf16),
            jax.ShapeDtypeStruct(fock_vir.shape, bf16),
        ),
        in_specs=[vmem, vmem],
        out_specs=(vmem, vmem),
        compiler_params=params(6),
        cost_estimate=cost(10**7, 2 * 10**6),
    )(fock_occ, fock_vir)

    flat_amps = amps.reshape(occupied, rows, virtuals)
    parts = (6, 2)
    wide = 2

    def fock_part(n, after):
        first, count = sum(parts[:n]), parts[n]
        return pl.pallas_call(
            functools.partial(fock_kernel, first),
            grid=(count // wide,),
            out_shape=(
                jax.ShapeDtypeStruct((2 * count, per_device, virtuals), f32),
                jax.ShapeDtypeStruct((count, per_device, LANES), bf16),
            ),
            in_specs=[
                smem,
                pl.BlockSpec((wide, rows, virtuals), lambda i: (i + first // wide, 0, 0)),
                whole(fock_vir.shape),
                whole(mix.shape),
                whole(u.shape),
                anywhere,
            ],
            out_specs=(
                pl.BlockSpec((2 * wide, per_device, virtuals), lambda i: (i, 0, 0)),
                pl.BlockSpec((wide, per_device, LANES), lambda i: (i, 0, 0)),
            ),
            scratch_shapes=[pltpu.VMEM((occupied, per_device, virtuals), f32)],
            compiler_params=params(12),
            cost_estimate=cost(3 * count * rows * virtuals * virtuals, 2 * 10**6),
        )(occ_irrep, flat_amps, fock, mix, u, after)

    z1, z2, z3 = [permute(block, m << 2, dests) for m in range(1, quarter)]
    block_y = permute(block, 2, dests)
    column = stack([z1, z2, z3], mix)
    column_y = permute(column, 2, dests)
    half0, cyc0 = fock_part(0, column)
    own_blocks = stack([block, column, block_y, column_y], half0)
    mate_blocks = permute(own_blocks, 1, dests)
    half1, cyc1 = fock_part(1, own_blocks)

    send_rows = tiles * per_device + 8
    groups = per_device // 8
    half, send = pl.pallas_call(
        functools.partial(half_kernel, groups, parts),
        out_shape=(
            jax.ShapeDtypeStruct((pairs, per_device, virtuals), f32),
            jax.ShapeDtypeStruct((dests, send_rows, LANES), bf16),
        ),
        in_specs=[smem, smem] + [vmem] * (4 + 2 * len(parts)),
        out_specs=(vmem, vmem),
        scratch_shapes=[
            pltpu.SMEM((occupied,), jnp.int32),
            pltpu.VMEM((occupied * occupied, LANES), f32),
            pltpu.VMEM((virtuals, occupied, LANES), f32),
            pltpu.VMEM((occupied, occupied, per_device, virtuals), f32),
            pltpu.VMEM((dests, send_rows, LANES), f32),
        ]
        + [pltpu.VMEM((tiles, 8 * pairs, LANES), f32)] * groups,
        compiler_params=params(28),
        cost_estimate=cost(6 * occupied * rows * virtuals * LANES, 15 * 10**6),
    )(
        pos, occ_irrep, own_blocks, mate_blocks, half0, half1, cyc0, cyc1, u, ladder_ints,
    )

    recv = lax.all_to_all(send, "vir", split_axis=0, concat_axis=0, tiled=True)

    return pl.pallas_call(
        join_kernel,
        out_shape=jax.ShapeDtypeStruct((occupied, occupied, per_device, virtuals), f32),
        in_specs=[smem, vmem, vmem, vmem],
        out_specs=anywhere,
        scratch_shapes=[
            pltpu.VMEM((virtuals, LANES), f32),
            pltpu.VMEM((tiles * LANES, virtuals), f32),
            pltpu.VMEM((occupied * occupied, per_device, virtuals), f32),
            pltpu.SemaphoreType.DMA((occupied * occupied,)),
        ],
        compiler_params=params(16),
        cost_estimate=cost(10**6, 5 * 10**6),
    )(occ_irrep, u, half, recv)


def solution(mesh):
    dests = mesh.shape["vir"]

    def run(amps, *rest):
        occupied, _, per_device, virtuals = amps.shape
        tiled = (
            dests == 16
            and per_device % 8 == 0
            and virtuals % LANES == 0
            and 2 * occupied * per_device == virtuals
            and rest[2].shape[2] == LANES
            and rest[3].shape[2] == LANES
        )
        return body(dests, amps, *rest) if tiled else plain_body(amps, *rest)

    return jax.shard_map(
        run,
        mesh=mesh,
        in_specs=(
            P("groups", None, "vir", None),
            P("groups", None),
            P("groups", None),
            P("vir", "groups", None),
            P("vir", "groups", None),
            P("groups"),
            P("groups"),
        ),
        out_specs=P("groups", None, "vir", None),
        check_vma=False,
    )
```

```python
import functools

import jax
import jax.numpy as jnp
from jax import lax
from jax.experimental import pallas as pl
from jax.experimental.pallas import tpu as pltpu
from jax.sharding import PartitionSpec as P

DW = 8
CW = 16
LANES = 128
POWER = 9
TOP_EXPONENT = 13


def contract_last(left_side, right_side):
    return lax.dot_general(
        left_side, right_side, (((1,), (1,)), ((), ())), preferred_element_type=jnp.float32
    )


def plain_body(amps, fock_vir, fock_occ, ladder_ints, cycle_ints, occ_irrep, vir_irrep):
    occupied = amps.shape[0]
    per_device = amps.shape[2]
    virtuals = amps.shape[3]
    pair_count = occupied * occupied
    position = lax.axis_index("vir")
    fock_term = jnp.dot(
        amps.reshape(pair_count * per_device, virtuals),
        fock_vir,
        preferred_element_type=jnp.float32,
    ).reshape(occupied, occupied, per_device, virtuals)
    occ_term = jnp.einsum("ikab,kj->ijab", amps, fock_occ, preferred_element_type=jnp.float32)
    flat_ints = ladder_ints.reshape(per_device * virtuals, ladder_ints.shape[2])
    local_window = amps[:, :, 0:1, :DW]
    local_cycle = amps[:, :, :, :CW]
    segment = lax.all_gather(local_window, "vir", axis=2, tiled=True)
    width = segment.shape[2] * DW
    ladder = contract_last(segment.reshape(pair_count, width), flat_ints)
    left_side = jnp.transpose(local_cycle, (0, 2, 1, 3)).reshape(
        occupied * per_device, occupied * CW
    )
    segment = lax.all_gather(cycle_ints, "vir", axis=0, tiled=True)
    right_side = segment.reshape(segment.shape[0] * occupied, occupied * CW)
    cycle_block = contract_last(left_side, right_side).reshape(
        occupied, per_device, segment.shape[0], occupied
    )
    cycle_part = jnp.transpose(cycle_block, (0, 3, 1, 2))
    half_sum = (
        fock_term - occ_term + ladder.reshape(occupied, occupied, per_device, virtuals) + cycle_part
    )
    vir_local = lax.dynamic_slice_in_dim(vir_irrep, position * per_device, per_device)
    occ_pair = jnp.bitwise_xor(occ_irrep[:, None], occ_irrep[None, :])
    vir_pair = jnp.bitwise_xor(vir_local[:, None], vir_irrep[None, :])
    received = lax.all_to_all(half_sum, "vir", split_axis=3, concat_axis=2, tiled=True)
    mirrored = jnp.transpose(received, (1, 0, 3, 2))
    product_irrep = jnp.bitwise_xor(occ_pair[:, :, None, None], vir_pair[None, None, :, :])
    allowed = jnp.where(product_irrep == 0, jnp.float32(1.0), jnp.float32(0.0))
    return allowed * (half_sum + mirrored)


def params(mib):
    return pltpu.CompilerParams(vmem_limit_bytes=mib * 2**20)


def labels_and_copies(occ_ref, occupied):
    labels = [occ_ref[j] for j in range(occupied)]
    copies = []
    for j in range(occupied):
        s = jnp.int32(0)
        for k in range(j):
            s = s + (labels[k] == labels[j]).astype(jnp.int32)
        copies.append(s)
    return labels, copies


def prep_kernel(cyc_ref, amps_ref, block_ref):
    occupied = amps_ref.shape[0]
    rows = cyc_ref.shape[0]
    block_ref[:rows, :] = cyc_ref[...]
    lane = lax.broadcasted_iota(jnp.int32, (occupied, LANES), 1)
    packed = jnp.zeros((occupied, LANES), jnp.float32)
    for j in range(occupied):
        w = jnp.where(lane < DW, amps_ref[:, j, 0, :].astype(jnp.float32), 0.0)
        packed = packed + (pltpu.roll(w, j * DW, axis=1) if j else w)
    packed = jnp.concatenate([packed, jnp.zeros_like(packed)], axis=0)
    block_ref[rows:, :] = packed.astype(jnp.bfloat16)


def mix_kernel(occ_vals_ref, fock_ref, mix_ref, fock_out_ref):
    fock_out_ref[...] = fock_ref[...]
    rows = mix_ref.shape[0]
    occupied = occ_vals_ref.shape[0]
    per_device = rows // occupied
    row = lax.broadcasted_iota(jnp.int32, (rows, occupied), 0)
    start = lax.broadcasted_iota(jnp.int32, (rows, occupied), 1) * per_device
    in_block = jnp.logical_and(row >= start, row < start + per_device).astype(jnp.bfloat16)
    row = lax.broadcasted_iota(jnp.int32, (rows, per_device), 0)
    at = lax.broadcasted_iota(jnp.int32, (rows, per_device), 1)
    same = row == at
    for n in range(1, occupied):
        same = jnp.logical_or(same, row == at + n * per_device)
    same = same.astype(jnp.bfloat16)
    left = contract_last(in_block, occ_vals_ref[...]).astype(jnp.bfloat16)
    mix = contract_last(left, in_block) * contract_last(same, same)
    mix_ref[...] = mix.astype(jnp.bfloat16)


def fock_kernel(first, occ_ref, amps_ref, fock_ref, mix_ref, u_ref, after_ref, half_ref, cyc_ref, hs_ref):
    wide, rows, virtuals = amps_ref.shape
    _, per_device, _ = half_ref.shape
    occupied = occ_ref.shape[0]
    labels, copies = labels_and_copies(occ_ref, occupied)
    u = u_ref[...]
    h = jnp.dot(
        amps_ref[...].reshape(wide * rows, virtuals),
        fock_ref[...],
        preferred_element_type=jnp.float32,
    )
    for w in range(wide):
        a = amps_ref[w]
        mixed = jnp.dot(mix_ref[...], a, preferred_element_type=jnp.float32)
        hs_ref[...] = (h[w * rows : (w + 1) * rows] - mixed).reshape(hs_ref.shape)
        own = occ_ref[pl.program_id(0) * wide + w + first]
        for j in range(occupied):
            at = 2 * w + copies[j]
            half_ref[at] = jnp.where(u == (own ^ labels[j]), hs_ref[j], half_ref[at])
        head = a[:, :LANES].astype(jnp.float32)
        lane = lax.broadcasted_iota(jnp.int32, (per_device, LANES), 1)
        acc = jnp.zeros((per_device, LANES), jnp.float32)
        for k in range(occupied):
            piece = jnp.where(lane < CW, head[k * per_device : (k + 1) * per_device], 0.0)
            acc = acc + (pltpu.roll(piece, k * CW, axis=1) if k else piece)
        cyc_ref[w] = acc.astype(jnp.bfloat16)


def stack(blocks, after):
    count = len(blocks)

    def kernel(*refs):
        out = refs[count + 1]
        at = 0
        for n in range(count):
            head = blocks[n].shape[0]
            out[at : at + head] = refs[n][...]
            at += head

    vmem = pl.BlockSpec(memory_space=pltpu.VMEM)
    shape = (sum(b.shape[0] for b in blocks),) + blocks[0].shape[1:]
    return pl.pallas_call(
        kernel,
        out_shape=jax.ShapeDtypeStruct(shape, blocks[0].dtype),
        in_specs=[vmem] * count + [pl.BlockSpec(memory_space=pl.ANY)],
        out_specs=vmem,
        compiler_params=params(4),
        cost_estimate=pl.CostEstimate(flops=0, bytes_accessed=10**6, transcendentals=0),
    )(*blocks, after)


def payload_pieces(per_device, pairs, dests):
    out = {}
    for q in range(dests):
        for e in range(pairs):
            start = 0
            while start < per_device:
                src = q * per_device + start
                dst = e * per_device + start
                length = min(LANES - src % LANES, LANES - dst % LANES, per_device - start)
                out.setdefault((q, dst // LANES), []).append(
                    (dst % LANES, e, src // LANES, (dst - src) % LANES)
                )
                start += length
    return out


def half_kernel(groups, parts, pos_ref, occ_ref, own_ref, mate_ref, *refs):
    halves, refs = refs[: len(parts)], refs[len(parts) :]
    cycs, refs = refs[: len(parts)], refs[len(parts) :]
    u_ref, lad_ref, out_ref, send_ref, orb_ref, w2_ref, xs_ref, cs_ref, pay_ref = refs[:9]
    ls_refs = refs[9:]
    occupied = occ_ref.shape[0]
    pairs, per_device, virtuals = out_ref.shape
    dests = pay_ref.shape[0]
    tiles = virtuals // LANES
    rows = occupied * per_device
    labels, copies = labels_and_copies(occ_ref, occupied)
    lane = lax.broadcasted_iota(jnp.int32, (8, LANES), 1)

    def block_of(r):
        ref = mate_ref if r & 1 else own_ref
        return ref[((r >> 1) & 1) * (dests // 4) + (r >> 2)]

    packed = [block_of(r)[rows:].astype(jnp.float32)[:8] for r in range(dests)]
    for j in range(occupied):
        orb_ref[2 * labels[j] + copies[j]] = jnp.int32(j)
        window = jnp.zeros((8, LANES), jnp.float32)
        for r in range(dests):
            w = jnp.where(jnp.logical_and(lane >= j * DW, lane < (j + 1) * DW), packed[r], 0.0)
            shift = lax.rem((pos_ref[0] ^ r) * DW - j * DW + LANES, LANES)
            window = window + pltpu.roll(w, shift, axis=1)
        for i in range(occupied):
            row = (labels[i] ^ labels[j]) * pairs + 2 * i + copies[j]
            w2_ref[pl.ds(row, 1), :] = window[i : i + 1, :]
    w2 = w2_ref[...]
    zero = jnp.zeros_like(w2)
    w2 = jnp.concatenate(
        [jnp.concatenate([w2, zero], axis=1), jnp.concatenate([zero, w2], axis=1)], axis=0
    ).astype(jnp.bfloat16)
    left = jnp.concatenate([ref[...].astype(jnp.float32) for ref in cycs], axis=0)
    left = left.reshape(rows, LANES).astype(jnp.bfloat16)
    choices = [
        [orb_ref[2 * (labels[e // 2] ^ n) + e % 2] for n in range(4)] for e in range(pairs)
    ]
    sources = [(part, n) for part in halves for n in range(part.shape[0])]
    pieces_of = payload_pieces(per_device, pairs, dests)
    tops = [jnp.zeros((8, LANES), jnp.float32)]

    def ladder(g, a):
        first = 8 * g + a
        product = contract_last(w2, jnp.concatenate([lad_ref[first], lad_ref[first + 1]], axis=1))
        for n in range(2):
            ua = u_ref[first + n : first + n + 1, :]
            start = n * occupied * occupied
            sel = product[start : start + pairs]
            for v in range(1, 4):
                at = start + v * pairs
                sel = jnp.where(ua == v, product[at : at + pairs], sel)
            for v in range(tiles):
                to = pl.ds(a + n, pairs, stride=8)
                ls_refs[g][v, to, :] = sel[:, v * LANES : (v + 1) * LANES]

    def gathered():
        for r in range(dests):
            x = block_of(r)[:rows].astype(jnp.float32).reshape(per_device, occupied, LANES)
            xs_ref[pl.ds((pos_ref[0] ^ r) * per_device, per_device)] = x
            if r % 2:
                yield

    def cycle():
        for j in range(occupied):
            c = contract_last(left, xs_ref[:, j, :].astype(jnp.bfloat16))
            cs_ref[j] = c.reshape(occupied, per_device, virtuals)
            yield

    def payload(g):
        group = slice(8 * g, 8 * g + 8)
        found = {}
        for t in range(tiles):
            last_e = min(((t + 1) * LANES - 1) // per_device, pairs - 1)
            for e in range(t * LANES // per_device, last_e + 1):
                if (e, 0) in found:
                    continue
                part, n = sources[e]
                for v in range(tiles):
                    at = slice(v * LANES, (v + 1) * LANES)
                    uv = u_ref[group, at]
                    x = cs_ref[choices[e][0], e // 2, group, at]
                    for m in range(1, 4):
                        x = jnp.where(uv == m, cs_ref[choices[e][m], e // 2, group, at], x)
                    x = x + (part[n, group, at] + ls_refs[g][v, 8 * e : 8 * e + 8, :])
                    out_ref[e, group, at] = x
                    tops[0] = jnp.maximum(tops[0], jnp.abs(x))
                    found[e, v] = x
            for q in range(dests):
                acc = None
                for first, e, v, shift in pieces_of[q, t]:
                    x = pltpu.roll(found[e, v], shift, axis=1) if shift else found[e, v]
                    acc = x if acc is None else jnp.where(lane >= first, x, acc)
                start = t * per_device + 8 * g
                pay_ref[q, start : start + 8, :] = acc
                if q % 8 == 7:
                    yield

    others = [gathered(), cycle()] + [payload(g) for g in range(groups)]
    for g, other in enumerate(others):
        for a in range(8):
            if g < groups and a % 2 == 0:
                ladder(g, a)
            next(other, None)
        for _ in other:
            pass
    most = jnp.max(jnp.max(tops[0], axis=0, keepdims=True), axis=1, keepdims=True)
    k = jnp.floor(TOP_EXPONENT - jnp.log2(jnp.maximum(most, 1e-30)))
    scale = jnp.exp2(k)
    row = lax.broadcasted_iota(jnp.int32, pay_ref.shape[1:], 0)
    for q in range(dests):
        z = pay_ref[q] * scale
        z2 = z * z
        z4 = z2 * z2
        y = jnp.where(row >= tiles * per_device, k, z4 * z4 * z)
        send_ref[q] = y.astype(jnp.bfloat16)


def join_kernel(occ_ref, u_ref, half_ref, recv_ref, out_ref, dec_ref, mir_ref, res_ref, sems):
    occupied = occ_ref.shape[0]
    per_device, virtuals = u_ref.shape
    labels, copies = labels_and_copies(occ_ref, occupied)
    spread = 2 * per_device
    ready = set()

    def decode(t):
        ready.add(t)
        start = t * per_device
        low, high = start // 16 * 16, (start + per_device + 15) // 16 * 16
        end = virtuals // LANES * per_device
        for p in range(recv_ref.shape[0]):
            tail = recv_ref[p, end // 16 * 16 : end // 16 * 16 + 16, :]
            k = tail.astype(jnp.float32)[end % 16 : end % 16 + 1, 0:1]
            y = recv_ref[p, low:high, :].astype(jnp.float32)
            y = y[start - low : start - low + per_device]
            size = jnp.log2(jnp.maximum(jnp.abs(y), 2.0**-126)) * (1.0 / POWER) - k
            size = jnp.exp2(size)
            x = jnp.where(y < 0, -size, jnp.where(y > 0, size, 0.0))
            dec_ref[p * per_device : (p + 1) * per_device, :] = x
        mir_ref[t * LANES : (t + 1) * LANES, :] = dec_ref[...].T

    stores = []
    for j in range(occupied):
        for t in range(j * spread // LANES, ((j + 1) * spread - 1) // LANES + 1):
            if t not in ready:
                decode(t)
        u = u_ref[...]
        for i in range(occupied):
            at = pl.ds(pl.multiple_of((2 * j + copies[i]) * per_device, 8), per_device)
            total = half_ref[2 * i + copies[j]] + mir_ref[at, :]
            n = j * occupied + i
            res_ref[n] = jnp.where(u == (labels[j] ^ labels[i]), total, 0.0)
            store = pltpu.make_async_copy(res_ref.at[n], out_ref.at[i, j], sems.at[n])
            store.start()
            stores.append(store)
    for store in stores:
        store.wait()


def permute(x, flip, size):
    return lax.ppermute(x, "vir", [(n, n ^ flip) for n in range(size)])


def body(dests, amps, fock_vir, fock_occ, ladder_ints, cycle_ints, occ_irrep, vir_irrep):
    occupied, _, per_device, virtuals = amps.shape
    pairs = 2 * occupied
    tiles = virtuals // LANES
    rows = occupied * per_device
    kw = ladder_ints.shape[2]
    f32, bf16 = jnp.float32, jnp.bfloat16
    position = lax.axis_index("vir").astype(jnp.int32)
    pos = position.reshape(1)
    vir_local = lax.dynamic_slice_in_dim(vir_irrep, position * per_device, per_device)
    u = jnp.bitwise_xor(vir_local[:, None], vir_irrep[None, :])
    smem = pl.BlockSpec(memory_space=pltpu.SMEM)

    def whole(shape):
        return pl.BlockSpec(shape, lambda n: (0,) * len(shape))

    def cost(flops, size):
        return pl.CostEstimate(flops=flops, bytes_accessed=size, transcendentals=0)

    anywhere = pl.BlockSpec(memory_space=pl.ANY)
    quarter = dests // 4
    block_rows = rows + 16
    block = pl.pallas_call(
        prep_kernel,
        grid=(1,),
        out_shape=jax.ShapeDtypeStruct((block_rows, LANES), bf16),
        in_specs=[
            whole((rows, LANES)),
            pl.BlockSpec((occupied, occupied, 16, LANES), lambda n: (0, 0, 0, 0)),
        ],
        out_specs=whole((block_rows, LANES)),
        compiler_params=params(60),
        cost_estimate=cost(0, 500000),
    )(cycle_ints.reshape(rows, LANES), amps)
    block = block.reshape(1, block_rows, LANES)
    vmem = pl.BlockSpec(memory_space=pltpu.VMEM)
    mix, fock = pl.pallas_call(
        mix_kernel,
        out_shape=(
            jax.ShapeDtypeStruct((rows, rows), bf16),
            jax.ShapeDtypeStruct(fock_vir.shape, bf16),
        ),
        in_specs=[vmem, vmem],
        out_specs=(vmem, vmem),
        compiler_params=params(6),
        cost_estimate=cost(10**7, 2 * 10**6),
    )(fock_occ, fock_vir)

    flat_amps = amps.reshape(occupied, rows, virtuals)
    parts = (6, 2)
    wide = 2

    def fock_part(n, after):
        first, count = sum(parts[:n]), parts[n]
        return pl.pallas_call(
            functools.partial(fock_kernel, first),
            grid=(count // wide,),
            out_shape=(
                jax.ShapeDtypeStruct((2 * count, per_device, virtuals), f32),
                jax.ShapeDtypeStruct((count, per_device, LANES), bf16),
            ),
            in_specs=[
                smem,
                pl.BlockSpec((wide, rows, virtuals), lambda i: (i + first // wide, 0, 0)),
                whole(fock_vir.shape),
                whole(mix.shape),
                whole(u.shape),
                anywhere,
            ],
            out_specs=(
                pl.BlockSpec((2 * wide, per_device, virtuals), lambda i: (i, 0, 0)),
                pl.BlockSpec((wide, per_device, LANES), lambda i: (i, 0, 0)),
            ),
            scratch_shapes=[pltpu.VMEM((occupied, per_device, virtuals), f32)],
            compiler_params=params(12),
            cost_estimate=cost(3 * count * rows * virtuals * virtuals, 2 * 10**6),
        )(occ_irrep, flat_amps, fock, mix, u, after)

    z1, z2, z3 = [permute(block, m << 2, dests) for m in range(1, quarter)]
    block_y = permute(block, 2, dests)
    column = stack([z1, z2, z3], mix)
    column_y = permute(column, 2, dests)
    half0, cyc0 = fock_part(0, column)
    own_blocks = stack([block, column, block_y, column_y], half0)
    mate_blocks = permute(own_blocks, 1, dests)
    half1, cyc1 = fock_part(1, own_blocks)

    send_rows = tiles * per_device + 8
    groups = per_device // 8
    half, send = pl.pallas_call(
        functools.partial(half_kernel, groups, parts),
        out_shape=(
            jax.ShapeDtypeStruct((pairs, per_device, virtuals), f32),
            jax.ShapeDtypeStruct((dests, send_rows, LANES), bf16),
        ),
        in_specs=[smem, smem] + [vmem] * (4 + 2 * len(parts)),
        out_specs=(vmem, vmem),
        scratch_shapes=[
            pltpu.SMEM((occupied,), jnp.int32),
            pltpu.VMEM((occupied * occupied, LANES), f32),
            pltpu.VMEM((virtuals, occupied, LANES), f32),
            pltpu.VMEM((occupied, occupied, per_device, virtuals), f32),
            pltpu.VMEM((dests, send_rows, LANES), f32),
        ]
        + [pltpu.VMEM((tiles, 8 * pairs, LANES), f32)] * groups,
        compiler_params=params(28),
        cost_estimate=cost(6 * occupied * rows * virtuals * LANES, 15 * 10**6),
    )(
        pos, occ_irrep, own_blocks, mate_blocks, half0, half1, cyc0, cyc1, u, ladder_ints,
    )

    recv = lax.all_to_all(send, "vir", split_axis=0, concat_axis=0, tiled=True)

    return pl.pallas_call(
        join_kernel,
        out_shape=jax.ShapeDtypeStruct((occupied, occupied, per_device, virtuals), f32),
        in_specs=[smem, vmem, vmem, vmem],
        out_specs=anywhere,
        scratch_shapes=[
            pltpu.VMEM((virtuals, LANES), f32),
            pltpu.VMEM((tiles * LANES, virtuals), f32),
            pltpu.VMEM((occupied * occupied, per_device, virtuals), f32),
            pltpu.SemaphoreType.DMA((occupied * occupied,)),
        ],
        compiler_params=params(16),
        cost_estimate=cost(10**6, 5 * 10**6),
    )(occ_irrep, u, half, recv)


def solution(mesh):
    dests = mesh.shape["vir"]

    def run(amps, *rest):
        occupied, _, per_device, virtuals = amps.shape
        tiled = (
            dests == 16
            and per_device % 8 == 0
            and virtuals % LANES == 0
            and 2 * occupied * per_device == virtuals
            and rest[2].shape[2] == LANES
            and rest[3].shape[2] == LANES
        )
        return body(dests, amps, *rest) if tiled else plain_body(amps, *rest)

    return jax.shard_map(
        run,
        mesh=mesh,
        in_specs=(
            P("groups", None, "vir", None),
            P("groups", None),
            P("groups", None),
            P("vir", "groups", None),
            P("vir", "groups", None),
            P("groups"),
            P("groups"),
        ),
        out_specs=P("groups", None, "vir", None),
        check_vma=False,
    )
```

```python
import functools

import jax
import jax.numpy as jnp
from jax import lax
from jax.experimental import pallas as pl
from jax.experimental.pallas import tpu as pltpu
from jax.sharding import PartitionSpec as P

DW = 8
CW = 16
LANES = 128
POWER = 9
TOP_EXPONENT = 13


def contract_last(left_side, right_side):
    return lax.dot_general(
        left_side, right_side, (((1,), (1,)), ((), ())), preferred_element_type=jnp.float32
    )


def plain_body(amps, fock_vir, fock_occ, ladder_ints, cycle_ints, occ_irrep, vir_irrep):
    occupied = amps.shape[0]
    per_device = amps.shape[2]
    virtuals = amps.shape[3]
    pair_count = occupied * occupied
    position = lax.axis_index("vir")
    fock_term = jnp.dot(
        amps.reshape(pair_count * per_device, virtuals),
        fock_vir,
        preferred_element_type=jnp.float32,
    ).reshape(occupied, occupied, per_device, virtuals)
    occ_term = jnp.einsum("ikab,kj->ijab", amps, fock_occ, preferred_element_type=jnp.float32)
    flat_ints = ladder_ints.reshape(per_device * virtuals, ladder_ints.shape[2])
    local_window = amps[:, :, 0:1, :DW]
    local_cycle = amps[:, :, :, :CW]
    segment = lax.all_gather(local_window, "vir", axis=2, tiled=True)
    width = segment.shape[2] * DW
    ladder = contract_last(segment.reshape(pair_count, width), flat_ints)
    left_side = jnp.transpose(local_cycle, (0, 2, 1, 3)).reshape(
        occupied * per_device, occupied * CW
    )
    segment = lax.all_gather(cycle_ints, "vir", axis=0, tiled=True)
    right_side = segment.reshape(segment.shape[0] * occupied, occupied * CW)
    cycle_block = contract_last(left_side, right_side).reshape(
        occupied, per_device, segment.shape[0], occupied
    )
    cycle_part = jnp.transpose(cycle_block, (0, 3, 1, 2))
    half_sum = (
        fock_term - occ_term + ladder.reshape(occupied, occupied, per_device, virtuals) + cycle_part
    )
    vir_local = lax.dynamic_slice_in_dim(vir_irrep, position * per_device, per_device)
    occ_pair = jnp.bitwise_xor(occ_irrep[:, None], occ_irrep[None, :])
    vir_pair = jnp.bitwise_xor(vir_local[:, None], vir_irrep[None, :])
    received = lax.all_to_all(half_sum, "vir", split_axis=3, concat_axis=2, tiled=True)
    mirrored = jnp.transpose(received, (1, 0, 3, 2))
    product_irrep = jnp.bitwise_xor(occ_pair[:, :, None, None], vir_pair[None, None, :, :])
    allowed = jnp.where(product_irrep == 0, jnp.float32(1.0), jnp.float32(0.0))
    return allowed * (half_sum + mirrored)


def params(mib):
    return pltpu.CompilerParams(vmem_limit_bytes=mib * 2**20)


def labels_and_copies(occ_ref, occupied):
    labels = [occ_ref[j] for j in range(occupied)]
    copies = []
    for j in range(occupied):
        s = jnp.int32(0)
        for k in range(j):
            s = s + (labels[k] == labels[j]).astype(jnp.int32)
        copies.append(s)
    return labels, copies


def prep_kernel(cyc_ref, amps_ref, block_ref):
    occupied = amps_ref.shape[0]
    rows = cyc_ref.shape[0]
    block_ref[:rows, :] = cyc_ref[...]
    lane = lax.broadcasted_iota(jnp.int32, (occupied, LANES), 1)
    packed = jnp.zeros((occupied, LANES), jnp.float32)
    for j in range(occupied):
        w = jnp.where(lane < DW, amps_ref[:, j, 0, :].astype(jnp.float32), 0.0)
        packed = packed + (pltpu.roll(w, j * DW, axis=1) if j else w)
    packed = jnp.concatenate([packed, jnp.zeros_like(packed)], axis=0)
    block_ref[rows:, :] = packed.astype(jnp.bfloat16)


def mix_kernel(occ_vals_ref, fock_ref, mix_ref, fock_out_ref):
    fock_out_ref[...] = fock_ref[...]
    rows = mix_ref.shape[0]
    occupied = occ_vals_ref.shape[0]
    per_device = rows // occupied
    row = lax.broadcasted_iota(jnp.int32, (rows, occupied), 0)
    start = lax.broadcasted_iota(jnp.int32, (rows, occupied), 1) * per_device
    in_block = jnp.logical_and(row >= start, row < start + per_device).astype(jnp.bfloat16)
    row = lax.broadcasted_iota(jnp.int32, (rows, per_device), 0)
    at = lax.broadcasted_iota(jnp.int32, (rows, per_device), 1)
    same = row == at
    for n in range(1, occupied):
        same = jnp.logical_or(same, row == at + n * per_device)
    same = same.astype(jnp.bfloat16)
    left = contract_last(in_block, occ_vals_ref[...]).astype(jnp.bfloat16)
    mix = contract_last(left, in_block) * contract_last(same, same)
    mix_ref[...] = mix.astype(jnp.bfloat16)


def fock_kernel(first, occ_ref, amps_ref, fock_ref, mix_ref, u_ref, after_ref, half_ref, cyc_ref, hs_ref):
    wide, rows, virtuals = amps_ref.shape
    _, per_device, _ = half_ref.shape
    occupied = occ_ref.shape[0]
    labels, copies = labels_and_copies(occ_ref, occupied)
    u = u_ref[...]
    h = jnp.dot(
        amps_ref[...].reshape(wide * rows, virtuals),
        fock_ref[...],
        preferred_element_type=jnp.float32,
    )
    for w in range(wide):
        a = amps_ref[w]
        mixed = jnp.dot(mix_ref[...], a, preferred_element_type=jnp.float32)
        hs_ref[...] = (h[w * rows : (w + 1) * rows] - mixed).reshape(hs_ref.shape)
        own = occ_ref[pl.program_id(0) * wide + w + first]
        for j in range(occupied):
            at = 2 * w + copies[j]
            half_ref[at] = jnp.where(u == (own ^ labels[j]), hs_ref[j], half_ref[at])
        head = a[:, :LANES].astype(jnp.float32)
        lane = lax.broadcasted_iota(jnp.int32, (per_device, LANES), 1)
        acc = jnp.zeros((per_device, LANES), jnp.float32)
        for k in range(occupied):
            piece = jnp.where(lane < CW, head[k * per_device : (k + 1) * per_device], 0.0)
            acc = acc + (pltpu.roll(piece, k * CW, axis=1) if k else piece)
        cyc_ref[w] = acc.astype(jnp.bfloat16)


def stack(blocks, after):
    count = len(blocks)

    def kernel(*refs):
        out = refs[count + 1]
        at = 0
        for n in range(count):
            head = blocks[n].shape[0]
            out[at : at + head] = refs[n][...]
            at += head

    vmem = pl.BlockSpec(memory_space=pltpu.VMEM)
    shape = (sum(b.shape[0] for b in blocks),) + blocks[0].shape[1:]
    return pl.pallas_call(
        kernel,
        out_shape=jax.ShapeDtypeStruct(shape, blocks[0].dtype),
        in_specs=[vmem] * count + [pl.BlockSpec(memory_space=pl.ANY)],
        out_specs=vmem,
        compiler_params=params(4),
        cost_estimate=pl.CostEstimate(flops=0, bytes_accessed=10**6, transcendentals=0),
    )(*blocks, after)


def payload_pieces(per_device, pairs, dests):
    out = {}
    for q in range(dests):
        for e in range(pairs):
            start = 0
            while start < per_device:
                src = q * per_device + start
                dst = e * per_device + start
                length = min(LANES - src % LANES, LANES - dst % LANES, per_device - start)
                out.setdefault((q, dst // LANES), []).append(
                    (dst % LANES, e, src // LANES, (dst - src) % LANES)
                )
                start += length
    return out


def half_kernel(groups, parts, pos_ref, occ_ref, own_ref, mate_ref, *refs):
    halves, refs = refs[: len(parts)], refs[len(parts) :]
    cycs, refs = refs[: len(parts)], refs[len(parts) :]
    u_ref, lad_ref, out_ref, send_ref, orb_ref, w2_ref, xs_ref, cs_ref, pay_ref = refs[:9]
    ls_refs = refs[9:]
    occupied = occ_ref.shape[0]
    pairs, per_device, virtuals = out_ref.shape
    dests = pay_ref.shape[0]
    tiles = virtuals // LANES
    rows = occupied * per_device
    labels, copies = labels_and_copies(occ_ref, occupied)
    lane = lax.broadcasted_iota(jnp.int32, (8, LANES), 1)

    def block_of(r):
        ref = mate_ref if r & 1 else own_ref
        return ref[((r >> 1) & 1) * (dests // 4) + (r >> 2)]

    packed = [block_of(r)[rows:].astype(jnp.float32)[:8] for r in range(dests)]
    for j in range(occupied):
        orb_ref[2 * labels[j] + copies[j]] = jnp.int32(j)
        window = jnp.zeros((8, LANES), jnp.float32)
        for r in range(dests):
            w = jnp.where(jnp.logical_and(lane >= j * DW, lane < (j + 1) * DW), packed[r], 0.0)
            shift = lax.rem((pos_ref[0] ^ r) * DW - j * DW + LANES, LANES)
            window = window + pltpu.roll(w, shift, axis=1)
        for i in range(occupied):
            row = (labels[i] ^ labels[j]) * pairs + 2 * i + copies[j]
            w2_ref[pl.ds(row, 1), :] = window[i : i + 1, :]
    w2 = w2_ref[...].astype(jnp.bfloat16)
    left = jnp.concatenate([ref[...].astype(jnp.float32) for ref in cycs], axis=0)
    left = left.reshape(rows, LANES).astype(jnp.bfloat16)
    choices = [
        [orb_ref[2 * (labels[e // 2] ^ n) + e % 2] for n in range(4)] for e in range(pairs)
    ]
    sources = [(part, n) for part in halves for n in range(part.shape[0])]
    pieces_of = payload_pieces(per_device, pairs, dests)
    tops = [jnp.zeros((8, LANES), jnp.float32)]

    def ladder(g, a):
        product = contract_last(w2, lad_ref[8 * g + a])
        ua = u_ref[8 * g + a : 8 * g + a + 1, :]
        sel = product[0:pairs]
        for v in range(1, 4):
            sel = jnp.where(ua == v, product[v * pairs : (v + 1) * pairs], sel)
        for v in range(tiles):
            ls_refs[g][v, pl.ds(a, pairs, stride=8), :] = sel[:, v * LANES : (v + 1) * LANES]

    def gathered():
        for r in range(dests):
            x = block_of(r)[:rows].astype(jnp.float32).reshape(per_device, occupied, LANES)
            xs_ref[pl.ds((pos_ref[0] ^ r) * per_device, per_device)] = x
            if r % 2:
                yield

    def cycle():
        for j in range(occupied):
            c = contract_last(left, xs_ref[:, j, :].astype(jnp.bfloat16))
            cs_ref[j] = c.reshape(occupied, per_device, virtuals)
            yield

    def payload(g):
        group = slice(8 * g, 8 * g + 8)
        found = {}
        rolled = {}
        for t in range(tiles):
            last_e = min(((t + 1) * LANES - 1) // per_device, pairs - 1)
            for e in range(t * LANES // per_device, last_e + 1):
                if (e, 0) in found:
                    continue
                part, n = sources[e]
                for v in range(tiles):
                    at = slice(v * LANES, (v + 1) * LANES)
                    uv = u_ref[group, at]
                    x = cs_ref[choices[e][0], e // 2, group, at]
                    for m in range(1, 4):
                        x = jnp.where(uv == m, cs_ref[choices[e][m], e // 2, group, at], x)
                    x = x + (part[n, group, at] + ls_refs[g][v, 8 * e : 8 * e + 8, :])
                    out_ref[e, group, at] = x
                    tops[0] = jnp.maximum(tops[0], jnp.abs(x))
                    found[e, v] = x
            for q in range(dests):
                acc = None
                for first, e, v, shift in pieces_of[q, t]:
                    if (e, v, shift) not in rolled:
                        x = found[e, v]
                        rolled[e, v, shift] = pltpu.roll(x, shift, axis=1) if shift else x
                    x = rolled[e, v, shift]
                    acc = x if acc is None else jnp.where(lane >= first, x, acc)
                start = t * per_device + 8 * g
                pay_ref[q, start : start + 8, :] = acc
                if q % 8 == 7:
                    yield

    others = [gathered(), cycle()] + [payload(g) for g in range(groups)]
    for g, other in enumerate(others):
        for a in range(8):
            if g < groups:
                ladder(g, a)
            next(other, None)
        for _ in other:
            pass
    most = jnp.max(jnp.max(tops[0], axis=0, keepdims=True), axis=1, keepdims=True)
    k = jnp.floor(TOP_EXPONENT - jnp.log2(jnp.maximum(most, 1e-30)))
    scale = jnp.exp2(k)
    row = lax.broadcasted_iota(jnp.int32, pay_ref.shape[1:], 0)
    for q in range(dests):
        z = pay_ref[q] * scale
        z2 = z * z
        z4 = z2 * z2
        y = jnp.where(row >= tiles * per_device, k, z4 * z4 * z)
        send_ref[q] = y.astype(jnp.bfloat16)


def join_kernel(occ_ref, u_ref, half_ref, recv_ref, out_ref, dec_ref, mir_ref, res_ref, sems):
    occupied = occ_ref.shape[0]
    per_device, virtuals = u_ref.shape
    labels, copies = labels_and_copies(occ_ref, occupied)
    spread = 2 * per_device
    ready = set()

    def decode(t):
        ready.add(t)
        start = t * per_device
        low, high = start // 16 * 16, (start + per_device + 15) // 16 * 16
        end = virtuals // LANES * per_device
        for p in range(recv_ref.shape[0]):
            tail = recv_ref[p, end // 16 * 16 : end // 16 * 16 + 16, :]
            k = tail.astype(jnp.float32)[end % 16 : end % 16 + 1, 0:1]
            y = recv_ref[p, low:high, :].astype(jnp.float32)
            y = y[start - low : start - low + per_device]
            size = jnp.log2(jnp.maximum(jnp.abs(y), 2.0**-126)) * (1.0 / POWER) - k
            size = jnp.exp2(size)
            x = jnp.where(y < 0, -size, jnp.where(y > 0, size, 0.0))
            dec_ref[p * per_device : (p + 1) * per_device, :] = x
        mir_ref[t * LANES : (t + 1) * LANES, :] = dec_ref[...].T

    stores = []
    for j in range(occupied):
        for t in range(j * spread // LANES, ((j + 1) * spread - 1) // LANES + 1):
            if t not in ready:
                decode(t)
        u = u_ref[...]
        for i in range(occupied):
            at = pl.ds(pl.multiple_of((2 * j + copies[i]) * per_device, 8), per_device)
            total = half_ref[2 * i + copies[j]] + mir_ref[at, :]
            n = j * occupied + i
            res_ref[n] = jnp.where(u == (labels[j] ^ labels[i]), total, 0.0)
            store = pltpu.make_async_copy(res_ref.at[n], out_ref.at[i, j], sems.at[n])
            store.start()
            stores.append(store)
    for store in stores:
        store.wait()


def permute(x, flip, size):
    return lax.ppermute(x, "vir", [(n, n ^ flip) for n in range(size)])


def body(dests, amps, fock_vir, fock_occ, ladder_ints, cycle_ints, occ_irrep, vir_irrep):
    occupied, _, per_device, virtuals = amps.shape
    pairs = 2 * occupied
    tiles = virtuals // LANES
    rows = occupied * per_device
    kw = ladder_ints.shape[2]
    f32, bf16 = jnp.float32, jnp.bfloat16
    position = lax.axis_index("vir").astype(jnp.int32)
    pos = position.reshape(1)
    vir_local = lax.dynamic_slice_in_dim(vir_irrep, position * per_device, per_device)
    u = jnp.bitwise_xor(vir_local[:, None], vir_irrep[None, :])
    smem = pl.BlockSpec(memory_space=pltpu.SMEM)

    def whole(shape):
        return pl.BlockSpec(shape, lambda n: (0,) * len(shape))

    def cost(flops, size):
        return pl.CostEstimate(flops=flops, bytes_accessed=size, transcendentals=0)

    anywhere = pl.BlockSpec(memory_space=pl.ANY)
    quarter = dests // 4
    block_rows = rows + 16
    block = pl.pallas_call(
        prep_kernel,
        grid=(1,),
        out_shape=jax.ShapeDtypeStruct((block_rows, LANES), bf16),
        in_specs=[
            whole((rows, LANES)),
            pl.BlockSpec((occupied, occupied, 16, LANES), lambda n: (0, 0, 0, 0)),
        ],
        out_specs=whole((block_rows, LANES)),
        compiler_params=params(60),
        cost_estimate=cost(0, 500000),
    )(cycle_ints.reshape(rows, LANES), amps)
    block = block.reshape(1, block_rows, LANES)
    vmem = pl.BlockSpec(memory_space=pltpu.VMEM)
    mix, fock = pl.pallas_call(
        mix_kernel,
        out_shape=(
            jax.ShapeDtypeStruct((rows, rows), bf16),
            jax.ShapeDtypeStruct(fock_vir.shape, bf16),
        ),
        in_specs=[vmem, vmem],
        out_specs=(vmem, vmem),
        compiler_params=params(6),
        cost_estimate=cost(10**7, 2 * 10**6),
    )(fock_occ, fock_vir)

    flat_amps = amps.reshape(occupied, rows, virtuals)
    parts = (6, 2)
    wide = 2

    def fock_part(n, after):
        first, count = sum(parts[:n]), parts[n]
        return pl.pallas_call(
            functools.partial(fock_kernel, first),
            grid=(count // wide,),
            out_shape=(
                jax.ShapeDtypeStruct((2 * count, per_device, virtuals), f32),
                jax.ShapeDtypeStruct((count, per_device, LANES), bf16),
            ),
            in_specs=[
                smem,
                pl.BlockSpec((wide, rows, virtuals), lambda i: (i + first // wide, 0, 0)),
                whole(fock_vir.shape),
                whole(mix.shape),
                whole(u.shape),
                anywhere,
            ],
            out_specs=(
                pl.BlockSpec((2 * wide, per_device, virtuals), lambda i: (i, 0, 0)),
                pl.BlockSpec((wide, per_device, LANES), lambda i: (i, 0, 0)),
            ),
            scratch_shapes=[pltpu.VMEM((occupied, per_device, virtuals), f32)],
            compiler_params=params(12),
            cost_estimate=cost(3 * count * rows * virtuals * virtuals, 2 * 10**6),
        )(occ_irrep, flat_amps, fock, mix, u, after)

    z1, z2, z3 = [permute(block, m << 2, dests) for m in range(1, quarter)]
    block_y = permute(block, 2, dests)
    diagonal = permute(block_y, 4, dests)
    column = stack([z2, z3], mix)
    column_y = permute(column, 2, dests)
    half0, cyc0 = fock_part(0, column)
    own_blocks = stack([block, z1, column, block_y, diagonal, column_y], half0)
    mate_blocks = permute(own_blocks, 1, dests)
    half1, cyc1 = fock_part(1, own_blocks)

    send_rows = tiles * per_device + 8
    groups = per_device // 8
    half, send = pl.pallas_call(
        functools.partial(half_kernel, groups, parts),
        out_shape=(
            jax.ShapeDtypeStruct((pairs, per_device, virtuals), f32),
            jax.ShapeDtypeStruct((dests, send_rows, LANES), bf16),
        ),
        in_specs=[smem, smem] + [vmem] * (4 + 2 * len(parts)),
        out_specs=(vmem, vmem),
        scratch_shapes=[
            pltpu.SMEM((occupied,), jnp.int32),
            pltpu.VMEM((occupied * occupied, LANES), f32),
            pltpu.VMEM((virtuals, occupied, LANES), f32),
            pltpu.VMEM((occupied, occupied, per_device, virtuals), f32),
            pltpu.VMEM((dests, send_rows, LANES), f32),
        ]
        + [pltpu.VMEM((tiles, 8 * pairs, LANES), f32)] * groups,
        compiler_params=params(28),
        cost_estimate=cost(6 * occupied * rows * virtuals * LANES, 15 * 10**6),
    )(
        pos, occ_irrep, own_blocks, mate_blocks, half0, half1, cyc0, cyc1, u, ladder_ints,
    )

    recv = lax.all_to_all(send, "vir", split_axis=0, concat_axis=0, tiled=True)

    return pl.pallas_call(
        join_kernel,
        out_shape=jax.ShapeDtypeStruct((occupied, occupied, per_device, virtuals), f32),
        in_specs=[smem, vmem, vmem, vmem],
        out_specs=anywhere,
        scratch_shapes=[
            pltpu.VMEM((virtuals, LANES), f32),
            pltpu.VMEM((tiles * LANES, virtuals), f32),
            pltpu.VMEM((occupied * occupied, per_device, virtuals), f32),
            pltpu.SemaphoreType.DMA((occupied * occupied,)),
        ],
        compiler_params=params(16),
        cost_estimate=cost(10**6, 5 * 10**6),
    )(occ_irrep, u, half, recv)


def solution(mesh):
    dests = mesh.shape["vir"]

    def run(amps, *rest):
        occupied, _, per_device, virtuals = amps.shape
        tiled = (
            dests == 16
            and per_device % 8 == 0
            and virtuals % LANES == 0
            and 2 * occupied * per_device == virtuals
            and rest[2].shape[2] == LANES
            and rest[3].shape[2] == LANES
        )
        return body(dests, amps, *rest) if tiled else plain_body(amps, *rest)

    return jax.shard_map(
        run,
        mesh=mesh,
        in_specs=(
            P("groups", None, "vir", None),
            P("groups", None),
            P("groups", None),
            P("vir", "groups", None),
            P("vir", "groups", None),
            P("groups"),
            P("groups"),
        ),
        out_specs=P("groups", None, "vir", None),
        check_vma=False,
    )
```

```python
import functools

import jax
import jax.numpy as jnp
from jax import lax
from jax.experimental import pallas as pl
from jax.experimental.pallas import tpu as pltpu
from jax.sharding import PartitionSpec as P

DW = 8
CW = 16
LANES = 128
POWER = 9
TOP_EXPONENT = 13


def contract_last(left_side, right_side):
    return lax.dot_general(
        left_side, right_side, (((1,), (1,)), ((), ())), preferred_element_type=jnp.float32
    )


def plain_body(amps, fock_vir, fock_occ, ladder_ints, cycle_ints, occ_irrep, vir_irrep):
    occupied = amps.shape[0]
    per_device = amps.shape[2]
    virtuals = amps.shape[3]
    pair_count = occupied * occupied
    position = lax.axis_index("vir")
    fock_term = jnp.dot(
        amps.reshape(pair_count * per_device, virtuals),
        fock_vir,
        preferred_element_type=jnp.float32,
    ).reshape(occupied, occupied, per_device, virtuals)
    occ_term = jnp.einsum("ikab,kj->ijab", amps, fock_occ, preferred_element_type=jnp.float32)
    flat_ints = ladder_ints.reshape(per_device * virtuals, ladder_ints.shape[2])
    local_window = amps[:, :, 0:1, :DW]
    local_cycle = amps[:, :, :, :CW]
    segment = lax.all_gather(local_window, "vir", axis=2, tiled=True)
    width = segment.shape[2] * DW
    ladder = contract_last(segment.reshape(pair_count, width), flat_ints)
    left_side = jnp.transpose(local_cycle, (0, 2, 1, 3)).reshape(
        occupied * per_device, occupied * CW
    )
    segment = lax.all_gather(cycle_ints, "vir", axis=0, tiled=True)
    right_side = segment.reshape(segment.shape[0] * occupied, occupied * CW)
    cycle_block = contract_last(left_side, right_side).reshape(
        occupied, per_device, segment.shape[0], occupied
    )
    cycle_part = jnp.transpose(cycle_block, (0, 3, 1, 2))
    half_sum = (
        fock_term - occ_term + ladder.reshape(occupied, occupied, per_device, virtuals) + cycle_part
    )
    vir_local = lax.dynamic_slice_in_dim(vir_irrep, position * per_device, per_device)
    occ_pair = jnp.bitwise_xor(occ_irrep[:, None], occ_irrep[None, :])
    vir_pair = jnp.bitwise_xor(vir_local[:, None], vir_irrep[None, :])
    received = lax.all_to_all(half_sum, "vir", split_axis=3, concat_axis=2, tiled=True)
    mirrored = jnp.transpose(received, (1, 0, 3, 2))
    product_irrep = jnp.bitwise_xor(occ_pair[:, :, None, None], vir_pair[None, None, :, :])
    allowed = jnp.where(product_irrep == 0, jnp.float32(1.0), jnp.float32(0.0))
    return allowed * (half_sum + mirrored)


def params(mib):
    return pltpu.CompilerParams(vmem_limit_bytes=mib * 2**20)


def labels_and_copies(occ_ref, occupied):
    labels = [occ_ref[j] for j in range(occupied)]
    copies = []
    for j in range(occupied):
        s = jnp.int32(0)
        for k in range(j):
            s = s + (labels[k] == labels[j]).astype(jnp.int32)
        copies.append(s)
    return labels, copies


def prep_kernel(cyc_ref, amps_ref, block_ref):
    occupied = amps_ref.shape[0]
    rows = cyc_ref.shape[0]
    block_ref[:rows, :] = cyc_ref[...]
    lane = lax.broadcasted_iota(jnp.int32, (occupied, LANES), 1)
    packed = jnp.zeros((occupied, LANES), jnp.float32)
    for j in range(occupied):
        w = jnp.where(lane < DW, amps_ref[:, j, 0, :].astype(jnp.float32), 0.0)
        packed = packed + (pltpu.roll(w, j * DW, axis=1) if j else w)
    packed = jnp.concatenate([packed, jnp.zeros_like(packed)], axis=0)
    block_ref[rows:, :] = packed.astype(jnp.bfloat16)


def mix_kernel(occ_vals_ref, fock_ref, mix_ref, fock_out_ref):
    fock_out_ref[...] = fock_ref[...]
    rows = mix_ref.shape[0]
    occupied = occ_vals_ref.shape[0]
    per_device = rows // occupied
    row = lax.broadcasted_iota(jnp.int32, (rows, occupied), 0)
    start = lax.broadcasted_iota(jnp.int32, (rows, occupied), 1) * per_device
    in_block = jnp.logical_and(row >= start, row < start + per_device).astype(jnp.bfloat16)
    row = lax.broadcasted_iota(jnp.int32, (rows, per_device), 0)
    at = lax.broadcasted_iota(jnp.int32, (rows, per_device), 1)
    same = row == at
    for n in range(1, occupied):
        same = jnp.logical_or(same, row == at + n * per_device)
    same = same.astype(jnp.bfloat16)
    left = contract_last(in_block, occ_vals_ref[...]).astype(jnp.bfloat16)
    mix = contract_last(left, in_block) * contract_last(same, same)
    mix_ref[...] = mix.astype(jnp.bfloat16)


def fock_kernel(first, occ_ref, amps_ref, fock_ref, mix_ref, u_ref, after_ref, half_ref, cyc_ref, hs_ref):
    wide, rows, virtuals = amps_ref.shape
    _, per_device, _ = half_ref.shape
    occupied = occ_ref.shape[0]
    labels, copies = labels_and_copies(occ_ref, occupied)
    u = u_ref[...]
    h = jnp.dot(
        amps_ref[...].reshape(wide * rows, virtuals),
        fock_ref[...],
        preferred_element_type=jnp.float32,
    )
    for w in range(wide):
        a = amps_ref[w]
        mixed = jnp.dot(mix_ref[...], a, preferred_element_type=jnp.float32)
        hs_ref[...] = (h[w * rows : (w + 1) * rows] - mixed).reshape(hs_ref.shape)
        own = occ_ref[pl.program_id(0) * wide + w + first]
        for j in range(occupied):
            at = 2 * w + copies[j]
            half_ref[at] = jnp.where(u == (own ^ labels[j]), hs_ref[j], half_ref[at])
        head = a[:, :LANES].astype(jnp.float32)
        lane = lax.broadcasted_iota(jnp.int32, (per_device, LANES), 1)
        acc = jnp.zeros((per_device, LANES), jnp.float32)
        for k in range(occupied):
            piece = jnp.where(lane < CW, head[k * per_device : (k + 1) * per_device], 0.0)
            acc = acc + (pltpu.roll(piece, k * CW, axis=1) if k else piece)
        cyc_ref[w] = acc.astype(jnp.bfloat16)


def stack(blocks, after):
    count = len(blocks)

    def kernel(*refs):
        out = refs[count + 1]
        at = 0
        for n in range(count):
            head = blocks[n].shape[0]
            out[at : at + head] = refs[n][...]
            at += head

    vmem = pl.BlockSpec(memory_space=pltpu.VMEM)
    shape = (sum(b.shape[0] for b in blocks),) + blocks[0].shape[1:]
    return pl.pallas_call(
        kernel,
        out_shape=jax.ShapeDtypeStruct(shape, blocks[0].dtype),
        in_specs=[vmem] * count + [pl.BlockSpec(memory_space=pl.ANY)],
        out_specs=vmem,
        compiler_params=params(4),
        cost_estimate=pl.CostEstimate(flops=0, bytes_accessed=10**6, transcendentals=0),
    )(*blocks, after)


def payload_pieces(per_device, pairs, dests):
    out = {}
    for q in range(dests):
        for e in range(pairs):
            start = 0
            while start < per_device:
                src = q * per_device + start
                dst = e * per_device + start
                length = min(LANES - src % LANES, LANES - dst % LANES, per_device - start)
                out.setdefault((q, dst // LANES), []).append(
                    (dst % LANES, e, src // LANES, (dst - src) % LANES)
                )
                start += length
    return out


def half_kernel(groups, parts, pos_ref, occ_ref, own_ref, mate_ref, *refs):
    halves, refs = refs[: len(parts)], refs[len(parts) :]
    cycs, refs = refs[: len(parts)], refs[len(parts) :]
    u_ref, lad_ref, out_ref, send_ref, orb_ref, w2_ref, xs_ref, cs_ref, pay_ref = refs[:9]
    ls_refs = refs[9:]
    occupied = occ_ref.shape[0]
    pairs, per_device, virtuals = out_ref.shape
    dests = pay_ref.shape[0]
    tiles = virtuals // LANES
    rows = occupied * per_device
    labels, copies = labels_and_copies(occ_ref, occupied)
    lane = lax.broadcasted_iota(jnp.int32, (8, LANES), 1)

    def block_of(r):
        ref = mate_ref if r & 1 else own_ref
        return ref[((r >> 1) & 1) * (dests // 4) + (r >> 2)]

    packed = [block_of(r)[rows:].astype(jnp.float32)[:8] for r in range(dests)]
    for j in range(occupied):
        orb_ref[2 * labels[j] + copies[j]] = jnp.int32(j)
        window = jnp.zeros((8, LANES), jnp.float32)
        for r in range(dests):
            w = jnp.where(jnp.logical_and(lane >= j * DW, lane < (j + 1) * DW), packed[r], 0.0)
            shift = lax.rem((pos_ref[0] ^ r) * DW - j * DW + LANES, LANES)
            window = window + pltpu.roll(w, shift, axis=1)
        for i in range(occupied):
            row = (labels[i] ^ labels[j]) * pairs + 2 * i + copies[j]
            w2_ref[pl.ds(row, 1), :] = window[i : i + 1, :]
    w2 = w2_ref[...].astype(jnp.bfloat16)
    left = jnp.concatenate([ref[...].astype(jnp.float32) for ref in cycs], axis=0)
    left = left.reshape(rows, LANES).astype(jnp.bfloat16)
    choices = [
        [orb_ref[2 * (labels[e // 2] ^ n) + e % 2] for n in range(4)] for e in range(pairs)
    ]
    sources = [(part, n) for part in halves for n in range(part.shape[0])]
    pieces_of = payload_pieces(per_device, pairs, dests)
    tops = [jnp.zeros((8, LANES), jnp.float32)]

    def ladder(g, a):
        product = contract_last(w2, lad_ref[8 * g + a])
        ua = u_ref[8 * g + a : 8 * g + a + 1, :]
        sel = product[0:pairs]
        for v in range(1, 4):
            sel = jnp.where(ua == v, product[v * pairs : (v + 1) * pairs], sel)
        for v in range(tiles):
            ls_refs[g][v, pl.ds(a, pairs, stride=8), :] = sel[:, v * LANES : (v + 1) * LANES]

    def gathered():
        for r in range(dests):
            x = block_of(r)[:rows].astype(jnp.float32).reshape(per_device, occupied, LANES)
            xs_ref[pl.ds((pos_ref[0] ^ r) * per_device, per_device)] = x
            if r % 2:
                yield

    def cycle():
        for j in range(occupied):
            c = contract_last(left, xs_ref[:, j, :].astype(jnp.bfloat16))
            cs_ref[j] = c.reshape(occupied, per_device, virtuals)
            yield

    def payload(g):
        group = slice(8 * g, 8 * g + 8)
        found = {}
        for t in range(tiles):
            last_e = min(((t + 1) * LANES - 1) // per_device, pairs - 1)
            for e in range(t * LANES // per_device, last_e + 1):
                if (e, 0) in found:
                    continue
                part, n = sources[e]
                for v in range(tiles):
                    at = slice(v * LANES, (v + 1) * LANES)
                    uv = u_ref[group, at]
                    x = cs_ref[choices[e][0], e // 2, group, at]
                    for m in range(1, 4):
                        x = jnp.where(uv == m, cs_ref[choices[e][m], e // 2, group, at], x)
                    x = x + (part[n, group, at] + ls_refs[g][v, 8 * e : 8 * e + 8, :])
                    out_ref[e, group, at] = x
                    tops[0] = jnp.maximum(tops[0], jnp.abs(x))
                    found[e, v] = x
            for q in range(dests):
                acc = None
                for first, e, v, shift in pieces_of[q, t]:
                    x = pltpu.roll(found[e, v], shift, axis=1) if shift else found[e, v]
                    acc = x if acc is None else jnp.where(lane >= first, x, acc)
                start = t * per_device + 8 * g
                pay_ref[q, start : start + 8, :] = acc
                if q % 8 == 7:
                    yield

    others = [gathered(), cycle()] + [payload(g) for g in range(groups)]
    for g, other in enumerate(others):
        for a in range(8):
            if g < groups:
                ladder(g, a)
            next(other, None)
        for _ in other:
            pass
    most = jnp.max(jnp.max(tops[0], axis=0, keepdims=True), axis=1, keepdims=True)
    k = jnp.floor(TOP_EXPONENT - jnp.log2(jnp.maximum(most, 1e-30)))
    scale = jnp.exp2(k)
    row = lax.broadcasted_iota(jnp.int32, pay_ref.shape[1:], 0)
    for q in range(dests):
        z = pay_ref[q] * scale
        z2 = z * z
        z4 = z2 * z2
        y = jnp.where(row >= tiles * per_device, k, z4 * z4 * z)
        send_ref[q] = y.astype(jnp.bfloat16)


def join_kernel(occ_ref, u_ref, half_ref, recv_ref, out_ref, dec_ref, mir_ref, res_ref, sems):
    occupied = occ_ref.shape[0]
    per_device, virtuals = u_ref.shape
    labels, copies = labels_and_copies(occ_ref, occupied)
    spread = 2 * per_device
    ready = set()

    def decode(t):
        ready.add(t)
        start = t * per_device
        low, high = start // 16 * 16, (start + per_device + 15) // 16 * 16
        end = virtuals // LANES * per_device
        for p in range(recv_ref.shape[0]):
            tail = recv_ref[p, end // 16 * 16 : end // 16 * 16 + 16, :]
            k = tail.astype(jnp.float32)[end % 16 : end % 16 + 1, 0:1]
            y = recv_ref[p, low:high, :].astype(jnp.float32)
            y = y[start - low : start - low + per_device]
            size = jnp.log2(jnp.maximum(jnp.abs(y), 2.0**-126)) * (1.0 / POWER) - k
            size = jnp.exp2(size)
            x = jnp.where(y < 0, -size, jnp.where(y > 0, size, 0.0))
            dec_ref[p * per_device : (p + 1) * per_device, :] = x
        mir_ref[t * LANES : (t + 1) * LANES, :] = dec_ref[...].T

    stores = []
    for j in range(occupied):
        for t in range(j * spread // LANES, ((j + 1) * spread - 1) // LANES + 1):
            if t not in ready:
                decode(t)
        u = u_ref[...]
        for i in range(occupied):
            at = pl.ds(pl.multiple_of((2 * j + copies[i]) * per_device, 8), per_device)
            total = half_ref[2 * i + copies[j]] + mir_ref[at, :]
            n = j * occupied + i
            res_ref[n] = jnp.where(u == (labels[j] ^ labels[i]), total, 0.0)
            store = pltpu.make_async_copy(res_ref.at[n], out_ref.at[i, j], sems.at[n])
            store.start()
            stores.append(store)
    for store in stores:
        store.wait()


def permute(x, flip, size):
    return lax.ppermute(x, "vir", [(n, n ^ flip) for n in range(size)])


def body(dests, amps, fock_vir, fock_occ, ladder_ints, cycle_ints, occ_irrep, vir_irrep):
    occupied, _, per_device, virtuals = amps.shape
    pairs = 2 * occupied
    tiles = virtuals // LANES
    rows = occupied * per_device
    kw = ladder_ints.shape[2]
    f32, bf16 = jnp.float32, jnp.bfloat16
    position = lax.axis_index("vir").astype(jnp.int32)
    pos = position.reshape(1)
    vir_local = lax.dynamic_slice_in_dim(vir_irrep, position * per_device, per_device)
    u = jnp.bitwise_xor(vir_local[:, None], vir_irrep[None, :])
    smem = pl.BlockSpec(memory_space=pltpu.SMEM)

    def whole(shape):
        return pl.BlockSpec(shape, lambda n: (0,) * len(shape))

    def cost(flops, size):
        return pl.CostEstimate(flops=flops, bytes_accessed=size, transcendentals=0)

    anywhere = pl.BlockSpec(memory_space=pl.ANY)
    quarter = dests // 4
    block_rows = rows + 16
    block = pl.pallas_call(
        prep_kernel,
        grid=(1,),
        out_shape=jax.ShapeDtypeStruct((block_rows, LANES), bf16),
        in_specs=[
            whole((rows, LANES)),
            pl.BlockSpec((occupied, occupied, 16, LANES), lambda n: (0, 0, 0, 0)),
        ],
        out_specs=whole((block_rows, LANES)),
        compiler_params=params(60),
        cost_estimate=cost(0, 500000),
    )(cycle_ints.reshape(rows, LANES), amps)
    block = block.reshape(1, block_rows, LANES)
    vmem = pl.BlockSpec(memory_space=pltpu.VMEM)
    mix, fock = pl.pallas_call(
        mix_kernel,
        out_shape=(
            jax.ShapeDtypeStruct((rows, rows), bf16),
            jax.ShapeDtypeStruct(fock_vir.shape, bf16),
        ),
        in_specs=[vmem, vmem],
        out_specs=(vmem, vmem),
        compiler_params=params(6),
        cost_estimate=cost(10**7, 2 * 10**6),
    )(fock_occ, fock_vir)

    flat_amps = amps.reshape(occupied, rows, virtuals)
    parts = (6, 2)

    def fock_part(n, after):
        first, count = sum(parts[:n]), parts[n]
        wide = 3 if count % 3 == 0 else 2
        return pl.pallas_call(
            functools.partial(fock_kernel, first),
            grid=(count // wide,),
            out_shape=(
                jax.ShapeDtypeStruct((2 * count, per_device, virtuals), f32),
                jax.ShapeDtypeStruct((count, per_device, LANES), bf16),
            ),
            in_specs=[
                smem,
                pl.BlockSpec((wide, rows, virtuals), lambda i: (i + first // wide, 0, 0)),
                whole(fock_vir.shape),
                whole(mix.shape),
                whole(u.shape),
                anywhere,
            ],
            out_specs=(
                pl.BlockSpec((2 * wide, per_device, virtuals), lambda i: (i, 0, 0)),
                pl.BlockSpec((wide, per_device, LANES), lambda i: (i, 0, 0)),
            ),
            scratch_shapes=[pltpu.VMEM((occupied, per_device, virtuals), f32)],
            compiler_params=params(16),
            cost_estimate=cost(3 * count * rows * virtuals * virtuals, 2 * 10**6),
        )(occ_irrep, flat_amps, fock, mix, u, after)

    z1, z2, z3 = [permute(block, m << 2, dests) for m in range(1, quarter)]
    block_y = permute(block, 2, dests)
    column = stack([z1, z2, z3], mix)
    column_y = permute(column, 2, dests)
    half0, cyc0 = fock_part(0, column)
    own_blocks = stack([block, column, block_y, column_y], half0)
    mate_blocks = permute(own_blocks, 1, dests)
    half1, cyc1 = fock_part(1, own_blocks)

    send_rows = tiles * per_device + 8
    groups = per_device // 8
    half, send = pl.pallas_call(
        functools.partial(half_kernel, groups, parts),
        out_shape=(
            jax.ShapeDtypeStruct((pairs, per_device, virtuals), f32),
            jax.ShapeDtypeStruct((dests, send_rows, LANES), bf16),
        ),
        in_specs=[smem, smem] + [vmem] * (4 + 2 * len(parts)),
        out_specs=(vmem, vmem),
        scratch_shapes=[
            pltpu.SMEM((occupied,), jnp.int32),
            pltpu.VMEM((occupied * occupied, LANES), f32),
            pltpu.VMEM((virtuals, occupied, LANES), f32),
            pltpu.VMEM((occupied, occupied, per_device, virtuals), f32),
            pltpu.VMEM((dests, send_rows, LANES), f32),
        ]
        + [pltpu.VMEM((tiles, 8 * pairs, LANES), f32)] * groups,
        compiler_params=params(28),
        cost_estimate=cost(6 * occupied * rows * virtuals * LANES, 15 * 10**6),
    )(
        pos, occ_irrep, own_blocks, mate_blocks, half0, half1, cyc0, cyc1, u, ladder_ints,
    )

    recv = lax.all_to_all(send, "vir", split_axis=0, concat_axis=0, tiled=True)

    return pl.pallas_call(
        join_kernel,
        out_shape=jax.ShapeDtypeStruct((occupied, occupied, per_device, virtuals), f32),
        in_specs=[smem, vmem, vmem, vmem],
        out_specs=anywhere,
        scratch_shapes=[
            pltpu.VMEM((virtuals, LANES), f32),
            pltpu.VMEM((tiles * LANES, virtuals), f32),
            pltpu.VMEM((occupied * occupied, per_device, virtuals), f32),
            pltpu.SemaphoreType.DMA((occupied * occupied,)),
        ],
        compiler_params=params(16),
        cost_estimate=cost(10**6, 5 * 10**6),
    )(occ_irrep, u, half, recv)


def solution(mesh):
    dests = mesh.shape["vir"]

    def run(amps, *rest):
        occupied, _, per_device, virtuals = amps.shape
        tiled = (
            dests == 16
            and per_device % 8 == 0
            and virtuals % LANES == 0
            and 2 * occupied * per_device == virtuals
            and rest[2].shape[2] == LANES
            and rest[3].shape[2] == LANES
        )
        return body(dests, amps, *rest) if tiled else plain_body(amps, *rest)

    return jax.shard_map(
        run,
        mesh=mesh,
        in_specs=(
            P("groups", None, "vir", None),
            P("groups", None),
            P("groups", None),
            P("vir", "groups", None),
            P("vir", "groups", None),
            P("groups"),
            P("groups"),
        ),
        out_specs=P("groups", None, "vir", None),
        check_vma=False,
    )
```
